32 devices in a mesh: seq: 8 (over z, y), tp: 4 (over x, core).
Axes of the slice: x: 2, y: 2, z: 4, core: 2. Of those that a mesh axis runs over, the one named last changes fastest.
Arguments:
- tokens: bfloat16 [4, 4096, 1024], P(None, 'seq'), may hold values from -6 to 6
- lengths: int32 [4], replicated, may hold values from 1024 to 4096, as said below
- gain_mix: float32 [1024], replicated, may hold values from 0.25 to 1.75
- w_in: bfloat16 [1024, 3, 1024], P(None, None, 'tp'), may hold values from -0.1875 to 0.1875
- conv_weight: float32 [3, 1024], P(None, 'tp'), may hold values from -3.5 to 3.5
- w_out: bfloat16 [1024, 1024], P('tp'), may hold values from -0.1875 to 0.1875
- gain_ffn: float32 [1024], replicated, may hold values from 0.25 to 1.75
- w_gate: bfloat16 [1024, 4608], P(None, 'tp'), may hold values from -0.1875 to 0.1875
- w_up: bfloat16 [1024, 4608], P(None, 'tp'), may hold values from -0.1875 to 0.1875
- w_down: bfloat16 [4608, 1024], P('tp'), may hold values from -0.125 to 0.125
- cotangent: bfloat16 [4, 4096, 1024], P(None, 'seq'), may hold values from -6 to 6
Outputs:
- block_out: bfloat16 [4, 4096, 1024], P(None, 'seq')
- grad_tokens: float32 [4, 4096, 1024], P(None, 'seq')
- grad_gain_mix: float32 [1024], replicated
- grad_w_in: float32 [1024, 3, 1024], P(None, None, 'tp')
- grad_conv: float32 [3, 1024], P(None, 'tp')
- grad_w_out: float32 [1024, 1024], P('tp')
- grad_gain_ffn: float32 [1024], replicated
- grad_w_gate: float32 [1024, 4608], P(None, 'tp')
- grad_w_up: float32 [1024, 4608], P(None, 'tp')
- grad_w_down: float32 [4608, 1024], P('tp')
The draws below stay inside these ranges and needn't reach their ends.
Inputs may be any that keep to these rules, and one draw needn't show every extreme that they name: Each slot holds one sequence in its first lengths[s] positions, the rest is padding; in every draw one slot is full, 4096 tokens.
All inputs are finite; a program needn't handle non-finite values.
Results may differ from the reference program's by a relative error of at most 0.0092.
Values sent between devices are 32-bit elements; how exact they have to be, the bound alone decides.
A program may use at most 192 MiB of HBM per device.

```python
import jax
import jax.numpy as jnp
from jax import lax

D = 1024
FF = 4608
KER = 3
SLOTS = 4
SLOT = 4096


def draw_lengths(key, part):
    key = jax.random.fold_in(key, 7)
    pick_key, length_key = jax.random.split(key)
    length_draw = jax.random.randint(length_key, (SLOTS,), SLOT // 4, SLOT + 1, dtype=jnp.int32)
    picked_slot = jax.random.randint(pick_key, (), 0, SLOTS, dtype=jnp.int32)
    return jnp.where(jnp.arange(SLOTS, dtype=jnp.int32) == picked_slot, SLOT, length_draw).astype(jnp.int32)


def level_of(own_key, shape, cuts, low, top_value):
    def one(axis_at, parts):
        steps = jax.random.uniform(jax.random.fold_in(jax.random.fold_in(own_key, 6), axis_at), (parts,), jnp.float32, low / len(cuts), top_value / len(cuts))
        return jnp.repeat(jnp.exp(steps), shape[axis_at] // parts).reshape((-1,) + (1,) * (len(shape) - axis_at - 1))

    loudness = one(*cuts[0])
    for cut in cuts[1:]:
        loudness = loudness * one(*cut)
    return loudness


def bell_draw(stream_key, shape, width, reach, pieces=(), held_as=jnp.bfloat16):
    loudness = level_of(stream_key, shape, pieces, -0.22, 0.18) if pieces else 1.0
    array = jax.random.normal(stream_key, shape, jnp.float32) * width * loudness
    return jnp.minimum(jnp.maximum(array, -reach), reach).astype(held_as)


def setup_inputs(seed: int = 0) -> dict:
    seeds = jax.random.split(jax.random.key(seed), 12)
    return {
        "tokens": bell_draw(seeds[0], (SLOTS, SLOT, D), 1.0, 6.0, ((1, 8),)),
        "lengths": draw_lengths(jax.random.fold_in(seeds[11], 71), 0),
        "gain_mix": jnp.clip(1.0 + 0.15 * jax.random.normal(seeds[2], (D,), jnp.float32), 0.25, 1.75),
        "w_in": bell_draw(seeds[3], (D, 3, D), D ** -0.5, 0.1875, ((2, 4),)),
        "conv_weight": bell_draw(seeds[4], (KER, D), KER ** -0.5, 3.5, ((1, 4),), jnp.float32),
        "w_out": bell_draw(seeds[5], (D, D), D ** -0.5, 0.1875, ((0, 4),)),
        "gain_ffn": jnp.clip(1.0 + 0.15 * jax.random.normal(seeds[6], (D,), jnp.float32), 0.25, 1.75),
        "w_gate": bell_draw(seeds[7], (D, FF), D ** -0.5, 0.1875, ((1, 4),)),
        "w_up": bell_draw(seeds[8], (D, FF), D ** -0.5, 0.1875, ((1, 4),)),
        "w_down": bell_draw(seeds[9], (FF, D), (FF // 2) ** -0.5, 0.125, ((0, 4),)),
        "cotangent": bell_draw(seeds[10], (SLOTS, SLOT, D), 1.0, 6.0, ((1, 8),)),
    }


NORM_EPS = 1e-05

@jax.custom_vjp
def low(v):
    return lax.optimization_barrier(v.astype(jnp.bfloat16)).astype(jnp.float32)

@jax.custom_vjp
def low_back(v):
    return v

def low_keep(v):
    return (low(v), None)

def low_pass(kept, grad):
    return (grad,)

def back_keep(v):
    return (v, None)

def back_low(kept, grad):
    return (low(grad),)
low.defvjp(low_keep, low_pass)
low_back.defvjp(back_keep, back_low)

def matmul_high(left, right):
    return jnp.dot(left, right, precision=lax.Precision.HIGHEST)

def rms_scale(values):
    return lax.rsqrt(lax.optimization_barrier(jnp.mean(values * values, axis=-1, keepdims=True)) + NORM_EPS)

def block_forward(slot_rows, gain_mix, w_in, conv_weight, w_out, gain_ffn, w_gate, w_up, w_down, valid_mask):
    normed_in = low(gain_mix * slot_rows * rms_scale(slot_rows))
    projected = low_back(matmul_high(normed_in, w_in.reshape(D, 3 * D)))
    in_gate = projected[:, :D]
    out_gate = projected[:, D:2 * D]
    conv_value = projected[:, 2 * D:]
    gated_seq = valid_mask * in_gate * conv_value
    padded_seq = jnp.concatenate([jnp.zeros((2, D), jnp.float32), gated_seq], axis=0)
    conv_sum = conv_weight[0] * padded_seq[0:SLOT] + conv_weight[1] * padded_seq[1:SLOT + 1] + conv_weight[2] * padded_seq[2:SLOT + 2]
    mixed_seq = low(out_gate * conv_sum)
    mixer_out = low_back(matmul_high(mixed_seq, w_out))
    hidden_res = slot_rows + mixer_out
    normed_mid = low(gain_ffn * hidden_res * rms_scale(hidden_res))
    gate_proj = low_back(matmul_high(normed_mid, w_gate))
    up_proj = low_back(matmul_high(normed_mid, w_up))
    activated = low(jax.nn.silu(gate_proj) * up_proj)
    ffn_out = low_back(matmul_high(activated, w_down))
    return valid_mask * (hidden_res + ffn_out)

def reference(tokens, lengths, gain_mix, w_in, conv_weight, w_out, gain_ffn, w_gate, w_up, w_down, cotangent):
    weights = tuple((value.astype(jnp.float32) for value in (gain_mix, w_in, conv_weight, w_out, gain_ffn, w_gate, w_up, w_down)))
    positions = jnp.arange(SLOT, dtype=jnp.int32)

    def one_slot(totals, inputs):
        slot_tokens, length, slot_cot = inputs
        valid_mask = (positions < length).astype(jnp.float32)[:, None]

        def forward_fn(slot_rows, *params):
            return block_forward(slot_rows, *params, valid_mask)
        slot_out, pull_back = jax.vjp(forward_fn, slot_tokens.astype(jnp.float32), *weights)
        slot_grads = pull_back(slot_cot.astype(jnp.float32))
        summed = tuple((total + grad for total, grad in zip(totals, slot_grads[1:])))
        return (summed, (slot_out.astype(jnp.bfloat16), slot_grads[0]))
    initial = tuple((jnp.zeros_like(value) for value in weights))
    totals, (block_out, grad_tokens) = lax.scan(one_slot, initial, (tokens, lengths, cotangent))
    return (block_out, grad_tokens, totals[0], totals[1], totals[2], totals[3], totals[4], totals[5], totals[6], totals[7])
```

```python
import functools

import jax
import jax.numpy as jnp
from jax import lax
from jax.experimental import pallas as pl
from jax.experimental.pallas import tpu as pltpu
from jax.sharding import PartitionSpec as P

NORM_EPS = 1e-05
LANES = 128
HALF = 128
SLOTS_IN_FLIGHT = 10


def rms_scale(values):
    return lax.rsqrt(jnp.mean(values * values, axis=-1, keepdims=True) + NORM_EPS)


def dot_rows(left, right):
    return lax.dot_general(
        left, right, (((0,), (0,)), ((), ())), preferred_element_type=jnp.float32
    )


def dot_cols(left, right):
    return lax.dot_general(
        left, right, (((1,), (1,)), ((), ())), preferred_element_type=jnp.float32
    )


def shift_seq(block, distance):
    count = lax.axis_size("seq")
    route = [(i - distance, i) for i in range(count) if 0 <= i - distance < count]
    return lax.ppermute(block, "seq", route)


def swap_tp(block, bit):
    return lax.ppermute(block, "tp", [(i, i ^ bit) for i in range(lax.axis_size("tp"))])


class SeqSum:
    def __init__(self, places, own, out, scratch):
        self.places, self.own, self.out = places, own, out
        self.y_in, self.p_left, self.p_right, self.p_acc = scratch[0:4]
        self.q_left, self.q_right, self.q_acc, self.q_in = scratch[4:8]
        self.sems = scratch[8]
        here = lax.axis_index("seq")
        self.place, self.side = here // 2, here % 2

    def greet(self):
        barrier = pltpu.get_barrier_semaphore()
        place, side = self.place, self.side

        def signal(index):
            pl.semaphore_signal(
                barrier, inc=1, device_id={"seq": index}, device_id_type=pl.DeviceIdType.MESH
            )

        signal(place * 2 + 1 - side)

        @pl.when(place > 0)
        def _():
            signal((place - 1) * 2 + side)

        @pl.when(place < self.places - 1)
        def _():
            signal((place + 1) * 2 + side)

        ends = jnp.where(place > 0, 1, 0) + jnp.where(place < self.places - 1, 1, 0)
        pl.semaphore_wait(barrier, 1 + ends)

    def remote(self, src, dst, slot, send, recv, place, side):
        return pltpu.make_async_remote_copy(
            src_ref=src,
            dst_ref=dst,
            send_sem=self.sems.at[send, slot],
            recv_sem=self.sems.at[recv, slot],
            device_id={"seq": place * 2 + side},
            device_id_type=pl.DeviceIdType.MESH,
        )

    def chain(self, root):
        last = self.places - 1
        left = jnp.maximum(self.place - 1, 0)
        right = jnp.minimum(self.place + 1, last)
        from_left = (self.place <= root) & (self.place > 0)
        from_right = (self.place >= root) & (self.place < last)
        return left, right, from_left, from_right

    def p_stage(self, which, k):
        place, side = self.place, self.side
        own, out = self.own, self.out
        slot = lax.rem(k, SLOTS_IN_FLIGHT)
        base = pl.multiple_of(k * 4 * HALF, 4 * HALF)
        mine = pl.ds(pl.multiple_of(base + side * HALF, HALF), HALF)
        theirs = pl.ds(pl.multiple_of(base + (1 - side) * HALF, HALF), HALF)
        root = self.places // 2 - 1 + lax.rem(k, 2)
        left, right, from_left, from_right = self.chain(root)
        acc, y_in = self.p_acc.at[slot], self.y_in.at[slot]
        from_l, from_r = self.p_left.at[slot], self.p_right.at[slot]
        remote = functools.partial(functools.partial, self.remote)

        to_side = remote(own.at[theirs], y_in, slot, 0, 1, place, 1 - side)
        up_right = remote(acc, from_l, slot, 2, 3, right, side)
        up_left = remote(acc, from_r, slot, 2, 4, left, side)

        def down(src):
            return (
                remote(src, out.at[mine], slot, 5, 7, left, side),
                remote(src, out.at[mine], slot, 6, 7, right, side),
                remote(src, out.at[mine], slot, 8, 9, place, 1 - side),
            )

        def keep():
            return pltpu.make_async_copy(acc, out.at[mine], self.sems.at[10, slot])

        def hand_down(src):
            down_left, down_right, down_side = down(src)
            down_side().start()
            pl.when(from_left)(lambda: down_left().start())
            pl.when(from_right)(lambda: down_right().start())

        if which == "split":
            to_side().start()

        if which == "up":
            to_side().wait_recv()
            acc[...] = own[mine, :] + y_in[...]

            @pl.when(place < root)
            def _():
                @pl.when(from_left)
                def _():
                    up_right().wait_recv()
                    acc[...] += from_l[...]

                up_right().start()

            @pl.when(place > root)
            def _():
                @pl.when(from_right)
                def _():
                    up_left().wait_recv()
                    acc[...] += from_r[...]

                up_left().start()

        if which == "root":

            @pl.when(place == root)
            def _():
                @pl.when(from_left)
                def _():
                    up_right().wait_recv()
                    acc[...] += from_l[...]

                @pl.when(from_right)
                def _():
                    up_left().wait_recv()
                    acc[...] += from_r[...]

                hand_down(acc)
                keep().start()

        if which == "down":

            @pl.when(place != root)
            def _():
                down(acc)[0]().wait_recv()
                hand_down(out.at[mine])

        if which == "end":
            down_left, down_right, down_side = down(acc)
            down_side().wait()
            to_side().wait_send()
            pl.when(from_left)(lambda: down_left().wait_send())
            pl.when(from_right)(lambda: down_right().wait_send())
            pl.when(place == root)(lambda: keep().wait())
            pl.when(place != root)(lambda: up_left().wait_send())

    def q_stage(self, which, k):
        place, side = self.place, self.side
        own, out = self.own, self.out
        slot = lax.rem(k, SLOTS_IN_FLIGHT)
        base = pl.multiple_of(k * 4 * HALF, 4 * HALF)
        wide = pl.ds(pl.multiple_of(base + 2 * HALF, 2 * HALF), 2 * HALF)
        root = self.places // 2 - lax.rem(k, 2)
        left, right, from_left, from_right = self.chain(root)
        acc, side_in = self.q_acc.at[slot], self.q_in.at[slot]
        from_l, from_r = self.q_left.at[slot], self.q_right.at[slot]
        remote = functools.partial(functools.partial, self.remote)

        up_right = remote(acc, from_l, slot, 11, 12, right, side)
        up_left = remote(acc, from_r, slot, 11, 13, left, side)
        to_side = remote(acc, side_in, slot, 14, 15, place, 1 - side)

        def down(src):
            return (
                remote(src, out.at[wide], slot, 16, 18, left, side),
                remote(src, out.at[wide], slot, 17, 18, right, side),
            )

        def keep():
            return pltpu.make_async_copy(side_in, out.at[wide], self.sems.at[19, slot])

        def hand_down(src):
            down_left, down_right = down(src)
            pl.when(from_left)(lambda: down_left().start())
            pl.when(from_right)(lambda: down_right().start())

        if which == "up":
            acc[...] = own[wide, :]

            @pl.when(place < root)
            def _():
                @pl.when(from_left)
                def _():
                    up_right().wait_recv()
                    acc[...] += from_l[...]

                up_right().start()

            @pl.when(place > root)
            def _():
                @pl.when(from_right)
                def _():
                    up_left().wait_recv()
                    acc[...] += from_r[...]

                up_left().start()

        if which == "root":

            @pl.when(place == root)
            def _():
                @pl.when(from_left)
                def _():
                    up_right().wait_recv()
                    acc[...] += from_l[...]

                @pl.when(from_right)
                def _():
                    up_left().wait_recv()
                    acc[...] += from_r[...]

                to_side().start()

        if which == "side":

            @pl.when(place == root)
            def _():
                to_side().wait_recv()
                side_in[...] += acc[...]
                hand_down(side_in)
                keep().start()

        if which == "down":

            @pl.when(place != root)
            def _():
                down(acc)[0]().wait_recv()
                hand_down(out.at[wide])

        if which == "end":
            down_left, down_right = down(acc)
            pl.when(from_left)(lambda: down_left().wait_send())
            pl.when(from_right)(lambda: down_right().wait_send())

            @pl.when(place == root)
            def _():
                to_side().wait_send()
                keep().wait()

            pl.when(place != root)(lambda: up_left().wait_send())

    P_LAGS = (("split", 0, 0), ("up", 2, 1), ("root", 3, 3), ("down", 6, 7), ("end", 9, 9))
    Q_LAGS = (("up", 1, 0), ("root", 2, 2), ("side", 4, 4), ("down", 6, 7), ("end", 9, 9))

    def tick(self, t, count):
        middle = (self.place == self.places // 2) | (self.place == self.places // 2 - 1)
        for stage, lags in ((self.p_stage, self.P_LAGS), (self.q_stage, self.Q_LAGS)):
            for which, mid_lag, outer_lag in lags:
                k = t - jnp.where(middle, mid_lag, outer_lag)

                @pl.when((k >= 0) & (k < count))
                def _(stage=stage, which=which, k=k):
                    stage(which, k)

    def run(self, count):
        @pl.loop(0, count + self.P_LAGS[-1][1])
        def _(t):
            self.tick(t, count)


def seq_sum_scratch():
    half = pltpu.VMEM((SLOTS_IN_FLIGHT, HALF, LANES), jnp.float32)
    wide = pltpu.VMEM((SLOTS_IN_FLIGHT, 2 * HALF, LANES), jnp.float32)
    return [half] * 4 + [wide] * 4 + [pltpu.SemaphoreType.DMA((20, SLOTS_IN_FLIGHT))]


def seq_sum_kernel(places, own, out, *scratch):
    summer = SeqSum(places, own, out, scratch)
    summer.greet()
    summer.run(own.shape[0] // (4 * HALF))


def seq_sum(block, collective_id, name):
    rows = block.shape[0]
    return pl.pallas_call(
        functools.partial(seq_sum_kernel, lax.axis_size("seq") // 2),
        out_shape=jax.ShapeDtypeStruct(block.shape, jnp.float32),
        in_specs=[pl.BlockSpec(memory_space=pltpu.VMEM)],
        out_specs=pl.BlockSpec(memory_space=pl.ANY),
        scratch_shapes=seq_sum_scratch(),
        compiler_params=pltpu.CompilerParams(
            collective_id=collective_id, has_side_effects=True, vmem_limit_bytes=40 << 20
        ),
        cost_estimate=pl.CostEstimate(
            flops=rows * 256, bytes_accessed=rows * 512 * 32, transcendentals=0
        ),
        name=name,
    )(block)


def to_panels(matrix):
    rows, cols = matrix.shape
    return matrix.reshape(rows, cols // LANES, LANES).transpose(1, 0, 2).reshape(-1, LANES)


def from_panels(panels, rows, cols):
    return panels.reshape(cols // LANES, rows, LANES).transpose(1, 0, 2).reshape(rows, cols)


def per_device(
    tokens, lengths, gain_mix, w_in, conv_weight, w_out, gain_ffn, w_gate, w_up, w_down, cotangent
):
    slot_count, local_len, width = tokens.shape
    chans = w_in.shape[2]
    group = lax.axis_size("tp")
    seq_count = lax.axis_size("seq")
    tp_at, seq_at = lax.axis_index("tp"), lax.axis_index("seq")
    core, chip = tp_at % 2, tp_at // 2
    half_slots = slot_count // 2
    half_rows = half_slots * local_len
    row_count = slot_count * local_len

    def pick(is_first, first, second):
        return jnp.where(is_first, first, second)

    def both_cores(own, other):
        return jnp.concatenate(
            [pick(core == 0, own, other), pick(core == 0, other, own)], axis=0
        )

    flat = jnp.concatenate([w_in.reshape(3 * width, chans), w_out.reshape(width, chans)], axis=0)
    taps8 = jnp.pad(conv_weight, ((0, 5), (0, 0)))
    share_rows = flat.shape[0] // seq_count
    share = lax.dynamic_slice(flat, (seq_at * share_rows, 0), (share_rows, chans))
    sent = jnp.concatenate([share.astype(jnp.float32), taps8], axis=0)
    sent = swap_tp(sent, 2)
    across = lax.all_gather(sent[:share_rows], "seq", axis=0, tiled=True)
    own_flat = jnp.concatenate([flat.astype(jnp.float32), taps8], axis=0)
    across_flat = jnp.concatenate([across, sent[share_rows:]], axis=0)
    sib_own = swap_tp(own_flat, 1)
    sib_across = swap_tp(across_flat, 1)
    pair_own = [pick(core == 0, own_flat, sib_own), pick(core == 0, sib_own, own_flat)]
    pair_across = [
        pick(core == 0, across_flat, sib_across),
        pick(core == 0, sib_across, across_flat),
    ]
    quad = [pick(chip == 0, a, b) for a, b in zip(pair_own, pair_across)] + [
        pick(chip == 0, b, a) for a, b in zip(pair_own, pair_across)
    ]
    quad = lax.optimization_barrier(quad)
    taps = jnp.stack([q[4 * width : 4 * width + 3] for q in quad])
    w_in_all = jnp.stack(
        [q[: 3 * width].reshape(width, 3 * chans).astype(jnp.bfloat16) for q in quad]
    )
    w_out_all = jnp.stack(
        [q[3 * width : 4 * width].reshape(chans, width).astype(jnp.bfloat16) for q in quad]
    )

    first_pos = seq_at * local_len
    positions = first_pos + jnp.arange(local_len, dtype=jnp.int32)
    valid = (positions[None, :] < lengths[:, None]).astype(jnp.float32)[:, :, None]
    valid_all = valid.reshape(row_count, 1)
    valid_own = lax.dynamic_slice(valid, (core * half_slots, 0, 0), (half_slots, local_len, 1))
    valid_rows = valid_own.reshape(half_rows, 1)
    tokens_own = lax.dynamic_slice(
        tokens, (core * half_slots, 0, 0), (half_slots, local_len, width)
    )
    inputs_f = tokens_own.astype(jnp.float32).reshape(half_rows, width)
    scale_mix = rms_scale(inputs_f)
    unit_mix = inputs_f * scale_mix
    normed_in = (gain_mix * unit_mix).astype(jnp.bfloat16)
    projected = jnp.stack(
        [
            jnp.dot(normed_in, w_in_all[j], preferred_element_type=jnp.float32)
            for j in range(group)
        ]
    )
    in_gate = projected[:, :, :chans]
    out_gate = projected[:, :, chans : 2 * chans]
    conv_value = projected[:, :, 2 * chans :]
    seq_shape = (group, half_slots, local_len, chans)
    gated_seq = (valid_rows * in_gate * conv_value).reshape(seq_shape)
    carried = shift_seq(gated_seq[:, :, local_len - 2 :], 1)
    padded_seq = jnp.concatenate([carried, gated_seq], axis=2)

    def tap(j):
        return taps[:, j][:, None, None, :]

    conv_sum = (
        tap(0) * padded_seq[:, :, 0:local_len]
        + tap(1) * padded_seq[:, :, 1 : local_len + 1]
        + tap(2) * padded_seq[:, :, 2 : local_len + 2]
    ).reshape(group, half_rows, chans)
    mixed_seq = (out_gate * conv_sum).astype(jnp.bfloat16)
    mixer_out = sum(
        jnp.dot(mixed_seq[j], w_out_all[j], preferred_element_type=jnp.float32)
        for j in range(group)
    )
    hidden_res = inputs_f + mixer_out
    scale_ffn = rms_scale(hidden_res)
    unit_ffn = hidden_res * scale_ffn
    unit_all = both_cores(unit_ffn, swap_tp(unit_ffn, 1))
    normed_mid = (gain_ffn * unit_all).astype(jnp.bfloat16)

    gate_proj = jnp.dot(normed_mid, w_gate, preferred_element_type=jnp.float32)
    up_proj = jnp.dot(normed_mid, w_up, preferred_element_type=jnp.float32)
    sigmoid_gate = jax.nn.sigmoid(gate_proj)
    silu_gate = gate_proj * sigmoid_gate
    activated = (silu_gate * up_proj).astype(jnp.bfloat16)
    ffn_part = jnp.dot(activated, w_down, preferred_element_type=jnp.float32)
    grad_out = valid_all * cotangent.astype(jnp.float32).reshape(row_count, width)
    grad_ffn = grad_out.astype(jnp.bfloat16)
    grad_act = dot_cols(grad_ffn, w_down)
    grad_w_down = dot_rows(activated, grad_ffn)
    silu_slope = sigmoid_gate * (1.0 + gate_proj * (1.0 - sigmoid_gate))
    grad_gate = (grad_act * up_proj * silu_slope).astype(jnp.bfloat16)
    grad_up = (grad_act * silu_gate).astype(jnp.bfloat16)
    grad_w_gate = dot_rows(normed_mid, grad_gate)
    grad_w_up = dot_rows(normed_mid, grad_up)
    mid_part = dot_cols(grad_gate, w_gate) + dot_cols(grad_up, w_up)

    def own_rows(block):
        return lax.dynamic_slice(block, (core * half_rows, 0), (half_rows, width))

    def other_rows(block):
        return lax.dynamic_slice(block, ((1 - core) * half_rows, 0), (half_rows, width))

    mid_chip = own_rows(mid_part) + swap_tp(other_rows(mid_part), 1)
    grad_mid = mid_chip + swap_tp(mid_chip, 2)
    ffn_chip = own_rows(ffn_part) + swap_tp(other_rows(ffn_part), 1)
    ffn_out = ffn_chip + swap_tp(ffn_chip, 2)
    ffn_panels = jnp.concatenate(
        [to_panels(grad_w_gate), to_panels(grad_w_up), to_panels(grad_w_down)], axis=0
    )
    ffn_sums = seq_sum(ffn_panels, 1, "sum_ffn_grads")

    block_own = hidden_res + ffn_out
    block_out = both_cores(block_own, swap_tp(block_own, 1))
    block_out = (valid_all * block_out).astype(jnp.bfloat16).reshape(slot_count, local_len, width)

    grad_gain_ffn = jnp.sum(grad_mid * unit_ffn, axis=0)
    scaled_mid = gain_ffn * grad_mid
    grad_hidden = own_rows(grad_out) + scale_ffn * (
        scaled_mid - unit_ffn * jnp.mean(scaled_mid * unit_ffn, axis=-1, keepdims=True)
    )

    grad_mixer = grad_hidden.astype(jnp.bfloat16)
    grad_mixed = jnp.stack([dot_cols(grad_mixer, w_out_all[j]) for j in range(group)])
    grad_out_gate = grad_mixed * conv_sum
    grad_conv_in = (grad_mixed * out_gate).reshape(seq_shape)
    next_grad = shift_seq(grad_conv_in[:, :, :2], -1)
    extended = jnp.concatenate([grad_conv_in, next_grad], axis=2)
    grad_gated = (
        tap(2) * extended[:, :, 0:local_len]
        + tap(1) * extended[:, :, 1 : local_len + 1]
        + tap(0) * extended[:, :, 2 : local_len + 2]
    ).reshape(group, half_rows, chans)
    grad_conv = jnp.stack(
        [
            jnp.sum(grad_conv_in * padded_seq[:, :, j : j + local_len], axis=(1, 2))
            for j in range(3)
        ],
        axis=1,
    )
    grad_in_gate = grad_gated * valid_rows * conv_value
    grad_value = grad_gated * valid_rows * in_gate
    grad_proj = jnp.concatenate([grad_in_gate, grad_out_gate, grad_value], axis=2).astype(
        jnp.bfloat16
    )
    grad_in = sum(dot_cols(grad_proj[j], w_in_all[j]) for j in range(group))
    grad_gain_mix = jnp.sum(grad_in * unit_mix, axis=0)
    scaled_in = gain_mix * grad_in
    tokens_grad = grad_hidden + scale_mix * (
        scaled_in - unit_mix * jnp.mean(scaled_in * unit_mix, axis=-1, keepdims=True)
    )
    grad_tokens = both_cores(tokens_grad, swap_tp(tokens_grad, 1))
    grad_tokens = grad_tokens.reshape(slot_count, local_len, width)

    def shard_of(stacked, which):
        at = chip * 2 + which
        return lax.dynamic_slice(
            stacked, (at,) + (0,) * (stacked.ndim - 1), (1,) + stacked.shape[1:]
        )[0]

    def mixer_panels(which):
        in_part = dot_rows(normed_in, shard_of(grad_proj, which))
        out_part = dot_rows(shard_of(mixed_seq, which), grad_mixer)
        small = jnp.concatenate(
            [grad_gain_mix, grad_gain_ffn, shard_of(grad_conv, which).reshape(-1)]
        ).reshape(-1, LANES)
        pad = -small.shape[0] % (4 * HALF)
        return jnp.concatenate(
            [to_panels(in_part), to_panels(out_part), jnp.pad(small, ((0, pad), (0, 0)))], axis=0
        )

    mixer_chip = mixer_panels(core) + swap_tp(mixer_panels(1 - core), 1)
    mixer_sums = seq_sum(mixer_chip, 2, "sum_mixer_grads")

    hidden = w_gate.shape[1]
    panel = hidden * width // LANES
    total_w_gate = from_panels(ffn_sums[:panel], width, hidden)
    total_w_up = from_panels(ffn_sums[panel : 2 * panel], width, hidden)
    total_w_down = from_panels(ffn_sums[2 * panel :], hidden, width)
    in_rows = width * 3 * chans // LANES
    out_rows = width * chans // LANES
    total_w_in = from_panels(mixer_sums[:in_rows], width, 3 * chans).reshape(width, 3, chans)
    total_w_out = from_panels(mixer_sums[in_rows : in_rows + out_rows], chans, width)
    small = mixer_sums[in_rows + out_rows :].reshape(-1)
    total_gain_mix = small[:width]
    total_gain_ffn = small[width : 2 * width]
    total_conv = small[2 * width : 2 * width + 3 * chans].reshape(3, chans)
    return (
        block_out,
        grad_tokens,
        total_gain_mix,
        total_w_in,
        total_conv,
        total_w_out,
        total_gain_ffn,
        total_w_gate,
        total_w_up,
        total_w_down,
    )


def solution(mesh):
    rows, cols = P("tp", None), P(None, "tp")
    tokens, whole, stacked = P(None, "seq", None), P(), P(None, None, "tp")
    return jax.shard_map(
        per_device,
        mesh=mesh,
        in_specs=(
            tokens, whole, whole, stacked, cols, rows, whole, cols, cols, rows, tokens,
        ),
        out_specs=(
            tokens, tokens, whole, stacked, cols, rows, whole, cols, cols, rows,
        ),
        check_vma=False,
    )
```

```python
import functools

import jax
import jax.numpy as jnp
from jax import lax
from jax.experimental import pallas as pl
from jax.experimental.pallas import tpu as pltpu
from jax.sharding import PartitionSpec as P

NORM_EPS = 1e-05
LANES = 128
VMEM_LIMIT = 64 << 20
HALF = 128
SLOTS_IN_FLIGHT = 10


def rms_scale(values):
    return lax.rsqrt(jnp.mean(values * values, axis=-1, keepdims=True) + NORM_EPS)


def dot_rows(left, right):
    return lax.dot_general(
        left, right, (((0,), (0,)), ((), ())), preferred_element_type=jnp.float32
    )


def dot_cols(left, right):
    return lax.dot_general(
        left, right, (((1,), (1,)), ((), ())), preferred_element_type=jnp.float32
    )


def shift_seq(block, distance):
    count = lax.axis_size("seq")
    route = [(i - distance, i) for i in range(count) if 0 <= i - distance < count]
    return lax.ppermute(block, "seq", route)


def swap_tp(block, bit):
    return lax.ppermute(block, "tp", [(i, i ^ bit) for i in range(lax.axis_size("tp"))])


class SeqSum:
    def __init__(self, places, own, out, scratch):
        self.places, self.own, self.out = places, own, out
        self.y_in, self.p_left, self.p_right, self.p_acc = scratch[0:4]
        self.q_left, self.q_right, self.q_acc, self.q_in = scratch[4:8]
        self.sems = scratch[8]
        here = lax.axis_index("seq")
        self.place, self.side = here // 2, here % 2

    def greet(self, others=()):
        barrier = pltpu.get_barrier_semaphore()
        place, side = self.place, self.side

        def signal(index):
            pl.semaphore_signal(
                barrier, inc=1, device_id={"seq": index}, device_id_type=pl.DeviceIdType.MESH
            )

        signal(place * 2 + 1 - side)
        for other in others:
            pl.semaphore_signal(
                barrier, inc=1, device_id=other, device_id_type=pl.DeviceIdType.MESH
            )

        @pl.when(place > 0)
        def _():
            signal((place - 1) * 2 + side)

        @pl.when(place < self.places - 1)
        def _():
            signal((place + 1) * 2 + side)

        ends = jnp.where(place > 0, 1, 0) + jnp.where(place < self.places - 1, 1, 0)
        pl.semaphore_wait(barrier, 1 + len(others) + ends)

    def remote(self, src, dst, slot, send, recv, place, side):
        return pltpu.make_async_remote_copy(
            src_ref=src,
            dst_ref=dst,
            send_sem=self.sems.at[send, slot],
            recv_sem=self.sems.at[recv, slot],
            device_id={"seq": place * 2 + side},
            device_id_type=pl.DeviceIdType.MESH,
        )

    def chain(self, root):
        last = self.places - 1
        left = jnp.maximum(self.place - 1, 0)
        right = jnp.minimum(self.place + 1, last)
        from_left = (self.place <= root) & (self.place > 0)
        from_right = (self.place >= root) & (self.place < last)
        return left, right, from_left, from_right

    def p_stage(self, which, k):
        place, side = self.place, self.side
        own, out = self.own, self.out
        slot = lax.rem(k, SLOTS_IN_FLIGHT)
        base = pl.multiple_of(k * 4 * HALF, 4 * HALF)
        mine = pl.ds(pl.multiple_of(base + side * HALF, HALF), HALF)
        theirs = pl.ds(pl.multiple_of(base + (1 - side) * HALF, HALF), HALF)
        root = self.places // 2 - 1 + lax.rem(k, 2)
        left, right, from_left, from_right = self.chain(root)
        acc, y_in = self.p_acc.at[slot], self.y_in.at[slot]
        from_l, from_r = self.p_left.at[slot], self.p_right.at[slot]
        remote = functools.partial(functools.partial, self.remote)

        to_side = remote(own.at[theirs], y_in, slot, 0, 1, place, 1 - side)
        up_right = remote(acc, from_l, slot, 2, 3, right, side)
        up_left = remote(acc, from_r, slot, 2, 4, left, side)

        def down(src):
            return (
                remote(src, out.at[mine], slot, 5, 7, left, side),
                remote(src, out.at[mine], slot, 6, 7, right, side),
                remote(src, out.at[mine], slot, 8, 9, place, 1 - side),
            )

        def keep():
            return pltpu.make_async_copy(acc, out.at[mine], self.sems.at[10, slot])

        def hand_down(src):
            down_left, down_right, down_side = down(src)
            down_side().start()
            pl.when(from_left)(lambda: down_left().start())
            pl.when(from_right)(lambda: down_right().start())

        if which == "split":
            to_side().start()

        if which == "up":
            to_side().wait_recv()
            acc[...] = own[mine, :] + y_in[...]

            @pl.when(place < root)
            def _():
                @pl.when(from_left)
                def _():
                    up_right().wait_recv()
                    acc[...] += from_l[...]

                up_right().start()

            @pl.when(place > root)
            def _():
                @pl.when(from_right)
                def _():
                    up_left().wait_recv()
                    acc[...] += from_r[...]

                up_left().start()

        if which == "root":

            @pl.when(place == root)
            def _():
                @pl.when(from_left)
                def _():
                    up_right().wait_recv()
                    acc[...] += from_l[...]

                @pl.when(from_right)
                def _():
                    up_left().wait_recv()
                    acc[...] += from_r[...]

                hand_down(acc)
                keep().start()

        if which == "down":

            @pl.when(place != root)
            def _():
                down(acc)[0]().wait_recv()
                hand_down(out.at[mine])

        if which == "end":
            down_left, down_right, down_side = down(acc)
            down_side().wait()
            to_side().wait_send()
            pl.when(from_left)(lambda: down_left().wait_send())
            pl.when(from_right)(lambda: down_right().wait_send())
            pl.when(place == root)(lambda: keep().wait())
            pl.when(place != root)(lambda: up_left().wait_send())

    def q_stage(self, which, k):
        place, side = self.place, self.side
        own, out = self.own, self.out
        slot = lax.rem(k, SLOTS_IN_FLIGHT)
        base = pl.multiple_of(k * 4 * HALF, 4 * HALF)
        wide = pl.ds(pl.multiple_of(base + 2 * HALF, 2 * HALF), 2 * HALF)
        root = self.places // 2 - lax.rem(k, 2)
        left, right, from_left, from_right = self.chain(root)
        acc, side_in = self.q_acc.at[slot], self.q_in.at[slot]
        from_l, from_r = self.q_left.at[slot], self.q_right.at[slot]
        remote = functools.partial(functools.partial, self.remote)

        up_right = remote(acc, from_l, slot, 11, 12, right, side)
        up_left = remote(acc, from_r, slot, 11, 13, left, side)
        to_side = remote(acc, side_in, slot, 14, 15, place, 1 - side)

        def down(src):
            return (
                remote(src, out.at[wide], slot, 16, 18, left, side),
                remote(src, out.at[wide], slot, 17, 18, right, side),
            )

        def keep():
            return pltpu.make_async_copy(side_in, out.at[wide], self.sems.at[19, slot])

        def hand_down(src):
            down_left, down_right = down(src)
            pl.when(from_left)(lambda: down_left().start())
            pl.when(from_right)(lambda: down_right().start())

        if which == "up":
            acc[...] = own[wide, :]

            @pl.when(place < root)
            def _():
                @pl.when(from_left)
                def _():
                    up_right().wait_recv()
                    acc[...] += from_l[...]

                up_right().start()

            @pl.when(place > root)
            def _():
                @pl.when(from_right)
                def _():
                    up_left().wait_recv()
                    acc[...] += from_r[...]

                up_left().start()

        if which == "root":

            @pl.when(place == root)
            def _():
                @pl.when(from_left)
                def _():
                    up_right().wait_recv()
                    acc[...] += from_l[...]

                @pl.when(from_right)
                def _():
                    up_left().wait_recv()
                    acc[...] += from_r[...]

                to_side().start()

        if which == "side":

            @pl.when(place == root)
            def _():
                to_side().wait_recv()
                side_in[...] += acc[...]
                hand_down(side_in)
                keep().start()

        if which == "down":

            @pl.when(place != root)
            def _():
                down(acc)[0]().wait_recv()
                hand_down(out.at[wide])

        if which == "end":
            down_left, down_right = down(acc)
            pl.when(from_left)(lambda: down_left().wait_send())
            pl.when(from_right)(lambda: down_right().wait_send())

            @pl.when(place == root)
            def _():
                to_side().wait_send()
                keep().wait()

            pl.when(place != root)(lambda: up_left().wait_send())

    P_LAGS = (("split", 0, 0), ("up", 2, 1), ("root", 3, 3), ("down", 6, 7), ("end", 9, 9))
    Q_LAGS = (("up", 1, 0), ("root", 2, 2), ("side", 4, 4), ("down", 6, 7), ("end", 9, 9))

    def tick(self, t, count):
        middle = (self.place == self.places // 2) | (self.place == self.places // 2 - 1)
        for stage, lags in ((self.p_stage, self.P_LAGS), (self.q_stage, self.Q_LAGS)):
            for which, mid_lag, outer_lag in lags:
                k = t - jnp.where(middle, mid_lag, outer_lag)

                @pl.when((k >= 0) & (k < count))
                def _(stage=stage, which=which, k=k):
                    stage(which, k)

    def run(self, count):
        @pl.loop(0, count + self.P_LAGS[-1][1])
        def _(t):
            self.tick(t, count)


def seq_sum_scratch():
    half = pltpu.VMEM((SLOTS_IN_FLIGHT, HALF, LANES), jnp.float32)
    wide = pltpu.VMEM((SLOTS_IN_FLIGHT, 2 * HALF, LANES), jnp.float32)
    return [half] * 4 + [wide] * 4 + [pltpu.SemaphoreType.DMA((20, SLOTS_IN_FLIGHT))]


def seq_sum_kernel(places, own, out, *scratch):
    summer = SeqSum(places, own, out, scratch)
    summer.greet()
    summer.run(own.shape[0] // (4 * HALF))


def seq_sum(block, collective_id, name):
    rows = block.shape[0]
    return pl.pallas_call(
        functools.partial(seq_sum_kernel, lax.axis_size("seq") // 2),
        out_shape=jax.ShapeDtypeStruct(block.shape, jnp.float32),
        in_specs=[pl.BlockSpec(memory_space=pltpu.VMEM)],
        out_specs=pl.BlockSpec(memory_space=pl.ANY),
        scratch_shapes=seq_sum_scratch(),
        compiler_params=pltpu.CompilerParams(
            collective_id=collective_id, has_side_effects=True, vmem_limit_bytes=40 << 20
        ),
        cost_estimate=pl.CostEstimate(
            flops=rows * 256, bytes_accessed=rows * 512 * 32, transcendentals=0
        ),
        name=name,
    )(block)


FFN_PARTS = 3
ROW_BLOCK = 512
OUT_BLOCK = 256


def ffn_kernel(places, *refs):
    (mid_hbm, mid_t_hbm, cot_hbm, cot_t_hbm, w_gu_hbm, w_d_hbm) = refs[0:6]
    (sums, mid_chip, mid_far, ffn_chip, ffn_far, mid_land, ffn_land) = refs[6:13]
    (mid, mid_t, cot, cot_t, w_gu, w_d, act, ggu, own, staged, fetched) = refs[13:24]
    load_sems, near_sems, far_sems, keep_sem, fetch_sem = refs[24:29]
    summer = SeqSum(places, own, sums, refs[29:])
    tp_at = lax.axis_index("tp")
    core = lax.rem(tp_at, 2)
    sibling = tp_at + 1 - 2 * core
    across = lax.rem(tp_at + 2, 4)
    rows, width = mid.shape
    parts, _, wide = w_gu.shape
    hidden = wide // 2
    panels = 3 * hidden // LANES

    loads = [
        pltpu.make_async_copy(src, dst, load_sems.at[i])
        for i, (src, dst) in enumerate(
            (
                (mid_hbm, mid),
                (w_gu_hbm, w_gu),
                (cot_hbm, cot),
                (w_d_hbm, w_d),
                (mid_t_hbm, mid_t),
                (cot_t_hbm, cot_t),
            )
        )
    ]
    for load in loads:
        load.start()
    summer.greet(({"tp": sibling}, {"tp": across}))
    count = own.shape[0] // (4 * HALF)
    for load in loads[:4]:
        load.wait()

    def part_cols(c):
        return pl.ds(pl.multiple_of(c * hidden, LANES), hidden)

    @pl.loop(0, parts)
    def _(c):
        @pl.loop(0, rows // ROW_BLOCK)
        def _(r):
            at = pl.ds(pl.multiple_of(r * ROW_BLOCK, ROW_BLOCK), ROW_BLOCK)
            both = jnp.dot(mid[at, :], w_gu[c], preferred_element_type=jnp.float32)
            gate, up = both[:, :hidden], both[:, hidden:]
            grad_act = dot_cols(cot[at, :], w_d[c])
            sigmoid = 1.0 / (1.0 + jnp.exp(-gate))
            silu = gate * sigmoid
            act[at, part_cols(c)] = (silu * up).astype(jnp.bfloat16)
            slope = sigmoid * (1.0 + gate * (1.0 - sigmoid))
            ggu[c, at, :hidden] = (grad_act * up * slope).astype(jnp.bfloat16)
            ggu[c, at, hidden:] = (grad_act * silu).astype(jnp.bfloat16)

        @pl.when(c == 0)
        def _():
            for load in loads[4:]:
                load.wait()

        @pl.loop(0, width // OUT_BLOCK)
        def _(m):
            first = pl.multiple_of(m * OUT_BLOCK, OUT_BLOCK)
            at = pl.ds(first, OUT_BLOCK)
            base = c * (panels * width) + first

            def put(block, panel):
                for j in range(block.shape[1] // LANES):
                    to = pl.multiple_of(base + (panel + j) * width, OUT_BLOCK)
                    own[pl.ds(to, OUT_BLOCK), :] = block[:, j * LANES : (j + 1) * LANES]

            put(jnp.dot(mid_t[at, :], ggu[c], preferred_element_type=jnp.float32), 0)
            put(
                jnp.dot(cot_t[at, :], act[:, part_cols(c)], preferred_element_type=jnp.float32),
                wide // LANES,
            )

            @pl.when(c > 0)
            def _():
                summer.tick((c - 1) * (width // OUT_BLOCK) + m, count)

    early = (parts - 1) * (width // OUT_BLOCK)
    blocks = rows // 2 // OUT_BLOCK

    def row_block(half, k):
        return pl.ds(pl.multiple_of((half * blocks + k) * OUT_BLOCK, OUT_BLOCK), OUT_BLOCK)

    def mid_part(at):
        return sum(dot_cols(ggu[c, at, :], w_gu[c]) for c in range(parts))

    def ffn_part(at):
        return sum(
            jnp.dot(
                act[at, c * hidden : (c + 1) * hidden],
                w_d[c],
                preferred_element_type=jnp.float32,
            )
            for c in range(parts)
        )

    def near(which, land, k):
        return pltpu.make_async_remote_copy(
            src_ref=staged.at[lax.rem(k, 2)],
            dst_ref=land.at[row_block(0, k)],
            send_sem=near_sems.at[which, 0, k],
            recv_sem=near_sems.at[which, 1, k],
            device_id={"tp": sibling},
            device_id_type=pl.DeviceIdType.MESH,
        )

    def far(which, chip, there, k):
        return pltpu.make_async_remote_copy(
            src_ref=chip.at[row_block(0, k)],
            dst_ref=there.at[row_block(0, k)],
            send_sem=far_sems.at[which, 0, k],
            recv_sem=far_sems.at[which, 1, k],
            device_id={"tp": across},
            device_id_type=pl.DeviceIdType.MESH,
        )

    def tp_sum(which, part, land, chip, there, first_tick):
        @pl.loop(0, blocks)
        def _(k):
            @pl.when(k >= 2)
            def _():
                near(which, land, k - 2).wait_send()

            staged[lax.rem(k, 2)] = part(row_block(1 - core, k))
            near(which, land, k).start()

        for k in range(max(blocks - 2, 0), blocks):
            near(which, land, k).wait_send()

        @pl.loop(0, blocks)
        def _(k):
            near(which, land, k).wait_recv()
            fetch = pltpu.make_async_copy(land.at[row_block(0, k)], fetched, fetch_sem)
            fetch.start()
            staged[0] = part(row_block(core, k))
            fetch.wait()
            staged[0] += fetched[...]
            keep = pltpu.make_async_copy(staged.at[0], chip.at[row_block(0, k)], keep_sem)
            keep.start()
            summer.tick(first_tick + k, count)
            keep.wait()
            far(which, chip, there, k).start()

    tp_sum(0, mid_part, mid_land, mid_chip, mid_far, early)
    tp_sum(1, ffn_part, ffn_land, ffn_chip, ffn_far, early + blocks)

    @pl.loop(early + 2 * blocks, count + summer.P_LAGS[-1][1])
    def _(t):
        summer.tick(t, count)

    for which, chip, there in ((0, mid_chip, mid_far), (1, ffn_chip, ffn_far)):

        @pl.loop(0, blocks)
        def _(k, which=which, chip=chip, there=there):
            far(which, chip, there, k).wait()


def ffn_both_ways(normed_mid, grad_ffn, w_gate, w_up, w_down, collective_id):
    rows, width = normed_mid.shape
    local = w_gate.shape[1]
    hidden = local // FFN_PARTS

    def in_parts(weights):
        return weights.reshape(width, FFN_PARTS, hidden)

    w_gu = jnp.concatenate([in_parts(w_gate), in_parts(w_up)], axis=2).transpose(1, 0, 2)
    w_d = w_down.reshape(FFN_PARTS, hidden, width)
    grad_rows = 3 * local * width // LANES
    half = jax.ShapeDtypeStruct((rows // 2, width), jnp.float32)
    low = jnp.bfloat16
    blocks = rows // 2 // OUT_BLOCK
    return pl.pallas_call(
        functools.partial(ffn_kernel, lax.axis_size("seq") // 2),
        out_shape=[jax.ShapeDtypeStruct((grad_rows, LANES), jnp.float32)] + [half] * 6,
        in_specs=[pl.BlockSpec(memory_space=pl.ANY)] * 6,
        out_specs=[pl.BlockSpec(memory_space=pl.ANY)] * 7,
        scratch_shapes=[
            pltpu.VMEM((rows, width), low),
            pltpu.VMEM((width, rows), low),
            pltpu.VMEM((rows, width), low),
            pltpu.VMEM((width, rows), low),
            pltpu.VMEM(w_gu.shape, low),
            pltpu.VMEM(w_d.shape, low),
            pltpu.VMEM((rows, local), low),
            pltpu.VMEM((FFN_PARTS, rows, 2 * hidden), low),
            pltpu.VMEM((grad_rows, LANES), jnp.float32),
            pltpu.VMEM((2, OUT_BLOCK, width), jnp.float32),
            pltpu.VMEM((OUT_BLOCK, width), jnp.float32),
            pltpu.SemaphoreType.DMA((6,)),
            pltpu.SemaphoreType.DMA((2, 2, blocks)),
            pltpu.SemaphoreType.DMA((2, 2, blocks)),
            pltpu.SemaphoreType.DMA,
            pltpu.SemaphoreType.DMA,
        ]
        + seq_sum_scratch(),
        compiler_params=pltpu.CompilerParams(
            collective_id=collective_id, has_side_effects=True, vmem_limit_bytes=VMEM_LIMIT
        ),
        cost_estimate=pl.CostEstimate(
            flops=18 * rows * width * local, bytes_accessed=800 << 20, transcendentals=0
        ),
        name="ffn_both_ways",
    )(normed_mid, normed_mid.T, grad_ffn, grad_ffn.T, w_gu, w_d)


def to_panels(matrix):
    rows, cols = matrix.shape
    return matrix.reshape(rows, cols // LANES, LANES).transpose(1, 0, 2).reshape(-1, LANES)


def from_panels(panels, rows, cols):
    return panels.reshape(cols // LANES, rows, LANES).transpose(1, 0, 2).reshape(rows, cols)


def per_device(
    tokens, lengths, gain_mix, w_in, conv_weight, w_out, gain_ffn, w_gate, w_up, w_down, cotangent
):
    slot_count, local_len, width = tokens.shape
    chans = w_in.shape[2]
    group = lax.axis_size("tp")
    seq_count = lax.axis_size("seq")
    tp_at, seq_at = lax.axis_index("tp"), lax.axis_index("seq")
    core, chip = tp_at % 2, tp_at // 2
    half_slots = slot_count // 2
    half_rows = half_slots * local_len
    row_count = slot_count * local_len

    def pick(is_first, first, second):
        return jnp.where(is_first, first, second)

    def both_cores(own, other):
        return jnp.concatenate(
            [pick(core == 0, own, other), pick(core == 0, other, own)], axis=0
        )

    flat = jnp.concatenate([w_in.reshape(3 * width, chans), w_out.reshape(width, chans)], axis=0)
    taps8 = jnp.pad(conv_weight, ((0, 5), (0, 0)))
    share_rows = flat.shape[0] // seq_count
    share = lax.dynamic_slice(flat, (seq_at * share_rows, 0), (share_rows, chans))
    sent = jnp.concatenate([share.astype(jnp.float32), taps8], axis=0)
    sent = swap_tp(sent, 2)
    across = lax.all_gather(sent[:share_rows], "seq", axis=0, tiled=True)
    own_flat = jnp.concatenate([flat.astype(jnp.float32), taps8], axis=0)
    across_flat = jnp.concatenate([across, sent[share_rows:]], axis=0)
    sib_own = swap_tp(own_flat, 1)
    sib_across = swap_tp(across_flat, 1)
    pair_own = [pick(core == 0, own_flat, sib_own), pick(core == 0, sib_own, own_flat)]
    pair_across = [
        pick(core == 0, across_flat, sib_across),
        pick(core == 0, sib_across, across_flat),
    ]
    quad = [pick(chip == 0, a, b) for a, b in zip(pair_own, pair_across)] + [
        pick(chip == 0, b, a) for a, b in zip(pair_own, pair_across)
    ]
    quad = lax.optimization_barrier(quad)
    taps = jnp.stack([q[4 * width : 4 * width + 3] for q in quad])
    w_in_all = jnp.stack(
        [q[: 3 * width].reshape(width, 3 * chans).astype(jnp.bfloat16) for q in quad]
    )
    w_out_all = jnp.stack(
        [q[3 * width : 4 * width].reshape(chans, width).astype(jnp.bfloat16) for q in quad]
    )

    first_pos = seq_at * local_len
    positions = first_pos + jnp.arange(local_len, dtype=jnp.int32)
    valid = (positions[None, :] < lengths[:, None]).astype(jnp.float32)[:, :, None]
    valid_all = valid.reshape(row_count, 1)
    valid_own = lax.dynamic_slice(valid, (core * half_slots, 0, 0), (half_slots, local_len, 1))
    valid_rows = valid_own.reshape(half_rows, 1)
    tokens_own = lax.dynamic_slice(
        tokens, (core * half_slots, 0, 0), (half_slots, local_len, width)
    )
    inputs_f = tokens_own.astype(jnp.float32).reshape(half_rows, width)
    scale_mix = rms_scale(inputs_f)
    unit_mix = inputs_f * scale_mix
    normed_in = (gain_mix * unit_mix).astype(jnp.bfloat16)
    projected = jnp.stack(
        [
            jnp.dot(normed_in, w_in_all[j], preferred_element_type=jnp.float32)
            for j in range(group)
        ]
    )
    in_gate = projected[:, :, :chans]
    out_gate = projected[:, :, chans : 2 * chans]
    conv_value = projected[:, :, 2 * chans :]
    seq_shape = (group, half_slots, local_len, chans)
    gated_seq = (valid_rows * in_gate * conv_value).reshape(seq_shape)
    carried = shift_seq(gated_seq[:, :, local_len - 2 :], 1)
    padded_seq = jnp.concatenate([carried, gated_seq], axis=2)

    def tap(j):
        return taps[:, j][:, None, None, :]

    conv_sum = (
        tap(0) * padded_seq[:, :, 0:local_len]
        + tap(1) * padded_seq[:, :, 1 : local_len + 1]
        + tap(2) * padded_seq[:, :, 2 : local_len + 2]
    ).reshape(group, half_rows, chans)
    mixed_seq = (out_gate * conv_sum).astype(jnp.bfloat16)
    mixer_out = sum(
        jnp.dot(mixed_seq[j], w_out_all[j], preferred_element_type=jnp.float32)
        for j in range(group)
    )
    hidden_res = inputs_f + mixer_out
    scale_ffn = rms_scale(hidden_res)
    unit_ffn = hidden_res * scale_ffn
    unit_all = both_cores(unit_ffn, swap_tp(unit_ffn, 1))
    normed_mid = (gain_ffn * unit_all).astype(jnp.bfloat16)

    grad_out = valid_all * cotangent.astype(jnp.float32).reshape(row_count, width)
    grad_ffn = grad_out.astype(jnp.bfloat16)
    ffn_sums, mid_chip, mid_far, ffn_chip, ffn_far = ffn_both_ways(
        normed_mid, grad_ffn, w_gate, w_up, w_down, 1
    )[:5]
    grad_mid = mid_chip + mid_far
    ffn_out = ffn_chip + ffn_far

    def own_rows(block):
        return lax.dynamic_slice(block, (core * half_rows, 0), (half_rows, width))

    block_own = hidden_res + ffn_out
    block_out = both_cores(block_own, swap_tp(block_own, 1))
    block_out = (valid_all * block_out).astype(jnp.bfloat16).reshape(slot_count, local_len, width)

    grad_gain_ffn = jnp.sum(grad_mid * unit_ffn, axis=0)
    scaled_mid = gain_ffn * grad_mid
    grad_hidden = own_rows(grad_out) + scale_ffn * (
        scaled_mid - unit_ffn * jnp.mean(scaled_mid * unit_ffn, axis=-1, keepdims=True)
    )

    grad_mixer = grad_hidden.astype(jnp.bfloat16)
    grad_mixed = jnp.stack([dot_cols(grad_mixer, w_out_all[j]) for j in range(group)])
    grad_out_gate = grad_mixed * conv_sum
    grad_conv_in = (grad_mixed * out_gate).reshape(seq_shape)
    next_grad = shift_seq(grad_conv_in[:, :, :2], -1)
    extended = jnp.concatenate([grad_conv_in, next_grad], axis=2)
    grad_gated = (
        tap(2) * extended[:, :, 0:local_len]
        + tap(1) * extended[:, :, 1 : local_len + 1]
        + tap(0) * extended[:, :, 2 : local_len + 2]
    ).reshape(group, half_rows, chans)
    grad_conv = jnp.stack(
        [
            jnp.sum(grad_conv_in * padded_seq[:, :, j : j + local_len], axis=(1, 2))
            for j in range(3)
        ],
        axis=1,
    )
    grad_in_gate = grad_gated * valid_rows * conv_value
    grad_value = grad_gated * valid_rows * in_gate
    grad_proj = jnp.concatenate([grad_in_gate, grad_out_gate, grad_value], axis=2).astype(
        jnp.bfloat16
    )
    grad_in = sum(dot_cols(grad_proj[j], w_in_all[j]) for j in range(group))
    grad_gain_mix = jnp.sum(grad_in * unit_mix, axis=0)
    scaled_in = gain_mix * grad_in
    tokens_grad = grad_hidden + scale_mix * (
        scaled_in - unit_mix * jnp.mean(scaled_in * unit_mix, axis=-1, keepdims=True)
    )
    grad_tokens = both_cores(tokens_grad, swap_tp(tokens_grad, 1))
    grad_tokens = grad_tokens.reshape(slot_count, local_len, width)

    def shard_of(stacked, which):
        at = chip * 2 + which
        return lax.dynamic_slice(
            stacked, (at,) + (0,) * (stacked.ndim - 1), (1,) + stacked.shape[1:]
        )[0]

    def mixer_panels(which):
        in_part = dot_rows(normed_in, shard_of(grad_proj, which))
        out_part = dot_rows(shard_of(mixed_seq, which), grad_mixer)
        small = jnp.concatenate(
            [grad_gain_mix, grad_gain_ffn, shard_of(grad_conv, which).reshape(-1)]
        ).reshape(-1, LANES)
        pad = -small.shape[0] % (4 * HALF)
        return jnp.concatenate(
            [to_panels(in_part), to_panels(out_part), jnp.pad(small, ((0, pad), (0, 0)))], axis=0
        )

    mixer_chip = mixer_panels(core) + swap_tp(mixer_panels(1 - core), 1)
    mixer_sums = seq_sum(mixer_chip, 2, "sum_mixer_grads")

    hidden = w_gate.shape[1]
    by_part = ffn_sums.reshape(FFN_PARTS, 3, hidden // FFN_PARTS // LANES, width, LANES)
    total_w_gate = by_part[:, 0].transpose(2, 0, 1, 3).reshape(width, hidden)
    total_w_up = by_part[:, 1].transpose(2, 0, 1, 3).reshape(width, hidden)
    total_w_down = by_part[:, 2].transpose(0, 1, 3, 2).reshape(hidden, width)
    in_rows = width * 3 * chans // LANES
    out_rows = width * chans // LANES
    total_w_in = from_panels(mixer_sums[:in_rows], width, 3 * chans).reshape(width, 3, chans)
    total_w_out = from_panels(mixer_sums[in_rows : in_rows + out_rows], chans, width)
    small = mixer_sums[in_rows + out_rows :].reshape(-1)
    total_gain_mix = small[:width]
    total_gain_ffn = small[width : 2 * width]
    total_conv = small[2 * width : 2 * width + 3 * chans].reshape(3, chans)
    return (
        block_out,
        grad_tokens,
        total_gain_mix,
        total_w_in,
        total_conv,
        total_w_out,
        total_gain_ffn,
        total_w_gate,
        total_w_up,
        total_w_down,
    )


def solution(mesh):
    rows, cols = P("tp", None), P(None, "tp")
    tokens, whole, stacked = P(None, "seq", None), P(), P(None, None, "tp")
    return jax.shard_map(
        per_device,
        mesh=mesh,
        in_specs=(
            tokens, whole, whole, stacked, cols, rows, whole, cols, cols, rows, tokens,
        ),
        out_specs=(
            tokens, tokens, whole, stacked, cols, rows, whole, cols, cols, rows,
        ),
        check_vma=False,
    )
```

```python
import functools

import jax
import jax.numpy as jnp
from jax import lax
from jax.experimental import pallas as pl
from jax.experimental.pallas import tpu as pltpu
from jax.sharding import PartitionSpec as P

NORM_EPS = 1e-05
LANES = 128
VMEM_LIMIT = 64 << 20
HALF = 128
SLOTS_IN_FLIGHT = 10


def rms_scale(values):
    return lax.rsqrt(jnp.mean(values * values, axis=-1, keepdims=True) + NORM_EPS)


def dot_rows(left, right):
    return lax.dot_general(
        left, right, (((0,), (0,)), ((), ())), preferred_element_type=jnp.float32
    )


def dot_cols(left, right):
    return lax.dot_general(
        left, right, (((1,), (1,)), ((), ())), preferred_element_type=jnp.float32
    )


def shift_seq(block, distance):
    count = lax.axis_size("seq")
    route = [(i - distance, i) for i in range(count) if 0 <= i - distance < count]
    return lax.ppermute(block, "seq", route)


def swap_tp(block, bit):
    return lax.ppermute(block, "tp", [(i, i ^ bit) for i in range(lax.axis_size("tp"))])


def greet_seq(places, others=()):
    barrier = pltpu.get_barrier_semaphore()
    here = lax.axis_index("seq")
    place, side = here // 2, lax.rem(here, 2)

    def signal(device):
        pl.semaphore_signal(
            barrier, inc=1, device_id=device, device_id_type=pl.DeviceIdType.MESH
        )

    signal({"seq": here + 1 - 2 * side})
    for other in others:
        signal(other)
    pl.when(place > 0)(lambda: signal({"seq": here - 2}))
    pl.when(place < places - 1)(lambda: signal({"seq": here + 2}))
    ends = jnp.where(place > 0, 1, 0) + jnp.where(place < places - 1, 1, 0)
    pl.semaphore_wait(barrier, 1 + len(others) + ends)


class SeqSum:
    def __init__(self, places, own, out, scratch):
        self.places, self.own, self.out = places, own, out
        self.y_in, self.p_left, self.p_right, self.p_acc = scratch[0:4]
        self.q_left, self.q_right, self.q_acc, self.q_in = scratch[4:8]
        self.sems = scratch[8]
        here = lax.axis_index("seq")
        self.place, self.side = here // 2, here % 2

    def remote(self, src, dst, slot, send, recv, place, side):
        return pltpu.make_async_remote_copy(
            src_ref=src,
            dst_ref=dst,
            send_sem=self.sems.at[send, slot],
            recv_sem=self.sems.at[recv, slot],
            device_id={"seq": place * 2 + side},
            device_id_type=pl.DeviceIdType.MESH,
        )

    def chain(self, root):
        last = self.places - 1
        left = jnp.maximum(self.place - 1, 0)
        right = jnp.minimum(self.place + 1, last)
        from_left = (self.place <= root) & (self.place > 0)
        from_right = (self.place >= root) & (self.place < last)
        return left, right, from_left, from_right

    def p_stage(self, which, k):
        place, side = self.place, self.side
        own, out = self.own, self.out
        slot = lax.rem(k, SLOTS_IN_FLIGHT)
        base = pl.multiple_of(k * 4 * HALF, 4 * HALF)
        mine = pl.ds(pl.multiple_of(base + side * HALF, HALF), HALF)
        theirs = pl.ds(pl.multiple_of(base + (1 - side) * HALF, HALF), HALF)
        root = self.places // 2 - 1 + lax.rem(k, 2)
        left, right, from_left, from_right = self.chain(root)
        acc, y_in = self.p_acc.at[slot], self.y_in.at[slot]
        from_l, from_r = self.p_left.at[slot], self.p_right.at[slot]
        remote = functools.partial(functools.partial, self.remote)

        to_side = remote(own.at[theirs], y_in, slot, 0, 1, place, 1 - side)
        up_right = remote(acc, from_l, slot, 2, 3, right, side)
        up_left = remote(acc, from_r, slot, 2, 4, left, side)

        def down(src):
            return (
                remote(src, out.at[mine], slot, 5, 7, left, side),
                remote(src, out.at[mine], slot, 6, 7, right, side),
                remote(src, out.at[mine], slot, 8, 9, place, 1 - side),
            )

        def keep():
            return pltpu.make_async_copy(acc, out.at[mine], self.sems.at[10, slot])

        def hand_down(src):
            down_left, down_right, down_side = down(src)
            down_side().start()
            pl.when(from_left)(lambda: down_left().start())
            pl.when(from_right)(lambda: down_right().start())

        if which == "split":
            to_side().start()

        if which == "up":
            to_side().wait_recv()
            acc[...] = own[mine, :] + y_in[...]

            @pl.when(place < root)
            def _():
                @pl.when(from_left)
                def _():
                    up_right().wait_recv()
                    acc[...] += from_l[...]

                up_right().start()

            @pl.when(place > root)
            def _():
                @pl.when(from_right)
                def _():
                    up_left().wait_recv()
                    acc[...] += from_r[...]

                up_left().start()

        if which == "root":

            @pl.when(place == root)
            def _():
                @pl.when(from_left)
                def _():
                    up_right().wait_recv()
                    acc[...] += from_l[...]

                @pl.when(from_right)
                def _():
                    up_left().wait_recv()
                    acc[...] += from_r[...]

                hand_down(acc)
                keep().start()

        if which == "down":

            @pl.when(place != root)
            def _():
                down(acc)[0]().wait_recv()
                hand_down(out.at[mine])

        if which == "end":
            down_left, down_right, down_side = down(acc)
            down_side().wait()
            to_side().wait_send()
            pl.when(from_left)(lambda: down_left().wait_send())
            pl.when(from_right)(lambda: down_right().wait_send())
            pl.when(place == root)(lambda: keep().wait())
            pl.when(place != root)(lambda: up_left().wait_send())

    def q_stage(self, which, k):
        place, side = self.place, self.side
        own, out = self.own, self.out
        slot = lax.rem(k, SLOTS_IN_FLIGHT)
        base = pl.multiple_of(k * 4 * HALF, 4 * HALF)
        wide = pl.ds(pl.multiple_of(base + 2 * HALF, 2 * HALF), 2 * HALF)
        root = self.places // 2 - lax.rem(k, 2)
        left, right, from_left, from_right = self.chain(root)
        acc, side_in = self.q_acc.at[slot], self.q_in.at[slot]
        from_l, from_r = self.q_left.at[slot], self.q_right.at[slot]
        remote = functools.partial(functools.partial, self.remote)

        up_right = remote(acc, from_l, slot, 11, 12, right, side)
        up_left = remote(acc, from_r, slot, 11, 13, left, side)
        to_side = remote(acc, side_in, slot, 14, 15, place, 1 - side)

        def down(src):
            return (
                remote(src, out.at[wide], slot, 16, 18, left, side),
                remote(src, out.at[wide], slot, 17, 18, right, side),
            )

        def keep():
            return pltpu.make_async_copy(side_in, out.at[wide], self.sems.at[19, slot])

        def hand_down(src):
            down_left, down_right = down(src)
            pl.when(from_left)(lambda: down_left().start())
            pl.when(from_right)(lambda: down_right().start())

        if which == "up":
            acc[...] = own[wide, :]

            @pl.when(place < root)
            def _():
                @pl.when(from_left)
                def _():
                    up_right().wait_recv()
                    acc[...] += from_l[...]

                up_right().start()

            @pl.when(place > root)
            def _():
                @pl.when(from_right)
                def _():
                    up_left().wait_recv()
                    acc[...] += from_r[...]

                up_left().start()

        if which == "root":

            @pl.when(place == root)
            def _():
                @pl.when(from_left)
                def _():
                    up_right().wait_recv()
                    acc[...] += from_l[...]

                @pl.when(from_right)
                def _():
                    up_left().wait_recv()
                    acc[...] += from_r[...]

                to_side().start()

        if which == "side":

            @pl.when(place == root)
            def _():
                to_side().wait_recv()
                side_in[...] += acc[...]
                hand_down(side_in)
                keep().start()

        if which == "down":

            @pl.when(place != root)
            def _():
                down(acc)[0]().wait_recv()
                hand_down(out.at[wide])

        if which == "end":
            down_left, down_right = down(acc)
            pl.when(from_left)(lambda: down_left().wait_send())
            pl.when(from_right)(lambda: down_right().wait_send())

            @pl.when(place == root)
            def _():
                to_side().wait_send()
                keep().wait()

            pl.when(place != root)(lambda: up_left().wait_send())

    P_LAGS = (("split", 0, 0), ("up", 2, 1), ("root", 3, 3), ("down", 6, 7), ("end", 9, 9))
    Q_LAGS = (("up", 1, 0), ("root", 2, 2), ("side", 4, 4), ("down", 6, 7), ("end", 9, 9))

    def tick(self, t, count):
        middle = (self.place == self.places // 2) | (self.place == self.places // 2 - 1)
        for stage, lags in ((self.p_stage, self.P_LAGS), (self.q_stage, self.Q_LAGS)):
            for which, mid_lag, outer_lag in lags:
                k = t - jnp.where(middle, mid_lag, outer_lag)

                @pl.when((k >= 0) & (k < count))
                def _(stage=stage, which=which, k=k):
                    stage(which, k)

    def run(self, count):
        @pl.loop(0, count + self.P_LAGS[-1][1])
        def _(t):
            self.tick(t, count)


def seq_sum_scratch():
    half = pltpu.VMEM((SLOTS_IN_FLIGHT, HALF, LANES), jnp.float32)
    wide = pltpu.VMEM((SLOTS_IN_FLIGHT, 2 * HALF, LANES), jnp.float32)
    return [half] * 4 + [wide] * 4 + [pltpu.SemaphoreType.DMA((20, SLOTS_IN_FLIGHT))]


def seq_sum_kernel(places, own, out, *scratch):
    summer = SeqSum(places, own, out, scratch)
    greet_seq(places)
    summer.run(own.shape[0] // (4 * HALF))


def seq_sum(block, collective_id, name):
    rows = block.shape[0]
    return pl.pallas_call(
        functools.partial(seq_sum_kernel, lax.axis_size("seq") // 2),
        out_shape=jax.ShapeDtypeStruct(block.shape, jnp.float32),
        in_specs=[pl.BlockSpec(memory_space=pltpu.VMEM)],
        out_specs=pl.BlockSpec(memory_space=pl.ANY),
        scratch_shapes=seq_sum_scratch(),
        compiler_params=pltpu.CompilerParams(
            collective_id=collective_id, has_side_effects=True, vmem_limit_bytes=40 << 20
        ),
        cost_estimate=pl.CostEstimate(
            flops=rows * 256, bytes_accessed=rows * 512 * 32, transcendentals=0
        ),
        name=name,
    )(block)


FFN_PARTS = 3
ROW_BLOCK = 512
OUT_BLOCK = 256


def ffn_kernel(places, *refs):
    (mid_hbm, mid_t_hbm, cot_hbm, cot_t_hbm, w_gu_hbm, w_d_hbm) = refs[0:6]
    (sums, mid_chip, mid_far, ffn_chip, ffn_far, mid_land, ffn_land) = refs[6:13]
    (mid, mid_t, cot, cot_t, w_gu, w_d, act, ggu, own, staged, fetched) = refs[13:24]
    load_sems, near_sems, far_sems, keep_sem, fetch_sem = refs[24:29]
    summer = SeqSum(places, own, sums, refs[29:])
    tp_at = lax.axis_index("tp")
    core = lax.rem(tp_at, 2)
    sibling = tp_at + 1 - 2 * core
    across = lax.rem(tp_at + 2, 4)
    rows, width = mid.shape
    parts, _, wide = w_gu.shape
    hidden = wide // 2
    panels = 3 * hidden // LANES

    loads = [
        pltpu.make_async_copy(src, dst, load_sems.at[i])
        for i, (src, dst) in enumerate(
            (
                (mid_hbm, mid),
                (w_gu_hbm, w_gu),
                (cot_hbm, cot),
                (w_d_hbm, w_d),
                (mid_t_hbm, mid_t),
                (cot_t_hbm, cot_t),
            )
        )
    ]
    for load in loads:
        load.start()
    greet_seq(places, ({"tp": sibling}, {"tp": across}))
    count = own.shape[0] // (4 * HALF)
    for load in loads[:4]:
        load.wait()

    def part_cols(c):
        return pl.ds(pl.multiple_of(c * hidden, LANES), hidden)

    @pl.loop(0, parts)
    def _(c):
        @pl.loop(0, rows // ROW_BLOCK)
        def _(r):
            at = pl.ds(pl.multiple_of(r * ROW_BLOCK, ROW_BLOCK), ROW_BLOCK)
            both = jnp.dot(mid[at, :], w_gu[c], preferred_element_type=jnp.float32)
            gate, up = both[:, :hidden], both[:, hidden:]
            grad_act = dot_cols(cot[at, :], w_d[c])
            sigmoid = 1.0 / (1.0 + jnp.exp(-gate))
            silu = gate * sigmoid
            act[at, part_cols(c)] = (silu * up).astype(jnp.bfloat16)
            slope = sigmoid * (1.0 + gate * (1.0 - sigmoid))
            ggu[c, at, :hidden] = (grad_act * up * slope).astype(jnp.bfloat16)
            ggu[c, at, hidden:] = (grad_act * silu).astype(jnp.bfloat16)

        @pl.when(c == 0)
        def _():
            for load in loads[4:]:
                load.wait()

        @pl.loop(0, width // OUT_BLOCK)
        def _(m):
            first = pl.multiple_of(m * OUT_BLOCK, OUT_BLOCK)
            at = pl.ds(first, OUT_BLOCK)
            base = c * (panels * width) + first

            def put(block, panel):
                for j in range(block.shape[1] // LANES):
                    to = pl.multiple_of(base + (panel + j) * width, OUT_BLOCK)
                    own[pl.ds(to, OUT_BLOCK), :] = block[:, j * LANES : (j + 1) * LANES]

            put(jnp.dot(mid_t[at, :], ggu[c], preferred_element_type=jnp.float32), 0)
            put(
                jnp.dot(cot_t[at, :], act[:, part_cols(c)], preferred_element_type=jnp.float32),
                wide // LANES,
            )

            @pl.when(c > 0)
            def _():
                summer.tick((c - 1) * (width // OUT_BLOCK) + m, count)

    early = (parts - 1) * (width // OUT_BLOCK)
    blocks = rows // 2 // OUT_BLOCK

    def row_block(half, k):
        return pl.ds(pl.multiple_of((half * blocks + k) * OUT_BLOCK, OUT_BLOCK), OUT_BLOCK)

    def mid_part(at):
        return sum(dot_cols(ggu[c, at, :], w_gu[c]) for c in range(parts))

    def ffn_part(at):
        return sum(
            jnp.dot(
                act[at, c * hidden : (c + 1) * hidden],
                w_d[c],
                preferred_element_type=jnp.float32,
            )
            for c in range(parts)
        )

    def near(which, land, k):
        return pltpu.make_async_remote_copy(
            src_ref=staged.at[lax.rem(k, 2)],
            dst_ref=land.at[row_block(0, k)],
            send_sem=near_sems.at[which, 0, k],
            recv_sem=near_sems.at[which, 1, k],
            device_id={"tp": sibling},
            device_id_type=pl.DeviceIdType.MESH,
        )

    def far(which, chip, there, k):
        return pltpu.make_async_remote_copy(
            src_ref=chip.at[row_block(0, k)],
            dst_ref=there.at[row_block(0, k)],
            send_sem=far_sems.at[which, 0, k],
            recv_sem=far_sems.at[which, 1, k],
            device_id={"tp": across},
            device_id_type=pl.DeviceIdType.MESH,
        )

    def tp_sum(which, part, land, chip, there, first_tick):
        @pl.loop(0, blocks)
        def _(k):
            @pl.when(k >= 2)
            def _():
                near(which, land, k - 2).wait_send()

            staged[lax.rem(k, 2)] = part(row_block(1 - core, k))
            near(which, land, k).start()

        for k in range(max(blocks - 2, 0), blocks):
            near(which, land, k).wait_send()

        @pl.loop(0, blocks)
        def _(k):
            near(which, land, k).wait_recv()
            fetch = pltpu.make_async_copy(land.at[row_block(0, k)], fetched, fetch_sem)
            fetch.start()
            staged[0] = part(row_block(core, k))
            fetch.wait()
            staged[0] += fetched[...]
            keep = pltpu.make_async_copy(staged.at[0], chip.at[row_block(0, k)], keep_sem)
            keep.start()
            summer.tick(first_tick + k, count)
            keep.wait()
            far(which, chip, there, k).start()

    tp_sum(0, mid_part, mid_land, mid_chip, mid_far, early)
    tp_sum(1, ffn_part, ffn_land, ffn_chip, ffn_far, early + blocks)

    @pl.loop(early + 2 * blocks, count + summer.P_LAGS[-1][1])
    def _(t):
        summer.tick(t, count)

    for which, chip, there in ((0, mid_chip, mid_far), (1, ffn_chip, ffn_far)):

        @pl.loop(0, blocks)
        def _(k, which=which, chip=chip, there=there):
            far(which, chip, there, k).wait()


def ffn_both_ways(normed_mid, grad_ffn, w_gate, w_up, w_down, collective_id):
    rows, width = normed_mid.shape
    local = w_gate.shape[1]
    hidden = local // FFN_PARTS

    def in_parts(weights):
        return weights.reshape(width, FFN_PARTS, hidden)

    w_gu = jnp.concatenate([in_parts(w_gate), in_parts(w_up)], axis=2).transpose(1, 0, 2)
    w_d = w_down.reshape(FFN_PARTS, hidden, width)
    grad_rows = 3 * local * width // LANES
    half = jax.ShapeDtypeStruct((rows // 2, width), jnp.float32)
    low = jnp.bfloat16
    blocks = rows // 2 // OUT_BLOCK
    return pl.pallas_call(
        functools.partial(ffn_kernel, lax.axis_size("seq") // 2),
        out_shape=[jax.ShapeDtypeStruct((grad_rows, LANES), jnp.float32)] + [half] * 6,
        in_specs=[pl.BlockSpec(memory_space=pl.ANY)] * 6,
        out_specs=[pl.BlockSpec(memory_space=pl.ANY)] * 7,
        scratch_shapes=[
            pltpu.VMEM((rows, width), low),
            pltpu.VMEM((width, rows), low),
            pltpu.VMEM((rows, width), low),
            pltpu.VMEM((width, rows), low),
            pltpu.VMEM(w_gu.shape, low),
            pltpu.VMEM(w_d.shape, low),
            pltpu.VMEM((rows, local), low),
            pltpu.VMEM((FFN_PARTS, rows, 2 * hidden), low),
            pltpu.VMEM((grad_rows, LANES), jnp.float32),
            pltpu.VMEM((2, OUT_BLOCK, width), jnp.float32),
            pltpu.VMEM((OUT_BLOCK, width), jnp.float32),
            pltpu.SemaphoreType.DMA((6,)),
            pltpu.SemaphoreType.DMA((2, 2, blocks)),
            pltpu.SemaphoreType.DMA((2, 2, blocks)),
            pltpu.SemaphoreType.DMA,
            pltpu.SemaphoreType.DMA,
        ]
        + seq_sum_scratch(),
        compiler_params=pltpu.CompilerParams(
            collective_id=collective_id, has_side_effects=True, vmem_limit_bytes=VMEM_LIMIT
        ),
        cost_estimate=pl.CostEstimate(
            flops=18 * rows * width * local, bytes_accessed=800 << 20, transcendentals=0
        ),
        name="ffn_both_ways",
    )(normed_mid, normed_mid.T, grad_ffn, grad_ffn.T, w_gu, w_d)


def gather_kernel(places, w_in, w_out, taps, full_in, full_out, full_taps, *scratch):
    own_in, own_out, far_in, far_out, sib_in, sib_out, sibfar_in, sibfar_out = scratch[0:8]
    own_taps, far_taps, sib_taps, sibfar_taps, share_in, share_out = scratch[8:14]
    sends, recvs, once = scratch[14:17]
    here = lax.axis_index("seq")
    place, side = here // 2, lax.rem(here, 2)
    last = places - 1
    tp_at = lax.axis_index("tp")
    core = lax.rem(tp_at, 2)
    sibling = tp_at + 1 - 2 * core
    across = lax.rem(tp_at + 2, 4)
    far_sibling = sibling + across - tp_at
    in_rows = w_in.shape[0] // (2 * places)
    out_rows = w_out.shape[0] // (2 * places)
    chans = w_in.shape[1] // 3
    width = w_out.shape[1]

    greet_seq(places, ({"tp": sibling}, {"tp": across}))

    def shares(j):
        return (
            pl.ds(pl.multiple_of(j * in_rows, in_rows), in_rows),
            pl.ds(pl.multiple_of(j * out_rows, out_rows), out_rows),
        )

    def copies(source, target, j, kind, device):
        for i, at in enumerate(shares(j)):
            yield pltpu.make_async_remote_copy(
                src_ref=source[i] if kind == 0 else source[i].at[at],
                dst_ref=target[i].at[at],
                send_sem=sends.at[kind, i, j],
                recv_sem=recvs.at[0 if kind < 4 else 1, i, j],
                device_id=device,
                device_id_type=pl.DeviceIdType.MESH,
            )

    share, far, sibfar = (share_in, share_out), (far_in, far_out), (sibfar_in, sibfar_out)

    def across_share():
        return copies(share, far, here, 0, {"tp": across})

    def to_right(j):
        return copies(far, far, j, 1, {"seq": here + 2})

    def to_left(j):
        return copies(far, far, j, 2, {"seq": here - 2})

    def to_side(j):
        return copies(far, far, j, 3, {"seq": here + 1 - 2 * side})

    def to_sibling(j):
        return copies(far, sibfar, j, 4, {"tp": sibling})

    def start(group):
        for copy in group:
            copy.start()

    def arrived(group):
        for copy in group:
            copy.wait_recv()

    def left_source(group):
        for copy in group:
            copy.wait_send()

    def single(i, src, dst, device):
        return pltpu.make_async_remote_copy(
            src_ref=src,
            dst_ref=dst,
            send_sem=once.at[0, i],
            recv_sem=once.at[1, i],
            device_id=device,
            device_id_type=pl.DeviceIdType.MESH,
        )

    for source, held, at in zip((w_in, w_out), share, shares(here)):
        held[...] = source[at, :].astype(jnp.float32)
    start(across_share())
    own_taps[...] = taps[...]
    taps_far = single(0, own_taps, far_taps, {"tp": across})
    taps_sib = single(1, own_taps, sib_taps, {"tp": sibling})
    taps_sibfar = single(2, far_taps, sibfar_taps, {"tp": sibling})
    own_in[...] = w_in[...].astype(jnp.float32)
    own_out[...] = w_out[...].astype(jnp.float32)
    in_sib = single(3, own_in, sib_in, {"tp": sibling})
    out_sib = single(4, own_out, sib_out, {"tp": sibling})
    for copy in (taps_far, taps_sib, in_sib, out_sib):
        copy.start()

    arrived(across_share())
    start(to_side(here))
    pl.when(place < last)(lambda: start(to_right(here)))
    pl.when(place > 0)(lambda: start(to_left(here)))
    start(to_sibling(here))
    taps_far.wait_recv()
    taps_sibfar.start()

    def place_shard(shard_in, shard_out, shard_taps, index):
        for g in range(3):
            cols = pl.ds(pl.multiple_of(g * width + index * chans, LANES), chans)
            full_in[:, cols] = shard_in[:, g * chans : (g + 1) * chans].astype(jnp.bfloat16)
        rows = pl.ds(pl.multiple_of(index * chans, chans), chans)
        full_out[rows, :] = shard_out[...].astype(jnp.bfloat16)
        cols = pl.ds(pl.multiple_of(index * chans, LANES), chans)
        full_taps[:, cols] = shard_taps[...]

    def from_side(q):
        j = 2 * q + 1 - side
        arrived(to_side(j))
        start(to_sibling(j))

    @pl.loop(1, places)
    def _(d):
        @pl.when(place - d >= 0)
        def _():
            j = here - 2 * d
            arrived(to_right(j))
            pl.when(place < last)(lambda: start(to_right(j)))
            start(to_side(j))
            start(to_sibling(j))

        @pl.when(place + d <= last)
        def _():
            j = here + 2 * d
            arrived(to_left(j))
            pl.when(place > 0)(lambda: start(to_left(j)))
            start(to_side(j))
            start(to_sibling(j))

        @pl.when(d == 1)
        def _():
            from_side(place)
            place_shard(own_in, own_out, own_taps, tp_at)
            in_sib.wait_recv()
            out_sib.wait_recv()
            taps_sib.wait_recv()
            place_shard(sib_in, sib_out, sib_taps, sibling)

        pl.when(place - d >= 0)(lambda: from_side(place - d))
        pl.when(place + d <= last)(lambda: from_side(place + d))

    place_shard(far_in, far_out, far_taps, across)
    taps_sibfar.wait_recv()

    @pl.loop(0, 2 * places)
    def _(j):
        arrived(to_sibling(j))

    place_shard(sibfar_in, sibfar_out, sibfar_taps, far_sibling)

    left_source(across_share())
    for copy in (taps_far, taps_sib, taps_sibfar, in_sib, out_sib):
        copy.wait_send()

    @pl.loop(0, places)
    def _(q):
        j = 2 * q + side
        left_source(to_side(j))
        pl.when((q <= place) & (place < last))(lambda: left_source(to_right(j)))
        pl.when((q >= place) & (place > 0))(lambda: left_source(to_left(j)))
        left_source(to_sibling(j))
        left_source(to_sibling(2 * q + 1 - side))


def gather_mixer(w_in, w_out, taps, collective_id):
    width, _, chans = w_in.shape
    count = lax.axis_size("seq")
    group = lax.axis_size("tp")
    f32 = jnp.float32
    pair = [pltpu.VMEM((width, 3 * chans), f32), pltpu.VMEM((chans, width), f32)]
    whole = pl.BlockSpec(memory_space=pltpu.VMEM)
    return pl.pallas_call(
        functools.partial(gather_kernel, count // 2),
        out_shape=[
            jax.ShapeDtypeStruct((width, 3 * chans * group), jnp.bfloat16),
            jax.ShapeDtypeStruct((chans * group, width), jnp.bfloat16),
            jax.ShapeDtypeStruct((8, chans * group), f32),
        ],
        in_specs=[whole] * 3,
        out_specs=[whole] * 3,
        scratch_shapes=pair * 4
        + [pltpu.VMEM((8, chans), f32)] * 4
        + [
            pltpu.VMEM((width // count, 3 * chans), f32),
            pltpu.VMEM((chans // count, width), f32),
        ]
        + [
            pltpu.SemaphoreType.DMA((5, 2, count)),
            pltpu.SemaphoreType.DMA((2, 2, count)),
            pltpu.SemaphoreType.DMA((2, 5)),
        ],
        compiler_params=pltpu.CompilerParams(
            collective_id=collective_id, has_side_effects=True, vmem_limit_bytes=48 << 20
        ),
        name="gather_mixer",
    )(w_in.reshape(width, 3 * chans), w_out, jnp.pad(taps, ((0, 5), (0, 0))))


def to_panels(matrix):
    rows, cols = matrix.shape
    return matrix.reshape(rows, cols // LANES, LANES).transpose(1, 0, 2).reshape(-1, LANES)


def from_panels(panels, rows, cols):
    return panels.reshape(cols // LANES, rows, LANES).transpose(1, 0, 2).reshape(rows, cols)


def per_device(
    tokens, lengths, gain_mix, w_in, conv_weight, w_out, gain_ffn, w_gate, w_up, w_down, cotangent
):
    slot_count, local_len, width = tokens.shape
    chans = w_in.shape[2]
    group = lax.axis_size("tp")
    seq_count = lax.axis_size("seq")
    tp_at, seq_at = lax.axis_index("tp"), lax.axis_index("seq")
    core, chip = tp_at % 2, tp_at // 2
    half_slots = slot_count // 2
    half_rows = half_slots * local_len
    row_count = slot_count * local_len

    def pick(is_first, first, second):
        return jnp.where(is_first, first, second)

    def both_cores(own, other):
        return jnp.concatenate(
            [pick(core == 0, own, other), pick(core == 0, other, own)], axis=0
        )

    w_in_all, w_out_all, taps = gather_mixer(w_in, w_out, conv_weight, 3)

    first_pos = seq_at * local_len
    positions = first_pos + jnp.arange(local_len, dtype=jnp.int32)
    valid = (positions[None, :] < lengths[:, None]).astype(jnp.float32)[:, :, None]
    valid_all = valid.reshape(row_count, 1)
    valid_own = lax.dynamic_slice(valid, (core * half_slots, 0, 0), (half_slots, local_len, 1))
    valid_rows = valid_own.reshape(half_rows, 1)
    tokens_own = lax.dynamic_slice(
        tokens, (core * half_slots, 0, 0), (half_slots, local_len, width)
    )
    inputs_f = tokens_own.astype(jnp.float32).reshape(half_rows, width)
    scale_mix = rms_scale(inputs_f)
    unit_mix = inputs_f * scale_mix
    normed_in = (gain_mix * unit_mix).astype(jnp.bfloat16)
    projected = jnp.dot(normed_in, w_in_all, preferred_element_type=jnp.float32)
    in_gate = projected[:, :width]
    out_gate = projected[:, width : 2 * width]
    conv_value = projected[:, 2 * width :]
    seq_shape = (half_slots, local_len, width)
    gated_seq = (valid_rows * in_gate * conv_value).reshape(seq_shape)
    carried = shift_seq(gated_seq[:, local_len - 2 :], 1)
    padded_seq = jnp.concatenate([carried, gated_seq], axis=1)
    conv_sum = (
        taps[0] * padded_seq[:, 0:local_len]
        + taps[1] * padded_seq[:, 1 : local_len + 1]
        + taps[2] * padded_seq[:, 2 : local_len + 2]
    ).reshape(half_rows, width)
    mixed_seq = (out_gate * conv_sum).astype(jnp.bfloat16)
    mixer_out = jnp.dot(mixed_seq, w_out_all, preferred_element_type=jnp.float32)
    hidden_res = inputs_f + mixer_out
    scale_ffn = rms_scale(hidden_res)
    unit_ffn = hidden_res * scale_ffn
    unit_all = both_cores(unit_ffn, swap_tp(unit_ffn, 1))
    normed_mid = (gain_ffn * unit_all).astype(jnp.bfloat16)

    grad_out = valid_all * cotangent.astype(jnp.float32).reshape(row_count, width)
    grad_ffn = grad_out.astype(jnp.bfloat16)
    ffn_sums, mid_chip, mid_far, ffn_chip, ffn_far = ffn_both_ways(
        normed_mid, grad_ffn, w_gate, w_up, w_down, 1
    )[:5]
    grad_mid = mid_chip + mid_far
    ffn_out = ffn_chip + ffn_far

    def own_rows(block):
        return lax.dynamic_slice(block, (core * half_rows, 0), (half_rows, width))

    block_own = hidden_res + ffn_out
    block_out = both_cores(block_own, swap_tp(block_own, 1))
    block_out = (valid_all * block_out).astype(jnp.bfloat16).reshape(slot_count, local_len, width)

    grad_gain_ffn = jnp.sum(grad_mid * unit_ffn, axis=0)
    scaled_mid = gain_ffn * grad_mid
    grad_hidden = own_rows(grad_out) + scale_ffn * (
        scaled_mid - unit_ffn * jnp.mean(scaled_mid * unit_ffn, axis=-1, keepdims=True)
    )

    grad_mixer = grad_hidden.astype(jnp.bfloat16)
    grad_mixed = dot_cols(grad_mixer, w_out_all)
    grad_out_gate = grad_mixed * conv_sum
    grad_conv_in = (grad_mixed * out_gate).reshape(seq_shape)
    next_grad = shift_seq(grad_conv_in[:, :2], -1)
    extended = jnp.concatenate([grad_conv_in, next_grad], axis=1)
    grad_gated = (
        taps[2] * extended[:, 0:local_len]
        + taps[1] * extended[:, 1 : local_len + 1]
        + taps[0] * extended[:, 2 : local_len + 2]
    ).reshape(half_rows, width)
    grad_conv = jnp.stack(
        [jnp.sum(grad_conv_in * padded_seq[:, j : j + local_len], axis=(0, 1)) for j in range(3)]
    )
    grad_in_gate = grad_gated * valid_rows * conv_value
    grad_value = grad_gated * valid_rows * in_gate
    grad_proj = jnp.concatenate([grad_in_gate, grad_out_gate, grad_value], axis=1).astype(
        jnp.bfloat16
    )
    grad_in = dot_cols(grad_proj, w_in_all)
    grad_gain_mix = jnp.sum(grad_in * unit_mix, axis=0)
    scaled_in = gain_mix * grad_in
    tokens_grad = grad_hidden + scale_mix * (
        scaled_in - unit_mix * jnp.mean(scaled_in * unit_mix, axis=-1, keepdims=True)
    )
    grad_tokens = both_cores(tokens_grad, swap_tp(tokens_grad, 1))
    grad_tokens = grad_tokens.reshape(slot_count, local_len, width)

    def chans_of(block, which):
        first = (chip * 2 + which) * chans
        return lax.dynamic_slice(block, (0, first), (block.shape[0], chans))

    def mixer_panels(which):
        proj = jnp.concatenate(
            [chans_of(grad_proj[:, g * width : (g + 1) * width], which) for g in range(3)], axis=1
        )
        in_part = dot_rows(normed_in, proj)
        out_part = dot_rows(chans_of(mixed_seq, which), grad_mixer)
        small = jnp.concatenate(
            [grad_gain_mix, grad_gain_ffn, chans_of(grad_conv, which).reshape(-1)]
        ).reshape(-1, LANES)
        pad = -small.shape[0] % (4 * HALF)
        return jnp.concatenate(
            [to_panels(in_part), to_panels(out_part), jnp.pad(small, ((0, pad), (0, 0)))], axis=0
        )

    mixer_chip = mixer_panels(core) + swap_tp(mixer_panels(1 - core), 1)
    mixer_sums = seq_sum(mixer_chip, 2, "sum_mixer_grads")

    hidden = w_gate.shape[1]
    by_part = ffn_sums.reshape(FFN_PARTS, 3, hidden // FFN_PARTS // LANES, width, LANES)
    total_w_gate = by_part[:, 0].transpose(2, 0, 1, 3).reshape(width, hidden)
    total_w_up = by_part[:, 1].transpose(2, 0, 1, 3).reshape(width, hidden)
    total_w_down = by_part[:, 2].transpose(0, 1, 3, 2).reshape(hidden, width)
    in_rows = width * 3 * chans // LANES
    out_rows = width * chans // LANES
    total_w_in = from_panels(mixer_sums[:in_rows], width, 3 * chans).reshape(width, 3, chans)
    total_w_out = from_panels(mixer_sums[in_rows : in_rows + out_rows], chans, width)
    small = mixer_sums[in_rows + out_rows :].reshape(-1)
    total_gain_mix = small[:width]
    total_gain_ffn = small[width : 2 * width]
    total_conv = small[2 * width : 2 * width + 3 * chans].reshape(3, chans)
    return (
        block_out,
        grad_tokens,
        total_gain_mix,
        total_w_in,
        total_conv,
        total_w_out,
        total_gain_ffn,
        total_w_gate,
        total_w_up,
        total_w_down,
    )


def solution(mesh):
    rows, cols = P("tp", None), P(None, "tp")
    tokens, whole, stacked = P(None, "seq", None), P(), P(None, None, "tp")
    return jax.shard_map(
        per_device,
        mesh=mesh,
        in_specs=(
            tokens, whole, whole, stacked, cols, rows, whole, cols, cols, rows, tokens,
        ),
        out_specs=(
            tokens, tokens, whole, stacked, cols, rows, whole, cols, cols, rows,
        ),
        check_vma=False,
    )
```

```python
import functools

import jax
import jax.numpy as jnp
from jax import lax
from jax.experimental import pallas as pl
from jax.experimental.pallas import tpu as pltpu
from jax.sharding import PartitionSpec as P

NORM_EPS = 1e-05
LANES = 128
VMEM_LIMIT = 64 << 20
HALF = 128
SLOTS_IN_FLIGHT = 10


def rms_scale(values):
    return lax.rsqrt(jnp.mean(values * values, axis=-1, keepdims=True) + NORM_EPS)


def dot_rows(left, right):
    return lax.dot_general(
        left, right, (((0,), (0,)), ((), ())), preferred_element_type=jnp.float32
    )


def dot_cols(left, right):
    return lax.dot_general(
        left, right, (((1,), (1,)), ((), ())), preferred_element_type=jnp.float32
    )


def shift_seq(block, distance):
    count = lax.axis_size("seq")
    route = [(i - distance, i) for i in range(count) if 0 <= i - distance < count]
    return lax.ppermute(block, "seq", route)


def swap_tp(block, bit):
    return lax.ppermute(block, "tp", [(i, i ^ bit) for i in range(lax.axis_size("tp"))])


def greet_seq(places, others=(), more=0):
    barrier = pltpu.get_barrier_semaphore()
    here = lax.axis_index("seq")
    place, side = here // 2, lax.rem(here, 2)

    def signal(device):
        pl.semaphore_signal(
            barrier, inc=1, device_id=device, device_id_type=pl.DeviceIdType.MESH
        )

    signal({"seq": here + 1 - 2 * side})
    for other in others:
        signal(other)
    pl.when(place > 0)(lambda: signal({"seq": here - 2}))
    pl.when(place < places - 1)(lambda: signal({"seq": here + 2}))
    ends = jnp.where(place > 0, 1, 0) + jnp.where(place < places - 1, 1, 0)
    pl.semaphore_wait(barrier, 1 + len(others) + ends + more)


class SeqSum:
    def __init__(self, places, own, out, scratch):
        self.places, self.own, self.out = places, own, out
        self.y_in, self.p_left, self.p_right, self.p_acc = scratch[0:4]
        self.q_left, self.q_right, self.q_acc, self.q_in = scratch[4:8]
        self.sems = scratch[8]
        here = lax.axis_index("seq")
        self.place, self.side = here // 2, here % 2

    def remote(self, src, dst, slot, send, recv, place, side):
        return pltpu.make_async_remote_copy(
            src_ref=src,
            dst_ref=dst,
            send_sem=self.sems.at[send, slot],
            recv_sem=self.sems.at[recv, slot],
            device_id={"seq": place * 2 + side},
            device_id_type=pl.DeviceIdType.MESH,
        )

    def chain(self, root):
        last = self.places - 1
        left = jnp.maximum(self.place - 1, 0)
        right = jnp.minimum(self.place + 1, last)
        from_left = (self.place <= root) & (self.place > 0)
        from_right = (self.place >= root) & (self.place < last)
        return left, right, from_left, from_right

    def p_stage(self, which, k):
        place, side = self.place, self.side
        own, out = self.own, self.out
        slot = lax.rem(k, SLOTS_IN_FLIGHT)
        base = pl.multiple_of(k * 4 * HALF, 4 * HALF)
        mine = pl.ds(pl.multiple_of(base + side * HALF, HALF), HALF)
        theirs = pl.ds(pl.multiple_of(base + (1 - side) * HALF, HALF), HALF)
        root = self.places // 2 - 1 + lax.rem(k, 2)
        left, right, from_left, from_right = self.chain(root)
        acc, y_in = self.p_acc.at[slot], self.y_in.at[slot]
        from_l, from_r = self.p_left.at[slot], self.p_right.at[slot]
        remote = functools.partial(functools.partial, self.remote)

        to_side = remote(own.at[theirs], y_in, slot, 0, 1, place, 1 - side)
        up_right = remote(acc, from_l, slot, 2, 3, right, side)
        up_left = remote(acc, from_r, slot, 2, 4, left, side)

        def down(src):
            return (
                remote(src, out.at[mine], slot, 5, 7, left, side),
                remote(src, out.at[mine], slot, 6, 7, right, side),
                remote(src, out.at[mine], slot, 8, 9, place, 1 - side),
            )

        def keep():
            return pltpu.make_async_copy(acc, out.at[mine], self.sems.at[10, slot])

        def hand_down(src):
            down_left, down_right, down_side = down(src)
            down_side().start()
            pl.when(from_left)(lambda: down_left().start())
            pl.when(from_right)(lambda: down_right().start())

        if which == "split":
            to_side().start()

        if which == "up":
            to_side().wait_recv()
            acc[...] = own[mine, :] + y_in[...]

            @pl.when(place < root)
            def _():
                @pl.when(from_left)
                def _():
                    up_right().wait_recv()
                    acc[...] += from_l[...]

                up_right().start()

            @pl.when(place > root)
            def _():
                @pl.when(from_right)
                def _():
                    up_left().wait_recv()
                    acc[...] += from_r[...]

                up_left().start()

        if which == "root":

            @pl.when(place == root)
            def _():
                @pl.when(from_left)
                def _():
                    up_right().wait_recv()
                    acc[...] += from_l[...]

                @pl.when(from_right)
                def _():
                    up_left().wait_recv()
                    acc[...] += from_r[...]

                hand_down(acc)
                keep().start()

        if which == "down":

            @pl.when(place != root)
            def _():
                down(acc)[0]().wait_recv()
                hand_down(out.at[mine])

        if which == "end":
            down_left, down_right, down_side = down(acc)
            down_side().wait()
            to_side().wait_send()
            pl.when(from_left)(lambda: down_left().wait_send())
            pl.when(from_right)(lambda: down_right().wait_send())
            pl.when(place == root)(lambda: keep().wait())
            pl.when(place != root)(lambda: up_left().wait_send())

    def q_stage(self, which, k):
        place, side = self.place, self.side
        own, out = self.own, self.out
        slot = lax.rem(k, SLOTS_IN_FLIGHT)
        base = pl.multiple_of(k * 4 * HALF, 4 * HALF)
        wide = pl.ds(pl.multiple_of(base + 2 * HALF, 2 * HALF), 2 * HALF)
        root = self.places // 2 - lax.rem(k, 2)
        left, right, from_left, from_right = self.chain(root)
        acc, side_in = self.q_acc.at[slot], self.q_in.at[slot]
        from_l, from_r = self.q_left.at[slot], self.q_right.at[slot]
        remote = functools.partial(functools.partial, self.remote)

        up_right = remote(acc, from_l, slot, 11, 12, right, side)
        up_left = remote(acc, from_r, slot, 11, 13, left, side)
        to_side = remote(acc, side_in, slot, 14, 15, place, 1 - side)

        def down(src):
            return (
                remote(src, out.at[wide], slot, 16, 18, left, side),
                remote(src, out.at[wide], slot, 17, 18, right, side),
            )

        def keep():
            return pltpu.make_async_copy(side_in, out.at[wide], self.sems.at[19, slot])

        def hand_down(src):
            down_left, down_right = down(src)
            pl.when(from_left)(lambda: down_left().start())
            pl.when(from_right)(lambda: down_right().start())

        if which == "up":
            acc[...] = own[wide, :]

            @pl.when(place < root)
            def _():
                @pl.when(from_left)
                def _():
                    up_right().wait_recv()
                    acc[...] += from_l[...]

                up_right().start()

            @pl.when(place > root)
            def _():
                @pl.when(from_right)
                def _():
                    up_left().wait_recv()
                    acc[...] += from_r[...]

                up_left().start()

        if which == "root":

            @pl.when(place == root)
            def _():
                @pl.when(from_left)
                def _():
                    up_right().wait_recv()
                    acc[...] += from_l[...]

                @pl.when(from_right)
                def _():
                    up_left().wait_recv()
                    acc[...] += from_r[...]

                to_side().start()

        if which == "side":

            @pl.when(place == root)
            def _():
                to_side().wait_recv()
                side_in[...] += acc[...]
                hand_down(side_in)
                keep().start()

        if which == "down":

            @pl.when(place != root)
            def _():
                down(acc)[0]().wait_recv()
                hand_down(out.at[wide])

        if which == "end":
            down_left, down_right = down(acc)
            pl.when(from_left)(lambda: down_left().wait_send())
            pl.when(from_right)(lambda: down_right().wait_send())

            @pl.when(place == root)
            def _():
                to_side().wait_send()
                keep().wait()

            pl.when(place != root)(lambda: up_left().wait_send())

    P_LAGS = (("split", 0, 0), ("up", 2, 1), ("root", 3, 3), ("down", 6, 7), ("end", 9, 9))
    Q_LAGS = (("up", 1, 0), ("root", 2, 2), ("side", 4, 4), ("down", 6, 7), ("end", 9, 9))

    def tick(self, t, count):
        middle = (self.place == self.places // 2) | (self.place == self.places // 2 - 1)
        for stage, lags in ((self.p_stage, self.P_LAGS), (self.q_stage, self.Q_LAGS)):
            for which, mid_lag, outer_lag in lags:
                k = t - jnp.where(middle, mid_lag, outer_lag)

                @pl.when((k >= 0) & (k < count))
                def _(stage=stage, which=which, k=k):
                    stage(which, k)

    def run(self, count):
        @pl.loop(0, count + self.P_LAGS[-1][1])
        def _(t):
            self.tick(t, count)


def seq_sum_scratch():
    half = pltpu.VMEM((SLOTS_IN_FLIGHT, HALF, LANES), jnp.float32)
    wide = pltpu.VMEM((SLOTS_IN_FLIGHT, 2 * HALF, LANES), jnp.float32)
    return [half] * 4 + [wide] * 4 + [pltpu.SemaphoreType.DMA((20, SLOTS_IN_FLIGHT))]


FFN_PIECES = 36
FFN_PARTS = 3
ROW_BLOCK = 512
OUT_BLOCK = 256


def ffn_kernel(places, *refs):
    (mid_hbm, mid_t_hbm, cot_hbm, cot_t_hbm, w_gu_hbm, w_d_hbm) = refs[0:6]
    (sums, rest, mid_chip, mid_far, ffn_chip, mid_land, ffn_land) = refs[6:13]
    (mid, mid_t, cot, cot_t, w_gu, w_d, act, ggu, own, staged, fetched) = refs[13:24]
    load_sems, near_sems, far_sems, keep_sem, fetch_sem = refs[24:29]
    summer = SeqSum(places, own, sums, refs[29:])
    tp_at = lax.axis_index("tp")
    core = lax.rem(tp_at, 2)
    sibling = tp_at + 1 - 2 * core
    across = lax.rem(tp_at + 2, 4)
    rows, width = mid.shape
    parts, _, wide = w_gu.shape
    hidden = wide // 2
    panels = 3 * hidden // LANES

    loads = [
        pltpu.make_async_copy(src, dst, load_sems.at[i])
        for i, (src, dst) in enumerate(
            (
                (mid_hbm, mid),
                (w_gu_hbm, w_gu),
                (cot_hbm, cot),
                (w_d_hbm, w_d),
                (mid_t_hbm, mid_t),
                (cot_t_hbm, cot_t),
            )
        )
    ]
    for load in loads:
        load.start()
    greet_seq(places, ({"tp": sibling}, {"tp": across}))
    count = FFN_PIECES
    for load in loads[:4]:
        load.wait()

    def part_cols(c):
        return pl.ds(pl.multiple_of(c * hidden, LANES), hidden)

    @pl.loop(0, parts)
    def _(c):
        @pl.loop(0, rows // ROW_BLOCK)
        def _(r):
            at = pl.ds(pl.multiple_of(r * ROW_BLOCK, ROW_BLOCK), ROW_BLOCK)
            both = jnp.dot(mid[at, :], w_gu[c], preferred_element_type=jnp.float32)
            gate, up = both[:, :hidden], both[:, hidden:]
            grad_act = dot_cols(cot[at, :], w_d[c])
            sigmoid = 1.0 / (1.0 + jnp.exp(-gate))
            silu = gate * sigmoid
            act[at, part_cols(c)] = (silu * up).astype(jnp.bfloat16)
            slope = sigmoid * (1.0 + gate * (1.0 - sigmoid))
            ggu[c, at, :hidden] = (grad_act * up * slope).astype(jnp.bfloat16)
            ggu[c, at, hidden:] = (grad_act * silu).astype(jnp.bfloat16)

        @pl.when(c == 0)
        def _():
            for load in loads[4:]:
                load.wait()

        @pl.loop(0, width // OUT_BLOCK)
        def _(m):
            first = pl.multiple_of(m * OUT_BLOCK, OUT_BLOCK)
            at = pl.ds(first, OUT_BLOCK)
            base = c * (panels * width) + first

            def put(block, panel):
                for j in range(block.shape[1] // LANES):
                    to = pl.multiple_of(base + (panel + j) * width, OUT_BLOCK)
                    own[pl.ds(to, OUT_BLOCK), :] = block[:, j * LANES : (j + 1) * LANES]

            put(jnp.dot(mid_t[at, :], ggu[c], preferred_element_type=jnp.float32), 0)
            put(
                jnp.dot(cot_t[at, :], act[:, part_cols(c)], preferred_element_type=jnp.float32),
                wide // LANES,
            )

            @pl.when(c > 0)
            def _():
                summer.tick((c - 1) * (width // OUT_BLOCK) + m, count)

    early = (parts - 1) * (width // OUT_BLOCK)
    blocks = rows // 2 // OUT_BLOCK
    for_later = pltpu.make_async_copy(
        own.at[pl.ds(count * 4 * HALF, rest.shape[0])], rest, load_sems.at[0]
    )
    for_later.start()

    def row_block(half, k):
        return pl.ds(pl.multiple_of((half * blocks + k) * OUT_BLOCK, OUT_BLOCK), OUT_BLOCK)

    def mid_part(at):
        return sum(dot_cols(ggu[c, at, :], w_gu[c]) for c in range(parts))

    def ffn_part(at):
        return sum(
            jnp.dot(
                act[at, c * hidden : (c + 1) * hidden],
                w_d[c],
                preferred_element_type=jnp.float32,
            )
            for c in range(parts)
        )

    def near(which, land, k):
        return pltpu.make_async_remote_copy(
            src_ref=staged.at[lax.rem(k, 2)],
            dst_ref=land.at[row_block(0, k)],
            send_sem=near_sems.at[which, 0, k],
            recv_sem=near_sems.at[which, 1, k],
            device_id={"tp": sibling},
            device_id_type=pl.DeviceIdType.MESH,
        )

    def far(k):
        return pltpu.make_async_remote_copy(
            src_ref=mid_chip.at[row_block(0, k)],
            dst_ref=mid_far.at[row_block(0, k)],
            send_sem=far_sems.at[0, k],
            recv_sem=far_sems.at[1, k],
            device_id={"tp": across},
            device_id_type=pl.DeviceIdType.MESH,
        )

    def tp_sum(which, part, land, chip, first_tick):
        @pl.loop(0, blocks)
        def _(k):
            @pl.when(k >= 2)
            def _():
                near(which, land, k - 2).wait_send()

            staged[lax.rem(k, 2)] = part(row_block(1 - core, k))
            near(which, land, k).start()

        for k in range(max(blocks - 2, 0), blocks):
            near(which, land, k).wait_send()

        @pl.loop(0, blocks)
        def _(k):
            near(which, land, k).wait_recv()
            fetch = pltpu.make_async_copy(land.at[row_block(0, k)], fetched, fetch_sem)
            fetch.start()
            staged[0] = part(row_block(core, k))
            fetch.wait()
            staged[0] += fetched[...]
            keep = pltpu.make_async_copy(staged.at[0], chip.at[row_block(0, k)], keep_sem)
            keep.start()
            summer.tick(first_tick + k, count)
            keep.wait()
            if which == 0:
                far(k).start()

    tp_sum(0, mid_part, mid_land, mid_chip, early)
    tp_sum(1, ffn_part, ffn_land, ffn_chip, early + blocks)

    @pl.loop(early + 2 * blocks, count + summer.P_LAGS[-1][1])
    def _(t):
        summer.tick(t, count)

    for_later.wait()

    @pl.loop(0, blocks)
    def _(k):
        far(k).wait()


def ffn_both_ways(normed_mid, grad_ffn, w_gate, w_up, w_down, collective_id):
    rows, width = normed_mid.shape
    local = w_gate.shape[1]
    hidden = local // FFN_PARTS

    def in_parts(weights):
        return weights.reshape(width, FFN_PARTS, hidden)

    w_gu = jnp.concatenate([in_parts(w_gate), in_parts(w_up)], axis=2).transpose(1, 0, 2)
    w_d = w_down.reshape(FFN_PARTS, hidden, width)
    grad_rows = 3 * local * width // LANES
    summed = FFN_PIECES * 4 * HALF
    half = jax.ShapeDtypeStruct((rows // 2, width), jnp.float32)
    low = jnp.bfloat16
    blocks = rows // 2 // OUT_BLOCK
    return pl.pallas_call(
        functools.partial(ffn_kernel, lax.axis_size("seq") // 2),
        out_shape=[
            jax.ShapeDtypeStruct((summed, LANES), jnp.float32),
            jax.ShapeDtypeStruct((grad_rows - summed, LANES), jnp.float32),
        ]
        + [half] * 5,
        in_specs=[pl.BlockSpec(memory_space=pl.ANY)] * 6,
        out_specs=[pl.BlockSpec(memory_space=pl.ANY)] * 7,
        scratch_shapes=[
            pltpu.VMEM((rows, width), low),
            pltpu.VMEM((width, rows), low),
            pltpu.VMEM((rows, width), low),
            pltpu.VMEM((width, rows), low),
            pltpu.VMEM(w_gu.shape, low),
            pltpu.VMEM(w_d.shape, low),
            pltpu.VMEM((rows, local), low),
            pltpu.VMEM((FFN_PARTS, rows, 2 * hidden), low),
            pltpu.VMEM((grad_rows, LANES), jnp.float32),
            pltpu.VMEM((2, OUT_BLOCK, width), jnp.float32),
            pltpu.VMEM((OUT_BLOCK, width), jnp.float32),
            pltpu.SemaphoreType.DMA((6,)),
            pltpu.SemaphoreType.DMA((2, 2, blocks)),
            pltpu.SemaphoreType.DMA((2, blocks)),
            pltpu.SemaphoreType.DMA,
            pltpu.SemaphoreType.DMA,
        ]
        + seq_sum_scratch(),
        compiler_params=pltpu.CompilerParams(
            collective_id=collective_id, has_side_effects=True, vmem_limit_bytes=VMEM_LIMIT
        ),
        cost_estimate=pl.CostEstimate(
            flops=18 * rows * width * local, bytes_accessed=800 << 20, transcendentals=0
        ),
        name="ffn_both_ways",
    )(normed_mid, normed_mid.T, grad_ffn, grad_ffn.T, w_gu, w_d)


def gather_kernel(places, w_in, w_out, taps, full_in, full_out, full_taps, *scratch):
    own_in, own_out, far_in, far_out, sib_in, sib_out, sibfar_in, sibfar_out = scratch[0:8]
    own_taps, far_taps, sib_taps, sibfar_taps, share_in, share_out = scratch[8:14]
    sends, recvs, once = scratch[14:17]
    here = lax.axis_index("seq")
    place, side = here // 2, lax.rem(here, 2)
    last = places - 1
    tp_at = lax.axis_index("tp")
    core = lax.rem(tp_at, 2)
    sibling = tp_at + 1 - 2 * core
    across = lax.rem(tp_at + 2, 4)
    far_sibling = sibling + across - tp_at
    in_rows = w_in.shape[0] // (2 * places)
    out_rows = w_out.shape[0] // (2 * places)
    chans = w_in.shape[1] // 3
    width = w_out.shape[1]

    greet_seq(places, ({"tp": sibling}, {"tp": across}))

    def shares(j):
        return (
            pl.ds(pl.multiple_of(j * in_rows, in_rows), in_rows),
            pl.ds(pl.multiple_of(j * out_rows, out_rows), out_rows),
        )

    def copies(source, target, j, kind, device):
        for i, at in enumerate(shares(j)):
            yield pltpu.make_async_remote_copy(
                src_ref=source[i] if kind == 0 else source[i].at[at],
                dst_ref=target[i].at[at],
                send_sem=sends.at[kind, i, j],
                recv_sem=recvs.at[0 if kind < 4 else 1, i, j],
                device_id=device,
                device_id_type=pl.DeviceIdType.MESH,
            )

    share, far, sibfar = (share_in, share_out), (far_in, far_out), (sibfar_in, sibfar_out)

    def across_share():
        return copies(share, far, here, 0, {"tp": across})

    def to_right(j):
        return copies(far, far, j, 1, {"seq": here + 2})

    def to_left(j):
        return copies(far, far, j, 2, {"seq": here - 2})

    def to_side(j):
        return copies(far, far, j, 3, {"seq": here + 1 - 2 * side})

    def to_sibling(j):
        return copies(far, sibfar, j, 4, {"tp": sibling})

    def start(group):
        for copy in group:
            copy.start()

    def arrived(group):
        for copy in group:
            copy.wait_recv()

    def left_source(group):
        for copy in group:
            copy.wait_send()

    def single(i, src, dst, device):
        return pltpu.make_async_remote_copy(
            src_ref=src,
            dst_ref=dst,
            send_sem=once.at[0, i],
            recv_sem=once.at[1, i],
            device_id=device,
            device_id_type=pl.DeviceIdType.MESH,
        )

    for source, held, at in zip((w_in, w_out), share, shares(here)):
        held[...] = source[at, :].astype(jnp.float32)
    start(across_share())
    own_taps[...] = taps[...]
    taps_far = single(0, own_taps, far_taps, {"tp": across})
    taps_sib = single(1, own_taps, sib_taps, {"tp": sibling})
    taps_sibfar = single(2, far_taps, sibfar_taps, {"tp": sibling})
    own_in[...] = w_in[...].astype(jnp.float32)
    own_out[...] = w_out[...].astype(jnp.float32)
    in_sib = single(3, own_in, sib_in, {"tp": sibling})
    out_sib = single(4, own_out, sib_out, {"tp": sibling})
    for copy in (taps_far, taps_sib, in_sib, out_sib):
        copy.start()

    arrived(across_share())
    start(to_side(here))
    pl.when(place < last)(lambda: start(to_right(here)))
    pl.when(place > 0)(lambda: start(to_left(here)))
    start(to_sibling(here))
    taps_far.wait_recv()
    taps_sibfar.start()

    def place_shard(shard_in, shard_out, shard_taps, index):
        for g in range(3):
            cols = pl.ds(pl.multiple_of(g * width + index * chans, LANES), chans)
            full_in[:, cols] = shard_in[:, g * chans : (g + 1) * chans].astype(jnp.bfloat16)
        rows = pl.ds(pl.multiple_of(index * chans, chans), chans)
        full_out[rows, :] = shard_out[...].astype(jnp.bfloat16)
        cols = pl.ds(pl.multiple_of(index * chans, LANES), chans)
        full_taps[:, cols] = shard_taps[...]

    def from_side(q):
        j = 2 * q + 1 - side
        arrived(to_side(j))
        start(to_sibling(j))

    @pl.loop(1, places)
    def _(d):
        @pl.when(place - d >= 0)
        def _():
            j = here - 2 * d
            arrived(to_right(j))
            pl.when(place < last)(lambda: start(to_right(j)))
            start(to_side(j))
            start(to_sibling(j))

        @pl.when(place + d <= last)
        def _():
            j = here + 2 * d
            arrived(to_left(j))
            pl.when(place > 0)(lambda: start(to_left(j)))
            start(to_side(j))
            start(to_sibling(j))

        @pl.when(d == 1)
        def _():
            from_side(place)
            place_shard(own_in, own_out, own_taps, tp_at)
            in_sib.wait_recv()
            out_sib.wait_recv()
            taps_sib.wait_recv()
            place_shard(sib_in, sib_out, sib_taps, sibling)

        pl.when(place - d >= 0)(lambda: from_side(place - d))
        pl.when(place + d <= last)(lambda: from_side(place + d))

    place_shard(far_in, far_out, far_taps, across)
    taps_sibfar.wait_recv()

    @pl.loop(0, 2 * places)
    def _(j):
        arrived(to_sibling(j))

    place_shard(sibfar_in, sibfar_out, sibfar_taps, far_sibling)

    left_source(across_share())
    for copy in (taps_far, taps_sib, taps_sibfar, in_sib, out_sib):
        copy.wait_send()

    @pl.loop(0, places)
    def _(q):
        j = 2 * q + side
        left_source(to_side(j))
        pl.when((q <= place) & (place < last))(lambda: left_source(to_right(j)))
        pl.when((q >= place) & (place > 0))(lambda: left_source(to_left(j)))
        left_source(to_sibling(j))
        left_source(to_sibling(2 * q + 1 - side))


def gather_mixer(w_in, w_out, taps, collective_id):
    width, _, chans = w_in.shape
    count = lax.axis_size("seq")
    group = lax.axis_size("tp")
    f32 = jnp.float32
    pair = [pltpu.VMEM((width, 3 * chans), f32), pltpu.VMEM((chans, width), f32)]
    whole = pl.BlockSpec(memory_space=pltpu.VMEM)
    return pl.pallas_call(
        functools.partial(gather_kernel, count // 2),
        out_shape=[
            jax.ShapeDtypeStruct((width, 3 * chans * group), jnp.bfloat16),
            jax.ShapeDtypeStruct((chans * group, width), jnp.bfloat16),
            jax.ShapeDtypeStruct((8, chans * group), f32),
        ],
        in_specs=[whole] * 3,
        out_specs=[whole] * 3,
        scratch_shapes=pair * 4
        + [pltpu.VMEM((8, chans), f32)] * 4
        + [
            pltpu.VMEM((width // count, 3 * chans), f32),
            pltpu.VMEM((chans // count, width), f32),
        ]
        + [
            pltpu.SemaphoreType.DMA((5, 2, count)),
            pltpu.SemaphoreType.DMA((2, 2, count)),
            pltpu.SemaphoreType.DMA((2, 5)),
        ],
        compiler_params=pltpu.CompilerParams(
            collective_id=collective_id, has_side_effects=True, vmem_limit_bytes=48 << 20
        ),
        name="gather_mixer",
    )(w_in.reshape(width, 3 * chans), w_out, jnp.pad(taps, ((0, 5), (0, 0))))


SUB_ROWS = 64
SUB_COLS = 256


def norm_back(grad, gain, unit, scale):
    scaled = gain * grad
    return scale * (scaled - unit * jnp.mean(scaled * unit, axis=-1, keepdims=True))


def mixer_kernel(places, *refs):
    (rest_hbm, mid_chip, mid_far, ffn_chip, hidden_hbm, proj_hbm, gated_hbm) = refs[0:7]
    (normed_t_hbm, mixed_t_hbm, w_in_hbm, w_out_hbm, cot_hbm, tokens_hbm) = refs[7:13]
    (valid, taps, gain_mix, gain_ffn) = refs[13:17]
    (sums, tokens_out, block_out, ffn_far, land_in, land_out, land_small) = refs[17:24]
    (own, normed_t, mixed_t, w_in, w_out, cot, tokens, grad_mixer, grad_proj) = refs[24:33]
    (chip, far, hidden, proj, gated, mixed_buf, conv_in, grad_hid, grad_tok) = refs[33:42]
    (halo_out, halo_in, halo_keep, small, small_stage, small_fetch) = refs[42:48]
    (stage_in, fetch_in, stage_out, fetch_out) = refs[48:52]
    (load_sems, row_sems, halo_sems, near_sems, far_sems, out_sems) = refs[52:58]
    summer = SeqSum(places, own, sums, refs[58:])
    here = lax.axis_index("seq")
    last = 2 * places - 1
    tp_at = lax.axis_index("tp")
    core = lax.rem(tp_at, 2)
    sibling = tp_at + 1 - 2 * core
    across = lax.rem(tp_at + 2, 4)
    rows, width = tokens.shape
    slots = halo_in.shape[0]
    slot_len = rows // slots
    per_slot = slot_len // OUT_BLOCK
    blocks = rows // OUT_BLOCK
    chans = w_out.shape[0] // 4
    count = own.shape[0] // (4 * HALF)
    early_rows = rest_hbm.shape[0]

    loads = [
        pltpu.make_async_copy(src, dst, load_sems.at[i])
        for i, (src, dst) in enumerate(
            (
                (rest_hbm, own.at[pl.ds(0, early_rows)]),
                (cot_hbm, cot),
                (w_out_hbm, w_out),
                (tokens_hbm, tokens),
                (w_in_hbm, w_in),
                (normed_t_hbm, normed_t),
                (mixed_t_hbm, mixed_t),
            )
        )
    ]
    for load in loads:
        load.start()

    def place_of(n):
        slot = n // per_slot
        block = per_slot - 1 - lax.rem(n, per_slot)
        return slot, block, pl.multiple_of(slot * slot_len + block * OUT_BLOCK, OUT_BLOCK)

    def mid_loads(first):
        at = pl.ds(first, OUT_BLOCK)
        return [
            pltpu.make_async_copy(src.at[at], dst, row_sems.at[i])
            for i, (src, dst) in enumerate(((mid_chip, chip), (mid_far, far), (hidden_hbm, hidden)))
        ]

    def proj_loads(slot, block, first):
        return [
            pltpu.make_async_copy(proj_hbm.at[pl.ds(first, OUT_BLOCK)], proj, row_sems.at[3]),
            pltpu.make_async_copy(
                gated_hbm.at[slot, pl.ds(pl.multiple_of(block * OUT_BLOCK, 8), OUT_BLOCK + 8)],
                gated,
                row_sems.at[4],
            ),
        ]

    def start(copies):
        for copy in copies:
            copy.start()

    def wait(copies):
        for copy in copies:
            copy.wait()

    def remote(src, dst, sems, i, device):
        return pltpu.make_async_remote_copy(
            src_ref=src,
            dst_ref=dst,
            send_sem=sems.at[0, i],
            recv_sem=sems.at[1, i],
            device_id=device,
            device_id_type=pl.DeviceIdType.MESH,
        )

    barrier = pltpu.get_barrier_semaphore()

    def signal(device):
        pl.semaphore_signal(barrier, inc=1, device_id=device, device_id_type=pl.DeviceIdType.MESH)

    pl.when(here > 0)(lambda: signal({"seq": here - 1}))
    pl.when(here < last)(lambda: signal({"seq": here + 1}))
    ends = jnp.where(here > 0, 1, 0) + jnp.where(here < last, 1, 0)
    greet_seq(places, ({"tp": sibling}, {"tp": across}), ends)

    def block_at(k):
        return pl.ds(pl.multiple_of(k * OUT_BLOCK, OUT_BLOCK), OUT_BLOCK)

    def ffn_across(k):
        at = block_at(k)
        return remote(ffn_chip.at[at], ffn_far.at[at], far_sems, k, {"tp": across})

    @pl.loop(0, blocks)
    def _(k):
        ffn_across(k).start()

    small[...] = jnp.zeros_like(small)
    wait(loads[:3])

    def hidden_grad(chip_rows, far_rows, hidden_rows, cot_rows):
        grad_mid = chip_rows + far_rows
        scale = rms_scale(hidden_rows)
        unit = hidden_rows * scale
        grad = cot_rows.astype(jnp.float32) + norm_back(grad_mid, gain_ffn[...], unit, scale)
        return grad, grad_mid * unit

    def halo_copy(slot, device):
        return remote(halo_out.at[slot], halo_in.at[slot], halo_sems, slot, {"seq": device})

    head = 16
    for slot in range(slots):
        at = pl.ds(slot * slot_len, head)
        top = pl.ds(0, head)
        copies = [
            pltpu.make_async_copy(src.at[at], dst, row_sems.at[i])
            for i, (src, dst) in enumerate(
                (
                    (mid_chip, chip.at[top]),
                    (mid_far, far.at[top]),
                    (hidden_hbm, hidden.at[top]),
                    (proj_hbm, proj.at[top]),
                )
            )
        ]
        start(copies)
        wait(copies)
        grad, _ = hidden_grad(chip[top, :], far[top, :], hidden[top, :], cot[at, :])
        grad_mixed = dot_cols(grad.astype(jnp.bfloat16), w_out[...])
        halo_out[slot] = (grad_mixed * proj[top, width : 2 * width])[:8]
        pl.when(here > 0)(lambda slot=slot: halo_copy(slot, here - 1).start())

    slot, block, first = place_of(0)
    start(mid_loads(first))
    start(proj_loads(slot, block, first))

    @pl.when(here == last)
    def _():
        halo_in[...] = jnp.zeros_like(halo_in)

    @pl.when(here < last)
    def _():
        for slot in range(slots):
            halo_copy(slot, here + 1).wait_recv()

    wait(loads[3:])

    def out_rows(first):
        return pl.ds(pl.multiple_of(core * rows + first, OUT_BLOCK), OUT_BLOCK)

    def hand_out(target, first, i):
        at = out_rows(first)
        return (
            pltpu.make_async_copy(grad_tok, target.at[at], out_sems.at[0, 2 * blocks]),
            remote(grad_tok, target.at[at], out_sems, i, {"tp": sibling}),
        )

    @pl.loop(0, blocks)
    def _(n):
        slot, block, first = place_of(n)
        at = pl.ds(first, OUT_BLOCK)
        wait(mid_loads(first))

        @pl.loop(0, OUT_BLOCK // SUB_ROWS)
        def _(r):
            sub = pl.ds(pl.multiple_of(r * SUB_ROWS, SUB_ROWS), SUB_ROWS)
            whole = pl.ds(pl.multiple_of(first + r * SUB_ROWS, SUB_ROWS), SUB_ROWS)
            grad, for_gain = hidden_grad(chip[sub, :], far[sub, :], hidden[sub, :], cot[whole, :])
            grad_hid[sub, :] = grad
            grad_mixer[whole, :] = grad.astype(jnp.bfloat16)
            small[1:2, :] += jnp.sum(for_gain, axis=0, keepdims=True)

        @pl.when(n < blocks - 1)
        def _():
            start(mid_loads(place_of(n + 1)[2]))

        mixed_buf[...] = dot_cols(grad_mixer[at, :], w_out[...])
        wait(proj_loads(slot, block, first))

        @pl.when(block == per_slot - 1)
        def _():
            conv_in[pl.ds(OUT_BLOCK, 8), :] = halo_in[slot]

        @pl.when(block < per_slot - 1)
        def _():
            conv_in[pl.ds(OUT_BLOCK, 8), :] = halo_keep[...]

        summer.tick(2 * n, count)
        mask = valid[at, :]

        @pl.loop(0, width // SUB_COLS)
        def _(c):
            def cols(gate):
                return pl.ds(pl.multiple_of(gate * width + c * SUB_COLS, SUB_COLS), SUB_COLS)

            here_cols = cols(0)
            in_gate, out_gate, conv_value = (proj[:, cols(g)] for g in range(3))
            grad_mixed = mixed_buf[:, here_cols]
            now = grad_mixed * out_gate
            conv_in[pl.ds(0, OUT_BLOCK), here_cols] = now
            seen = [gated[pl.ds(6 + j, OUT_BLOCK), here_cols] for j in range(3)]
            tap = [taps[j : j + 1, here_cols] for j in range(3)]
            conv_sum = tap[0] * seen[0] + tap[1] * seen[1] + tap[2] * seen[2]
            for j in range(3):
                small[2 + j : 3 + j, here_cols] += jnp.sum(now * seen[j], axis=0, keepdims=True)
            grad_proj[at, cols(1)] = (grad_mixed * conv_sum).astype(jnp.bfloat16)
            grad_gated = mask * (
                tap[2] * now
                + tap[1] * conv_in[pl.ds(1, OUT_BLOCK), here_cols]
                + tap[0] * conv_in[pl.ds(2, OUT_BLOCK), here_cols]
            )
            grad_proj[at, cols(0)] = (grad_gated * conv_value).astype(jnp.bfloat16)
            grad_proj[at, cols(2)] = (grad_gated * in_gate).astype(jnp.bfloat16)

        halo_keep[...] = conv_in[pl.ds(0, 8), :]

        @pl.when(n < blocks - 1)
        def _():
            start(proj_loads(*place_of(n + 1)))

        mixed_buf[...] = dot_cols(grad_proj[at, :], w_in[...])

        @pl.when(n > 0)
        def _():
            local, there = hand_out(tokens_out, place_of(n - 1)[2], n - 1)
            local.wait()
            there.wait_send()

        @pl.loop(0, OUT_BLOCK // SUB_ROWS)
        def _(r):
            sub = pl.ds(pl.multiple_of(r * SUB_ROWS, SUB_ROWS), SUB_ROWS)
            whole = pl.ds(pl.multiple_of(first + r * SUB_ROWS, SUB_ROWS), SUB_ROWS)
            inputs = tokens[whole, :].astype(jnp.float32)
            scale = rms_scale(inputs)
            unit = inputs * scale
            grad_in = mixed_buf[sub, :]
            grad_tok[sub, :] = grad_hid[sub, :] + norm_back(grad_in, gain_mix[...], unit, scale)
            small[0:1, :] += jnp.sum(grad_in * unit, axis=0, keepdims=True)

        start(hand_out(tokens_out, first, n))
        summer.tick(2 * n + 1, count)

    def near(src, dst, i):
        return remote(src, dst, near_sems, i, {"tp": sibling})

    in_blocks = width // OUT_BLOCK
    panels_in = 3 * chans // LANES

    def near_in(m):
        return near(stage_in.at[lax.rem(m, 2)], land_in.at[m], m)

    near_out = near(stage_out, land_out, in_blocks)
    near_small = near(small_stage, land_small, in_blocks + 1)

    def in_part(m, g, shard):
        at = pl.ds(pl.multiple_of(m * OUT_BLOCK, OUT_BLOCK), OUT_BLOCK)
        cols = pl.ds(pl.multiple_of(g * width + shard * chans, LANES), chans)
        return jnp.dot(normed_t[at, :], grad_proj[:, cols], preferred_element_type=jnp.float32)

    def out_part(shard):
        at = pl.ds(pl.multiple_of(shard * chans, chans), chans)
        return jnp.dot(mixed_t[at, :], grad_mixer[...], preferred_element_type=jnp.float32)

    for p in range(width // LANES):
        small_stage[8 * p : 8 * p + 8, :] = small[:, p * LANES : (p + 1) * LANES]
    near_small.start()
    halves = chans // LANES

    @pl.loop(0, in_blocks)
    def _(m):
        @pl.when(m >= 2)
        def _():
            near_in(m - 2).wait_send()

        for g in range(3):
            part = in_part(m, g, sibling)
            for h in range(halves):
                stage_in[lax.rem(m, 2), g * halves + h] = part[:, h * LANES : (h + 1) * LANES]
        near_in(m).start()
        summer.tick(2 * blocks + m, count)

    part = out_part(sibling)
    for p in range(width // LANES):
        stage_out[p] = part[:, p * LANES : (p + 1) * LANES]
    near_out.start()

    @pl.loop(0, in_blocks)
    def _(m):
        near_in(m).wait_recv()
        fetch = pltpu.make_async_copy(land_in.at[m], fetch_in, row_sems.at[0])
        fetch.start()
        parts = [in_part(m, g, tp_at) for g in range(3)]
        fetch.wait()
        for g in range(3):
            for h in range(halves):
                i = g * halves + h
                to = pl.multiple_of(early_rows + i * width + m * OUT_BLOCK, OUT_BLOCK)
                own[pl.ds(to, OUT_BLOCK), :] = (
                    parts[g][:, h * LANES : (h + 1) * LANES] + fetch_in[i]
                )

        summer.tick(2 * blocks + in_blocks + m, count)

    near_out.wait_recv()
    near_small.wait_recv()
    fetches = [
        pltpu.make_async_copy(land_out, fetch_out, row_sems.at[0]),
        pltpu.make_async_copy(land_small, small_fetch, row_sems.at[1]),
    ]
    start(fetches)
    part = out_part(tp_at)
    wait(fetches)
    out_first = early_rows + panels_in * width
    for p in range(width // LANES):
        own[pl.ds(out_first + p * chans, chans), :] = (
            part[:, p * LANES : (p + 1) * LANES] + fetch_out[p]
        )
    small_first = out_first + width // LANES * chans
    small_rows = small_stage.shape[0]
    own[pl.ds(small_first, small_rows), :] = small_stage[...] + small_fetch[...]
    unused = own.shape[0] - small_first - small_rows
    own[pl.ds(small_first + small_rows, unused), :] = jnp.zeros((unused, LANES), jnp.float32)

    local, there = hand_out(tokens_out, place_of(blocks - 1)[2], blocks - 1)
    local.wait()
    there.wait_send()
    done = 2 * blocks + 2 * in_blocks
    pause = min(done + 10, count)

    @pl.loop(done, pause)
    def _(t):
        summer.tick(t, count)

    @pl.loop(0, blocks)
    def _(k):
        ffn_across(k).wait_recv()
        at = block_at(k)
        copies = [
            pltpu.make_async_copy(src.at[at], dst, row_sems.at[i])
            for i, (src, dst) in enumerate(((ffn_chip, chip), (ffn_far, far), (hidden_hbm, hidden)))
        ]
        start(copies)

        @pl.when(k > 0)
        def _():
            local, there = hand_out(block_out, (k - 1) * OUT_BLOCK, blocks + k - 1)
            local.wait()
            there.wait_send()

        wait(copies)
        grad_tok[...] = hidden[...] + (chip[...] + far[...])
        start(hand_out(block_out, k * OUT_BLOCK, blocks + k))
        summer.tick(pause + k, count)

    @pl.loop(pause + blocks, count + summer.P_LAGS[-1][1])
    def _(t):
        summer.tick(t, count)

    local, there = hand_out(block_out, (blocks - 1) * OUT_BLOCK, 2 * blocks - 1)
    local.wait()
    there.wait_send()

    @pl.loop(0, blocks)
    def _(k):
        ffn_across(k).wait_send()
        hand_out(tokens_out, place_of(k)[2], k)[1].wait_recv()
        hand_out(block_out, k * OUT_BLOCK, blocks + k)[1].wait_recv()

    for m in range(max(in_blocks - 2, 0), in_blocks):
        near_in(m).wait_send()
    near_out.wait_send()
    near_small.wait_send()

    @pl.when(here > 0)
    def _():
        for slot in range(slots):
            halo_copy(slot, here - 1).wait_send()


def mixer_back(hbm, vmem, slots, collective_id):
    rest, _, _, _, hidden, _, gated, normed_t, mixed_t, w_in, w_out, _, tokens = hbm
    rows, width = tokens.shape
    chans = w_out.shape[0] // 4
    blocks = rows // OUT_BLOCK
    in_blocks = width // OUT_BLOCK
    f32, low = jnp.float32, jnp.bfloat16
    panels_in = 3 * chans // LANES
    grad_rows = rest.shape[0] + panels_in * width + width // LANES * chans + 4 * HALF
    small_rows = 8 * width // LANES
    block = pltpu.VMEM((OUT_BLOCK, width), f32)
    full = jax.ShapeDtypeStruct((2 * rows, width), f32)
    anywhere = pl.BlockSpec(memory_space=pl.ANY)
    return pl.pallas_call(
        functools.partial(mixer_kernel, lax.axis_size("seq") // 2),
        out_shape=[
            jax.ShapeDtypeStruct((grad_rows, LANES), f32),
            full,
            full,
            jax.ShapeDtypeStruct((rows, width), f32),
            jax.ShapeDtypeStruct((in_blocks, panels_in, OUT_BLOCK, LANES), f32),
            jax.ShapeDtypeStruct((width // LANES, chans, LANES), f32),
            jax.ShapeDtypeStruct((small_rows, LANES), f32),
        ],
        in_specs=[anywhere] * len(hbm) + [pl.BlockSpec(memory_space=pltpu.VMEM)] * len(vmem),
        out_specs=[anywhere] * 7,
        scratch_shapes=[
            pltpu.VMEM((grad_rows, LANES), f32),
            pltpu.VMEM(normed_t.shape, low),
            pltpu.VMEM(mixed_t.shape, low),
            pltpu.VMEM(w_in.shape, low),
            pltpu.VMEM(w_out.shape, low),
            pltpu.VMEM((rows, width), low),
            pltpu.VMEM((rows, width), low),
            pltpu.VMEM((rows, width), low),
            pltpu.VMEM((rows, 3 * width), low),
            block,
            block,
            block,
            pltpu.VMEM((OUT_BLOCK, 3 * width), f32),
            pltpu.VMEM((OUT_BLOCK + 8, width), f32),
            block,
            pltpu.VMEM((OUT_BLOCK + 8, width), f32),
            block,
            block,
            pltpu.VMEM((slots, 8, width), f32),
            pltpu.VMEM((slots, 8, width), f32),
            pltpu.VMEM((8, width), f32),
            pltpu.VMEM((8, width), f32),
            pltpu.VMEM((small_rows, LANES), f32),
            pltpu.VMEM((small_rows, LANES), f32),
            pltpu.VMEM((2, panels_in, OUT_BLOCK, LANES), f32),
            pltpu.VMEM((panels_in, OUT_BLOCK, LANES), f32),
            pltpu.VMEM((width // LANES, chans, LANES), f32),
            pltpu.VMEM((width // LANES, chans, LANES), f32),
            pltpu.SemaphoreType.DMA((7,)),
            pltpu.SemaphoreType.DMA((5,)),
            pltpu.SemaphoreType.DMA((2, slots)),
            pltpu.SemaphoreType.DMA((2, in_blocks + 2)),
            pltpu.SemaphoreType.DMA((2, blocks)),
            pltpu.SemaphoreType.DMA((2, 2 * blocks + 1)),
        ]
        + seq_sum_scratch(),
        compiler_params=pltpu.CompilerParams(
            collective_id=collective_id, has_side_effects=True, vmem_limit_bytes=VMEM_LIMIT
        ),
        cost_estimate=pl.CostEstimate(
            flops=26 * rows * width * width, bytes_accessed=400 << 20, transcendentals=0
        ),
        name="mixer_back",
    )(*hbm, *vmem)


def from_panels(panels, rows, cols):
    return panels.reshape(cols // LANES, rows, LANES).transpose(1, 0, 2).reshape(rows, cols)


def per_device(
    tokens, lengths, gain_mix, w_in, conv_weight, w_out, gain_ffn, w_gate, w_up, w_down, cotangent
):
    slot_count, local_len, width = tokens.shape
    chans = w_in.shape[2]
    group = lax.axis_size("tp")
    seq_count = lax.axis_size("seq")
    tp_at, seq_at = lax.axis_index("tp"), lax.axis_index("seq")
    core, chip = tp_at % 2, tp_at // 2
    half_slots = slot_count // 2
    half_rows = half_slots * local_len
    row_count = slot_count * local_len

    def pick(is_first, first, second):
        return jnp.where(is_first, first, second)

    def both_cores(own, other):
        return jnp.concatenate(
            [pick(core == 0, own, other), pick(core == 0, other, own)], axis=0
        )

    w_in_all, w_out_all, taps = gather_mixer(w_in, w_out, conv_weight, 3)

    first_pos = seq_at * local_len
    positions = first_pos + jnp.arange(local_len, dtype=jnp.int32)
    valid = (positions[None, :] < lengths[:, None]).astype(jnp.float32)[:, :, None]
    valid_all = valid.reshape(row_count, 1)
    valid_own = lax.dynamic_slice(valid, (core * half_slots, 0, 0), (half_slots, local_len, 1))
    valid_rows = valid_own.reshape(half_rows, 1)
    tokens_own = lax.dynamic_slice(
        tokens, (core * half_slots, 0, 0), (half_slots, local_len, width)
    )
    inputs_f = tokens_own.astype(jnp.float32).reshape(half_rows, width)
    scale_mix = rms_scale(inputs_f)
    unit_mix = inputs_f * scale_mix
    normed_in = (gain_mix * unit_mix).astype(jnp.bfloat16)
    projected = jnp.dot(normed_in, w_in_all, preferred_element_type=jnp.float32)
    in_gate = projected[:, :width]
    out_gate = projected[:, width : 2 * width]
    conv_value = projected[:, 2 * width :]
    seq_shape = (half_slots, local_len, width)
    gated_seq = (valid_rows * in_gate * conv_value).reshape(seq_shape)
    carried = shift_seq(gated_seq[:, local_len - 2 :], 1)
    padded_seq = jnp.concatenate([carried, gated_seq], axis=1)
    conv_sum = (
        taps[0] * padded_seq[:, 0:local_len]
        + taps[1] * padded_seq[:, 1 : local_len + 1]
        + taps[2] * padded_seq[:, 2 : local_len + 2]
    ).reshape(half_rows, width)
    mixed_seq = (out_gate * conv_sum).astype(jnp.bfloat16)
    mixer_out = jnp.dot(mixed_seq, w_out_all, preferred_element_type=jnp.float32)
    hidden_res = inputs_f + mixer_out
    scale_ffn = rms_scale(hidden_res)
    unit_ffn = hidden_res * scale_ffn
    unit_all = both_cores(unit_ffn, swap_tp(unit_ffn, 1))
    normed_mid = (gain_ffn * unit_all).astype(jnp.bfloat16)

    grad_out = valid_all * cotangent.astype(jnp.float32).reshape(row_count, width)
    grad_ffn = grad_out.astype(jnp.bfloat16)
    ffn_sums, rest, mid_chip, mid_far, ffn_chip = ffn_both_ways(
        normed_mid, grad_ffn, w_gate, w_up, w_down, 1
    )[:5]
    cot_own = lax.dynamic_slice(grad_ffn, (core * half_rows, 0), (half_rows, width))
    lead = jnp.zeros((half_slots, 6, width), jnp.float32)
    gated_rows = jnp.concatenate([lead, padded_seq], axis=1)
    mixer_sums, grad_tokens, block_sum = mixer_back(
        (
            rest,
            mid_chip,
            mid_far,
            ffn_chip,
            hidden_res,
            projected,
            gated_rows,
            normed_in.T,
            mixed_seq.T,
            w_in_all,
            w_out_all,
            cot_own,
            tokens_own.reshape(half_rows, width),
        ),
        (valid_rows, taps, gain_mix.reshape(1, width), gain_ffn.reshape(1, width)),
        half_slots,
        2,
    )[:3]
    grad_tokens = grad_tokens.reshape(slot_count, local_len, width)
    block_out = (valid_all * block_sum).astype(jnp.bfloat16)
    block_out = block_out.reshape(slot_count, local_len, width)

    hidden = w_gate.shape[1]
    ffn_sums = jnp.concatenate([ffn_sums, mixer_sums[: rest.shape[0]]], axis=0)
    mixer_sums = mixer_sums[rest.shape[0] :]
    by_part = ffn_sums.reshape(FFN_PARTS, 3, hidden // FFN_PARTS // LANES, width, LANES)
    total_w_gate = by_part[:, 0].transpose(2, 0, 1, 3).reshape(width, hidden)
    total_w_up = by_part[:, 1].transpose(2, 0, 1, 3).reshape(width, hidden)
    total_w_down = by_part[:, 2].transpose(0, 1, 3, 2).reshape(hidden, width)
    in_rows = width * 3 * chans // LANES
    out_rows = width * chans // LANES
    total_w_in = from_panels(mixer_sums[:in_rows], width, 3 * chans).reshape(width, 3, chans)
    total_w_out = from_panels(mixer_sums[in_rows : in_rows + out_rows], chans, width)
    small = mixer_sums[in_rows + out_rows :][: 8 * width // LANES]
    small = small.reshape(width // LANES, 8, LANES).transpose(1, 0, 2).reshape(8, width)
    total_gain_mix, total_gain_ffn = small[0], small[1]
    total_conv = lax.dynamic_slice(small, (2, tp_at * chans), (3, chans))
    return (
        block_out,
        grad_tokens,
        total_gain_mix,
        total_w_in,
        total_conv,
        total_w_out,
        total_gain_ffn,
        total_w_gate,
        total_w_up,
        total_w_down,
    )


def solution(mesh):
    rows, cols = P("tp", None), P(None, "tp")
    tokens, whole, stacked = P(None, "seq", None), P(), P(None, None, "tp")
    return jax.shard_map(
        per_device,
        mesh=mesh,
        in_specs=(
            tokens, whole, whole, stacked, cols, rows, whole, cols, cols, rows, tokens,
        ),
        out_specs=(
            tokens, tokens, whole, stacked, cols, rows, whole, cols, cols, rows,
        ),
        check_vma=False,
    )
```

```python
import functools

import jax
import jax.numpy as jnp
from jax import lax
from jax.experimental import pallas as pl
from jax.experimental.pallas import tpu as pltpu
from jax.sharding import PartitionSpec as P

NORM_EPS = 1e-05
LANES = 128
VMEM_LIMIT = 64 << 20
HALF = 128
SLOTS_IN_FLIGHT = 10


def rms_scale(values):
    return lax.rsqrt(jnp.mean(values * values, axis=-1, keepdims=True) + NORM_EPS)


def dot_rows(left, right):
    return lax.dot_general(
        left, right, (((0,), (0,)), ((), ())), preferred_element_type=jnp.float32
    )


def dot_cols(left, right):
    return lax.dot_general(
        left, right, (((1,), (1,)), ((), ())), preferred_element_type=jnp.float32
    )


def shift_seq(block, distance):
    count = lax.axis_size("seq")
    route = [(i - distance, i) for i in range(count) if 0 <= i - distance < count]
    return lax.ppermute(block, "seq", route)


def swap_tp(block, bit):
    return lax.ppermute(block, "tp", [(i, i ^ bit) for i in range(lax.axis_size("tp"))])


def greet_seq(places, others=(), more=0):
    barrier = pltpu.get_barrier_semaphore()
    here = lax.axis_index("seq")
    place, side = here // 2, lax.rem(here, 2)

    def signal(device):
        pl.semaphore_signal(
            barrier, inc=1, device_id=device, device_id_type=pl.DeviceIdType.MESH
        )

    signal({"seq": here + 1 - 2 * side})
    for other in others:
        signal(other)
    pl.when(place > 0)(lambda: signal({"seq": here - 2}))
    pl.when(place < places - 1)(lambda: signal({"seq": here + 2}))
    ends = jnp.where(place > 0, 1, 0) + jnp.where(place < places - 1, 1, 0)
    pl.semaphore_wait(barrier, 1 + len(others) + ends + more)


class SeqSum:
    def __init__(self, places, own, out, panel_of, scratch):
        self.places, self.own, self.out, self.panel_of = places, own, out, panel_of
        self.y_in, self.p_left, self.p_right, self.p_acc = scratch[0:4]
        self.q_left, self.q_right, self.q_acc, self.q_in = scratch[4:8]
        self.sems = scratch[8]
        here = lax.axis_index("seq")
        self.place, self.side = here // 2, here % 2

    def remote(self, src, dst, slot, send, recv, place, side):
        return pltpu.make_async_remote_copy(
            src_ref=src,
            dst_ref=dst,
            send_sem=self.sems.at[send, slot],
            recv_sem=self.sems.at[recv, slot],
            device_id={"seq": place * 2 + side},
            device_id_type=pl.DeviceIdType.MESH,
        )

    def chain(self, root):
        last = self.places - 1
        left = jnp.maximum(self.place - 1, 0)
        right = jnp.minimum(self.place + 1, last)
        from_left = (self.place <= root) & (self.place > 0)
        from_right = (self.place >= root) & (self.place < last)
        return left, right, from_left, from_right

    def out_at(self, k, first, size):
        per_panel = self.out.shape[0] // (4 * HALF)
        panel = self.panel_of(k // per_panel)
        row = lax.rem(k, per_panel) * 4 * HALF + first
        return self.out.at[
            pl.ds(pl.multiple_of(row, size), size), pl.ds(pl.multiple_of(panel * LANES, LANES), LANES)
        ]

    def p_stage(self, which, k):
        place, side = self.place, self.side
        own = self.own
        slot = lax.rem(k, SLOTS_IN_FLIGHT)
        base = pl.multiple_of(k * 4 * HALF, 4 * HALF)
        mine = pl.ds(pl.multiple_of(base + side * HALF, HALF), HALF)
        theirs = pl.ds(pl.multiple_of(base + (1 - side) * HALF, HALF), HALF)
        out_mine = self.out_at(k, side * HALF, HALF)
        root = self.places // 2 - 1 + lax.rem(k, 2)
        left, right, from_left, from_right = self.chain(root)
        acc, y_in = self.p_acc.at[slot], self.y_in.at[slot]
        from_l, from_r = self.p_left.at[slot], self.p_right.at[slot]
        remote = functools.partial(functools.partial, self.remote)

        to_side = remote(own.at[theirs], y_in, slot, 0, 1, place, 1 - side)
        up_right = remote(acc, from_l, slot, 2, 3, right, side)
        up_left = remote(acc, from_r, slot, 2, 4, left, side)

        def down(src):
            return (
                remote(src, out_mine, slot, 5, 7, left, side),
                remote(src, out_mine, slot, 6, 7, right, side),
                remote(src, out_mine, slot, 8, 9, place, 1 - side),
            )

        def keep():
            return pltpu.make_async_copy(acc, out_mine, self.sems.at[10, slot])

        def hand_down(src):
            down_left, down_right, down_side = down(src)
            down_side().start()
            pl.when(from_left)(lambda: down_left().start())
            pl.when(from_right)(lambda: down_right().start())

        if which == "split":
            to_side().start()

        if which == "up":
            to_side().wait_recv()
            acc[...] = own[mine, :] + y_in[...]

            @pl.when(place < root)
            def _():
                @pl.when(from_left)
                def _():
                    up_right().wait_recv()
                    acc[...] += from_l[...]

                up_right().start()

            @pl.when(place > root)
            def _():
                @pl.when(from_right)
                def _():
                    up_left().wait_recv()
                    acc[...] += from_r[...]

                up_left().start()

        if which == "root":

            @pl.when(place == root)
            def _():
                @pl.when(from_left)
                def _():
                    up_right().wait_recv()
                    acc[...] += from_l[...]

                @pl.when(from_right)
                def _():
                    up_left().wait_recv()
                    acc[...] += from_r[...]

                hand_down(acc)
                keep().start()

        if which == "down":

            @pl.when(place != root)
            def _():
                down(acc)[0]().wait_recv()
                hand_down(out_mine)

        if which == "end":
            down_left, down_right, down_side = down(acc)
            down_side().wait()
            to_side().wait_send()
            pl.when(from_left)(lambda: down_left().wait_send())
            pl.when(from_right)(lambda: down_right().wait_send())
            pl.when(place == root)(lambda: keep().wait())
            pl.when(place != root)(lambda: up_left().wait_send())

    def q_stage(self, which, k):
        place, side = self.place, self.side
        own = self.own
        slot = lax.rem(k, SLOTS_IN_FLIGHT)
        base = pl.multiple_of(k * 4 * HALF, 4 * HALF)
        wide = pl.ds(pl.multiple_of(base + 2 * HALF, 2 * HALF), 2 * HALF)
        out_wide = self.out_at(k, 2 * HALF, 2 * HALF)
        root = self.places // 2 - lax.rem(k, 2)
        left, right, from_left, from_right = self.chain(root)
        acc, side_in = self.q_acc.at[slot], self.q_in.at[slot]
        from_l, from_r = self.q_left.at[slot], self.q_right.at[slot]
        remote = functools.partial(functools.partial, self.remote)

        up_right = remote(acc, from_l, slot, 11, 12, right, side)
        up_left = remote(acc, from_r, slot, 11, 13, left, side)
        to_side = remote(acc, side_in, slot, 14, 15, place, 1 - side)

        def down(src):
            return (
                remote(src, out_wide, slot, 16, 18, left, side),
                remote(src, out_wide, slot, 17, 18, right, side),
            )

        def keep():
            return pltpu.make_async_copy(side_in, out_wide, self.sems.at[19, slot])

        def hand_down(src):
            down_left, down_right = down(src)
            pl.when(from_left)(lambda: down_left().start())
            pl.when(from_right)(lambda: down_right().start())

        if which == "up":
            acc[...] = own[wide, :]

            @pl.when(place < root)
            def _():
                @pl.when(from_left)
                def _():
                    up_right().wait_recv()
                    acc[...] += from_l[...]

                up_right().start()

            @pl.when(place > root)
            def _():
                @pl.when(from_right)
                def _():
                    up_left().wait_recv()
                    acc[...] += from_r[...]

                up_left().start()

        if which == "root":

            @pl.when(place == root)
            def _():
                @pl.when(from_left)
                def _():
                    up_right().wait_recv()
                    acc[...] += from_l[...]

                @pl.when(from_right)
                def _():
                    up_left().wait_recv()
                    acc[...] += from_r[...]

                to_side().start()

        if which == "side":

            @pl.when(place == root)
            def _():
                to_side().wait_recv()
                side_in[...] += acc[...]
                hand_down(side_in)
                keep().start()

        if which == "down":

            @pl.when(place != root)
            def _():
                down(acc)[0]().wait_recv()
                hand_down(out_wide)

        if which == "end":
            down_left, down_right = down(acc)
            pl.when(from_left)(lambda: down_left().wait_send())
            pl.when(from_right)(lambda: down_right().wait_send())

            @pl.when(place == root)
            def _():
                to_side().wait_send()
                keep().wait()

            pl.when(place != root)(lambda: up_left().wait_send())

    P_LAGS = (("split", 0, 0), ("up", 2, 1), ("root", 3, 3), ("down", 6, 7), ("end", 9, 9))
    Q_LAGS = (("up", 1, 0), ("root", 2, 2), ("side", 4, 4), ("down", 6, 7), ("end", 9, 9))

    def tick(self, t, count):
        middle = (self.place == self.places // 2) | (self.place == self.places // 2 - 1)
        for stage, lags in ((self.p_stage, self.P_LAGS), (self.q_stage, self.Q_LAGS)):
            for which, mid_lag, outer_lag in lags:
                k = t - jnp.where(middle, mid_lag, outer_lag)

                @pl.when((k >= 0) & (k < count))
                def _(stage=stage, which=which, k=k):
                    stage(which, k)

    def run(self, count):
        @pl.loop(0, count + self.P_LAGS[-1][1])
        def _(t):
            self.tick(t, count)


def seq_sum_scratch():
    half = pltpu.VMEM((SLOTS_IN_FLIGHT, HALF, LANES), jnp.float32)
    wide = pltpu.VMEM((SLOTS_IN_FLIGHT, 2 * HALF, LANES), jnp.float32)
    return [half] * 4 + [wide] * 4 + [pltpu.SemaphoreType.DMA((20, SLOTS_IN_FLIGHT))]


FFN_PIECES = 36
FFN_PANELS = 27
FFN_PARTS = 3
ROW_BLOCK = 512
OUT_BLOCK = 256


def panel_in_sums(panel):
    per_part = FFN_PANELS // FFN_PARTS
    third = per_part // 3
    inside = lax.rem(panel, per_part)
    kind = inside // third
    return kind * (FFN_PANELS // 3) + panel // per_part * third + lax.rem(inside, third)


def ffn_kernel(places, *refs):
    (mid_hbm, mid_t_hbm, cot_hbm, cot_t_hbm, w_gu_hbm, w_d_hbm) = refs[0:6]
    (sums, rest, mid_chip, mid_far, ffn_chip, mid_land, ffn_land) = refs[6:13]
    (mid, mid_t, cot, cot_t, w_gu, w_d, act, ggu, own, staged, fetched) = refs[13:24]
    load_sems, near_sems, far_sems, keep_sem, fetch_sem = refs[24:29]
    summer = SeqSum(places, own, sums, panel_in_sums, refs[29:])
    tp_at = lax.axis_index("tp")
    core = lax.rem(tp_at, 2)
    sibling = tp_at + 1 - 2 * core
    across = lax.rem(tp_at + 2, 4)
    rows, width = mid.shape
    parts, _, wide = w_gu.shape
    hidden = wide // 2
    panels = 3 * hidden // LANES

    loads = [
        pltpu.make_async_copy(src, dst, load_sems.at[i])
        for i, (src, dst) in enumerate(
            (
                (mid_hbm, mid),
                (w_gu_hbm, w_gu),
                (cot_hbm, cot),
                (w_d_hbm, w_d),
                (mid_t_hbm, mid_t),
                (cot_t_hbm, cot_t),
            )
        )
    ]
    for load in loads:
        load.start()
    greet_seq(places, ({"tp": sibling}, {"tp": across}))
    count = FFN_PIECES
    for load in loads[:4]:
        load.wait()

    def part_cols(c):
        return pl.ds(pl.multiple_of(c * hidden, LANES), hidden)

    @pl.loop(0, parts)
    def _(c):
        @pl.loop(0, rows // ROW_BLOCK)
        def _(r):
            at = pl.ds(pl.multiple_of(r * ROW_BLOCK, ROW_BLOCK), ROW_BLOCK)
            both = jnp.dot(mid[at, :], w_gu[c], preferred_element_type=jnp.float32)
            gate, up = both[:, :hidden], both[:, hidden:]
            grad_act = dot_cols(cot[at, :], w_d[c])
            sigmoid = 1.0 / (1.0 + jnp.exp(-gate))
            silu = gate * sigmoid
            act[at, part_cols(c)] = (silu * up).astype(jnp.bfloat16)
            slope = sigmoid * (1.0 + gate * (1.0 - sigmoid))
            ggu[c, at, :hidden] = (grad_act * up * slope).astype(jnp.bfloat16)
            ggu[c, at, hidden:] = (grad_act * silu).astype(jnp.bfloat16)

        @pl.when(c == 0)
        def _():
            for load in loads[4:]:
                load.wait()

        @pl.loop(0, width // OUT_BLOCK)
        def _(m):
            first = pl.multiple_of(m * OUT_BLOCK, OUT_BLOCK)
            at = pl.ds(first, OUT_BLOCK)
            base = c * (panels * width) + first

            def put(block, panel):
                for j in range(block.shape[1] // LANES):
                    to = pl.multiple_of(base + (panel + j) * width, OUT_BLOCK)
                    own[pl.ds(to, OUT_BLOCK), :] = block[:, j * LANES : (j + 1) * LANES]

            put(jnp.dot(mid_t[at, :], ggu[c], preferred_element_type=jnp.float32), 0)
            put(
                jnp.dot(cot_t[at, :], act[:, part_cols(c)], preferred_element_type=jnp.float32),
                wide // LANES,
            )

            @pl.when(c > 0)
            def _():
                summer.tick((c - 1) * (width // OUT_BLOCK) + m, count)

    early = (parts - 1) * (width // OUT_BLOCK)
    blocks = rows // 2 // OUT_BLOCK
    for_later = pltpu.make_async_copy(
        own.at[pl.ds(count * 4 * HALF, rest.shape[0])], rest, load_sems.at[0]
    )
    for_later.start()

    def row_block(half, k):
        return pl.ds(pl.multiple_of((half * blocks + k) * OUT_BLOCK, OUT_BLOCK), OUT_BLOCK)

    def mid_part(at):
        return sum(dot_cols(ggu[c, at, :], w_gu[c]) for c in range(parts))

    def ffn_part(at):
        return sum(
            jnp.dot(
                act[at, c * hidden : (c + 1) * hidden],
                w_d[c],
                preferred_element_type=jnp.float32,
            )
            for c in range(parts)
        )

    def near(which, land, k):
        return pltpu.make_async_remote_copy(
            src_ref=staged.at[lax.rem(k, 2)],
            dst_ref=land.at[row_block(0, k)],
            send_sem=near_sems.at[which, 0, k],
            recv_sem=near_sems.at[which, 1, k],
            device_id={"tp": sibling},
            device_id_type=pl.DeviceIdType.MESH,
        )

    def far(k):
        return pltpu.make_async_remote_copy(
            src_ref=mid_chip.at[row_block(0, k)],
            dst_ref=mid_far.at[row_block(0, k)],
            send_sem=far_sems.at[0, k],
            recv_sem=far_sems.at[1, k],
            device_id={"tp": across},
            device_id_type=pl.DeviceIdType.MESH,
        )

    def tp_sum(which, part, land, chip, first_tick):
        @pl.loop(0, blocks)
        def _(k):
            @pl.when(k >= 2)
            def _():
                near(which, land, k - 2).wait_send()

            staged[lax.rem(k, 2)] = part(row_block(1 - core, k))
            near(which, land, k).start()

        for k in range(max(blocks - 2, 0), blocks):
            near(which, land, k).wait_send()

        @pl.loop(0, blocks)
        def _(k):
            near(which, land, k).wait_recv()
            fetch = pltpu.make_async_copy(land.at[row_block(0, k)], fetched, fetch_sem)
            fetch.start()
            staged[0] = part(row_block(core, k))
            fetch.wait()
            staged[0] += fetched[...]
            keep = pltpu.make_async_copy(staged.at[0], chip.at[row_block(0, k)], keep_sem)
            keep.start()
            summer.tick(first_tick + k, count)
            keep.wait()
            if which == 0:
                far(k).start()

    tp_sum(0, mid_part, mid_land, mid_chip, early)
    tp_sum(1, ffn_part, ffn_land, ffn_chip, early + blocks)

    @pl.loop(early + 2 * blocks, count + summer.P_LAGS[-1][1])
    def _(t):
        summer.tick(t, count)

    for_later.wait()

    @pl.loop(0, blocks)
    def _(k):
        far(k).wait()


def ffn_both_ways(normed_mid, grad_ffn, w_gate, w_up, w_down, sum_cols, collective_id):
    rows, width = normed_mid.shape
    local = w_gate.shape[1]
    hidden = local // FFN_PARTS

    def in_parts(weights):
        return weights.reshape(width, FFN_PARTS, hidden)

    w_gu = jnp.concatenate([in_parts(w_gate), in_parts(w_up)], axis=2).transpose(1, 0, 2)
    w_d = w_down.reshape(FFN_PARTS, hidden, width)
    grad_rows = 3 * local * width // LANES
    summed = FFN_PIECES * 4 * HALF
    half = jax.ShapeDtypeStruct((rows // 2, width), jnp.float32)
    low = jnp.bfloat16
    blocks = rows // 2 // OUT_BLOCK
    return pl.pallas_call(
        functools.partial(ffn_kernel, lax.axis_size("seq") // 2),
        out_shape=[
            jax.ShapeDtypeStruct((width, sum_cols), jnp.float32),
            jax.ShapeDtypeStruct((grad_rows - summed, LANES), jnp.float32),
        ]
        + [half] * 5,
        in_specs=[pl.BlockSpec(memory_space=pl.ANY)] * 6,
        out_specs=[pl.BlockSpec(memory_space=pl.ANY)] * 7,
        scratch_shapes=[
            pltpu.VMEM((rows, width), low),
            pltpu.VMEM((width, rows), low),
            pltpu.VMEM((rows, width), low),
            pltpu.VMEM((width, rows), low),
            pltpu.VMEM(w_gu.shape, low),
            pltpu.VMEM(w_d.shape, low),
            pltpu.VMEM((rows, local), low),
            pltpu.VMEM((FFN_PARTS, rows, 2 * hidden), low),
            pltpu.VMEM((grad_rows, LANES), jnp.float32),
            pltpu.VMEM((2, OUT_BLOCK, width), jnp.float32),
            pltpu.VMEM((OUT_BLOCK, width), jnp.float32),
            pltpu.SemaphoreType.DMA((6,)),
            pltpu.SemaphoreType.DMA((2, 2, blocks)),
            pltpu.SemaphoreType.DMA((2, blocks)),
            pltpu.SemaphoreType.DMA,
            pltpu.SemaphoreType.DMA,
        ]
        + seq_sum_scratch(),
        compiler_params=pltpu.CompilerParams(
            collective_id=collective_id, has_side_effects=True, vmem_limit_bytes=VMEM_LIMIT
        ),
        cost_estimate=pl.CostEstimate(
            flops=18 * rows * width * local, bytes_accessed=800 << 20, transcendentals=0
        ),
        name="ffn_both_ways",
    )(normed_mid, normed_mid.T, grad_ffn, grad_ffn.T, w_gu, w_d)


def gather_kernel(places, w_in, w_out, taps, full_in, full_out, full_taps, *scratch):
    own_in, own_out, far_in, far_out, sib_in, sib_out, sibfar_in, sibfar_out = scratch[0:8]
    own_taps, far_taps, sib_taps, sibfar_taps, share_in, share_out = scratch[8:14]
    sends, recvs, once = scratch[14:17]
    here = lax.axis_index("seq")
    place, side = here // 2, lax.rem(here, 2)
    last = places - 1
    tp_at = lax.axis_index("tp")
    core = lax.rem(tp_at, 2)
    sibling = tp_at + 1 - 2 * core
    across = lax.rem(tp_at + 2, 4)
    far_sibling = sibling + across - tp_at
    in_rows = w_in.shape[0] // (2 * places)
    out_rows = w_out.shape[0] // (2 * places)
    chans = w_in.shape[1] // 3
    width = w_out.shape[1]

    greet_seq(places, ({"tp": sibling}, {"tp": across}))

    def shares(j):
        return (
            pl.ds(pl.multiple_of(j * in_rows, in_rows), in_rows),
            pl.ds(pl.multiple_of(j * out_rows, out_rows), out_rows),
        )

    def copies(source, target, j, kind, device):
        for i, at in enumerate(shares(j)):
            yield pltpu.make_async_remote_copy(
                src_ref=source[i] if kind == 0 else source[i].at[at],
                dst_ref=target[i].at[at],
                send_sem=sends.at[kind, i, j],
                recv_sem=recvs.at[0 if kind < 4 else 1, i, j],
                device_id=device,
                device_id_type=pl.DeviceIdType.MESH,
            )

    share, far, sibfar = (share_in, share_out), (far_in, far_out), (sibfar_in, sibfar_out)

    def across_share():
        return copies(share, far, here, 0, {"tp": across})

    def to_right(j):
        return copies(far, far, j, 1, {"seq": here + 2})

    def to_left(j):
        return copies(far, far, j, 2, {"seq": here - 2})

    def to_side(j):
        return copies(far, far, j, 3, {"seq": here + 1 - 2 * side})

    def to_sibling(j):
        return copies(far, sibfar, j, 4, {"tp": sibling})

    def start(group):
        for copy in group:
            copy.start()

    def arrived(group):
        for copy in group:
            copy.wait_recv()

    def left_source(group):
        for copy in group:
            copy.wait_send()

    def single(i, src, dst, device):
        return pltpu.make_async_remote_copy(
            src_ref=src,
            dst_ref=dst,
            send_sem=once.at[0, i],
            recv_sem=once.at[1, i],
            device_id=device,
            device_id_type=pl.DeviceIdType.MESH,
        )

    for source, held, at in zip((w_in, w_out), share, shares(here)):
        held[...] = source[at, :].astype(jnp.float32)
    start(across_share())
    own_taps[...] = taps[...]
    taps_far = single(0, own_taps, far_taps, {"tp": across})
    taps_sib = single(1, own_taps, sib_taps, {"tp": sibling})
    taps_sibfar = single(2, far_taps, sibfar_taps, {"tp": sibling})
    own_in[...] = w_in[...].astype(jnp.float32)
    own_out[...] = w_out[...].astype(jnp.float32)
    in_sib = single(3, own_in, sib_in, {"tp": sibling})
    out_sib = single(4, own_out, sib_out, {"tp": sibling})
    for copy in (taps_far, taps_sib, in_sib, out_sib):
        copy.start()

    arrived(across_share())
    start(to_side(here))
    pl.when(place < last)(lambda: start(to_right(here)))
    pl.when(place > 0)(lambda: start(to_left(here)))
    start(to_sibling(here))
    taps_far.wait_recv()
    taps_sibfar.start()

    def place_shard(shard_in, shard_out, shard_taps, index):
        for g in range(3):
            cols = pl.ds(pl.multiple_of(g * width + index * chans, LANES), chans)
            full_in[:, cols] = shard_in[:, g * chans : (g + 1) * chans].astype(jnp.bfloat16)
        rows = pl.ds(pl.multiple_of(index * chans, chans), chans)
        full_out[rows, :] = shard_out[...].astype(jnp.bfloat16)
        cols = pl.ds(pl.multiple_of(index * chans, LANES), chans)
        full_taps[:, cols] = shard_taps[...]

    def from_side(q):
        j = 2 * q + 1 - side
        arrived(to_side(j))
        start(to_sibling(j))

    @pl.loop(1, places)
    def _(d):
        @pl.when(place - d >= 0)
        def _():
            j = here - 2 * d
            arrived(to_right(j))
            pl.when(place < last)(lambda: start(to_right(j)))
            start(to_side(j))
            start(to_sibling(j))

        @pl.when(place + d <= last)
        def _():
            j = here + 2 * d
            arrived(to_left(j))
            pl.when(place > 0)(lambda: start(to_left(j)))
            start(to_side(j))
            start(to_sibling(j))

        @pl.when(d == 1)
        def _():
            from_side(place)
            place_shard(own_in, own_out, own_taps, tp_at)
            in_sib.wait_recv()
            out_sib.wait_recv()
            taps_sib.wait_recv()
            place_shard(sib_in, sib_out, sib_taps, sibling)

        pl.when(place - d >= 0)(lambda: from_side(place - d))
        pl.when(place + d <= last)(lambda: from_side(place + d))

    place_shard(far_in, far_out, far_taps, across)
    taps_sibfar.wait_recv()

    @pl.loop(0, 2 * places)
    def _(j):
        arrived(to_sibling(j))

    place_shard(sibfar_in, sibfar_out, sibfar_taps, far_sibling)

    left_source(across_share())
    for copy in (taps_far, taps_sib, taps_sibfar, in_sib, out_sib):
        copy.wait_send()

    @pl.loop(0, places)
    def _(q):
        j = 2 * q + side
        left_source(to_side(j))
        pl.when((q <= place) & (place < last))(lambda: left_source(to_right(j)))
        pl.when((q >= place) & (place > 0))(lambda: left_source(to_left(j)))
        left_source(to_sibling(j))
        left_source(to_sibling(2 * q + 1 - side))


def gather_mixer(w_in, w_out, taps, collective_id):
    width, _, chans = w_in.shape
    count = lax.axis_size("seq")
    group = lax.axis_size("tp")
    f32 = jnp.float32
    pair = [pltpu.VMEM((width, 3 * chans), f32), pltpu.VMEM((chans, width), f32)]
    whole = pl.BlockSpec(memory_space=pltpu.VMEM)
    return pl.pallas_call(
        functools.partial(gather_kernel, count // 2),
        out_shape=[
            jax.ShapeDtypeStruct((width, 3 * chans * group), jnp.bfloat16),
            jax.ShapeDtypeStruct((chans * group, width), jnp.bfloat16),
            jax.ShapeDtypeStruct((8, chans * group), f32),
        ],
        in_specs=[whole] * 3,
        out_specs=[whole] * 3,
        scratch_shapes=pair * 4
        + [pltpu.VMEM((8, chans), f32)] * 4
        + [
            pltpu.VMEM((width // count, 3 * chans), f32),
            pltpu.VMEM((chans // count, width), f32),
        ]
        + [
            pltpu.SemaphoreType.DMA((5, 2, count)),
            pltpu.SemaphoreType.DMA((2, 2, count)),
            pltpu.SemaphoreType.DMA((2, 5)),
        ],
        compiler_params=pltpu.CompilerParams(
            collective_id=collective_id, has_side_effects=True, vmem_limit_bytes=48 << 20
        ),
        name="gather_mixer",
    )(w_in.reshape(width, 3 * chans), w_out, jnp.pad(taps, ((0, 5), (0, 0))))


SUB_ROWS = 64
SUB_COLS = 256


def norm_back(grad, gain, unit, scale):
    scaled = gain * grad
    return scale * (scaled - unit * jnp.mean(scaled * unit, axis=-1, keepdims=True))


def mixer_kernel(places, *refs):
    (rest_hbm, mid_chip, mid_far, ffn_chip, hidden_hbm, proj_hbm, gated_hbm) = refs[0:7]
    (normed_t_hbm, mixed_t_hbm, w_in_hbm, w_out_hbm, cot_hbm, tokens_hbm) = refs[7:13]
    (valid, taps, gain_mix, gain_ffn) = refs[13:17]
    (sums, tokens_out, block_out, ffn_far, land_in, land_out, land_small) = refs[18:25]
    (own, normed_t, mixed_t, w_in, w_out, cot, tokens, grad_mixer, grad_proj) = refs[25:34]
    (chip, far, hidden, proj, gated, mixed_buf, conv_in, grad_hid, grad_tok) = refs[34:43]
    (halo_out, halo_in, halo_keep, small, small_stage, small_fetch) = refs[43:49]
    (stage_in, fetch_in, stage_out, fetch_out) = refs[49:53]
    (load_sems, row_sems, halo_sems, near_sems, far_sems, out_sems) = refs[53:59]
    first_panel = FFN_PIECES * 4 * HALF // LANES // 8

    def panel_of(panel):
        panel = first_panel + panel
        return jnp.where(panel < FFN_PANELS, panel_in_sums(panel), panel)

    summer = SeqSum(places, own, sums, panel_of, refs[59:])
    here = lax.axis_index("seq")
    last = 2 * places - 1
    tp_at = lax.axis_index("tp")
    core = lax.rem(tp_at, 2)
    sibling = tp_at + 1 - 2 * core
    across = lax.rem(tp_at + 2, 4)
    rows, width = tokens.shape
    slots = halo_in.shape[0]
    slot_len = rows // slots
    per_slot = slot_len // OUT_BLOCK
    blocks = rows // OUT_BLOCK
    chans = w_out.shape[0] // 4
    count = own.shape[0] // (4 * HALF)
    early_rows = rest_hbm.shape[0]

    loads = [
        pltpu.make_async_copy(src, dst, load_sems.at[i])
        for i, (src, dst) in enumerate(
            (
                (rest_hbm, own.at[pl.ds(0, early_rows)]),
                (cot_hbm, cot),
                (w_out_hbm, w_out),
                (tokens_hbm, tokens),
                (w_in_hbm, w_in),
                (normed_t_hbm, normed_t),
                (mixed_t_hbm, mixed_t),
            )
        )
    ]
    for load in loads:
        load.start()

    def place_of(n):
        slot = n // per_slot
        block = per_slot - 1 - lax.rem(n, per_slot)
        return slot, block, pl.multiple_of(slot * slot_len + block * OUT_BLOCK, OUT_BLOCK)

    def mid_loads(first):
        at = pl.ds(first, OUT_BLOCK)
        return [
            pltpu.make_async_copy(src.at[at], dst, row_sems.at[i])
            for i, (src, dst) in enumerate(((mid_chip, chip), (mid_far, far), (hidden_hbm, hidden)))
        ]

    def proj_loads(slot, block, first):
        return [
            pltpu.make_async_copy(proj_hbm.at[pl.ds(first, OUT_BLOCK)], proj, row_sems.at[3]),
            pltpu.make_async_copy(
                gated_hbm.at[slot, pl.ds(pl.multiple_of(block * OUT_BLOCK, 8), OUT_BLOCK + 8)],
                gated,
                row_sems.at[4],
            ),
        ]

    def start(copies):
        for copy in copies:
            copy.start()

    def wait(copies):
        for copy in copies:
            copy.wait()

    def remote(src, dst, sems, i, device):
        return pltpu.make_async_remote_copy(
            src_ref=src,
            dst_ref=dst,
            send_sem=sems.at[0, i],
            recv_sem=sems.at[1, i],
            device_id=device,
            device_id_type=pl.DeviceIdType.MESH,
        )

    barrier = pltpu.get_barrier_semaphore()

    def signal(device):
        pl.semaphore_signal(barrier, inc=1, device_id=device, device_id_type=pl.DeviceIdType.MESH)

    pl.when(here > 0)(lambda: signal({"seq": here - 1}))
    pl.when(here < last)(lambda: signal({"seq": here + 1}))
    ends = jnp.where(here > 0, 1, 0) + jnp.where(here < last, 1, 0)
    greet_seq(places, ({"tp": sibling}, {"tp": across}), ends)

    def block_at(k):
        return pl.ds(pl.multiple_of(k * OUT_BLOCK, OUT_BLOCK), OUT_BLOCK)

    def ffn_across(k):
        at = block_at(k)
        return remote(ffn_chip.at[at], ffn_far.at[at], far_sems, k, {"tp": across})

    @pl.loop(0, blocks)
    def _(k):
        ffn_across(k).start()

    small[...] = jnp.zeros_like(small)
    wait(loads[:3])

    def hidden_grad(chip_rows, far_rows, hidden_rows, cot_rows):
        grad_mid = chip_rows + far_rows
        scale = rms_scale(hidden_rows)
        unit = hidden_rows * scale
        grad = cot_rows.astype(jnp.float32) + norm_back(grad_mid, gain_ffn[...], unit, scale)
        return grad, grad_mid * unit

    def halo_copy(slot, device):
        return remote(halo_out.at[slot], halo_in.at[slot], halo_sems, slot, {"seq": device})

    head = 16
    for slot in range(slots):
        at = pl.ds(slot * slot_len, head)
        top = pl.ds(0, head)
        copies = [
            pltpu.make_async_copy(src.at[at], dst, row_sems.at[i])
            for i, (src, dst) in enumerate(
                (
                    (mid_chip, chip.at[top]),
                    (mid_far, far.at[top]),
                    (hidden_hbm, hidden.at[top]),
                    (proj_hbm, proj.at[top]),
                )
            )
        ]
        start(copies)
        wait(copies)
        grad, _ = hidden_grad(chip[top, :], far[top, :], hidden[top, :], cot[at, :])
        grad_mixed = dot_cols(grad.astype(jnp.bfloat16), w_out[...])
        halo_out[slot] = (grad_mixed * proj[top, width : 2 * width])[:8]
        pl.when(here > 0)(lambda slot=slot: halo_copy(slot, here - 1).start())

    slot, block, first = place_of(0)
    start(mid_loads(first))
    start(proj_loads(slot, block, first))

    @pl.when(here == last)
    def _():
        halo_in[...] = jnp.zeros_like(halo_in)

    @pl.when(here < last)
    def _():
        for slot in range(slots):
            halo_copy(slot, here + 1).wait_recv()

    wait(loads[3:])

    def out_rows(first):
        return pl.ds(pl.multiple_of(core * rows + first, OUT_BLOCK), OUT_BLOCK)

    def hand_out(target, first, i):
        at = out_rows(first)
        return (
            pltpu.make_async_copy(grad_tok, target.at[at], out_sems.at[0, 2 * blocks]),
            remote(grad_tok, target.at[at], out_sems, i, {"tp": sibling}),
        )

    @pl.loop(0, blocks)
    def _(n):
        slot, block, first = place_of(n)
        at = pl.ds(first, OUT_BLOCK)
        wait(mid_loads(first))

        @pl.loop(0, OUT_BLOCK // SUB_ROWS)
        def _(r):
            sub = pl.ds(pl.multiple_of(r * SUB_ROWS, SUB_ROWS), SUB_ROWS)
            whole = pl.ds(pl.multiple_of(first + r * SUB_ROWS, SUB_ROWS), SUB_ROWS)
            grad, for_gain = hidden_grad(chip[sub, :], far[sub, :], hidden[sub, :], cot[whole, :])
            grad_hid[sub, :] = grad
            grad_mixer[whole, :] = grad.astype(jnp.bfloat16)
            small[1:2, :] += jnp.sum(for_gain, axis=0, keepdims=True)

        @pl.when(n < blocks - 1)
        def _():
            start(mid_loads(place_of(n + 1)[2]))

        mixed_buf[...] = dot_cols(grad_mixer[at, :], w_out[...])
        wait(proj_loads(slot, block, first))

        @pl.when(block == per_slot - 1)
        def _():
            conv_in[pl.ds(OUT_BLOCK, 8), :] = halo_in[slot]

        @pl.when(block < per_slot - 1)
        def _():
            conv_in[pl.ds(OUT_BLOCK, 8), :] = halo_keep[...]

        summer.tick(2 * n, count)
        mask = valid[at, :]

        @pl.loop(0, width // SUB_COLS)
        def _(c):
            def cols(gate):
                return pl.ds(pl.multiple_of(gate * width + c * SUB_COLS, SUB_COLS), SUB_COLS)

            here_cols = cols(0)
            in_gate, out_gate, conv_value = (proj[:, cols(g)] for g in range(3))
            grad_mixed = mixed_buf[:, here_cols]
            now = grad_mixed * out_gate
            conv_in[pl.ds(0, OUT_BLOCK), here_cols] = now
            seen = [gated[pl.ds(6 + j, OUT_BLOCK), here_cols] for j in range(3)]
            tap = [taps[j : j + 1, here_cols] for j in range(3)]
            conv_sum = tap[0] * seen[0] + tap[1] * seen[1] + tap[2] * seen[2]
            for j in range(3):
                small[2 + j : 3 + j, here_cols] += jnp.sum(now * seen[j], axis=0, keepdims=True)
            grad_proj[at, cols(1)] = (grad_mixed * conv_sum).astype(jnp.bfloat16)
            grad_gated = mask * (
                tap[2] * now
                + tap[1] * conv_in[pl.ds(1, OUT_BLOCK), here_cols]
                + tap[0] * conv_in[pl.ds(2, OUT_BLOCK), here_cols]
            )
            grad_proj[at, cols(0)] = (grad_gated * conv_value).astype(jnp.bfloat16)
            grad_proj[at, cols(2)] = (grad_gated * in_gate).astype(jnp.bfloat16)

        halo_keep[...] = conv_in[pl.ds(0, 8), :]

        @pl.when(n < blocks - 1)
        def _():
            start(proj_loads(*place_of(n + 1)))

        mixed_buf[...] = dot_cols(grad_proj[at, :], w_in[...])

        @pl.when(n > 0)
        def _():
            local, there = hand_out(tokens_out, place_of(n - 1)[2], n - 1)
            local.wait()
            there.wait_send()

        @pl.loop(0, OUT_BLOCK // SUB_ROWS)
        def _(r):
            sub = pl.ds(pl.multiple_of(r * SUB_ROWS, SUB_ROWS), SUB_ROWS)
            whole = pl.ds(pl.multiple_of(first + r * SUB_ROWS, SUB_ROWS), SUB_ROWS)
            inputs = tokens[whole, :].astype(jnp.float32)
            scale = rms_scale(inputs)
            unit = inputs * scale
            grad_in = mixed_buf[sub, :]
            grad_tok[sub, :] = grad_hid[sub, :] + norm_back(grad_in, gain_mix[...], unit, scale)
            small[0:1, :] += jnp.sum(grad_in * unit, axis=0, keepdims=True)

        start(hand_out(tokens_out, first, n))
        summer.tick(2 * n + 1, count)

    def near(src, dst, i):
        return remote(src, dst, near_sems, i, {"tp": sibling})

    in_blocks = width // OUT_BLOCK
    panels_in = 3 * chans // LANES

    def near_in(m):
        return near(stage_in.at[lax.rem(m, 2)], land_in.at[m], m)

    near_out = near(stage_out, land_out, in_blocks)
    near_small = near(small_stage, land_small, in_blocks + 1)

    def in_part(m, g, shard):
        at = pl.ds(pl.multiple_of(m * OUT_BLOCK, OUT_BLOCK), OUT_BLOCK)
        cols = pl.ds(pl.multiple_of(g * width + shard * chans, LANES), chans)
        return jnp.dot(normed_t[at, :], grad_proj[:, cols], preferred_element_type=jnp.float32)

    def out_part(shard):
        at = pl.ds(pl.multiple_of(shard * chans, chans), chans)
        return jnp.dot(mixed_t[at, :], grad_mixer[...], preferred_element_type=jnp.float32)

    for p in range(width // LANES):
        small_stage[8 * p : 8 * p + 8, :] = small[:, p * LANES : (p + 1) * LANES]
    near_small.start()
    halves = chans // LANES

    @pl.loop(0, in_blocks)
    def _(m):
        @pl.when(m >= 2)
        def _():
            near_in(m - 2).wait_send()

        for g in range(3):
            part = in_part(m, g, sibling)
            for h in range(halves):
                stage_in[lax.rem(m, 2), g * halves + h] = part[:, h * LANES : (h + 1) * LANES]
        near_in(m).start()
        summer.tick(2 * blocks + m, count)

    part = out_part(sibling)
    for p in range(width // LANES):
        stage_out[p] = part[:, p * LANES : (p + 1) * LANES]
    near_out.start()

    @pl.loop(0, in_blocks)
    def _(m):
        near_in(m).wait_recv()
        fetch = pltpu.make_async_copy(land_in.at[m], fetch_in, row_sems.at[0])
        fetch.start()
        parts = [in_part(m, g, tp_at) for g in range(3)]
        fetch.wait()
        for g in range(3):
            for h in range(halves):
                i = g * halves + h
                to = pl.multiple_of(early_rows + i * width + m * OUT_BLOCK, OUT_BLOCK)
                own[pl.ds(to, OUT_BLOCK), :] = (
                    parts[g][:, h * LANES : (h + 1) * LANES] + fetch_in[i]
                )

        summer.tick(2 * blocks + in_blocks + m, count)

    near_out.wait_recv()
    near_small.wait_recv()
    fetches = [
        pltpu.make_async_copy(land_out, fetch_out, row_sems.at[0]),
        pltpu.make_async_copy(land_small, small_fetch, row_sems.at[1]),
    ]
    start(fetches)
    part = out_part(tp_at)
    wait(fetches)
    out_first = early_rows + panels_in * width
    for p in range(width // LANES):
        own[pl.ds(out_first + p * chans, chans), :] = (
            part[:, p * LANES : (p + 1) * LANES] + fetch_out[p]
        )
    small_first = out_first + width // LANES * chans
    small_rows = small_stage.shape[0]
    own[pl.ds(small_first, small_rows), :] = small_stage[...] + small_fetch[...]
    unused = own.shape[0] - small_first - small_rows
    own[pl.ds(small_first + small_rows, unused), :] = jnp.zeros((unused, LANES), jnp.float32)

    local, there = hand_out(tokens_out, place_of(blocks - 1)[2], blocks - 1)
    local.wait()
    there.wait_send()
    done = 2 * blocks + 2 * in_blocks
    pause = min(done + 10, count)

    @pl.loop(done, pause)
    def _(t):
        summer.tick(t, count)

    @pl.loop(0, blocks)
    def _(k):
        ffn_across(k).wait_recv()
        at = block_at(k)
        copies = [
            pltpu.make_async_copy(src.at[at], dst, row_sems.at[i])
            for i, (src, dst) in enumerate(((ffn_chip, chip), (ffn_far, far), (hidden_hbm, hidden)))
        ]
        start(copies)

        @pl.when(k > 0)
        def _():
            local, there = hand_out(block_out, (k - 1) * OUT_BLOCK, blocks + k - 1)
            local.wait()
            there.wait_send()

        wait(copies)
        grad_tok[...] = hidden[...] + (chip[...] + far[...])
        start(hand_out(block_out, k * OUT_BLOCK, blocks + k))
        summer.tick(pause + k, count)

    @pl.loop(pause + blocks, count + summer.P_LAGS[-1][1])
    def _(t):
        summer.tick(t, count)

    local, there = hand_out(block_out, (blocks - 1) * OUT_BLOCK, 2 * blocks - 1)
    local.wait()
    there.wait_send()

    @pl.loop(0, blocks)
    def _(k):
        ffn_across(k).wait_send()
        hand_out(tokens_out, place_of(k)[2], k)[1].wait_recv()
        hand_out(block_out, k * OUT_BLOCK, blocks + k)[1].wait_recv()

    for m in range(max(in_blocks - 2, 0), in_blocks):
        near_in(m).wait_send()
    near_out.wait_send()
    near_small.wait_send()

    @pl.when(here > 0)
    def _():
        for slot in range(slots):
            halo_copy(slot, here - 1).wait_send()


def mixer_back(hbm, vmem, sums, slots, collective_id):
    rest, _, _, _, hidden, _, gated, normed_t, mixed_t, w_in, w_out, _, tokens = hbm
    rows, width = tokens.shape
    chans = w_out.shape[0] // 4
    blocks = rows // OUT_BLOCK
    in_blocks = width // OUT_BLOCK
    f32, low = jnp.float32, jnp.bfloat16
    panels_in = 3 * chans // LANES
    grad_rows = rest.shape[0] + panels_in * width + width // LANES * chans + 4 * HALF
    small_rows = 8 * width // LANES
    block = pltpu.VMEM((OUT_BLOCK, width), f32)
    full = jax.ShapeDtypeStruct((2 * rows, width), f32)
    anywhere = pl.BlockSpec(memory_space=pl.ANY)
    return pl.pallas_call(
        functools.partial(mixer_kernel, lax.axis_size("seq") // 2),
        out_shape=[
            jax.ShapeDtypeStruct(sums.shape, f32),
            full,
            full,
            jax.ShapeDtypeStruct((rows, width), f32),
            jax.ShapeDtypeStruct((in_blocks, panels_in, OUT_BLOCK, LANES), f32),
            jax.ShapeDtypeStruct((width // LANES, chans, LANES), f32),
            jax.ShapeDtypeStruct((small_rows, LANES), f32),
        ],
        in_specs=[anywhere] * len(hbm)
        + [pl.BlockSpec(memory_space=pltpu.VMEM)] * len(vmem)
        + [anywhere],
        input_output_aliases={len(hbm) + len(vmem): 0},
        out_specs=[anywhere] * 7,
        scratch_shapes=[
            pltpu.VMEM((grad_rows, LANES), f32),
            pltpu.VMEM(normed_t.shape, low),
            pltpu.VMEM(mixed_t.shape, low),
            pltpu.VMEM(w_in.shape, low),
            pltpu.VMEM(w_out.shape, low),
            pltpu.VMEM((rows, width), low),
            pltpu.VMEM((rows, width), low),
            pltpu.VMEM((rows, width), low),
            pltpu.VMEM((rows, 3 * width), low),
            block,
            block,
            block,
            pltpu.VMEM((OUT_BLOCK, 3 * width), f32),
            pltpu.VMEM((OUT_BLOCK + 8, width), f32),
            block,
            pltpu.VMEM((OUT_BLOCK + 8, width), f32),
            block,
            block,
            pltpu.VMEM((slots, 8, width), f32),
            pltpu.VMEM((slots, 8, width), f32),
            pltpu.VMEM((8, width), f32),
            pltpu.VMEM((8, width), f32),
            pltpu.VMEM((small_rows, LANES), f32),
            pltpu.VMEM((small_rows, LANES), f32),
            pltpu.VMEM((2, panels_in, OUT_BLOCK, LANES), f32),
            pltpu.VMEM((panels_in, OUT_BLOCK, LANES), f32),
            pltpu.VMEM((width // LANES, chans, LANES), f32),
            pltpu.VMEM((width // LANES, chans, LANES), f32),
            pltpu.SemaphoreType.DMA((7,)),
            pltpu.SemaphoreType.DMA((5,)),
            pltpu.SemaphoreType.DMA((2, slots)),
            pltpu.SemaphoreType.DMA((2, in_blocks + 2)),
            pltpu.SemaphoreType.DMA((2, blocks)),
            pltpu.SemaphoreType.DMA((2, 2 * blocks + 1)),
        ]
        + seq_sum_scratch(),
        compiler_params=pltpu.CompilerParams(
            collective_id=collective_id, has_side_effects=True, vmem_limit_bytes=VMEM_LIMIT
        ),
        cost_estimate=pl.CostEstimate(
            flops=26 * rows * width * width, bytes_accessed=400 << 20, transcendentals=0
        ),
        name="mixer_back",
    )(*hbm, *vmem, sums)


def per_device(
    tokens, lengths, gain_mix, w_in, conv_weight, w_out, gain_ffn, w_gate, w_up, w_down, cotangent
):
    slot_count, local_len, width = tokens.shape
    chans = w_in.shape[2]
    group = lax.axis_size("tp")
    seq_count = lax.axis_size("seq")
    tp_at, seq_at = lax.axis_index("tp"), lax.axis_index("seq")
    core, chip = tp_at % 2, tp_at // 2
    half_slots = slot_count // 2
    half_rows = half_slots * local_len
    row_count = slot_count * local_len

    def pick(is_first, first, second):
        return jnp.where(is_first, first, second)

    def both_cores(own, other):
        return jnp.concatenate(
            [pick(core == 0, own, other), pick(core == 0, other, own)], axis=0
        )

    w_in_all, w_out_all, taps = gather_mixer(w_in, w_out, conv_weight, 3)

    first_pos = seq_at * local_len
    positions = first_pos + jnp.arange(local_len, dtype=jnp.int32)
    valid = (positions[None, :] < lengths[:, None]).astype(jnp.float32)[:, :, None]
    valid_all = valid.reshape(row_count, 1)
    valid_own = lax.dynamic_slice(valid, (core * half_slots, 0, 0), (half_slots, local_len, 1))
    valid_rows = valid_own.reshape(half_rows, 1)
    tokens_own = lax.dynamic_slice(
        tokens, (core * half_slots, 0, 0), (half_slots, local_len, width)
    )
    inputs_f = tokens_own.astype(jnp.float32).reshape(half_rows, width)
    scale_mix = rms_scale(inputs_f)
    unit_mix = inputs_f * scale_mix
    normed_in = (gain_mix * unit_mix).astype(jnp.bfloat16)
    projected = jnp.dot(normed_in, w_in_all, preferred_element_type=jnp.float32)
    in_gate = projected[:, :width]
    out_gate = projected[:, width : 2 * width]
    conv_value = projected[:, 2 * width :]
    seq_shape = (half_slots, local_len, width)
    gated_seq = (valid_rows * in_gate * conv_value).reshape(seq_shape)
    carried = shift_seq(gated_seq[:, local_len - 2 :], 1)
    padded_seq = jnp.concatenate([carried, gated_seq], axis=1)
    conv_sum = (
        taps[0] * padded_seq[:, 0:local_len]
        + taps[1] * padded_seq[:, 1 : local_len + 1]
        + taps[2] * padded_seq[:, 2 : local_len + 2]
    ).reshape(half_rows, width)
    mixed_seq = (out_gate * conv_sum).astype(jnp.bfloat16)
    mixer_out = jnp.dot(mixed_seq, w_out_all, preferred_element_type=jnp.float32)
    hidden_res = inputs_f + mixer_out
    scale_ffn = rms_scale(hidden_res)
    unit_ffn = hidden_res * scale_ffn
    unit_all = both_cores(unit_ffn, swap_tp(unit_ffn, 1))
    normed_mid = (gain_ffn * unit_all).astype(jnp.bfloat16)

    grad_out = valid_all * cotangent.astype(jnp.float32).reshape(row_count, width)
    grad_ffn = grad_out.astype(jnp.bfloat16)
    mixer_cols = 4 * chans
    sum_cols = FFN_PANELS * LANES + mixer_cols + LANES
    ffn_sums, rest, mid_chip, mid_far, ffn_chip = ffn_both_ways(
        normed_mid, grad_ffn, w_gate, w_up, w_down, sum_cols, 1
    )[:5]
    cot_own = lax.dynamic_slice(grad_ffn, (core * half_rows, 0), (half_rows, width))
    lead = jnp.zeros((half_slots, 6, width), jnp.float32)
    gated_rows = jnp.concatenate([lead, padded_seq], axis=1)
    sums, grad_tokens, block_sum = mixer_back(
        (
            rest,
            mid_chip,
            mid_far,
            ffn_chip,
            hidden_res,
            projected,
            gated_rows,
            normed_in.T,
            mixed_seq.T,
            w_in_all,
            w_out_all,
            cot_own,
            tokens_own.reshape(half_rows, width),
        ),
        (valid_rows, taps, gain_mix.reshape(1, width), gain_ffn.reshape(1, width)),
        ffn_sums,
        half_slots,
        2,
    )[:3]
    grad_tokens = grad_tokens.reshape(slot_count, local_len, width)
    block_out = (valid_all * block_sum).astype(jnp.bfloat16)
    block_out = block_out.reshape(slot_count, local_len, width)

    hidden = w_gate.shape[1]
    total_w_gate = sums[:, :hidden]
    total_w_up = sums[:, hidden : 2 * hidden]
    total_w_down = sums[:, 2 * hidden : 3 * hidden].T
    mixer_sums = sums[:, 3 * hidden :]
    total_w_in = mixer_sums[:, : 3 * chans].reshape(width, 3, chans)
    out_parts = mixer_sums[:, 3 * chans : 4 * chans]
    out_parts = out_parts.reshape(width // chans, chans, chans // LANES, LANES)
    total_w_out = out_parts.transpose(1, 2, 0, 3).reshape(chans, width)
    small = mixer_sums[: 8 * width // LANES, 4 * chans :]
    small = small.reshape(width // LANES, 8, LANES).transpose(1, 0, 2).reshape(8, width)
    total_gain_mix, total_gain_ffn = small[0], small[1]
    total_conv = lax.dynamic_slice(small, (2, tp_at * chans), (3, chans))
    return (
        block_out,
        grad_tokens,
        total_gain_mix,
        total_w_in,
        total_conv,
        total_w_out,
        total_gain_ffn,
        total_w_gate,
        total_w_up,
        total_w_down,
    )


def solution(mesh):
    rows, cols = P("tp", None), P(None, "tp")
    tokens, whole, stacked = P(None, "seq", None), P(), P(None, None, "tp")
    return jax.shard_map(
        per_device,
        mesh=mesh,
        in_specs=(
            tokens, whole, whole, stacked, cols, rows, whole, cols, cols, rows, tokens,
        ),
        out_specs=(
            tokens, tokens, whole, stacked, cols, rows, whole, cols, cols, rows,
        ),
        check_vma=False,
    )
```

```python
import functools

import jax
import jax.numpy as jnp
from jax import lax
from jax.experimental import pallas as pl
from jax.experimental.pallas import tpu as pltpu
from jax.sharding import PartitionSpec as P

NORM_EPS = 1e-05
LANES = 128
VMEM_LIMIT = 64 << 20
HALF = 128
SLOTS_IN_FLIGHT = 10


def rms_scale(values):
    return lax.rsqrt(jnp.mean(values * values, axis=-1, keepdims=True) + NORM_EPS)


def dot_rows(left, right):
    return lax.dot_general(
        left, right, (((0,), (0,)), ((), ())), preferred_element_type=jnp.float32
    )


def dot_cols(left, right):
    return lax.dot_general(
        left, right, (((1,), (1,)), ((), ())), preferred_element_type=jnp.float32
    )


def greet_seq(places, others=(), more=0):
    barrier = pltpu.get_barrier_semaphore()
    here = lax.axis_index("seq")
    place, side = here // 2, lax.rem(here, 2)

    def signal(device):
        pl.semaphore_signal(
            barrier, inc=1, device_id=device, device_id_type=pl.DeviceIdType.MESH
        )

    signal({"seq": here + 1 - 2 * side})
    for other in others:
        signal(other)
    pl.when(place > 0)(lambda: signal({"seq": here - 2}))
    pl.when(place < places - 1)(lambda: signal({"seq": here + 2}))
    ends = jnp.where(place > 0, 1, 0) + jnp.where(place < places - 1, 1, 0)
    pl.semaphore_wait(barrier, 1 + len(others) + ends + more)


class SeqSum:
    def __init__(self, places, own, out, panel_of, scratch):
        self.places, self.own, self.out, self.panel_of = places, own, out, panel_of
        self.y_in, self.p_left, self.p_right, self.p_acc = scratch[0:4]
        self.q_left, self.q_right, self.q_acc, self.q_in = scratch[4:8]
        self.sems = scratch[8]
        here = lax.axis_index("seq")
        self.place, self.side = here // 2, here % 2

    def remote(self, src, dst, slot, send, recv, place, side):
        return pltpu.make_async_remote_copy(
            src_ref=src,
            dst_ref=dst,
            send_sem=self.sems.at[send, slot],
            recv_sem=self.sems.at[recv, slot],
            device_id={"seq": place * 2 + side},
            device_id_type=pl.DeviceIdType.MESH,
        )

    def chain(self, root):
        last = self.places - 1
        left = jnp.maximum(self.place - 1, 0)
        right = jnp.minimum(self.place + 1, last)
        from_left = (self.place <= root) & (self.place > 0)
        from_right = (self.place >= root) & (self.place < last)
        return left, right, from_left, from_right

    def out_at(self, k, first, size):
        per_panel = self.out.shape[0] // (4 * HALF)
        panel = self.panel_of(k // per_panel)
        row = lax.rem(k, per_panel) * 4 * HALF + first
        return self.out.at[
            pl.ds(pl.multiple_of(row, size), size), pl.ds(pl.multiple_of(panel * LANES, LANES), LANES)
        ]

    def p_stage(self, which, k):
        place, side = self.place, self.side
        own = self.own
        slot = lax.rem(k, SLOTS_IN_FLIGHT)
        base = pl.multiple_of(k * 4 * HALF, 4 * HALF)
        mine = pl.ds(pl.multiple_of(base + side * HALF, HALF), HALF)
        theirs = pl.ds(pl.multiple_of(base + (1 - side) * HALF, HALF), HALF)
        out_mine = self.out_at(k, side * HALF, HALF)
        root = self.places // 2 - 1 + lax.rem(k, 2)
        left, right, from_left, from_right = self.chain(root)
        acc, y_in = self.p_acc.at[slot], self.y_in.at[slot]
        from_l, from_r = self.p_left.at[slot], self.p_right.at[slot]
        remote = functools.partial(functools.partial, self.remote)

        to_side = remote(own.at[theirs], y_in, slot, 0, 1, place, 1 - side)
        up_right = remote(acc, from_l, slot, 2, 3, right, side)
        up_left = remote(acc, from_r, slot, 2, 4, left, side)

        def down(src):
            return (
                remote(src, out_mine, slot, 5, 7, left, side),
                remote(src, out_mine, slot, 6, 7, right, side),
                remote(src, out_mine, slot, 8, 9, place, 1 - side),
            )

        def keep():
            return pltpu.make_async_copy(acc, out_mine, self.sems.at[10, slot])

        def hand_down(src):
            down_left, down_right, down_side = down(src)
            down_side().start()
            pl.when(from_left)(lambda: down_left().start())
            pl.when(from_right)(lambda: down_right().start())

        if which == "split":
            to_side().start()

        if which == "up":
            to_side().wait_recv()
            acc[...] = own[mine, :] + y_in[...]

            @pl.when(place < root)
            def _():
                @pl.when(from_left)
                def _():
                    up_right().wait_recv()
                    acc[...] += from_l[...]

                up_right().start()

            @pl.when(place > root)
            def _():
                @pl.when(from_right)
                def _():
                    up_left().wait_recv()
                    acc[...] += from_r[...]

                up_left().start()

        if which == "root":

            @pl.when(place == root)
            def _():
                @pl.when(from_left)
                def _():
                    up_right().wait_recv()
                    acc[...] += from_l[...]

                @pl.when(from_right)
                def _():
                    up_left().wait_recv()
                    acc[...] += from_r[...]

                hand_down(acc)
                keep().start()

        if which == "down":

            @pl.when(place != root)
            def _():
                down(acc)[0]().wait_recv()
                hand_down(out_mine)

        if which == "end":
            down_left, down_right, down_side = down(acc)
            down_side().wait()
            to_side().wait_send()
            pl.when(from_left)(lambda: down_left().wait_send())
            pl.when(from_right)(lambda: down_right().wait_send())
            pl.when(place == root)(lambda: keep().wait())
            pl.when(place != root)(lambda: up_left().wait_send())

    def q_stage(self, which, k):
        place, side = self.place, self.side
        own = self.own
        slot = lax.rem(k, SLOTS_IN_FLIGHT)
        base = pl.multiple_of(k * 4 * HALF, 4 * HALF)
        wide = pl.ds(pl.multiple_of(base + 2 * HALF, 2 * HALF), 2 * HALF)
        out_wide = self.out_at(k, 2 * HALF, 2 * HALF)
        root = self.places // 2 - lax.rem(k, 2)
        left, right, from_left, from_right = self.chain(root)
        acc, side_in = self.q_acc.at[slot], self.q_in.at[slot]
        from_l, from_r = self.q_left.at[slot], self.q_right.at[slot]
        remote = functools.partial(functools.partial, self.remote)

        up_right = remote(acc, from_l, slot, 11, 12, right, side)
        up_left = remote(acc, from_r, slot, 11, 13, left, side)
        to_side = remote(acc, side_in, slot, 14, 15, place, 1 - side)

        def down(src):
            return (
                remote(src, out_wide, slot, 16, 18, left, side),
                remote(src, out_wide, slot, 17, 18, right, side),
            )

        def keep():
            return pltpu.make_async_copy(side_in, out_wide, self.sems.at[19, slot])

        def hand_down(src):
            down_left, down_right = down(src)
            pl.when(from_left)(lambda: down_left().start())
            pl.when(from_right)(lambda: down_right().start())

        if which == "up":
            acc[...] = own[wide, :]

            @pl.when(place < root)
            def _():
                @pl.when(from_left)
                def _():
                    up_right().wait_recv()
                    acc[...] += from_l[...]

                up_right().start()

            @pl.when(place > root)
            def _():
                @pl.when(from_right)
                def _():
                    up_left().wait_recv()
                    acc[...] += from_r[...]

                up_left().start()

        if which == "root":

            @pl.when(place == root)
            def _():
                @pl.when(from_left)
                def _():
                    up_right().wait_recv()
                    acc[...] += from_l[...]

                @pl.when(from_right)
                def _():
                    up_left().wait_recv()
                    acc[...] += from_r[...]

                to_side().start()

        if which == "side":

            @pl.when(place == root)
            def _():
                to_side().wait_recv()
                side_in[...] += acc[...]
                hand_down(side_in)
                keep().start()

        if which == "down":

            @pl.when(place != root)
            def _():
                down(acc)[0]().wait_recv()
                hand_down(out_wide)

        if which == "end":
            down_left, down_right = down(acc)
            pl.when(from_left)(lambda: down_left().wait_send())
            pl.when(from_right)(lambda: down_right().wait_send())

            @pl.when(place == root)
            def _():
                to_side().wait_send()
                keep().wait()

            pl.when(place != root)(lambda: up_left().wait_send())

    P_LAGS = (("split", 0, 0), ("up", 2, 1), ("root", 3, 3), ("down", 6, 7), ("end", 9, 9))
    Q_LAGS = (("up", 1, 0), ("root", 2, 2), ("side", 4, 4), ("down", 6, 7), ("end", 9, 9))

    def tick(self, t, count):
        middle = (self.place == self.places // 2) | (self.place == self.places // 2 - 1)
        for stage, lags in ((self.p_stage, self.P_LAGS), (self.q_stage, self.Q_LAGS)):
            for which, mid_lag, outer_lag in lags:
                k = t - jnp.where(middle, mid_lag, outer_lag)

                @pl.when((k >= 0) & (k < count))
                def _(stage=stage, which=which, k=k):
                    stage(which, k)

    def run(self, count):
        @pl.loop(0, count + self.P_LAGS[-1][1])
        def _(t):
            self.tick(t, count)


def seq_sum_scratch():
    half = pltpu.VMEM((SLOTS_IN_FLIGHT, HALF, LANES), jnp.float32)
    wide = pltpu.VMEM((SLOTS_IN_FLIGHT, 2 * HALF, LANES), jnp.float32)
    return [half] * 4 + [wide] * 4 + [pltpu.SemaphoreType.DMA((20, SLOTS_IN_FLIGHT))]


SUB_ROWS = 64
SUB_COLS = 256
FFN_PIECES = 36
FFN_PANELS = 27
FFN_PARTS = 3
ROW_BLOCK = 512
OUT_BLOCK = 256


def panel_in_sums(panel):
    per_part = FFN_PANELS // FFN_PARTS
    third = per_part // 3
    inside = lax.rem(panel, per_part)
    kind = inside // third
    return kind * (FFN_PANELS // 3) + panel // per_part * third + lax.rem(inside, third)


def ffn_kernel(places, *refs):
    (mid_hbm, cot_hbm, w_gate_hbm, w_up_hbm, w_d_hbm, valid) = refs[0:6]
    (sums, rest, mid_chip, mid_far, ffn_chip, mid_land, ffn_land) = refs[6:13]
    (mid, cot, w_gu, w_d, act, ggu, own, staged, fetched) = refs[13:22]
    load_sems, near_sems, far_sems, keep_sem, fetch_sem = refs[22:27]
    summer = SeqSum(places, own, sums, panel_in_sums, refs[27:])
    tp_at = lax.axis_index("tp")
    core = lax.rem(tp_at, 2)
    sibling = tp_at + 1 - 2 * core
    across = lax.rem(tp_at + 2, 4)
    rows, width = mid.shape
    parts, _, wide = w_gu.shape
    hidden = wide // 2
    panels = 3 * hidden // LANES

    moves = [(mid_hbm, mid), (cot_hbm, cot), (w_d_hbm, w_d)]
    for c in range(parts):
        for i, source in enumerate((w_gate_hbm, w_up_hbm)):
            moves.append(
                (
                    source.at[:, c * hidden : (c + 1) * hidden],
                    w_gu.at[c, :, i * hidden : (i + 1) * hidden],
                )
            )
    loads = [
        pltpu.make_async_copy(src, dst, load_sems.at[i]) for i, (src, dst) in enumerate(moves)
    ]
    for load in loads:
        load.start()
    greet_seq(places, ({"tp": sibling}, {"tp": across}))
    count = FFN_PIECES
    for load in loads:
        load.wait()

    def part_cols(c):
        return pl.ds(pl.multiple_of(c * hidden, LANES), hidden)

    @pl.loop(0, parts)
    def _(c):
        @pl.loop(0, rows // ROW_BLOCK)
        def _(r):
            at = pl.ds(pl.multiple_of(r * ROW_BLOCK, ROW_BLOCK), ROW_BLOCK)

            @pl.when(c == 0)
            def _():
                cot[at, :] = (valid[at, :] * cot[at, :].astype(jnp.float32)).astype(jnp.bfloat16)

            both = jnp.dot(mid[at, :], w_gu[c], preferred_element_type=jnp.float32)
            gate, up = both[:, :hidden], both[:, hidden:]
            grad_act = dot_cols(cot[at, :], w_d[c])
            sigmoid = 1.0 / (1.0 + jnp.exp(-gate))
            silu = gate * sigmoid
            act[at, part_cols(c)] = (silu * up).astype(jnp.bfloat16)
            slope = sigmoid * (1.0 + gate * (1.0 - sigmoid))
            ggu[c, at, :hidden] = (grad_act * up * slope).astype(jnp.bfloat16)
            ggu[c, at, hidden:] = (grad_act * silu).astype(jnp.bfloat16)

        @pl.loop(0, width // OUT_BLOCK)
        def _(m):
            first = pl.multiple_of(m * OUT_BLOCK, OUT_BLOCK)
            at = pl.ds(first, OUT_BLOCK)
            base = c * (panels * width) + first

            def put(block, panel):
                for j in range(block.shape[1] // LANES):
                    to = pl.multiple_of(base + (panel + j) * width, OUT_BLOCK)
                    own[pl.ds(to, OUT_BLOCK), :] = block[:, j * LANES : (j + 1) * LANES]

            put(dot_rows(mid[:, at], ggu[c]), 0)
            put(dot_rows(cot[:, at], act[:, part_cols(c)]), wide // LANES)

            @pl.when(c > 0)
            def _():
                summer.tick((c - 1) * (width // OUT_BLOCK) + m, count)

    early = (parts - 1) * (width // OUT_BLOCK)
    blocks = rows // 2 // OUT_BLOCK
    for_later = pltpu.make_async_copy(
        own.at[pl.ds(count * 4 * HALF, rest.shape[0])], rest, load_sems.at[0]
    )
    for_later.start()

    def row_block(half, k):
        return pl.ds(pl.multiple_of((half * blocks + k) * OUT_BLOCK, OUT_BLOCK), OUT_BLOCK)

    def mid_part(at):
        return sum(dot_cols(ggu[c, at, :], w_gu[c]) for c in range(parts))

    def ffn_part(at):
        return sum(
            jnp.dot(
                act[at, c * hidden : (c + 1) * hidden],
                w_d[c],
                preferred_element_type=jnp.float32,
            )
            for c in range(parts)
        )

    def near(which, land, k):
        return pltpu.make_async_remote_copy(
            src_ref=staged.at[lax.rem(k, 2)],
            dst_ref=land.at[row_block(0, k)],
            send_sem=near_sems.at[which, 0, k],
            recv_sem=near_sems.at[which, 1, k],
            device_id={"tp": sibling},
            device_id_type=pl.DeviceIdType.MESH,
        )

    def far(k):
        return pltpu.make_async_remote_copy(
            src_ref=mid_chip.at[row_block(0, k)],
            dst_ref=mid_far.at[row_block(0, k)],
            send_sem=far_sems.at[0, k],
            recv_sem=far_sems.at[1, k],
            device_id={"tp": across},
            device_id_type=pl.DeviceIdType.MESH,
        )

    def tp_sum(which, part, land, chip, first_tick):
        @pl.loop(0, blocks)
        def _(k):
            @pl.when(k >= 2)
            def _():
                near(which, land, k - 2).wait_send()

            staged[lax.rem(k, 2)] = part(row_block(1 - core, k))
            near(which, land, k).start()

        for k in range(max(blocks - 2, 0), blocks):
            near(which, land, k).wait_send()

        @pl.loop(0, blocks)
        def _(k):
            near(which, land, k).wait_recv()
            fetch = pltpu.make_async_copy(land.at[row_block(0, k)], fetched, fetch_sem)
            fetch.start()
            staged[0] = part(row_block(core, k))
            fetch.wait()
            staged[0] += fetched[...]
            keep = pltpu.make_async_copy(staged.at[0], chip.at[row_block(0, k)], keep_sem)
            keep.start()
            summer.tick(first_tick + k, count)
            keep.wait()
            if which == 0:
                far(k).start()

    tp_sum(0, mid_part, mid_land, mid_chip, early)
    tp_sum(1, ffn_part, ffn_land, ffn_chip, early + blocks)

    @pl.loop(early + 2 * blocks, count + summer.P_LAGS[-1][1])
    def _(t):
        summer.tick(t, count)

    for_later.wait()

    @pl.loop(0, blocks)
    def _(k):
        far(k).wait()


def ffn_both_ways(normed_mid, cotangent, w_gate, w_up, w_down, valid, sum_cols, collective_id):
    rows, width = normed_mid.shape
    local = w_gate.shape[1]
    hidden = local // FFN_PARTS

    w_d = w_down.reshape(FFN_PARTS, hidden, width)
    grad_rows = 3 * local * width // LANES
    summed = FFN_PIECES * 4 * HALF
    half = jax.ShapeDtypeStruct((rows // 2, width), jnp.float32)
    low = jnp.bfloat16
    blocks = rows // 2 // OUT_BLOCK
    return pl.pallas_call(
        functools.partial(ffn_kernel, lax.axis_size("seq") // 2),
        out_shape=[
            jax.ShapeDtypeStruct((width, sum_cols), jnp.float32),
            jax.ShapeDtypeStruct((grad_rows - summed, LANES), jnp.float32),
        ]
        + [half] * 5,
        in_specs=[pl.BlockSpec(memory_space=pl.ANY)] * 5
        + [pl.BlockSpec(memory_space=pltpu.VMEM)],
        out_specs=[pl.BlockSpec(memory_space=pl.ANY)] * 7,
        scratch_shapes=[
            pltpu.VMEM((rows, width), low),
            pltpu.VMEM((rows, width), low),
            pltpu.VMEM((FFN_PARTS, width, 2 * hidden), low),
            pltpu.VMEM(w_d.shape, low),
            pltpu.VMEM((rows, local), low),
            pltpu.VMEM((FFN_PARTS, rows, 2 * hidden), low),
            pltpu.VMEM((grad_rows, LANES), jnp.float32),
            pltpu.VMEM((2, OUT_BLOCK, width), jnp.float32),
            pltpu.VMEM((OUT_BLOCK, width), jnp.float32),
            pltpu.SemaphoreType.DMA((3 + 2 * FFN_PARTS,)),
            pltpu.SemaphoreType.DMA((2, 2, blocks)),
            pltpu.SemaphoreType.DMA((2, blocks)),
            pltpu.SemaphoreType.DMA,
            pltpu.SemaphoreType.DMA,
        ]
        + seq_sum_scratch(),
        compiler_params=pltpu.CompilerParams(
            collective_id=collective_id, has_side_effects=True, vmem_limit_bytes=VMEM_LIMIT
        ),
        cost_estimate=pl.CostEstimate(
            flops=18 * rows * width * local, bytes_accessed=800 << 20, transcendentals=0
        ),
        name="ffn_both_ways",
    )(normed_mid, cotangent, w_gate, w_up, w_d, valid)


def front_kernel(places, slots, *refs):
    (w_in, w_out, taps, gain_mix, gain_ffn, valid, tokens_hbm) = refs[0:7]
    (in_hbm, out_hbm, full_taps, mid_hbm, hidden_hbm, proj_hbm, gated_hbm) = refs[7:14]
    (normed_hbm, mixed_hbm) = refs[14:16]
    own_in, own_out, far_in, far_out, sib_in, sib_out, sibfar_in, sibfar_out = refs[16:24]
    own_taps, far_taps, sib_taps, sibfar_taps, share_in, share_out = refs[24:30]
    (full_in, full_out, tokens, normed, mixed, out_gate, gates, gated) = refs[30:38]
    (unit_out, unit_in, hidden) = refs[38:41]
    sends, recvs, once, halo_sems, gate_sems, unit_sems, keep_sems, mid_sems = refs[41:49]
    here = lax.axis_index("seq")
    place, side = here // 2, lax.rem(here, 2)
    last = places - 1
    end = 2 * places - 1
    tp_at = lax.axis_index("tp")
    core = lax.rem(tp_at, 2)
    sibling = tp_at + 1 - 2 * core
    across = lax.rem(tp_at + 2, 4)
    far_sibling = sibling + across - tp_at
    in_rows = w_in.shape[0] // (2 * places)
    out_rows = w_out.shape[0] // (2 * places)
    chans = w_in.shape[1] // 3
    rows, width = tokens.shape
    slot_len = rows // slots
    low = jnp.bfloat16

    load_tokens = pltpu.make_async_copy(
        tokens_hbm.at[pl.ds(pl.multiple_of(core * rows, rows), rows)], tokens, keep_sems.at[0]
    )
    load_tokens.start()
    barrier = pltpu.get_barrier_semaphore()

    def signal(device):
        pl.semaphore_signal(barrier, inc=1, device_id=device, device_id_type=pl.DeviceIdType.MESH)

    pl.when(here > 0)(lambda: signal({"seq": here - 1}))
    pl.when(here < end)(lambda: signal({"seq": here + 1}))
    ends = jnp.where(here > 0, 1, 0) + jnp.where(here < end, 1, 0)
    greet_seq(places, ({"tp": sibling}, {"tp": across}), ends)

    def shares(j):
        return (
            pl.ds(pl.multiple_of(j * in_rows, in_rows), in_rows),
            pl.ds(pl.multiple_of(j * out_rows, out_rows), out_rows),
        )

    def remote(src, dst, send, recv, device):
        return pltpu.make_async_remote_copy(
            src_ref=src,
            dst_ref=dst,
            send_sem=send,
            recv_sem=recv,
            device_id=device,
            device_id_type=pl.DeviceIdType.MESH,
        )

    def copies(source, target, j, kind, device):
        for i, at in enumerate(shares(j)):
            yield remote(
                source[i] if kind == 0 else source[i].at[at],
                target[i].at[at],
                sends.at[kind, i, j],
                recvs.at[0 if kind < 4 else 1, i, j],
                device,
            )

    share, far, sibfar = (share_in, share_out), (far_in, far_out), (sibfar_in, sibfar_out)

    def across_share():
        return copies(share, far, here, 0, {"tp": across})

    def to_right(j):
        return copies(far, far, j, 1, {"seq": here + 2})

    def to_left(j):
        return copies(far, far, j, 2, {"seq": here - 2})

    def to_side(j):
        return copies(far, far, j, 3, {"seq": here + 1 - 2 * side})

    def to_sibling(j):
        return copies(far, sibfar, j, 4, {"tp": sibling})

    def start(group):
        for copy in group:
            copy.start()

    def arrived(group):
        for copy in group:
            copy.wait_recv()

    def left_source(group):
        for copy in group:
            copy.wait_send()

    def single(i, src, dst, device):
        return remote(src, dst, once.at[0, i], once.at[1, i], device)

    for source, held, at in zip((w_in, w_out), share, shares(here)):
        held[...] = source[at, :].astype(jnp.float32)
    start(across_share())
    own_taps[...] = taps[...]
    taps_far = single(0, own_taps, far_taps, {"tp": across})
    taps_sib = single(1, own_taps, sib_taps, {"tp": sibling})
    taps_sibfar = single(2, far_taps, sibfar_taps, {"tp": sibling})
    own_in[...] = w_in[...].astype(jnp.float32)
    own_out[...] = w_out[...].astype(jnp.float32)
    in_sib = single(3, own_in, sib_in, {"tp": sibling})
    out_sib = single(4, own_out, sib_out, {"tp": sibling})
    for copy in (taps_far, taps_sib, in_sib, out_sib):
        copy.start()

    def gate_cols(g, index):
        return pl.ds(pl.multiple_of(g * width + index * chans, LANES), chans)

    def place_shard(shard_in, shard_out, shard_taps, index):
        for g in range(3):
            full_in[:, gate_cols(g, index)] = shard_in[:, g * chans : (g + 1) * chans].astype(low)
        at = pl.ds(pl.multiple_of(index * chans, chans), chans)
        full_out[at, :] = shard_out[...].astype(low)
        full_taps[:, gate_cols(0, index)] = shard_taps[...]

    def gate_out(turn, index, g):
        if g == 1:
            return pltpu.make_async_copy(
                out_gate.at[:, gate_cols(0, index)],
                proj_hbm.at[:, gate_cols(1, index)],
                gate_sems.at[turn, 1],
            )
        return pltpu.make_async_copy(
            gates.at[turn % 2, g // 2], proj_hbm.at[:, gate_cols(g, index)], gate_sems.at[turn, g]
        )

    def halo(turn, index, slot):
        return remote(
            gated.at[slot, pl.ds(slot_len, 8), gate_cols(0, index)],
            gated.at[slot, pl.ds(0, 8), gate_cols(0, index)],
            halo_sems.at[0, turn, slot],
            halo_sems.at[1, turn, slot],
            {"seq": here + 1},
        )

    order = (tp_at, sibling, across, far_sibling)

    def project(turn):
        index = order[turn]
        cols = gate_cols(0, index)
        if turn >= 2:
            gate_out(turn - 2, order[turn - 2], 0).wait()
            gate_out(turn - 2, order[turn - 2], 2).wait()

        @pl.loop(0, slots)
        def _(s):
            at = pl.ds(pl.multiple_of(s * slot_len, slot_len), slot_len)

            def gate(g):
                return jnp.dot(
                    normed[at, :], full_in[:, gate_cols(g, index)],
                    preferred_element_type=jnp.float32,
                )

            in_gate, value = gate(0), gate(2)
            gates[turn % 2, 0, at, :] = in_gate
            gates[turn % 2, 1, at, :] = value
            gated[s, pl.ds(8, slot_len), cols] = valid[at, :] * in_gate * value
            out_gate[at, cols] = gate(1)

        for g in range(3):
            gate_out(turn, index, g).start()

        @pl.when(here < end)
        def _():
            for slot in range(slots):
                halo(turn, index, slot).start()

    def convolve(turn):
        index = order[turn]
        cols = gate_cols(0, index)

        @pl.when(here > 0)
        def _():
            for slot in range(slots):
                halo(turn, index, slot).wait_recv()

        @pl.loop(0, slots)
        def _(s):
            at = pl.ds(pl.multiple_of(s * slot_len, slot_len), slot_len)
            seen = [gated[s, pl.ds(6 + j, slot_len), cols] for j in range(3)]
            tap = [full_taps[j : j + 1, cols] for j in range(3)]
            conv_sum = tap[0] * seen[0] + tap[1] * seen[1] + tap[2] * seen[2]
            mixed[at, cols] = (out_gate[at, cols] * conv_sum).astype(low)

    @pl.when(here == 0)
    def _():
        for slot in range(slots):
            gated[slot, pl.ds(0, 8), :] = jnp.zeros((8, width), jnp.float32)

    load_tokens.wait()

    @pl.loop(0, rows // SUB_ROWS)
    def _(r):
        at = pl.ds(pl.multiple_of(r * SUB_ROWS, SUB_ROWS), SUB_ROWS)
        inputs = tokens[at, :].astype(jnp.float32)
        normed[at, :] = (gain_mix[...] * (inputs * rms_scale(inputs))).astype(low)

    keep_normed = pltpu.make_async_copy(normed, normed_hbm, keep_sems.at[0])
    keep_normed.start()
    place_shard(own_in, own_out, own_taps, tp_at)
    project(0)

    arrived(across_share())
    pl.when(place < last)(lambda: start(to_right(here)))
    pl.when(place > 0)(lambda: start(to_left(here)))
    start(to_side(here))
    start(to_sibling(here))
    taps_far.wait_recv()
    taps_sibfar.start()
    in_sib.wait_recv()
    out_sib.wait_recv()
    taps_sib.wait_recv()
    place_shard(sib_in, sib_out, sib_taps, sibling)
    project(1)

    def from_side(q):
        j = 2 * q + 1 - side
        arrived(to_side(j))
        start(to_sibling(j))

    @pl.loop(1, places)
    def _(d):
        @pl.when(place - d >= 0)
        def _():
            j = here - 2 * d
            arrived(to_right(j))
            pl.when(place < last)(lambda: start(to_right(j)))
            start(to_side(j))
            start(to_sibling(j))

        @pl.when(place + d <= last)
        def _():
            j = here + 2 * d
            arrived(to_left(j))
            pl.when(place > 0)(lambda: start(to_left(j)))
            start(to_side(j))
            start(to_sibling(j))

        @pl.when(d == 1)
        def _():
            from_side(place)
            convolve(0)
            convolve(1)

        pl.when(place - d >= 0)(lambda: from_side(place - d))
        pl.when(place + d <= last)(lambda: from_side(place + d))

    place_shard(far_in, far_out, far_taps, across)
    project(2)
    taps_sibfar.wait_recv()

    @pl.loop(0, 2 * places)
    def _(j):
        arrived(to_sibling(j))

    place_shard(sibfar_in, sibfar_out, sibfar_taps, far_sibling)
    project(3)
    keep_in = pltpu.make_async_copy(full_in, in_hbm, keep_sems.at[1])
    keep_out = pltpu.make_async_copy(full_out, out_hbm, keep_sems.at[2])
    keep_in.start()
    keep_out.start()
    convolve(2)
    convolve(3)
    keep_gated = pltpu.make_async_copy(gated, gated_hbm, keep_sems.at[3])
    keep_mixed = pltpu.make_async_copy(mixed, mixed_hbm, keep_sems.at[4])
    keep_gated.start()
    keep_mixed.start()
    keep_normed.wait()

    blocks = rows // OUT_BLOCK

    def block_at(k, first=0):
        return pl.ds(pl.multiple_of(first + k * OUT_BLOCK, OUT_BLOCK), OUT_BLOCK)

    def unit_copy(k):
        return remote(
            unit_out.at[block_at(k)], unit_in.at[block_at(k)],
            unit_sems.at[0, k], unit_sems.at[1, k], {"tp": sibling},
        )

    def hidden_copy(k):
        return pltpu.make_async_copy(
            hidden.at[lax.rem(k, 2)], hidden_hbm.at[block_at(k)], mid_sems.at[0, lax.rem(k, 2)]
        )

    def mid_copy(half, held, whose, k):
        return pltpu.make_async_copy(
            held.at[block_at(k)], mid_hbm.at[block_at(k, whose * rows)], mid_sems.at[half, k]
        )

    @pl.loop(0, blocks)
    def _(k):
        slot = lax.rem(k, 2)
        at = block_at(k)
        pl.when(k >= 2)(lambda: hidden_copy(k - 2).wait())
        hidden[slot] = jnp.dot(mixed[at, :], full_out[...], preferred_element_type=jnp.float32)

        @pl.loop(0, OUT_BLOCK // SUB_ROWS)
        def _(r):
            sub = pl.ds(pl.multiple_of(r * SUB_ROWS, SUB_ROWS), SUB_ROWS)
            whole = pl.ds(pl.multiple_of(k * OUT_BLOCK + r * SUB_ROWS, SUB_ROWS), SUB_ROWS)
            hidden_rows = tokens[whole, :].astype(jnp.float32) + hidden[slot, sub, :]
            hidden[slot, sub, :] = hidden_rows
            unit = hidden_rows * rms_scale(hidden_rows)
            unit_out[whole, :] = unit
            normed[whole, :] = (gain_ffn[...] * unit).astype(low)

        unit_copy(k).start()
        hidden_copy(k).start()
        mid_copy(1, normed, core, k).start()

    keep_mixed.wait()

    @pl.loop(0, blocks)
    def _(k):
        unit_copy(k).wait_recv()

        @pl.loop(0, OUT_BLOCK // SUB_ROWS)
        def _(r):
            whole = pl.ds(pl.multiple_of(k * OUT_BLOCK + r * SUB_ROWS, SUB_ROWS), SUB_ROWS)
            mixed[whole, :] = (gain_ffn[...] * unit_in[whole, :]).astype(low)

        mid_copy(2, mixed, 1 - core, k).start()

    @pl.loop(0, blocks)
    def _(k):
        unit_copy(k).wait_send()
        mid_copy(1, normed, core, k).wait()
        mid_copy(2, mixed, 1 - core, k).wait()

    for k in range(max(blocks - 2, 0), blocks):
        hidden_copy(k).wait()
    keep_in.wait()
    keep_out.wait()
    keep_gated.wait()
    for turn in range(4):
        for g in range(3):
            if turn >= 2 or g == 1:
                gate_out(turn, order[turn], g).wait()

    @pl.when(here < end)
    def _():
        for turn in range(4):
            for slot in range(slots):
                halo(turn, order[turn], slot).wait_send()

    left_source(across_share())
    for copy in (taps_far, taps_sib, taps_sibfar, in_sib, out_sib):
        copy.wait_send()

    @pl.loop(0, places)
    def _(q):
        j = 2 * q + side
        left_source(to_side(j))
        pl.when((q <= place) & (place < last))(lambda: left_source(to_right(j)))
        pl.when((q >= place) & (place > 0))(lambda: left_source(to_left(j)))
        left_source(to_sibling(j))
        left_source(to_sibling(2 * q + 1 - side))


def mixer_front(w_in, w_out, taps, gain_mix, gain_ffn, valid, tokens, slots, collective_id):
    width, _, chans = w_in.shape
    rows = valid.shape[0]
    count = lax.axis_size("seq")
    group = lax.axis_size("tp")
    f32, low = jnp.float32, jnp.bfloat16
    blocks = rows // OUT_BLOCK
    pair = [pltpu.VMEM((width, 3 * chans), f32), pltpu.VMEM((chans, width), f32)]
    whole = pl.BlockSpec(memory_space=pltpu.VMEM)
    anywhere = pl.BlockSpec(memory_space=pl.ANY)
    padded = (slots, rows // slots + 8, width)
    return pl.pallas_call(
        functools.partial(front_kernel, count // 2, slots),
        out_shape=[
            jax.ShapeDtypeStruct((width, 3 * chans * group), low),
            jax.ShapeDtypeStruct((chans * group, width), low),
            jax.ShapeDtypeStruct((8, chans * group), f32),
            jax.ShapeDtypeStruct((2 * rows, width), low),
            jax.ShapeDtypeStruct((rows, width), f32),
            jax.ShapeDtypeStruct((rows, 3 * width), f32),
            jax.ShapeDtypeStruct(padded, f32),
            jax.ShapeDtypeStruct((rows, width), low),
            jax.ShapeDtypeStruct((rows, width), low),
        ],
        in_specs=[whole] * 6 + [anywhere],
        out_specs=[anywhere] * 2 + [whole] + [anywhere] * 6,
        scratch_shapes=pair * 4
        + [pltpu.VMEM((8, chans), f32)] * 4
        + [
            pltpu.VMEM((width // count, 3 * chans), f32),
            pltpu.VMEM((chans // count, width), f32),
            pltpu.VMEM((width, 3 * chans * group), low),
            pltpu.VMEM((chans * group, width), low),
            pltpu.VMEM((rows, width), low),
            pltpu.VMEM((rows, width), low),
            pltpu.VMEM((rows, width), low),
            pltpu.VMEM((rows, width), f32),
            pltpu.VMEM((2, 2, rows, chans), f32),
            pltpu.VMEM(padded, f32),
            pltpu.VMEM((rows, width), f32),
            pltpu.VMEM((rows, width), f32),
            pltpu.VMEM((2, OUT_BLOCK, width), f32),
            pltpu.SemaphoreType.DMA((5, 2, count)),
            pltpu.SemaphoreType.DMA((2, 2, count)),
            pltpu.SemaphoreType.DMA((2, 5)),
            pltpu.SemaphoreType.DMA((2, 4, slots)),
            pltpu.SemaphoreType.DMA((4, 3)),
            pltpu.SemaphoreType.DMA((2, blocks)),
            pltpu.SemaphoreType.DMA((5,)),
            pltpu.SemaphoreType.DMA((3, blocks)),
        ],
        compiler_params=pltpu.CompilerParams(
            collective_id=collective_id, has_side_effects=True, vmem_limit_bytes=VMEM_LIMIT
        ),
        name="mixer_front",
    )(
        w_in.reshape(width, 3 * chans),
        w_out,
        jnp.pad(taps, ((0, 5), (0, 0))),
        gain_mix,
        gain_ffn,
        valid,
        tokens,
    )


def norm_back(grad, gain, unit, scale):
    scaled = gain * grad
    return scale * (scaled - unit * jnp.mean(scaled * unit, axis=-1, keepdims=True))


def mixer_kernel(places, *refs):
    (rest_hbm, mid_chip, mid_far, ffn_chip, hidden_hbm, proj_hbm, gated_hbm) = refs[0:7]
    (normed_hbm, mixed_hbm, w_in_hbm, w_out_hbm, cot_hbm, tokens_hbm) = refs[7:13]
    (valid, taps, gain_mix, gain_ffn) = refs[13:17]
    (sums, tokens_out, block_out, ffn_far, land_in, land_out, land_small) = refs[18:25]
    (own, normed, mixed, w_in, w_out, cot, tokens, grad_mixer, grad_proj) = refs[25:34]
    (chip, far, hidden, proj, gated, mixed_buf, conv_in, grad_hid, grad_tok) = refs[34:43]
    (halo_out, halo_in, halo_keep, small, small_stage, small_fetch) = refs[43:49]
    (stage_in, fetch_in, stage_out, fetch_out) = refs[49:53]
    (load_sems, row_sems, halo_sems, near_sems, far_sems, out_sems) = refs[53:59]
    first_panel = FFN_PIECES * 4 * HALF // LANES // 8

    def panel_of(panel):
        panel = first_panel + panel
        return jnp.where(panel < FFN_PANELS, panel_in_sums(panel), panel)

    summer = SeqSum(places, own, sums, panel_of, refs[59:])
    here = lax.axis_index("seq")
    last = 2 * places - 1
    tp_at = lax.axis_index("tp")
    core = lax.rem(tp_at, 2)
    sibling = tp_at + 1 - 2 * core
    across = lax.rem(tp_at + 2, 4)
    rows, width = tokens.shape
    slots = halo_in.shape[0]
    slot_len = rows // slots
    per_slot = slot_len // OUT_BLOCK
    blocks = rows // OUT_BLOCK
    chans = w_out.shape[0] // 4
    count = own.shape[0] // (4 * HALF)
    early_rows = rest_hbm.shape[0]
    own_half = pl.ds(pl.multiple_of(core * rows, rows), rows)

    loads = [
        pltpu.make_async_copy(src, dst, load_sems.at[i])
        for i, (src, dst) in enumerate(
            (
                (rest_hbm, own.at[pl.ds(0, early_rows)]),
                (cot_hbm.at[own_half], cot),
                (w_out_hbm, w_out),
                (tokens_hbm.at[own_half], tokens),
                (w_in_hbm, w_in),
                (normed_hbm, normed),
                (mixed_hbm, mixed),
            )
        )
    ]
    for load in loads:
        load.start()

    def place_of(n):
        slot = n // per_slot
        block = per_slot - 1 - lax.rem(n, per_slot)
        return slot, block, pl.multiple_of(slot * slot_len + block * OUT_BLOCK, OUT_BLOCK)

    def mid_loads(first):
        at = pl.ds(first, OUT_BLOCK)
        return [
            pltpu.make_async_copy(src.at[at], dst, row_sems.at[i])
            for i, (src, dst) in enumerate(((mid_chip, chip), (mid_far, far), (hidden_hbm, hidden)))
        ]

    def proj_loads(slot, block, first):
        return [
            pltpu.make_async_copy(proj_hbm.at[pl.ds(first, OUT_BLOCK)], proj, row_sems.at[3]),
            pltpu.make_async_copy(
                gated_hbm.at[slot, pl.ds(pl.multiple_of(block * OUT_BLOCK, 8), OUT_BLOCK + 8)],
                gated,
                row_sems.at[4],
            ),
        ]

    def start(copies):
        for copy in copies:
            copy.start()

    def wait(copies):
        for copy in copies:
            copy.wait()

    def remote(src, dst, sems, i, device):
        return pltpu.make_async_remote_copy(
            src_ref=src,
            dst_ref=dst,
            send_sem=sems.at[0, i],
            recv_sem=sems.at[1, i],
            device_id=device,
            device_id_type=pl.DeviceIdType.MESH,
        )

    barrier = pltpu.get_barrier_semaphore()

    def signal(device):
        pl.semaphore_signal(barrier, inc=1, device_id=device, device_id_type=pl.DeviceIdType.MESH)

    pl.when(here > 0)(lambda: signal({"seq": here - 1}))
    pl.when(here < last)(lambda: signal({"seq": here + 1}))
    ends = jnp.where(here > 0, 1, 0) + jnp.where(here < last, 1, 0)
    greet_seq(places, ({"tp": sibling}, {"tp": across}), ends)

    def block_at(k):
        return pl.ds(pl.multiple_of(k * OUT_BLOCK, OUT_BLOCK), OUT_BLOCK)

    def ffn_across(k):
        at = block_at(k)
        return remote(ffn_chip.at[at], ffn_far.at[at], far_sems, k, {"tp": across})

    @pl.loop(0, blocks)
    def _(k):
        ffn_across(k).start()

    small[...] = jnp.zeros_like(small)
    wait(loads[:3])

    def hidden_grad(chip_rows, far_rows, hidden_rows, cot_rows, mask):
        grad_mid = chip_rows + far_rows
        scale = rms_scale(hidden_rows)
        unit = hidden_rows * scale
        grad = mask * cot_rows.astype(jnp.float32) + norm_back(grad_mid, gain_ffn[...], unit, scale)
        return grad, grad_mid * unit

    def halo_copy(slot, device):
        return remote(halo_out.at[slot], halo_in.at[slot], halo_sems, slot, {"seq": device})

    head = 16
    for slot in range(slots):
        at = pl.ds(slot * slot_len, head)
        top = pl.ds(0, head)
        copies = [
            pltpu.make_async_copy(src.at[at], dst, row_sems.at[i])
            for i, (src, dst) in enumerate(
                (
                    (mid_chip, chip.at[top]),
                    (mid_far, far.at[top]),
                    (hidden_hbm, hidden.at[top]),
                    (proj_hbm, proj.at[top]),
                )
            )
        ]
        start(copies)
        wait(copies)
        grad, _ = hidden_grad(
            chip[top, :], far[top, :], hidden[top, :], cot[at, :], valid[at, :]
        )
        grad_mixed = dot_cols(grad.astype(jnp.bfloat16), w_out[...])
        halo_out[slot] = (grad_mixed * proj[top, width : 2 * width])[:8]
        pl.when(here > 0)(lambda slot=slot: halo_copy(slot, here - 1).start())

    slot, block, first = place_of(0)
    start(mid_loads(first))
    start(proj_loads(slot, block, first))

    @pl.when(here == last)
    def _():
        halo_in[...] = jnp.zeros_like(halo_in)

    @pl.when(here < last)
    def _():
        for slot in range(slots):
            halo_copy(slot, here + 1).wait_recv()

    wait(loads[3:])

    def out_rows(first):
        return pl.ds(pl.multiple_of(core * rows + first, OUT_BLOCK), OUT_BLOCK)

    def hand_out(target, first, i):
        at = out_rows(first)
        return (
            pltpu.make_async_copy(grad_tok, target.at[at], out_sems.at[0, 2 * blocks]),
            remote(grad_tok, target.at[at], out_sems, i, {"tp": sibling}),
        )

    @pl.loop(0, blocks)
    def _(n):
        slot, block, first = place_of(n)
        at = pl.ds(first, OUT_BLOCK)
        wait(mid_loads(first))

        @pl.loop(0, OUT_BLOCK // SUB_ROWS)
        def _(r):
            sub = pl.ds(pl.multiple_of(r * SUB_ROWS, SUB_ROWS), SUB_ROWS)
            whole = pl.ds(pl.multiple_of(first + r * SUB_ROWS, SUB_ROWS), SUB_ROWS)
            grad, for_gain = hidden_grad(
                chip[sub, :], far[sub, :], hidden[sub, :], cot[whole, :], valid[whole, :]
            )
            grad_hid[sub, :] = grad
            grad_mixer[whole, :] = grad.astype(jnp.bfloat16)
            small[1:2, :] += jnp.sum(for_gain, axis=0, keepdims=True)

        @pl.when(n < blocks - 1)
        def _():
            start(mid_loads(place_of(n + 1)[2]))

        mixed_buf[...] = dot_cols(grad_mixer[at, :], w_out[...])
        wait(proj_loads(slot, block, first))

        @pl.when(block == per_slot - 1)
        def _():
            conv_in[pl.ds(OUT_BLOCK, 8), :] = halo_in[slot]

        @pl.when(block < per_slot - 1)
        def _():
            conv_in[pl.ds(OUT_BLOCK, 8), :] = halo_keep[...]

        summer.tick(2 * n, count)
        mask = valid[at, :]

        @pl.loop(0, width // SUB_COLS)
        def _(c):
            def cols(gate):
                return pl.ds(pl.multiple_of(gate * width + c * SUB_COLS, SUB_COLS), SUB_COLS)

            here_cols = cols(0)
            in_gate, out_gate, conv_value = (proj[:, cols(g)] for g in range(3))
            grad_mixed = mixed_buf[:, here_cols]
            now = grad_mixed * out_gate
            conv_in[pl.ds(0, OUT_BLOCK), here_cols] = now
            seen = [gated[pl.ds(6 + j, OUT_BLOCK), here_cols] for j in range(3)]
            tap = [taps[j : j + 1, here_cols] for j in range(3)]
            conv_sum = tap[0] * seen[0] + tap[1] * seen[1] + tap[2] * seen[2]
            for j in range(3):
                small[2 + j : 3 + j, here_cols] += jnp.sum(now * seen[j], axis=0, keepdims=True)
            grad_proj[at, cols(1)] = (grad_mixed * conv_sum).astype(jnp.bfloat16)
            grad_gated = mask * (
                tap[2] * now
                + tap[1] * conv_in[pl.ds(1, OUT_BLOCK), here_cols]
                + tap[0] * conv_in[pl.ds(2, OUT_BLOCK), here_cols]
            )
            grad_proj[at, cols(0)] = (grad_gated * conv_value).astype(jnp.bfloat16)
            grad_proj[at, cols(2)] = (grad_gated * in_gate).astype(jnp.bfloat16)

        halo_keep[...] = conv_in[pl.ds(0, 8), :]

        @pl.when(n < blocks - 1)
        def _():
            start(proj_loads(*place_of(n + 1)))

        mixed_buf[...] = dot_cols(grad_proj[at, :], w_in[...])

        @pl.when(n > 0)
        def _():
            local, there = hand_out(tokens_out, place_of(n - 1)[2], n - 1)
            local.wait()
            there.wait_send()

        @pl.loop(0, OUT_BLOCK // SUB_ROWS)
        def _(r):
            sub = pl.ds(pl.multiple_of(r * SUB_ROWS, SUB_ROWS), SUB_ROWS)
            whole = pl.ds(pl.multiple_of(first + r * SUB_ROWS, SUB_ROWS), SUB_ROWS)
            inputs = tokens[whole, :].astype(jnp.float32)
            scale = rms_scale(inputs)
            unit = inputs * scale
            grad_in = mixed_buf[sub, :]
            grad_tok[sub, :] = grad_hid[sub, :] + norm_back(grad_in, gain_mix[...], unit, scale)
            small[0:1, :] += jnp.sum(grad_in * unit, axis=0, keepdims=True)

        start(hand_out(tokens_out, first, n))
        summer.tick(2 * n + 1, count)

    def near(src, dst, i):
        return remote(src, dst, near_sems, i, {"tp": sibling})

    in_blocks = width // OUT_BLOCK
    panels_in = 3 * chans // LANES

    def near_in(m):
        return near(stage_in.at[lax.rem(m, 2)], land_in.at[m], m)

    near_out = near(stage_out, land_out, in_blocks)
    near_small = near(small_stage, land_small, in_blocks + 1)

    def in_part(m, g, shard):
        at = pl.ds(pl.multiple_of(m * OUT_BLOCK, OUT_BLOCK), OUT_BLOCK)
        cols = pl.ds(pl.multiple_of(g * width + shard * chans, LANES), chans)
        return dot_rows(normed[:, at], grad_proj[:, cols])

    def out_part(shard):
        at = pl.ds(pl.multiple_of(shard * chans, LANES), chans)
        return dot_rows(mixed[:, at], grad_mixer[...])

    for p in range(width // LANES):
        small_stage[8 * p : 8 * p + 8, :] = small[:, p * LANES : (p + 1) * LANES]
    near_small.start()
    halves = chans // LANES

    @pl.loop(0, in_blocks)
    def _(m):
        @pl.when(m >= 2)
        def _():
            near_in(m - 2).wait_send()

        for g in range(3):
            part = in_part(m, g, sibling)
            for h in range(halves):
                stage_in[lax.rem(m, 2), g * halves + h] = part[:, h * LANES : (h + 1) * LANES]
        near_in(m).start()
        summer.tick(2 * blocks + m, count)

    part = out_part(sibling)
    for p in range(width // LANES):
        stage_out[p] = part[:, p * LANES : (p + 1) * LANES]
    near_out.start()

    @pl.loop(0, in_blocks)
    def _(m):
        near_in(m).wait_recv()
        fetch = pltpu.make_async_copy(land_in.at[m], fetch_in, row_sems.at[0])
        fetch.start()
        parts = [in_part(m, g, tp_at) for g in range(3)]
        fetch.wait()
        for g in range(3):
            for h in range(halves):
                i = g * halves + h
                to = pl.multiple_of(early_rows + i * width + m * OUT_BLOCK, OUT_BLOCK)
                own[pl.ds(to, OUT_BLOCK), :] = (
                    parts[g][:, h * LANES : (h + 1) * LANES] + fetch_in[i]
                )

        summer.tick(2 * blocks + in_blocks + m, count)

    near_out.wait_recv()
    near_small.wait_recv()
    fetches = [
        pltpu.make_async_copy(land_out, fetch_out, row_sems.at[0]),
        pltpu.make_async_copy(land_small, small_fetch, row_sems.at[1]),
    ]
    start(fetches)
    part = out_part(tp_at)
    wait(fetches)
    out_first = early_rows + panels_in * width
    for p in range(width // LANES):
        own[pl.ds(out_first + p * chans, chans), :] = (
            part[:, p * LANES : (p + 1) * LANES] + fetch_out[p]
        )
    small_first = out_first + width // LANES * chans
    small_rows = small_stage.shape[0]
    own[pl.ds(small_first, small_rows), :] = small_stage[...] + small_fetch[...]
    unused = own.shape[0] - small_first - small_rows
    own[pl.ds(small_first + small_rows, unused), :] = jnp.zeros((unused, LANES), jnp.float32)

    local, there = hand_out(tokens_out, place_of(blocks - 1)[2], blocks - 1)
    local.wait()
    there.wait_send()
    done = 2 * blocks + 2 * in_blocks
    pause = min(done + 10, count)

    @pl.loop(done, pause)
    def _(t):
        summer.tick(t, count)

    @pl.loop(0, blocks)
    def _(k):
        ffn_across(k).wait_recv()
        at = block_at(k)
        copies = [
            pltpu.make_async_copy(src.at[at], dst, row_sems.at[i])
            for i, (src, dst) in enumerate(((ffn_chip, chip), (ffn_far, far), (hidden_hbm, hidden)))
        ]
        start(copies)

        @pl.when(k > 0)
        def _():
            local, there = hand_out(block_out, (k - 1) * OUT_BLOCK, blocks + k - 1)
            local.wait()
            there.wait_send()

        wait(copies)
        grad_tok[...] = hidden[...] + (chip[...] + far[...])
        start(hand_out(block_out, k * OUT_BLOCK, blocks + k))
        summer.tick(pause + k, count)

    @pl.loop(pause + blocks, count + summer.P_LAGS[-1][1])
    def _(t):
        summer.tick(t, count)

    local, there = hand_out(block_out, (blocks - 1) * OUT_BLOCK, 2 * blocks - 1)
    local.wait()
    there.wait_send()

    @pl.loop(0, blocks)
    def _(k):
        ffn_across(k).wait_send()
        hand_out(tokens_out, place_of(k)[2], k)[1].wait_recv()
        hand_out(block_out, k * OUT_BLOCK, blocks + k)[1].wait_recv()

    for m in range(max(in_blocks - 2, 0), in_blocks):
        near_in(m).wait_send()
    near_out.wait_send()
    near_small.wait_send()

    @pl.when(here > 0)
    def _():
        for slot in range(slots):
            halo_copy(slot, here - 1).wait_send()


def mixer_back(hbm, vmem, sums, slots, collective_id):
    rest, _, _, _, hidden, _, gated, normed, mixed, w_in, w_out, _, _ = hbm
    rows, width = normed.shape
    chans = w_out.shape[0] // 4
    blocks = rows // OUT_BLOCK
    in_blocks = width // OUT_BLOCK
    f32, low = jnp.float32, jnp.bfloat16
    panels_in = 3 * chans // LANES
    grad_rows = rest.shape[0] + panels_in * width + width // LANES * chans + 4 * HALF
    small_rows = 8 * width // LANES
    block = pltpu.VMEM((OUT_BLOCK, width), f32)
    full = jax.ShapeDtypeStruct((2 * rows, width), f32)
    anywhere = pl.BlockSpec(memory_space=pl.ANY)
    return pl.pallas_call(
        functools.partial(mixer_kernel, lax.axis_size("seq") // 2),
        out_shape=[
            jax.ShapeDtypeStruct(sums.shape, f32),
            full,
            full,
            jax.ShapeDtypeStruct((rows, width), f32),
            jax.ShapeDtypeStruct((in_blocks, panels_in, OUT_BLOCK, LANES), f32),
            jax.ShapeDtypeStruct((width // LANES, chans, LANES), f32),
            jax.ShapeDtypeStruct((small_rows, LANES), f32),
        ],
        in_specs=[anywhere] * len(hbm)
        + [pl.BlockSpec(memory_space=pltpu.VMEM)] * len(vmem)
        + [anywhere],
        input_output_aliases={len(hbm) + len(vmem): 0},
        out_specs=[anywhere] * 7,
        scratch_shapes=[
            pltpu.VMEM((grad_rows, LANES), f32),
            pltpu.VMEM(normed.shape, low),
            pltpu.VMEM(mixed.shape, low),
            pltpu.VMEM(w_in.shape, low),
            pltpu.VMEM(w_out.shape, low),
            pltpu.VMEM((rows, width), low),
            pltpu.VMEM((rows, width), low),
            pltpu.VMEM((rows, width), low),
            pltpu.VMEM((rows, 3 * width), low),
            block,
            block,
            block,
            pltpu.VMEM((OUT_BLOCK, 3 * width), f32),
            pltpu.VMEM((OUT_BLOCK + 8, width), f32),
            block,
            pltpu.VMEM((OUT_BLOCK + 8, width), f32),
            block,
            block,
            pltpu.VMEM((slots, 8, width), f32),
            pltpu.VMEM((slots, 8, width), f32),
            pltpu.VMEM((8, width), f32),
            pltpu.VMEM((8, width), f32),
            pltpu.VMEM((small_rows, LANES), f32),
            pltpu.VMEM((small_rows, LANES), f32),
            pltpu.VMEM((2, panels_in, OUT_BLOCK, LANES), f32),
            pltpu.VMEM((panels_in, OUT_BLOCK, LANES), f32),
            pltpu.VMEM((width // LANES, chans, LANES), f32),
            pltpu.VMEM((width // LANES, chans, LANES), f32),
            pltpu.SemaphoreType.DMA((7,)),
            pltpu.SemaphoreType.DMA((5,)),
            pltpu.SemaphoreType.DMA((2, slots)),
            pltpu.SemaphoreType.DMA((2, in_blocks + 2)),
            pltpu.SemaphoreType.DMA((2, blocks)),
            pltpu.SemaphoreType.DMA((2, 2 * blocks + 1)),
        ]
        + seq_sum_scratch(),
        compiler_params=pltpu.CompilerParams(
            collective_id=collective_id, has_side_effects=True, vmem_limit_bytes=VMEM_LIMIT
        ),
        cost_estimate=pl.CostEstimate(
            flops=26 * rows * width * width, bytes_accessed=400 << 20, transcendentals=0
        ),
        name="mixer_back",
    )(*hbm, *vmem, sums)


def per_device(
    tokens, lengths, gain_mix, w_in, conv_weight, w_out, gain_ffn, w_gate, w_up, w_down, cotangent
):
    slot_count, local_len, width = tokens.shape
    chans = w_in.shape[2]
    tp_at, seq_at = lax.axis_index("tp"), lax.axis_index("seq")
    core = tp_at % 2
    half_slots = slot_count // 2
    half_rows = half_slots * local_len
    row_count = slot_count * local_len

    positions = seq_at * local_len + jnp.arange(local_len, dtype=jnp.int32)
    valid = (positions[None, :] < lengths[:, None]).astype(jnp.float32)
    valid_all = valid.reshape(row_count, 1)
    valid_rows = lax.dynamic_slice(valid_all, (core * half_rows, 0), (half_rows, 1))
    token_rows = tokens.reshape(row_count, width)
    cot_rows = cotangent.reshape(row_count, width)
    gains = gain_mix.reshape(1, width), gain_ffn.reshape(1, width)
    w_in_all, w_out_all, taps, normed_mid, hidden_res, projected, gated_rows, normed_in, mixed = (
        mixer_front(w_in, w_out, conv_weight, *gains, valid_rows, token_rows, half_slots, 3)
    )
    mixer_cols = 4 * chans
    sum_cols = FFN_PANELS * LANES + mixer_cols + LANES
    ffn_sums, rest, mid_chip, mid_far, ffn_chip = ffn_both_ways(
        normed_mid, cot_rows, w_gate, w_up, w_down, valid_all, sum_cols, 1
    )[:5]
    sums, grad_tokens, block_sum = mixer_back(
        (
            rest,
            mid_chip,
            mid_far,
            ffn_chip,
            hidden_res,
            projected,
            gated_rows,
            normed_in,
            mixed,
            w_in_all,
            w_out_all,
            cot_rows,
            token_rows,
        ),
        (valid_rows, taps, *gains),
        ffn_sums,
        half_slots,
        2,
    )[:3]
    grad_tokens = grad_tokens.reshape(slot_count, local_len, width)
    block_out = (valid_all * block_sum).astype(jnp.bfloat16)
    block_out = block_out.reshape(slot_count, local_len, width)

    hidden = w_gate.shape[1]
    total_w_gate = sums[:, :hidden]
    total_w_up = sums[:, hidden : 2 * hidden]
    total_w_down = sums[:, 2 * hidden : 3 * hidden].T
    mixer_sums = sums[:, 3 * hidden :]
    total_w_in = mixer_sums[:, : 3 * chans].reshape(width, 3, chans)
    out_parts = mixer_sums[:, 3 * chans : 4 * chans]
    out_parts = out_parts.reshape(width // chans, chans, chans // LANES, LANES)
    total_w_out = out_parts.transpose(1, 2, 0, 3).reshape(chans, width)
    small = mixer_sums[: 8 * width // LANES, 4 * chans :]
    small = small.reshape(width // LANES, 8, LANES).transpose(1, 0, 2).reshape(8, width)
    total_gain_mix, total_gain_ffn = small[0], small[1]
    total_conv = lax.dynamic_slice(small, (2, tp_at * chans), (3, chans))
    return (
        block_out,
        grad_tokens,
        total_gain_mix,
        total_w_in,
        total_conv,
        total_w_out,
        total_gain_ffn,
        total_w_gate,
        total_w_up,
        total_w_down,
    )


def solution(mesh):
    rows, cols = P("tp", None), P(None, "tp")
    tokens, whole, stacked = P(None, "seq", None), P(), P(None, None, "tp")
    return jax.shard_map(
        per_device,
        mesh=mesh,
        in_specs=(
            tokens, whole, whole, stacked, cols, rows, whole, cols, cols, rows, tokens,
        ),
        out_specs=(
            tokens, tokens, whole, stacked, cols, rows, whole, cols, cols, rows,
        ),
        check_vma=False,
    )
```

```python
import functools

import jax
import jax.numpy as jnp
from jax import lax
from jax.experimental import pallas as pl
from jax.experimental.pallas import tpu as pltpu
from jax.sharding import PartitionSpec as P

NORM_EPS = 1e-05
LANES = 128
VMEM_LIMIT = 64 << 20
HALF = 128
SLOTS_IN_FLIGHT = 10


def rms_scale(values):
    return lax.rsqrt(jnp.mean(values * values, axis=-1, keepdims=True) + NORM_EPS)


def dot_rows(left, right):
    return lax.dot_general(
        left, right, (((0,), (0,)), ((), ())), preferred_element_type=jnp.float32
    )


def dot_cols(left, right):
    return lax.dot_general(
        left, right, (((1,), (1,)), ((), ())), preferred_element_type=jnp.float32
    )


def greet_seq(places, others=(), more=0):
    barrier = pltpu.get_barrier_semaphore()
    here = lax.axis_index("seq")
    place, side = here // 2, lax.rem(here, 2)

    def signal(device):
        pl.semaphore_signal(
            barrier, inc=1, device_id=device, device_id_type=pl.DeviceIdType.MESH
        )

    signal({"seq": here + 1 - 2 * side})
    for other in others:
        signal(other)
    pl.when(place > 0)(lambda: signal({"seq": here - 2}))
    pl.when(place < places - 1)(lambda: signal({"seq": here + 2}))
    ends = jnp.where(place > 0, 1, 0) + jnp.where(place < places - 1, 1, 0)
    pl.semaphore_wait(barrier, 1 + len(others) + ends + more)


class SeqSum:
    def __init__(self, places, own, out, panel_of, scratch):
        self.places, self.own, self.out, self.panel_of = places, own, out, panel_of
        self.y_in, self.p_left, self.p_right, self.p_acc = scratch[0:4]
        self.q_left, self.q_right, self.q_acc, self.q_in = scratch[4:8]
        self.sems = scratch[8]
        here = lax.axis_index("seq")
        self.place, self.side = here // 2, here % 2

    def remote(self, src, dst, slot, send, recv, place, side):
        return pltpu.make_async_remote_copy(
            src_ref=src,
            dst_ref=dst,
            send_sem=self.sems.at[send, slot],
            recv_sem=self.sems.at[recv, slot],
            device_id={"seq": place * 2 + side},
            device_id_type=pl.DeviceIdType.MESH,
        )

    def chain(self, root):
        last = self.places - 1
        left = jnp.maximum(self.place - 1, 0)
        right = jnp.minimum(self.place + 1, last)
        from_left = (self.place <= root) & (self.place > 0)
        from_right = (self.place >= root) & (self.place < last)
        return left, right, from_left, from_right

    def own_base(self, k):
        held = self.own.shape[0] // (4 * HALF)
        return pl.multiple_of(lax.rem(k, held) * 4 * HALF, 4 * HALF)

    def out_at(self, k, first, size):
        per_panel = self.out.shape[0] // (4 * HALF)
        panel = self.panel_of(k // per_panel)
        row = lax.rem(k, per_panel) * 4 * HALF + first
        return self.out.at[
            pl.ds(pl.multiple_of(row, size), size), pl.ds(pl.multiple_of(panel * LANES, LANES), LANES)
        ]

    def p_stage(self, which, k):
        place, side = self.place, self.side
        own = self.own
        slot = lax.rem(k, SLOTS_IN_FLIGHT)
        base = self.own_base(k)
        mine = pl.ds(pl.multiple_of(base + side * HALF, HALF), HALF)
        theirs = pl.ds(pl.multiple_of(base + (1 - side) * HALF, HALF), HALF)
        out_mine = self.out_at(k, side * HALF, HALF)
        root = self.places // 2 - 1 + lax.rem(k, 2)
        left, right, from_left, from_right = self.chain(root)
        acc, y_in = self.p_acc.at[slot], self.y_in.at[slot]
        from_l, from_r = self.p_left.at[slot], self.p_right.at[slot]
        remote = functools.partial(functools.partial, self.remote)

        to_side = remote(own.at[theirs], y_in, slot, 0, 1, place, 1 - side)
        up_right = remote(acc, from_l, slot, 2, 3, right, side)
        up_left = remote(acc, from_r, slot, 2, 4, left, side)

        def down(src):
            return (
                remote(src, out_mine, slot, 5, 7, left, side),
                remote(src, out_mine, slot, 6, 7, right, side),
                remote(src, out_mine, slot, 8, 9, place, 1 - side),
            )

        def keep():
            return pltpu.make_async_copy(acc, out_mine, self.sems.at[10, slot])

        def hand_down(src):
            down_left, down_right, down_side = down(src)
            down_side().start()
            pl.when(from_left)(lambda: down_left().start())
            pl.when(from_right)(lambda: down_right().start())

        if which == "split":
            to_side().start()

        if which == "up":
            to_side().wait_recv()
            acc[...] = own[mine, :] + y_in[...]

            @pl.when(place < root)
            def _():
                @pl.when(from_left)
                def _():
                    up_right().wait_recv()
                    acc[...] += from_l[...]

                up_right().start()

            @pl.when(place > root)
            def _():
                @pl.when(from_right)
                def _():
                    up_left().wait_recv()
                    acc[...] += from_r[...]

                up_left().start()

        if which == "root":

            @pl.when(place == root)
            def _():
                @pl.when(from_left)
                def _():
                    up_right().wait_recv()
                    acc[...] += from_l[...]

                @pl.when(from_right)
                def _():
                    up_left().wait_recv()
                    acc[...] += from_r[...]

                hand_down(acc)
                keep().start()

        if which == "down":

            @pl.when(place != root)
            def _():
                down(acc)[0]().wait_recv()
                hand_down(out_mine)

        if which == "end":
            down_left, down_right, down_side = down(acc)
            down_side().wait()
            to_side().wait_send()
            pl.when(from_left)(lambda: down_left().wait_send())
            pl.when(from_right)(lambda: down_right().wait_send())
            pl.when(place == root)(lambda: keep().wait())
            pl.when(place != root)(lambda: up_left().wait_send())

    def q_stage(self, which, k):
        place, side = self.place, self.side
        own = self.own
        slot = lax.rem(k, SLOTS_IN_FLIGHT)
        base = self.own_base(k)
        wide = pl.ds(pl.multiple_of(base + 2 * HALF, 2 * HALF), 2 * HALF)
        out_wide = self.out_at(k, 2 * HALF, 2 * HALF)
        root = self.places // 2 - lax.rem(k, 2)
        left, right, from_left, from_right = self.chain(root)
        acc, side_in = self.q_acc.at[slot], self.q_in.at[slot]
        from_l, from_r = self.q_left.at[slot], self.q_right.at[slot]
        remote = functools.partial(functools.partial, self.remote)

        up_right = remote(acc, from_l, slot, 11, 12, right, side)
        up_left = remote(acc, from_r, slot, 11, 13, left, side)
        to_side = remote(acc, side_in, slot, 14, 15, place, 1 - side)

        def down(src):
            return (
                remote(src, out_wide, slot, 16, 18, left, side),
                remote(src, out_wide, slot, 17, 18, right, side),
            )

        def keep():
            return pltpu.make_async_copy(side_in, out_wide, self.sems.at[19, slot])

        def hand_down(src):
            down_left, down_right = down(src)
            pl.when(from_left)(lambda: down_left().start())
            pl.when(from_right)(lambda: down_right().start())

        if which == "up":
            acc[...] = own[wide, :]

            @pl.when(place < root)
            def _():
                @pl.when(from_left)
                def _():
                    up_right().wait_recv()
                    acc[...] += from_l[...]

                up_right().start()

            @pl.when(place > root)
            def _():
                @pl.when(from_right)
                def _():
                    up_left().wait_recv()
                    acc[...] += from_r[...]

                up_left().start()

        if which == "root":

            @pl.when(place == root)
            def _():
                @pl.when(from_left)
                def _():
                    up_right().wait_recv()
                    acc[...] += from_l[...]

                @pl.when(from_right)
                def _():
                    up_left().wait_recv()
                    acc[...] += from_r[...]

                to_side().start()

        if which == "side":

            @pl.when(place == root)
            def _():
                to_side().wait_recv()
                side_in[...] += acc[...]
                hand_down(side_in)
                keep().start()

        if which == "down":

            @pl.when(place != root)
            def _():
                down(acc)[0]().wait_recv()
                hand_down(out_wide)

        if which == "end":
            down_left, down_right = down(acc)
            pl.when(from_left)(lambda: down_left().wait_send())
            pl.when(from_right)(lambda: down_right().wait_send())

            @pl.when(place == root)
            def _():
                to_side().wait_send()
                keep().wait()

            pl.when(place != root)(lambda: up_left().wait_send())

    P_LAGS = (("split", 0, 0), ("up", 2, 1), ("root", 3, 3), ("down", 6, 7), ("end", 9, 9))
    Q_LAGS = (("up", 1, 0), ("root", 2, 2), ("side", 4, 4), ("down", 6, 7), ("end", 9, 9))

    def tick(self, t, count):
        middle = (self.place == self.places // 2) | (self.place == self.places // 2 - 1)
        for stage, lags in ((self.p_stage, self.P_LAGS), (self.q_stage, self.Q_LAGS)):
            for which, mid_lag, outer_lag in lags:
                k = t - jnp.where(middle, mid_lag, outer_lag)

                @pl.when((k >= 0) & (k < count))
                def _(stage=stage, which=which, k=k):
                    stage(which, k)

    def run(self, count):
        @pl.loop(0, count + self.P_LAGS[-1][1])
        def _(t):
            self.tick(t, count)


def seq_sum_scratch():
    half = pltpu.VMEM((SLOTS_IN_FLIGHT, HALF, LANES), jnp.float32)
    wide = pltpu.VMEM((SLOTS_IN_FLIGHT, 2 * HALF, LANES), jnp.float32)
    return [half] * 4 + [wide] * 4 + [pltpu.SemaphoreType.DMA((20, SLOTS_IN_FLIGHT))]


SUB_ROWS = 64
FIRST_MIXER_TICK = 36
BLOCK_TICK = 56
FFN_PANELS = 27
FFN_PARTS = 3
ROW_BLOCK = 256
ROW_TICK = 2
OUT_BLOCK = 256


def panel_in_sums(panel):
    per_part = FFN_PANELS // FFN_PARTS
    third = per_part // 3
    inside = lax.rem(panel, per_part)
    kind = inside // third
    return kind * (FFN_PANELS // 3) + panel // per_part * third + lax.rem(inside, third)


def norm_back(grad, gain, unit, scale):
    scaled = gain * grad
    return scale * (scaled - unit * jnp.mean(scaled * unit, axis=-1, keepdims=True))


def back_kernel(places, slots, *refs):
    (mid_hbm, cot_hbm, w_gate_hbm, w_up_hbm, w_d_hbm, hidden_hbm, proj_hbm) = refs[0:7]
    (gated_hbm, normed_hbm, mixed_hbm, w_in_hbm, w_out_hbm, tokens_hbm) = refs[7:13]
    (lengths, taps, gain_mix, gain_ffn) = refs[13:17]
    (sums, tokens_out, block_out, mid_chip, mid_far, ffn_chip, ffn_far) = refs[17:24]
    (mid_land, ffn_land, land_in, land_out, land_small) = refs[24:29]
    (mid, cot, w_gu, w_d, act, ggu, own, staged, fetched) = refs[29:38]
    (proj, gated, mixed_buf, conv_in, grad_hid, grad_tok) = refs[38:44]
    (halo_out, halo_in, halo_keep, small, small_in) = refs[44:49]
    load_sems, near_sems, far_sems, keep_sem, fetch_sem = refs[49:54]
    (later_sems, row_sems, halo_sems, weight_sems, out_sems) = refs[54:59]

    def panel_of(panel):
        return jnp.where(panel < FFN_PANELS, panel_in_sums(panel), panel)

    summer = SeqSum(places, own, sums, panel_of, refs[59:])
    here = lax.axis_index("seq")
    last = 2 * places - 1
    tp_at = lax.axis_index("tp")
    core = lax.rem(tp_at, 2)
    sibling = tp_at + 1 - 2 * core
    across = lax.rem(tp_at + 2, 4)
    rows, width = mid.shape
    parts, _, wide = w_gu.shape
    half_rows = rows // 2
    chans = wide // 3
    hidden = wide // 2
    panels = 3 * hidden // LANES

    moves = [(mid_hbm, mid), (cot_hbm, cot), (w_d_hbm, w_d)]
    for c in range(parts):
        for i, source in enumerate((w_gate_hbm, w_up_hbm)):
            moves.append(
                (
                    source.at[:, c * hidden : (c + 1) * hidden],
                    w_gu.at[c, :, i * hidden : (i + 1) * hidden],
                )
            )
    loads = [
        pltpu.make_async_copy(src, dst, load_sems.at[i]) for i, (src, dst) in enumerate(moves)
    ]
    for load in loads:
        load.start()

    barrier = pltpu.get_barrier_semaphore()

    def signal(device):
        pl.semaphore_signal(barrier, inc=1, device_id=device, device_id_type=pl.DeviceIdType.MESH)

    pl.when(here > 0)(lambda: signal({"seq": here - 1}))
    pl.when(here < last)(lambda: signal({"seq": here + 1}))
    ends = jnp.where(here > 0, 1, 0) + jnp.where(here < last, 1, 0)
    greet_seq(places, ({"tp": sibling}, {"tp": across}), ends)
    ffn_pieces = own.shape[0] // (4 * HALF)
    mixer_pieces = 4 * chans * width // LANES // (4 * HALF) + 1
    count = ffn_pieces + mixer_pieces
    for load in loads:
        load.wait()

    slot_len = rows // 2 // slots

    def valid_rows(slot, first, size):
        at = lax.broadcasted_iota(jnp.int32, (size, 1), 0) + (here * slot_len + first)
        return (at < lengths[slot]).astype(jnp.float32)

    part_ticks = rows // ROW_BLOCK // ROW_TICK + width // OUT_BLOCK

    def part_cols(c):
        return pl.ds(pl.multiple_of(c * hidden, LANES), hidden)

    @pl.loop(0, parts)
    def _(c):
        @pl.loop(0, rows // ROW_BLOCK)
        def _(r):
            at = pl.ds(pl.multiple_of(r * ROW_BLOCK, ROW_BLOCK), ROW_BLOCK)

            @pl.when(c == 0)
            def _():
                per_slot = slot_len // ROW_BLOCK
                mask = valid_rows(r // per_slot, lax.rem(r, per_slot) * ROW_BLOCK, ROW_BLOCK)
                cot[at, :] = (mask * cot[at, :].astype(jnp.float32)).astype(jnp.bfloat16)

            both = jnp.dot(mid[at, :], w_gu[c], preferred_element_type=jnp.float32)
            gate, up = both[:, :hidden], both[:, hidden:]
            grad_act = dot_cols(cot[at, :], w_d[part_cols(c), :])
            sigmoid = 1.0 / (1.0 + jnp.exp(-gate))
            silu = gate * sigmoid
            act[at, part_cols(c)] = (silu * up).astype(jnp.bfloat16)
            slope = sigmoid * (1.0 + gate * (1.0 - sigmoid))
            ggu[c, at, :hidden] = (grad_act * up * slope).astype(jnp.bfloat16)
            ggu[c, at, hidden:] = (grad_act * silu).astype(jnp.bfloat16)

            @pl.when((c > 0) & (lax.rem(r, ROW_TICK) == ROW_TICK - 1))
            def _():
                summer.tick((c - 1) * part_ticks + r // ROW_TICK, count)

        @pl.loop(0, width // OUT_BLOCK)
        def _(m):
            first = pl.multiple_of(m * OUT_BLOCK, OUT_BLOCK)
            at = pl.ds(first, OUT_BLOCK)
            base = c * (panels * width) + first

            def put(block, panel):
                for j in range(block.shape[1] // LANES):
                    to = pl.multiple_of(base + (panel + j) * width, OUT_BLOCK)
                    own[pl.ds(to, OUT_BLOCK), :] = block[:, j * LANES : (j + 1) * LANES]

            put(dot_rows(mid[:, at], ggu[c]), 0)
            put(dot_rows(cot[:, at], act[:, part_cols(c)]), wide // LANES)

            @pl.when(c > 0)
            def _():
                summer.tick((c - 1) * part_ticks + rows // ROW_BLOCK // ROW_TICK + m, count)

    early = (parts - 1) * part_ticks
    blocks = rows // 2 // OUT_BLOCK
    def row_block(half, k):
        return pl.ds(pl.multiple_of((half * blocks + k) * OUT_BLOCK, OUT_BLOCK), OUT_BLOCK)

    def mid_part(at):
        return sum(dot_cols(ggu[c, at, :], w_gu[c]) for c in range(parts))

    def ffn_part(at):
        return sum(
            jnp.dot(
                act[at, c * hidden : (c + 1) * hidden],
                w_d[c * hidden : (c + 1) * hidden, :],
                preferred_element_type=jnp.float32,
            )
            for c in range(parts)
        )

    def near(which, land, k):
        return pltpu.make_async_remote_copy(
            src_ref=staged.at[lax.rem(k, 2)],
            dst_ref=land.at[row_block(0, k)],
            send_sem=near_sems.at[which, 0, k],
            recv_sem=near_sems.at[which, 1, k],
            device_id={"tp": sibling},
            device_id_type=pl.DeviceIdType.MESH,
        )

    def far(which, chip, there, k):
        return pltpu.make_async_remote_copy(
            src_ref=chip.at[row_block(0, k)],
            dst_ref=there.at[row_block(0, k)],
            send_sem=far_sems.at[which, 0, k],
            recv_sem=far_sems.at[which, 1, k],
            device_id={"tp": across},
            device_id_type=pl.DeviceIdType.MESH,
        )

    def ffn_across(k):
        return far(1, ffn_chip, ffn_far, k)

    def tp_sum(which, part, land, chip, first_tick):
        @pl.loop(0, blocks)
        def _(k):
            @pl.when(k >= 2)
            def _():
                near(which, land, k - 2).wait_send()

            staged[lax.rem(k, 2)] = part(row_block(1 - core, k))
            near(which, land, k).start()

        for k in range(max(blocks - 2, 0), blocks):
            near(which, land, k).wait_send()

        @pl.loop(0, blocks)
        def _(k):
            near(which, land, k).wait_recv()
            fetch = pltpu.make_async_copy(land.at[row_block(0, k)], fetched, fetch_sem)
            fetch.start()
            staged[0] = part(row_block(core, k))
            fetch.wait()
            staged[0] += fetched[...]
            keep = pltpu.make_async_copy(staged.at[0], chip.at[row_block(0, k)], keep_sem)
            keep.start()
            summer.tick(first_tick + k, count)
            keep.wait()
            if which == 0:
                far(0, mid_chip, mid_far, k).start()

    tp_sum(0, mid_part, mid_land, mid_chip, early)
    tp_sum(1, ffn_part, ffn_land, ffn_chip, early + blocks)

    own_half = pl.ds(pl.multiple_of(core * half_rows, half_rows), half_rows)
    low_half, high_half = pl.ds(0, half_rows), pl.ds(half_rows, half_rows)
    w_out, grad_mixer = mid.at[low_half], mid.at[high_half]
    normed, mixed = act.at[low_half, pl.ds(0, width)], act.at[high_half, pl.ds(0, width)]
    tokens = w_d.at[low_half]
    w_in = (ggu.at[2, low_half], ggu.at[2, high_half], w_gu.at[0], w_gu.at[1])
    moves = [
        (w_out_hbm, w_out),
        (tokens_hbm.at[own_half], tokens),
        (normed_hbm, normed),
        (mixed_hbm, mixed),
    ]
    for j in range(4):
        for g in range(3):
            first = g * width + j * chans
            moves.append(
                (w_in_hbm.at[:, first : first + chans], w_in[j].at[:, g * chans : (g + 1) * chans])
            )
    loads = [
        pltpu.make_async_copy(src, dst, later_sems.at[i]) for i, (src, dst) in enumerate(moves)
    ]
    for load in loads:
        load.start()
    chip, far_rows, hidden_rows = staged.at[0], staged.at[1], fetched
    per_slot = slot_len // OUT_BLOCK
    small[...] = jnp.zeros_like(small)
    ticked = early + 2 * blocks

    @pl.loop(ticked, FIRST_MIXER_TICK)
    def _(t):
        summer.tick(t, count)

    @pl.loop(0, blocks)
    def _(k):
        far(0, mid_chip, mid_far, k).wait()
        ffn_across(k).start()

    for load in loads:
        load.wait()

    def shard_rows(shard, first, size):
        at = lax.rem(shard, 2) * half_rows + first
        return shard // 2, pl.ds(pl.multiple_of(at, size), size)

    def place_of(n):
        slot = n // per_slot
        block = per_slot - 1 - lax.rem(n, per_slot)
        return slot, block, pl.multiple_of(slot * slot_len + block * OUT_BLOCK, OUT_BLOCK)

    def mid_loads(first):
        at = pl.ds(first, OUT_BLOCK)
        return [
            pltpu.make_async_copy(src.at[at], dst, row_sems.at[i])
            for i, (src, dst) in enumerate(((mid_chip, chip), (mid_far, far_rows), (hidden_hbm, hidden_rows)))
        ]

    def proj_loads(slot, block, first):
        return [
            pltpu.make_async_copy(proj_hbm.at[pl.ds(first, OUT_BLOCK)], proj, row_sems.at[3]),
            pltpu.make_async_copy(
                gated_hbm.at[slot, pl.ds(pl.multiple_of(block * OUT_BLOCK, 8), OUT_BLOCK + 8)],
                gated,
                row_sems.at[4],
            ),
        ]

    def start(copies):
        for copy in copies:
            copy.start()

    def wait(copies):
        for copy in copies:
            copy.wait()

    def remote(src, dst, sems, i, device):
        return pltpu.make_async_remote_copy(
            src_ref=src,
            dst_ref=dst,
            send_sem=sems.at[0, i],
            recv_sem=sems.at[1, i],
            device_id=device,
            device_id_type=pl.DeviceIdType.MESH,
        )

    def block_at(k):
        return pl.ds(pl.multiple_of(k * OUT_BLOCK, OUT_BLOCK), OUT_BLOCK)

    def own_rows(first, size):
        return pl.ds(pl.multiple_of(core * half_rows + first, size), size)

    def hidden_grad(chip_part, far_part, hidden_part, cot_part):
        grad_mid = chip_part + far_part
        scale = rms_scale(hidden_part)
        unit = hidden_part * scale
        grad = cot_part.astype(jnp.float32) + norm_back(grad_mid, gain_ffn[...], unit, scale)
        return grad, grad_mid * unit

    def halo_copy(slot, device):
        return remote(halo_out.at[slot], halo_in.at[slot], halo_sems, slot, {"seq": device})

    head = 16
    for slot in range(slots):
        at = pl.ds(slot * slot_len, head)
        top = pl.ds(0, head)
        copies = [
            pltpu.make_async_copy(src.at[at], dst, row_sems.at[i])
            for i, (src, dst) in enumerate(
                (
                    (mid_chip, chip.at[top]),
                    (mid_far, far_rows.at[top]),
                    (hidden_hbm, hidden_rows.at[top]),
                    (proj_hbm, proj.at[top]),
                )
            )
        ]
        start(copies)
        wait(copies)
        grad, _ = hidden_grad(
            chip[top, :], far_rows[top, :], hidden_rows[top, :], cot[own_rows(slot * slot_len, head), :]
        )
        grad_mixed = dot_cols(grad.astype(jnp.bfloat16), w_out[...])
        halo_out[slot] = (grad_mixed * proj[top, width : 2 * width])[:8]
        pl.when(here > 0)(lambda slot=slot: halo_copy(slot, here - 1).start())

    slot, block, first = place_of(0)
    start(mid_loads(first))
    start(proj_loads(slot, block, first))

    @pl.when(here == last)
    def _():
        halo_in[...] = jnp.zeros_like(halo_in)

    @pl.when(here < last)
    def _():
        for slot in range(slots):
            halo_copy(slot, here + 1).wait_recv()

    def out_rows(first):
        return own_rows(first, OUT_BLOCK)

    def hand_out(target, first, i):
        at = out_rows(first)
        return (
            pltpu.make_async_copy(grad_tok, target.at[at], out_sems.at[0, 2 * blocks]),
            remote(grad_tok, target.at[at], out_sems, i, {"tp": sibling}),
        )

    @pl.loop(0, blocks)
    def _(n):
        slot, block, first = place_of(n)
        at = pl.ds(first, OUT_BLOCK)
        wait(mid_loads(first))

        @pl.loop(0, OUT_BLOCK // SUB_ROWS)
        def _(r):
            sub = pl.ds(pl.multiple_of(r * SUB_ROWS, SUB_ROWS), SUB_ROWS)
            whole = pl.ds(pl.multiple_of(first + r * SUB_ROWS, SUB_ROWS), SUB_ROWS)
            grad, for_gain = hidden_grad(
                chip[sub, :],
                far_rows[sub, :],
                hidden_rows[sub, :],
                cot[own_rows(first + r * SUB_ROWS, SUB_ROWS), :],
            )
            grad_hid[sub, :] = grad
            grad_mixer[whole, :] = grad.astype(jnp.bfloat16)
            small[1:2, :] += jnp.sum(for_gain, axis=0, keepdims=True)

        @pl.when(n < blocks - 1)
        def _():
            start(mid_loads(place_of(n + 1)[2]))

        mixed_buf[...] = dot_cols(grad_mixer[at, :], w_out[...])
        wait(proj_loads(slot, block, first))

        @pl.when(block == per_slot - 1)
        def _():
            conv_in[pl.ds(OUT_BLOCK, 8), :] = halo_in[slot]

        @pl.when(block < per_slot - 1)
        def _():
            conv_in[pl.ds(OUT_BLOCK, 8), :] = halo_keep[...]

        summer.tick(FIRST_MIXER_TICK + 2 * n, count)
        mask = valid_rows(core * slots + slot, block * OUT_BLOCK, OUT_BLOCK)

        @pl.loop(0, width // chans)
        def _(c):
            def cols(gate):
                return pl.ds(pl.multiple_of(gate * width + c * chans, chans), chans)

            here_cols = cols(0)
            pair, shard_at = shard_rows(c, first, OUT_BLOCK)
            in_gate, out_gate, conv_value = (proj[:, cols(g)] for g in range(3))
            grad_mixed = mixed_buf[:, here_cols]
            now = grad_mixed * out_gate
            conv_in[pl.ds(0, OUT_BLOCK), here_cols] = now
            seen = [gated[pl.ds(6 + j, OUT_BLOCK), here_cols] for j in range(3)]
            tap = [taps[j : j + 1, here_cols] for j in range(3)]
            conv_sum = tap[0] * seen[0] + tap[1] * seen[1] + tap[2] * seen[2]
            for j in range(3):
                small[2 + j : 3 + j, here_cols] += jnp.sum(now * seen[j], axis=0, keepdims=True)
            ggu[pair, shard_at, chans : 2 * chans] = (grad_mixed * conv_sum).astype(jnp.bfloat16)
            grad_gated = mask * (
                tap[2] * now
                + tap[1] * conv_in[pl.ds(1, OUT_BLOCK), here_cols]
                + tap[0] * conv_in[pl.ds(2, OUT_BLOCK), here_cols]
            )
            ggu[pair, shard_at, :chans] = (grad_gated * conv_value).astype(jnp.bfloat16)
            ggu[pair, shard_at, 2 * chans : 3 * chans] = (grad_gated * in_gate).astype(jnp.bfloat16)

        halo_keep[...] = conv_in[pl.ds(0, 8), :]

        @pl.when(n < blocks - 1)
        def _():
            start(proj_loads(*place_of(n + 1)))

        def shard_grad(j):
            pair, shard_at = shard_rows(j, first, OUT_BLOCK)
            return dot_cols(ggu[pair, shard_at, :], w_in[j][...])

        mixed_buf[...] = sum(shard_grad(j) for j in range(4))

        @pl.when(n > 0)
        def _():
            local, there = hand_out(tokens_out, place_of(n - 1)[2], n - 1)
            local.wait()
            there.wait_send()

        @pl.loop(0, OUT_BLOCK // SUB_ROWS)
        def _(r):
            sub = pl.ds(pl.multiple_of(r * SUB_ROWS, SUB_ROWS), SUB_ROWS)
            whole = pl.ds(pl.multiple_of(first + r * SUB_ROWS, SUB_ROWS), SUB_ROWS)
            inputs = tokens[whole, :].astype(jnp.float32)
            scale = rms_scale(inputs)
            unit = inputs * scale
            grad_in = mixed_buf[sub, :]
            grad_tok[sub, :] = grad_hid[sub, :] + norm_back(grad_in, gain_mix[...], unit, scale)
            small[0:1, :] += jnp.sum(grad_in * unit, axis=0, keepdims=True)

        start(hand_out(tokens_out, first, n))
        summer.tick(FIRST_MIXER_TICK + 2 * n + 1, count)

    in_blocks = width // OUT_BLOCK
    stages = [proj.at[:, i * wide : (i + 1) * wide] for i in range(3)]

    def to_near(src, dst, i):
        return remote(src, dst, weight_sems, i, {"tp": sibling})

    def near_in(m):
        cols = pl.ds(pl.multiple_of(lax.rem(m, 2) * wide, LANES), wide)
        return to_near(proj.at[:, cols], land_in.at[m], m)

    near_out = to_near(grad_hid, land_out, in_blocks)
    near_small = to_near(small, land_small, in_blocks + 1)

    def in_part(m, shard):
        pair, shard_at = shard_rows(shard, 0, half_rows)
        return dot_rows(normed[:, block_at(m)], ggu[pair, shard_at, :])

    def out_part(shard):
        at = pl.ds(pl.multiple_of(shard * chans, LANES), chans)
        return dot_rows(mixed[:, at], grad_mixer[...])

    near_small.start()
    first_tick = FIRST_MIXER_TICK + 2 * blocks

    @pl.loop(0, in_blocks)
    def _(m):
        @pl.when(m >= 2)
        def _():
            near_in(m - 2).wait_send()

        cols = pl.ds(pl.multiple_of(lax.rem(m, 2) * wide, LANES), wide)
        proj[:, cols] = in_part(m, sibling)
        near_in(m).start()
        summer.tick(first_tick + m, count)

    grad_hid[...] = out_part(sibling)
    near_out.start()

    @pl.loop(0, in_blocks)
    def _(m):
        near_in(m).wait_recv()
        fetch = pltpu.make_async_copy(land_in.at[m], stages[2], row_sems.at[0])
        fetch.start()
        part = in_part(m, tp_at)
        fetch.wait()
        for i in range(wide // LANES):
            to = pl.multiple_of(i * width + m * OUT_BLOCK, OUT_BLOCK)
            own[pl.ds(to, OUT_BLOCK), :] = (
                part[:, i * LANES : (i + 1) * LANES]
                + proj[:, 2 * wide + i * LANES : 2 * wide + (i + 1) * LANES]
            )

        summer.tick(first_tick + in_blocks + m, count)

    near_out.wait_recv()
    near_small.wait_recv()
    fetches = [
        pltpu.make_async_copy(land_out, mixed_buf, row_sems.at[0]),
        pltpu.make_async_copy(land_small, small_in, row_sems.at[1]),
    ]
    start(fetches)
    part = out_part(tp_at)
    wait(fetches)
    out_first = wide // LANES * width
    small_first = out_first + width // LANES * chans
    for p in range(width // LANES):
        cols = slice(p * LANES, (p + 1) * LANES)
        own[pl.ds(out_first + p * chans, chans), :] = part[:, cols] + mixed_buf[:, cols]
        own[pl.ds(small_first + 8 * p, 8), :] = small[:, cols] + small_in[:, cols]
    unused = 4 * HALF - 8 * (width // LANES)
    own[pl.ds(small_first + 4 * HALF - unused, unused), :] = jnp.zeros((unused, LANES), jnp.float32)

    local, there = hand_out(tokens_out, place_of(blocks - 1)[2], blocks - 1)
    local.wait()
    there.wait_send()
    done = first_tick + 2 * in_blocks
    pause = BLOCK_TICK

    @pl.loop(done, pause)
    def _(t):
        summer.tick(t, count)

    @pl.loop(0, blocks)
    def _(k):
        ffn_across(k).wait_recv()
        at = block_at(k)
        copies = [
            pltpu.make_async_copy(src.at[at], dst, row_sems.at[i])
            for i, (src, dst) in enumerate(((ffn_chip, chip), (ffn_far, far_rows), (hidden_hbm, hidden_rows)))
        ]
        start(copies)

        @pl.when(k > 0)
        def _():
            local, there = hand_out(block_out, (k - 1) * OUT_BLOCK, blocks + k - 1)
            local.wait()
            there.wait_send()

        wait(copies)
        grad_tok[...] = hidden_rows[...] + (chip[...] + far_rows[...])
        start(hand_out(block_out, k * OUT_BLOCK, blocks + k))
        summer.tick(pause + k, count)

    @pl.loop(pause + blocks, count + summer.P_LAGS[-1][1])
    def _(t):
        summer.tick(t, count)

    local, there = hand_out(block_out, (blocks - 1) * OUT_BLOCK, 2 * blocks - 1)
    local.wait()
    there.wait_send()

    @pl.loop(0, blocks)
    def _(k):
        ffn_across(k).wait_send()
        hand_out(tokens_out, place_of(k)[2], k)[1].wait_recv()
        hand_out(block_out, k * OUT_BLOCK, blocks + k)[1].wait_recv()

    for m in range(max(in_blocks - 2, 0), in_blocks):
        near_in(m).wait_send()
    near_out.wait_send()
    near_small.wait_send()

    @pl.when(here > 0)
    def _():
        for slot in range(slots):
            halo_copy(slot, here - 1).wait_send()


def back_both(hbm, vmem, slots, sum_cols, collective_id):
    normed_mid, _, w_gate, _, w_d, _, _, gated, _, _, _, _, _ = hbm
    rows, width = normed_mid.shape
    half_rows = rows // 2
    local = w_gate.shape[1]
    hidden = local // FFN_PARTS
    chans = 2 * hidden // 3
    blocks = half_rows // OUT_BLOCK
    in_blocks = width // OUT_BLOCK
    f32, low = jnp.float32, jnp.bfloat16
    half = jax.ShapeDtypeStruct((half_rows, width), f32)
    full = jax.ShapeDtypeStruct((rows, width), f32)
    block = pltpu.VMEM((OUT_BLOCK, width), f32)
    row8 = pltpu.VMEM((8, width), f32)
    anywhere = pl.BlockSpec(memory_space=pl.ANY)
    return pl.pallas_call(
        functools.partial(back_kernel, lax.axis_size("seq") // 2, slots),
        out_shape=[jax.ShapeDtypeStruct((width, sum_cols), f32)]
        + [full] * 2
        + [half] * 6
        + [
            jax.ShapeDtypeStruct((in_blocks, OUT_BLOCK, 2 * hidden), f32),
            jax.ShapeDtypeStruct((chans, width), f32),
            jax.ShapeDtypeStruct((8, width), f32),
        ],
        in_specs=[anywhere] * len(hbm)
        + [pl.BlockSpec(memory_space=pltpu.SMEM)]
        + [pl.BlockSpec(memory_space=pltpu.VMEM)] * (len(vmem) - 1),
        out_specs=[anywhere] * 12,
        scratch_shapes=[
            pltpu.VMEM((rows, width), low),
            pltpu.VMEM((rows, width), low),
            pltpu.VMEM((FFN_PARTS, width, 2 * hidden), low),
            pltpu.VMEM(w_d.shape, low),
            pltpu.VMEM((rows, local), low),
            pltpu.VMEM((FFN_PARTS, rows, 2 * hidden), low),
            pltpu.VMEM((3 * local * width // LANES, LANES), f32),
            pltpu.VMEM((2, OUT_BLOCK, width), f32),
            block,
            pltpu.VMEM((OUT_BLOCK, 3 * width), f32),
            pltpu.VMEM((OUT_BLOCK + 8, width), f32),
            block,
            pltpu.VMEM((OUT_BLOCK + 8, width), f32),
            block,
            block,
            pltpu.VMEM((slots, 8, width), f32),
            pltpu.VMEM((slots, 8, width), f32),
            row8,
            row8,
            row8,
            pltpu.SemaphoreType.DMA((3 + 2 * FFN_PARTS,)),
            pltpu.SemaphoreType.DMA((2, 2, blocks)),
            pltpu.SemaphoreType.DMA((2, 2, blocks)),
            pltpu.SemaphoreType.DMA,
            pltpu.SemaphoreType.DMA,
            pltpu.SemaphoreType.DMA((16,)),
            pltpu.SemaphoreType.DMA((5,)),
            pltpu.SemaphoreType.DMA((2, slots)),
            pltpu.SemaphoreType.DMA((2, in_blocks + 2)),
            pltpu.SemaphoreType.DMA((2, 2 * blocks + 1)),
        ]
        + seq_sum_scratch(),
        compiler_params=pltpu.CompilerParams(
            collective_id=collective_id, has_side_effects=True, vmem_limit_bytes=VMEM_LIMIT
        ),
        cost_estimate=pl.CostEstimate(
            flops=18 * rows * width * local, bytes_accessed=800 << 20, transcendentals=0
        ),
        name="back_both",
    )(*hbm, *vmem)


def front_kernel(places, slots, *refs):
    (w_in, w_out, taps, gain_mix, gain_ffn, valid, tokens_hbm) = refs[0:7]
    (in_hbm, out_hbm, full_taps, mid_hbm, hidden_hbm, proj_hbm, gated_hbm) = refs[7:14]
    (normed_hbm, mixed_hbm) = refs[14:16]
    own_in, own_out, far_in, far_out, sib_in, sib_out, sibfar_in, sibfar_out = refs[16:24]
    own_taps, far_taps, sib_taps, sibfar_taps, share_in, share_out = refs[24:30]
    (full_in, full_out, tokens, normed, mixed, out_gate, gates, gated) = refs[30:38]
    (unit_out, unit_in, hidden) = refs[38:41]
    sends, recvs, once, halo_sems, gate_sems, unit_sems, keep_sems, mid_sems = refs[41:49]
    here = lax.axis_index("seq")
    place, side = here // 2, lax.rem(here, 2)
    last = places - 1
    end = 2 * places - 1
    tp_at = lax.axis_index("tp")
    core = lax.rem(tp_at, 2)
    sibling = tp_at + 1 - 2 * core
    across = lax.rem(tp_at + 2, 4)
    far_sibling = sibling + across - tp_at
    in_rows = w_in.shape[0] // (2 * places)
    out_rows = w_out.shape[0] // (2 * places)
    chans = w_in.shape[1] // 3
    rows, width = tokens.shape
    slot_len = rows // slots
    low = jnp.bfloat16

    load_tokens = pltpu.make_async_copy(
        tokens_hbm.at[pl.ds(pl.multiple_of(core * rows, rows), rows)], tokens, keep_sems.at[0]
    )
    load_tokens.start()
    barrier = pltpu.get_barrier_semaphore()

    def signal(device):
        pl.semaphore_signal(barrier, inc=1, device_id=device, device_id_type=pl.DeviceIdType.MESH)

    pl.when(here > 0)(lambda: signal({"seq": here - 1}))
    pl.when(here < end)(lambda: signal({"seq": here + 1}))
    ends = jnp.where(here > 0, 1, 0) + jnp.where(here < end, 1, 0)
    greet_seq(places, ({"tp": sibling}, {"tp": across}), ends)

    def shares(j):
        return (
            pl.ds(pl.multiple_of(j * in_rows, in_rows), in_rows),
            pl.ds(pl.multiple_of(j * out_rows, out_rows), out_rows),
        )

    def remote(src, dst, send, recv, device):
        return pltpu.make_async_remote_copy(
            src_ref=src,
            dst_ref=dst,
            send_sem=send,
            recv_sem=recv,
            device_id=device,
            device_id_type=pl.DeviceIdType.MESH,
        )

    def copies(source, target, j, kind, device):
        for i, at in enumerate(shares(j)):
            yield remote(
                source[i] if kind == 0 else source[i].at[at],
                target[i].at[at],
                sends.at[kind, i, j],
                recvs.at[0 if kind < 4 else 1, i, j],
                device,
            )

    share, far, sibfar = (share_in, share_out), (far_in, far_out), (sibfar_in, sibfar_out)

    def across_share():
        return copies(share, far, here, 0, {"tp": across})

    def to_right(j):
        return copies(far, far, j, 1, {"seq": here + 2})

    def to_left(j):
        return copies(far, far, j, 2, {"seq": here - 2})

    def to_side(j):
        return copies(far, far, j, 3, {"seq": here + 1 - 2 * side})

    def to_sibling(j):
        return copies(far, sibfar, j, 4, {"tp": sibling})

    def start(group):
        for copy in group:
            copy.start()

    def arrived(group):
        for copy in group:
            copy.wait_recv()

    def left_source(group):
        for copy in group:
            copy.wait_send()

    def single(i, src, dst, device):
        return remote(src, dst, once.at[0, i], once.at[1, i], device)

    for source, held, at in zip((w_in, w_out), share, shares(here)):
        held[...] = source[at, :].astype(jnp.float32)
    start(across_share())
    own_taps[...] = taps[...]
    taps_far = single(0, own_taps, far_taps, {"tp": across})
    taps_sib = single(1, own_taps, sib_taps, {"tp": sibling})
    taps_sibfar = single(2, far_taps, sibfar_taps, {"tp": sibling})
    own_in[...] = w_in[...].astype(jnp.float32)
    own_out[...] = w_out[...].astype(jnp.float32)
    in_sib = single(3, own_in, sib_in, {"tp": sibling})
    out_sib = single(4, own_out, sib_out, {"tp": sibling})
    for copy in (taps_far, taps_sib, in_sib, out_sib):
        copy.start()

    def gate_cols(g, index):
        return pl.ds(pl.multiple_of(g * width + index * chans, LANES), chans)

    def place_shard(shard_in, shard_out, shard_taps, index):
        for g in range(3):
            full_in[:, gate_cols(g, index)] = shard_in[:, g * chans : (g + 1) * chans].astype(low)
        at = pl.ds(pl.multiple_of(index * chans, chans), chans)
        full_out[at, :] = shard_out[...].astype(low)
        full_taps[:, gate_cols(0, index)] = shard_taps[...]

    def gate_out(turn, index, g):
        if g == 1:
            return pltpu.make_async_copy(
                out_gate.at[:, gate_cols(0, index)],
                proj_hbm.at[:, gate_cols(1, index)],
                gate_sems.at[turn, 1],
            )
        return pltpu.make_async_copy(
            gates.at[turn % 2, g // 2], proj_hbm.at[:, gate_cols(g, index)], gate_sems.at[turn, g]
        )

    def halo(turn, index, slot):
        return remote(
            gated.at[slot, pl.ds(slot_len, 8), gate_cols(0, index)],
            gated.at[slot, pl.ds(0, 8), gate_cols(0, index)],
            halo_sems.at[0, turn, slot],
            halo_sems.at[1, turn, slot],
            {"seq": here + 1},
        )

    order = (tp_at, sibling, across, far_sibling)

    def project(turn):
        index = order[turn]
        cols = gate_cols(0, index)
        if turn >= 2:
            gate_out(turn - 2, order[turn - 2], 0).wait()
            gate_out(turn - 2, order[turn - 2], 2).wait()

        @pl.loop(0, slots)
        def _(s):
            at = pl.ds(pl.multiple_of(s * slot_len, slot_len), slot_len)

            def gate(g):
                return jnp.dot(
                    normed[at, :], full_in[:, gate_cols(g, index)],
                    preferred_element_type=jnp.float32,
                )

            in_gate, value = gate(0), gate(2)
            gates[turn % 2, 0, at, :] = in_gate
            gates[turn % 2, 1, at, :] = value
            gated[s, pl.ds(8, slot_len), cols] = valid[at, :] * in_gate * value
            out_gate[at, cols] = gate(1)

        for g in range(3):
            gate_out(turn, index, g).start()

        @pl.when(here < end)
        def _():
            for slot in range(slots):
                halo(turn, index, slot).start()

    def convolve(turn):
        index = order[turn]
        cols = gate_cols(0, index)

        @pl.when(here > 0)
        def _():
            for slot in range(slots):
                halo(turn, index, slot).wait_recv()

        @pl.loop(0, slots)
        def _(s):
            at = pl.ds(pl.multiple_of(s * slot_len, slot_len), slot_len)
            seen = [gated[s, pl.ds(6 + j, slot_len), cols] for j in range(3)]
            tap = [full_taps[j : j + 1, cols] for j in range(3)]
            conv_sum = tap[0] * seen[0] + tap[1] * seen[1] + tap[2] * seen[2]
            mixed[at, cols] = (out_gate[at, cols] * conv_sum).astype(low)

    @pl.when(here == 0)
    def _():
        for slot in range(slots):
            gated[slot, pl.ds(0, 8), :] = jnp.zeros((8, width), jnp.float32)

    load_tokens.wait()

    @pl.loop(0, rows // SUB_ROWS)
    def _(r):
        at = pl.ds(pl.multiple_of(r * SUB_ROWS, SUB_ROWS), SUB_ROWS)
        inputs = tokens[at, :].astype(jnp.float32)
        normed[at, :] = (gain_mix[...] * (inputs * rms_scale(inputs))).astype(low)

    keep_normed = pltpu.make_async_copy(normed, normed_hbm, keep_sems.at[0])
    keep_normed.start()
    place_shard(own_in, own_out, own_taps, tp_at)
    project(0)

    arrived(across_share())
    pl.when(place < last)(lambda: start(to_right(here)))
    pl.when(place > 0)(lambda: start(to_left(here)))
    start(to_side(here))
    start(to_sibling(here))
    taps_far.wait_recv()
    taps_sibfar.start()
    in_sib.wait_recv()
    out_sib.wait_recv()
    taps_sib.wait_recv()
    place_shard(sib_in, sib_out, sib_taps, sibling)
    project(1)

    def from_side(q):
        j = 2 * q + 1 - side
        arrived(to_side(j))
        start(to_sibling(j))

    @pl.loop(1, places)
    def _(d):
        @pl.when(place - d >= 0)
        def _():
            j = here - 2 * d
            arrived(to_right(j))
            pl.when(place < last)(lambda: start(to_right(j)))
            start(to_side(j))
            start(to_sibling(j))

        @pl.when(place + d <= last)
        def _():
            j = here + 2 * d
            arrived(to_left(j))
            pl.when(place > 0)(lambda: start(to_left(j)))
            start(to_side(j))
            start(to_sibling(j))

        @pl.when(d == 1)
        def _():
            from_side(place)
            convolve(0)
            convolve(1)

        pl.when(place - d >= 0)(lambda: from_side(place - d))
        pl.when(place + d <= last)(lambda: from_side(place + d))

    place_shard(far_in, far_out, far_taps, across)
    project(2)
    taps_sibfar.wait_recv()

    @pl.loop(0, 2 * places)
    def _(j):
        arrived(to_sibling(j))

    place_shard(sibfar_in, sibfar_out, sibfar_taps, far_sibling)
    project(3)
    keep_in = pltpu.make_async_copy(full_in, in_hbm, keep_sems.at[1])
    keep_out = pltpu.make_async_copy(full_out, out_hbm, keep_sems.at[2])
    keep_in.start()
    keep_out.start()
    convolve(2)
    convolve(3)
    keep_gated = pltpu.make_async_copy(gated, gated_hbm, keep_sems.at[3])
    keep_mixed = pltpu.make_async_copy(mixed, mixed_hbm, keep_sems.at[4])
    keep_gated.start()
    keep_mixed.start()
    keep_normed.wait()

    blocks = rows // OUT_BLOCK

    def block_at(k, first=0):
        return pl.ds(pl.multiple_of(first + k * OUT_BLOCK, OUT_BLOCK), OUT_BLOCK)

    def unit_copy(k):
        return remote(
            unit_out.at[block_at(k)], unit_in.at[block_at(k)],
            unit_sems.at[0, k], unit_sems.at[1, k], {"tp": sibling},
        )

    def hidden_copy(k):
        return pltpu.make_async_copy(
            hidden.at[lax.rem(k, 2)], hidden_hbm.at[block_at(k)], mid_sems.at[0, lax.rem(k, 2)]
        )

    def mid_copy(half, held, whose, k):
        return pltpu.make_async_copy(
            held.at[block_at(k)], mid_hbm.at[block_at(k, whose * rows)], mid_sems.at[half, k]
        )

    @pl.loop(0, blocks)
    def _(k):
        slot = lax.rem(k, 2)
        at = block_at(k)
        pl.when(k >= 2)(lambda: hidden_copy(k - 2).wait())
        hidden[slot] = jnp.dot(mixed[at, :], full_out[...], preferred_element_type=jnp.float32)

        @pl.loop(0, OUT_BLOCK // SUB_ROWS)
        def _(r):
            sub = pl.ds(pl.multiple_of(r * SUB_ROWS, SUB_ROWS), SUB_ROWS)
            whole = pl.ds(pl.multiple_of(k * OUT_BLOCK + r * SUB_ROWS, SUB_ROWS), SUB_ROWS)
            hidden_rows = tokens[whole, :].astype(jnp.float32) + hidden[slot, sub, :]
            hidden[slot, sub, :] = hidden_rows
            unit = hidden_rows * rms_scale(hidden_rows)
            unit_out[whole, :] = unit
            normed[whole, :] = (gain_ffn[...] * unit).astype(low)

        unit_copy(k).start()
        hidden_copy(k).start()
        mid_copy(1, normed, core, k).start()

    keep_mixed.wait()

    @pl.loop(0, blocks)
    def _(k):
        unit_copy(k).wait_recv()

        @pl.loop(0, OUT_BLOCK // SUB_ROWS)
        def _(r):
            whole = pl.ds(pl.multiple_of(k * OUT_BLOCK + r * SUB_ROWS, SUB_ROWS), SUB_ROWS)
            mixed[whole, :] = (gain_ffn[...] * unit_in[whole, :]).astype(low)

        mid_copy(2, mixed, 1 - core, k).start()

    @pl.loop(0, blocks)
    def _(k):
        unit_copy(k).wait_send()
        mid_copy(1, normed, core, k).wait()
        mid_copy(2, mixed, 1 - core, k).wait()

    for k in range(max(blocks - 2, 0), blocks):
        hidden_copy(k).wait()
    keep_in.wait()
    keep_out.wait()
    keep_gated.wait()
    for turn in range(4):
        for g in range(3):
            if turn >= 2 or g == 1:
                gate_out(turn, order[turn], g).wait()

    @pl.when(here < end)
    def _():
        for turn in range(4):
            for slot in range(slots):
                halo(turn, order[turn], slot).wait_send()

    left_source(across_share())
    for copy in (taps_far, taps_sib, taps_sibfar, in_sib, out_sib):
        copy.wait_send()

    @pl.loop(0, places)
    def _(q):
        j = 2 * q + side
        left_source(to_side(j))
        pl.when((q <= place) & (place < last))(lambda: left_source(to_right(j)))
        pl.when((q >= place) & (place > 0))(lambda: left_source(to_left(j)))
        left_source(to_sibling(j))
        left_source(to_sibling(2 * q + 1 - side))


def mixer_front(w_in, w_out, taps, gain_mix, gain_ffn, valid, tokens, slots, collective_id):
    width, _, chans = w_in.shape
    rows = valid.shape[0]
    count = lax.axis_size("seq")
    group = lax.axis_size("tp")
    f32, low = jnp.float32, jnp.bfloat16
    blocks = rows // OUT_BLOCK
    pair = [pltpu.VMEM((width, 3 * chans), f32), pltpu.VMEM((chans, width), f32)]
    whole = pl.BlockSpec(memory_space=pltpu.VMEM)
    anywhere = pl.BlockSpec(memory_space=pl.ANY)
    padded = (slots, rows // slots + 8, width)
    return pl.pallas_call(
        functools.partial(front_kernel, count // 2, slots),
        out_shape=[
            jax.ShapeDtypeStruct((width, 3 * chans * group), low),
            jax.ShapeDtypeStruct((chans * group, width), low),
            jax.ShapeDtypeStruct((8, chans * group), f32),
            jax.ShapeDtypeStruct((2 * rows, width), low),
            jax.ShapeDtypeStruct((rows, width), f32),
            jax.ShapeDtypeStruct((rows, 3 * width), f32),
            jax.ShapeDtypeStruct(padded, f32),
            jax.ShapeDtypeStruct((rows, width), low),
            jax.ShapeDtypeStruct((rows, width), low),
        ],
        in_specs=[whole] * 6 + [anywhere],
        out_specs=[anywhere] * 2 + [whole] + [anywhere] * 6,
        scratch_shapes=pair * 4
        + [pltpu.VMEM((8, chans), f32)] * 4
        + [
            pltpu.VMEM((width // count, 3 * chans), f32),
            pltpu.VMEM((chans // count, width), f32),
            pltpu.VMEM((width, 3 * chans * group), low),
            pltpu.VMEM((chans * group, width), low),
            pltpu.VMEM((rows, width), low),
            pltpu.VMEM((rows, width), low),
            pltpu.VMEM((rows, width), low),
            pltpu.VMEM((rows, width), f32),
            pltpu.VMEM((2, 2, rows, chans), f32),
            pltpu.VMEM(padded, f32),
            pltpu.VMEM((rows, width), f32),
            pltpu.VMEM((rows, width), f32),
            pltpu.VMEM((2, OUT_BLOCK, width), f32),
            pltpu.SemaphoreType.DMA((5, 2, count)),
            pltpu.SemaphoreType.DMA((2, 2, count)),
            pltpu.SemaphoreType.DMA((2, 5)),
            pltpu.SemaphoreType.DMA((2, 4, slots)),
            pltpu.SemaphoreType.DMA((4, 3)),
            pltpu.SemaphoreType.DMA((2, blocks)),
            pltpu.SemaphoreType.DMA((5,)),
            pltpu.SemaphoreType.DMA((3, blocks)),
        ],
        compiler_params=pltpu.CompilerParams(
            collective_id=collective_id, has_side_effects=True, vmem_limit_bytes=VMEM_LIMIT
        ),
        name="mixer_front",
    )(
        w_in.reshape(width, 3 * chans),
        w_out,
        jnp.pad(taps, ((0, 5), (0, 0))),
        gain_mix,
        gain_ffn,
        valid,
        tokens,
    )


def per_device(
    tokens, lengths, gain_mix, w_in, conv_weight, w_out, gain_ffn, w_gate, w_up, w_down, cotangent
):
    slot_count, local_len, width = tokens.shape
    chans = w_in.shape[2]
    tp_at, seq_at = lax.axis_index("tp"), lax.axis_index("seq")
    core = tp_at % 2
    half_slots = slot_count // 2
    half_rows = half_slots * local_len
    row_count = slot_count * local_len

    positions = seq_at * local_len + jnp.arange(local_len, dtype=jnp.int32)
    valid = (positions[None, :] < lengths[:, None]).astype(jnp.float32)
    valid_all = valid.reshape(row_count, 1)
    valid_rows = lax.dynamic_slice(valid_all, (core * half_rows, 0), (half_rows, 1))
    token_rows = tokens.reshape(row_count, width)
    cot_rows = cotangent.reshape(row_count, width)
    gains = gain_mix.reshape(1, width), gain_ffn.reshape(1, width)
    w_in_all, w_out_all, taps, normed_mid, hidden_res, projected, gated_rows, normed_in, mixed = (
        mixer_front(w_in, w_out, conv_weight, *gains, valid_rows, token_rows, half_slots, 3)
    )
    mixer_cols = 4 * chans
    sum_cols = FFN_PANELS * LANES + mixer_cols + LANES
    sums, grad_tokens, block_sum = back_both(
        (
            normed_mid,
            cot_rows,
            w_gate,
            w_up,
            w_down,
            hidden_res,
            projected,
            gated_rows,
            normed_in,
            mixed,
            w_in_all,
            w_out_all,
            token_rows,
        ),
        (lengths, taps, *gains),
        half_slots,
        sum_cols,
        1,
    )[:3]
    grad_tokens = grad_tokens.reshape(slot_count, local_len, width)
    block_out = (valid_all * block_sum).astype(jnp.bfloat16)
    block_out = block_out.reshape(slot_count, local_len, width)

    hidden = w_gate.shape[1]
    total_w_gate = sums[:, :hidden]
    total_w_up = sums[:, hidden : 2 * hidden]
    total_w_down = sums[:, 2 * hidden : 3 * hidden].T
    mixer_sums = sums[:, 3 * hidden :]
    total_w_in = mixer_sums[:, : 3 * chans].reshape(width, 3, chans)
    out_parts = mixer_sums[:, 3 * chans : 4 * chans]
    out_parts = out_parts.reshape(width // chans, chans, chans // LANES, LANES)
    total_w_out = out_parts.transpose(1, 2, 0, 3).reshape(chans, width)
    small = mixer_sums[: 8 * width // LANES, 4 * chans :]
    small = small.reshape(width // LANES, 8, LANES).transpose(1, 0, 2).reshape(8, width)
    total_gain_mix, total_gain_ffn = small[0], small[1]
    total_conv = lax.dynamic_slice(small, (2, tp_at * chans), (3, chans))
    return (
        block_out,
        grad_tokens,
        total_gain_mix,
        total_w_in,
        total_conv,
        total_w_out,
        total_gain_ffn,
        total_w_gate,
        total_w_up,
        total_w_down,
    )


def solution(mesh):
    rows, cols = P("tp", None), P(None, "tp")
    tokens, whole, stacked = P(None, "seq", None), P(), P(None, None, "tp")
    return jax.shard_map(
        per_device,
        mesh=mesh,
        in_specs=(
            tokens, whole, whole, stacked, cols, rows, whole, cols, cols, rows, tokens,
        ),
        out_specs=(
            tokens, tokens, whole, stacked, cols, rows, whole, cols, cols, rows,
        ),
        check_vma=False,
    )
```

```python
import functools

import jax
import jax.numpy as jnp
from jax import lax
from jax.experimental import pallas as pl
from jax.experimental.pallas import tpu as pltpu
from jax.sharding import PartitionSpec as P

NORM_EPS = 1e-05
LANES = 128
VMEM_LIMIT = 64 << 20
HALF = 128
SLOTS_IN_FLIGHT = 10


def rms_scale(values):
    return lax.rsqrt(jnp.mean(values * values, axis=-1, keepdims=True) + NORM_EPS)


def dot_rows(left, right):
    return lax.dot_general(
        left, right, (((0,), (0,)), ((), ())), preferred_element_type=jnp.float32
    )


def dot_cols(left, right):
    return lax.dot_general(
        left, right, (((1,), (1,)), ((), ())), preferred_element_type=jnp.float32
    )


def greet_seq(places, others=(), more=0):
    barrier = pltpu.get_barrier_semaphore()
    here = lax.axis_index("seq")
    place, side = here // 2, lax.rem(here, 2)

    def signal(device):
        pl.semaphore_signal(
            barrier, inc=1, device_id=device, device_id_type=pl.DeviceIdType.MESH
        )

    signal({"seq": here + 1 - 2 * side})
    for other in others:
        signal(other)
    pl.when(place > 0)(lambda: signal({"seq": here - 2}))
    pl.when(place < places - 1)(lambda: signal({"seq": here + 2}))
    ends = jnp.where(place > 0, 1, 0) + jnp.where(place < places - 1, 1, 0)
    pl.semaphore_wait(barrier, 1 + len(others) + ends + more)


class SeqSum:
    def __init__(self, places, own, out, panel_of, scratch):
        self.places, self.own, self.out, self.panel_of = places, own, out, panel_of
        self.y_in, self.p_left, self.p_right, self.p_acc = scratch[0:4]
        self.q_left, self.q_right, self.q_acc, self.q_in = scratch[4:8]
        self.sems = scratch[8]
        here = lax.axis_index("seq")
        self.place, self.side = here // 2, here % 2

    def remote(self, src, dst, slot, send, recv, place, side):
        return pltpu.make_async_remote_copy(
            src_ref=src,
            dst_ref=dst,
            send_sem=self.sems.at[send, slot],
            recv_sem=self.sems.at[recv, slot],
            device_id={"seq": place * 2 + side},
            device_id_type=pl.DeviceIdType.MESH,
        )

    def chain(self, root):
        last = self.places - 1
        left = jnp.maximum(self.place - 1, 0)
        right = jnp.minimum(self.place + 1, last)
        from_left = (self.place <= root) & (self.place > 0)
        from_right = (self.place >= root) & (self.place < last)
        return left, right, from_left, from_right

    def own_base(self, k):
        held = self.own.shape[0] // (4 * HALF)
        return pl.multiple_of(lax.rem(k, held) * 4 * HALF, 4 * HALF)

    def out_at(self, k, first, size):
        per_panel = self.out.shape[0] // (4 * HALF)
        panel = self.panel_of(k // per_panel)
        row = lax.rem(k, per_panel) * 4 * HALF + first
        return self.out.at[
            pl.ds(pl.multiple_of(row, size), size), pl.ds(pl.multiple_of(panel * LANES, LANES), LANES)
        ]

    def p_stage(self, which, k):
        place, side = self.place, self.side
        own = self.own
        slot = lax.rem(k, SLOTS_IN_FLIGHT)
        base = self.own_base(k)
        mine = pl.ds(pl.multiple_of(base + side * HALF, HALF), HALF)
        theirs = pl.ds(pl.multiple_of(base + (1 - side) * HALF, HALF), HALF)
        out_mine = self.out_at(k, side * HALF, HALF)
        root = self.places // 2 - 1 + lax.rem(k, 2)
        left, right, from_left, from_right = self.chain(root)
        acc, y_in = self.p_acc.at[slot], self.y_in.at[slot]
        from_l, from_r = self.p_left.at[slot], self.p_right.at[slot]
        remote = functools.partial(functools.partial, self.remote)

        to_side = remote(own.at[theirs], y_in, slot, 0, 1, place, 1 - side)
        up_right = remote(acc, from_l, slot, 2, 3, right, side)
        up_left = remote(acc, from_r, slot, 2, 4, left, side)

        def down(src):
            return (
                remote(src, out_mine, slot, 5, 7, left, side),
                remote(src, out_mine, slot, 6, 7, right, side),
                remote(src, out_mine, slot, 8, 9, place, 1 - side),
            )

        def keep():
            return pltpu.make_async_copy(acc, out_mine, self.sems.at[10, slot])

        def hand_down(src):
            down_left, down_right, down_side = down(src)
            down_side().start()
            pl.when(from_left)(lambda: down_left().start())
            pl.when(from_right)(lambda: down_right().start())

        if which == "split":
            to_side().start()

        if which == "up":
            to_side().wait_recv()
            acc[...] = own[mine, :] + y_in[...]

            @pl.when(place < root)
            def _():
                @pl.when(from_left)
                def _():
                    up_right().wait_recv()
                    acc[...] += from_l[...]

                up_right().start()

            @pl.when(place > root)
            def _():
                @pl.when(from_right)
                def _():
                    up_left().wait_recv()
                    acc[...] += from_r[...]

                up_left().start()

        if which == "root":

            @pl.when(place == root)
            def _():
                @pl.when(from_left)
                def _():
                    up_right().wait_recv()
                    acc[...] += from_l[...]

                @pl.when(from_right)
                def _():
                    up_left().wait_recv()
                    acc[...] += from_r[...]

                hand_down(acc)
                keep().start()

        if which == "down":

            @pl.when(place != root)
            def _():
                down(acc)[0]().wait_recv()
                hand_down(out_mine)

        if which == "end":
            down_left, down_right, down_side = down(acc)
            down_side().wait()
            to_side().wait_send()
            pl.when(from_left)(lambda: down_left().wait_send())
            pl.when(from_right)(lambda: down_right().wait_send())
            pl.when(place == root)(lambda: keep().wait())
            pl.when(place != root)(lambda: up_left().wait_send())

    def q_stage(self, which, k):
        place, side = self.place, self.side
        own = self.own
        slot = lax.rem(k, SLOTS_IN_FLIGHT)
        base = self.own_base(k)
        wide = pl.ds(pl.multiple_of(base + 2 * HALF, 2 * HALF), 2 * HALF)
        out_wide = self.out_at(k, 2 * HALF, 2 * HALF)
        root = self.places // 2 - lax.rem(k, 2)
        left, right, from_left, from_right = self.chain(root)
        acc, side_in = self.q_acc.at[slot], self.q_in.at[slot]
        from_l, from_r = self.q_left.at[slot], self.q_right.at[slot]
        remote = functools.partial(functools.partial, self.remote)

        up_right = remote(acc, from_l, slot, 11, 12, right, side)
        up_left = remote(acc, from_r, slot, 11, 13, left, side)
        to_side = remote(acc, side_in, slot, 14, 15, place, 1 - side)

        def down(src):
            return (
                remote(src, out_wide, slot, 16, 18, left, side),
                remote(src, out_wide, slot, 17, 18, right, side),
            )

        def keep():
            return pltpu.make_async_copy(side_in, out_wide, self.sems.at[19, slot])

        def hand_down(src):
            down_left, down_right = down(src)
            pl.when(from_left)(lambda: down_left().start())
            pl.when(from_right)(lambda: down_right().start())

        if which == "up":
            acc[...] = own[wide, :]

            @pl.when(place < root)
            def _():
                @pl.when(from_left)
                def _():
                    up_right().wait_recv()
                    acc[...] += from_l[...]

                up_right().start()

            @pl.when(place > root)
            def _():
                @pl.when(from_right)
                def _():
                    up_left().wait_recv()
                    acc[...] += from_r[...]

                up_left().start()

        if which == "root":

            @pl.when(place == root)
            def _():
                @pl.when(from_left)
                def _():
                    up_right().wait_recv()
                    acc[...] += from_l[...]

                @pl.when(from_right)
                def _():
                    up_left().wait_recv()
                    acc[...] += from_r[...]

                to_side().start()

        if which == "side":

            @pl.when(place == root)
            def _():
                to_side().wait_recv()
                side_in[...] += acc[...]
                hand_down(side_in)
                keep().start()

        if which == "down":

            @pl.when(place != root)
            def _():
                down(acc)[0]().wait_recv()
                hand_down(out_wide)

        if which == "end":
            down_left, down_right = down(acc)
            pl.when(from_left)(lambda: down_left().wait_send())
            pl.when(from_right)(lambda: down_right().wait_send())

            @pl.when(place == root)
            def _():
                to_side().wait_send()
                keep().wait()

            pl.when(place != root)(lambda: up_left().wait_send())

    P_LAGS = (("split", 0, 0), ("up", 2, 1), ("root", 3, 3), ("down", 6, 7), ("end", 9, 9))
    Q_LAGS = (("up", 1, 0), ("root", 2, 2), ("side", 4, 4), ("down", 6, 7), ("end", 9, 9))

    def tick(self, t, count):
        middle = (self.place == self.places // 2) | (self.place == self.places // 2 - 1)
        for stage, lags in ((self.p_stage, self.P_LAGS), (self.q_stage, self.Q_LAGS)):
            for which, mid_lag, outer_lag in lags:
                k = t - jnp.where(middle, mid_lag, outer_lag)

                @pl.when((k >= 0) & (k < count))
                def _(stage=stage, which=which, k=k):
                    stage(which, k)

    def run(self, count):
        @pl.loop(0, count + self.P_LAGS[-1][1])
        def _(t):
            self.tick(t, count)


def seq_sum_scratch():
    half = pltpu.VMEM((SLOTS_IN_FLIGHT, HALF, LANES), jnp.float32)
    wide = pltpu.VMEM((SLOTS_IN_FLIGHT, 2 * HALF, LANES), jnp.float32)
    return [half] * 4 + [wide] * 4 + [pltpu.SemaphoreType.DMA((20, SLOTS_IN_FLIGHT))]


SUB_ROWS = 64
FIRST_MIXER_TICK = 36
BLOCK_TICK = 56
FFN_PANELS = 27
FFN_PARTS = 3
ROW_BLOCK = 256
ROW_TICK = 2
OUT_BLOCK = 256


def panel_in_sums(panel):
    per_part = FFN_PANELS // FFN_PARTS
    third = per_part // 3
    inside = lax.rem(panel, per_part)
    kind = inside // third
    return kind * (FFN_PANELS // 3) + panel // per_part * third + lax.rem(inside, third)


def norm_back(grad, gain, unit, scale):
    scaled = gain * grad
    return scale * (scaled - unit * jnp.mean(scaled * unit, axis=-1, keepdims=True))


def back_kernel(places, slots, *refs):
    (mid_hbm, cot_hbm, w_gate_hbm, w_up_hbm, w_d_hbm, hidden_hbm, proj_hbm) = refs[0:7]
    (gated_hbm, normed_hbm, mixed_hbm, w_in_hbm, w_out_hbm, tokens_hbm) = refs[7:13]
    (lengths, taps, gain_mix, gain_ffn) = refs[13:17]
    (sums, tokens_out, block_out, mid_chip, mid_far, ffn_chip, ffn_far) = refs[17:24]
    (mid_land, ffn_land, land_in, land_out, land_small) = refs[24:29]
    (mid, cot, w_gu, w_d, act, ggu, own, staged, fetched) = refs[29:38]
    (proj, gated, mixed_buf, conv_in, grad_hid, grad_tok) = refs[38:44]
    (halo_out, halo_in, halo_keep, small, small_in) = refs[44:49]
    load_sems, near_sems, far_sems, keep_sem, fetch_sem = refs[49:54]
    (later_sems, row_sems, halo_sems, weight_sems, out_sems) = refs[54:59]

    def panel_of(panel):
        return jnp.where(panel < FFN_PANELS, panel_in_sums(panel), panel)

    summer = SeqSum(places, own, sums, panel_of, refs[59:])
    here = lax.axis_index("seq")
    last = 2 * places - 1
    tp_at = lax.axis_index("tp")
    core = lax.rem(tp_at, 2)
    sibling = tp_at + 1 - 2 * core
    across = lax.rem(tp_at + 2, 4)
    rows, width = mid.shape
    parts, _, wide = w_gu.shape
    half_rows = rows // 2
    chans = wide // 3
    hidden = wide // 2
    panels = 3 * hidden // LANES

    moves = [(mid_hbm, mid), (cot_hbm, cot), (w_d_hbm, w_d)]
    for c in range(parts):
        for i, source in enumerate((w_gate_hbm, w_up_hbm)):
            moves.append(
                (
                    source.at[:, c * hidden : (c + 1) * hidden],
                    w_gu.at[c, :, i * hidden : (i + 1) * hidden],
                )
            )
    loads = [
        pltpu.make_async_copy(src, dst, load_sems.at[i]) for i, (src, dst) in enumerate(moves)
    ]
    for load in loads:
        load.start()

    barrier = pltpu.get_barrier_semaphore()

    def signal(device):
        pl.semaphore_signal(barrier, inc=1, device_id=device, device_id_type=pl.DeviceIdType.MESH)

    pl.when(here > 0)(lambda: signal({"seq": here - 1}))
    pl.when(here < last)(lambda: signal({"seq": here + 1}))
    ends = jnp.where(here > 0, 1, 0) + jnp.where(here < last, 1, 0)
    greet_seq(places, ({"tp": sibling}, {"tp": across}), ends)
    ffn_pieces = own.shape[0] // (4 * HALF)
    mixer_pieces = 4 * chans * width // LANES // (4 * HALF) + 1
    count = ffn_pieces + mixer_pieces
    for load in loads:
        load.wait()

    slot_len = rows // 2 // slots

    def valid_rows(slot, first, size):
        at = lax.broadcasted_iota(jnp.int32, (size, 1), 0) + (here * slot_len + first)
        return (at < lengths[slot]).astype(jnp.float32)

    part_ticks = rows // ROW_BLOCK // ROW_TICK + width // OUT_BLOCK

    def part_cols(c):
        return pl.ds(pl.multiple_of(c * hidden, LANES), hidden)

    @pl.loop(0, parts)
    def _(c):
        @pl.loop(0, rows // ROW_BLOCK)
        def _(r):
            at = pl.ds(pl.multiple_of(r * ROW_BLOCK, ROW_BLOCK), ROW_BLOCK)

            @pl.when(c == 0)
            def _():
                per_slot = slot_len // ROW_BLOCK
                mask = valid_rows(r // per_slot, lax.rem(r, per_slot) * ROW_BLOCK, ROW_BLOCK)
                cot[at, :] = (mask * cot[at, :].astype(jnp.float32)).astype(jnp.bfloat16)

            both = jnp.dot(mid[at, :], w_gu[c], preferred_element_type=jnp.float32)
            gate, up = both[:, :hidden], both[:, hidden:]
            grad_act = dot_cols(cot[at, :], w_d[part_cols(c), :])
            sigmoid = 1.0 / (1.0 + jnp.exp(-gate))
            silu = gate * sigmoid
            act[at, part_cols(c)] = (silu * up).astype(jnp.bfloat16)
            slope = sigmoid * (1.0 + gate * (1.0 - sigmoid))
            ggu[c, at, :hidden] = (grad_act * up * slope).astype(jnp.bfloat16)
            ggu[c, at, hidden:] = (grad_act * silu).astype(jnp.bfloat16)

            @pl.when((c > 0) & (lax.rem(r, ROW_TICK) == ROW_TICK - 1))
            def _():
                summer.tick((c - 1) * part_ticks + r // ROW_TICK, count)

        @pl.loop(0, width // OUT_BLOCK)
        def _(m):
            first = pl.multiple_of(m * OUT_BLOCK, OUT_BLOCK)
            at = pl.ds(first, OUT_BLOCK)
            base = c * (panels * width) + first

            def put(block, panel):
                for j in range(block.shape[1] // LANES):
                    to = pl.multiple_of(base + (panel + j) * width, OUT_BLOCK)
                    own[pl.ds(to, OUT_BLOCK), :] = block[:, j * LANES : (j + 1) * LANES]

            put(dot_rows(mid[:, at], ggu[c]), 0)
            put(dot_rows(cot[:, at], act[:, part_cols(c)]), wide // LANES)

            @pl.when(c > 0)
            def _():
                summer.tick((c - 1) * part_ticks + rows // ROW_BLOCK // ROW_TICK + m, count)

    early = (parts - 1) * part_ticks
    blocks = rows // 2 // OUT_BLOCK
    def row_block(half, k):
        return pl.ds(pl.multiple_of((half * blocks + k) * OUT_BLOCK, OUT_BLOCK), OUT_BLOCK)

    def mid_part(at):
        return sum(dot_cols(ggu[c, at, :], w_gu[c]) for c in range(parts))

    def ffn_part(at):
        return sum(
            jnp.dot(
                act[at, c * hidden : (c + 1) * hidden],
                w_d[c * hidden : (c + 1) * hidden, :],
                preferred_element_type=jnp.float32,
            )
            for c in range(parts)
        )

    def near(which, land, k):
        return pltpu.make_async_remote_copy(
            src_ref=staged.at[lax.rem(k, 2)],
            dst_ref=land.at[row_block(0, k)],
            send_sem=near_sems.at[which, 0, k],
            recv_sem=near_sems.at[which, 1, k],
            device_id={"tp": sibling},
            device_id_type=pl.DeviceIdType.MESH,
        )

    def far(which, chip, there, k):
        return pltpu.make_async_remote_copy(
            src_ref=chip.at[row_block(0, k)],
            dst_ref=there.at[row_block(0, k)],
            send_sem=far_sems.at[which, 0, k],
            recv_sem=far_sems.at[which, 1, k],
            device_id={"tp": across},
            device_id_type=pl.DeviceIdType.MESH,
        )

    def ffn_across(k):
        return far(1, ffn_chip, ffn_far, k)

    def tp_sum(which, part, land, chip, first_tick):
        @pl.loop(0, blocks)
        def _(k):
            @pl.when(k >= 2)
            def _():
                near(which, land, k - 2).wait_send()

            staged[lax.rem(k, 2)] = part(row_block(1 - core, k))
            near(which, land, k).start()

        for k in range(max(blocks - 2, 0), blocks):
            near(which, land, k).wait_send()

        @pl.loop(0, blocks)
        def _(k):
            near(which, land, k).wait_recv()
            fetch = pltpu.make_async_copy(land.at[row_block(0, k)], fetched, fetch_sem)
            fetch.start()
            staged[0] = part(row_block(core, k))
            fetch.wait()
            staged[0] += fetched[...]
            keep = pltpu.make_async_copy(staged.at[0], chip.at[row_block(0, k)], keep_sem)
            keep.start()
            summer.tick(first_tick + k, count)
            keep.wait()
            if which == 0:
                far(0, mid_chip, mid_far, k).start()

    tp_sum(0, mid_part, mid_land, mid_chip, early)
    tp_sum(1, ffn_part, ffn_land, ffn_chip, early + blocks)

    own_half = pl.ds(pl.multiple_of(core * half_rows, half_rows), half_rows)
    low_half, high_half = pl.ds(0, half_rows), pl.ds(half_rows, half_rows)
    w_out, grad_mixer = mid.at[low_half], mid.at[high_half]
    normed, mixed = act.at[low_half, pl.ds(0, width)], act.at[high_half, pl.ds(0, width)]
    tokens = w_d.at[low_half]
    w_in = (ggu.at[2, low_half], ggu.at[2, high_half], w_gu.at[0], w_gu.at[1])
    moves = [
        (w_out_hbm, w_out),
        (tokens_hbm.at[own_half], tokens),
        (normed_hbm, normed),
        (mixed_hbm, mixed),
    ]
    for j in range(4):
        for g in range(3):
            first = g * width + j * chans
            moves.append(
                (w_in_hbm.at[:, first : first + chans], w_in[j].at[:, g * chans : (g + 1) * chans])
            )
    loads = [
        pltpu.make_async_copy(src, dst, later_sems.at[i]) for i, (src, dst) in enumerate(moves)
    ]
    for load in loads:
        load.start()
    chip, far_rows, hidden_rows = staged.at[0], staged.at[1], fetched
    per_slot = slot_len // OUT_BLOCK
    small[...] = jnp.zeros_like(small)
    ticked = early + 2 * blocks

    @pl.loop(ticked, FIRST_MIXER_TICK)
    def _(t):
        summer.tick(t, count)

    @pl.loop(0, blocks)
    def _(k):
        far(0, mid_chip, mid_far, k).wait()
        ffn_across(k).start()

    for load in loads:
        load.wait()

    def shard_rows(shard, first, size):
        at = lax.rem(shard, 2) * half_rows + first
        return shard // 2, pl.ds(pl.multiple_of(at, size), size)

    def place_of(n):
        slot = n // per_slot
        block = per_slot - 1 - lax.rem(n, per_slot)
        return slot, block, pl.multiple_of(slot * slot_len + block * OUT_BLOCK, OUT_BLOCK)

    def mid_loads(first):
        at = pl.ds(first, OUT_BLOCK)
        return [
            pltpu.make_async_copy(src.at[at], dst, row_sems.at[i])
            for i, (src, dst) in enumerate(((mid_chip, chip), (mid_far, far_rows), (hidden_hbm, hidden_rows)))
        ]

    def proj_loads(slot, block, first):
        return [
            pltpu.make_async_copy(proj_hbm.at[pl.ds(first, OUT_BLOCK)], proj, row_sems.at[3]),
            pltpu.make_async_copy(
                gated_hbm.at[slot, pl.ds(pl.multiple_of(block * OUT_BLOCK, 8), OUT_BLOCK + 8)],
                gated,
                row_sems.at[4],
            ),
        ]

    def start(copies):
        for copy in copies:
            copy.start()

    def wait(copies):
        for copy in copies:
            copy.wait()

    def remote(src, dst, sems, i, device):
        return pltpu.make_async_remote_copy(
            src_ref=src,
            dst_ref=dst,
            send_sem=sems.at[0, i],
            recv_sem=sems.at[1, i],
            device_id=device,
            device_id_type=pl.DeviceIdType.MESH,
        )

    def block_at(k):
        return pl.ds(pl.multiple_of(k * OUT_BLOCK, OUT_BLOCK), OUT_BLOCK)

    def own_rows(first, size):
        return pl.ds(pl.multiple_of(core * half_rows + first, size), size)

    def hidden_grad(chip_part, far_part, hidden_part, cot_part):
        grad_mid = chip_part + far_part
        scale = rms_scale(hidden_part)
        unit = hidden_part * scale
        grad = cot_part.astype(jnp.float32) + norm_back(grad_mid, gain_ffn[...], unit, scale)
        return grad, grad_mid * unit

    def halo_copy(slot, device):
        return remote(halo_out.at[slot], halo_in.at[slot], halo_sems, slot, {"seq": device})

    head = 16
    for slot in range(slots):
        at = pl.ds(slot * slot_len, head)
        top = pl.ds(0, head)
        copies = [
            pltpu.make_async_copy(src.at[at], dst, row_sems.at[i])
            for i, (src, dst) in enumerate(
                (
                    (mid_chip, chip.at[top]),
                    (mid_far, far_rows.at[top]),
                    (hidden_hbm, hidden_rows.at[top]),
                    (proj_hbm, proj.at[top]),
                )
            )
        ]
        start(copies)
        wait(copies)
        grad, _ = hidden_grad(
            chip[top, :], far_rows[top, :], hidden_rows[top, :], cot[own_rows(slot * slot_len, head), :]
        )
        grad_mixed = dot_cols(grad.astype(jnp.bfloat16), w_out[...])
        halo_out[slot] = (grad_mixed * proj[top, width : 2 * width])[:8]
        pl.when(here > 0)(lambda slot=slot: halo_copy(slot, here - 1).start())

    slot, block, first = place_of(0)
    start(mid_loads(first))
    start(proj_loads(slot, block, first))

    @pl.when(here == last)
    def _():
        halo_in[...] = jnp.zeros_like(halo_in)

    @pl.when(here < last)
    def _():
        for slot in range(slots):
            halo_copy(slot, here + 1).wait_recv()

    def out_rows(first):
        return own_rows(first, OUT_BLOCK)

    def hand_out(target, first, i):
        at = out_rows(first)
        return (
            pltpu.make_async_copy(grad_tok, target.at[at], out_sems.at[0, 2 * blocks]),
            remote(grad_tok, target.at[at], out_sems, i, {"tp": sibling}),
        )

    @pl.loop(0, blocks)
    def _(n):
        slot, block, first = place_of(n)
        at = pl.ds(first, OUT_BLOCK)
        wait(mid_loads(first))

        @pl.loop(0, OUT_BLOCK // SUB_ROWS)
        def _(r):
            sub = pl.ds(pl.multiple_of(r * SUB_ROWS, SUB_ROWS), SUB_ROWS)
            whole = pl.ds(pl.multiple_of(first + r * SUB_ROWS, SUB_ROWS), SUB_ROWS)
            grad, for_gain = hidden_grad(
                chip[sub, :],
                far_rows[sub, :],
                hidden_rows[sub, :],
                cot[own_rows(first + r * SUB_ROWS, SUB_ROWS), :],
            )
            grad_hid[sub, :] = grad
            grad_mixer[whole, :] = grad.astype(jnp.bfloat16)
            small[1:2, :] += jnp.sum(for_gain, axis=0, keepdims=True)

        @pl.when(n < blocks - 1)
        def _():
            start(mid_loads(place_of(n + 1)[2]))

        mixed_buf[...] = dot_cols(grad_mixer[at, :], w_out[...])
        wait(proj_loads(slot, block, first))

        @pl.when(block == per_slot - 1)
        def _():
            conv_in[pl.ds(OUT_BLOCK, 8), :] = halo_in[slot]

        @pl.when(block < per_slot - 1)
        def _():
            conv_in[pl.ds(OUT_BLOCK, 8), :] = halo_keep[...]

        summer.tick(FIRST_MIXER_TICK + 2 * n, count)
        mask = valid_rows(core * slots + slot, block * OUT_BLOCK, OUT_BLOCK)

        @pl.loop(0, width // chans)
        def _(c):
            def cols(gate):
                return pl.ds(pl.multiple_of(gate * width + c * chans, chans), chans)

            here_cols = cols(0)
            pair, shard_at = shard_rows(c, first, OUT_BLOCK)
            in_gate, out_gate, conv_value = (proj[:, cols(g)] for g in range(3))
            grad_mixed = mixed_buf[:, here_cols]
            now = grad_mixed * out_gate
            conv_in[pl.ds(0, OUT_BLOCK), here_cols] = now
            seen = [gated[pl.ds(6 + j, OUT_BLOCK), here_cols] for j in range(3)]
            tap = [taps[j : j + 1, here_cols] for j in range(3)]
            conv_sum = tap[0] * seen[0] + tap[1] * seen[1] + tap[2] * seen[2]
            for j in range(3):
                small[2 + j : 3 + j, here_cols] += jnp.sum(now * seen[j], axis=0, keepdims=True)
            ggu[pair, shard_at, chans : 2 * chans] = (grad_mixed * conv_sum).astype(jnp.bfloat16)
            grad_gated = mask * (
                tap[2] * now
                + tap[1] * conv_in[pl.ds(1, OUT_BLOCK), here_cols]
                + tap[0] * conv_in[pl.ds(2, OUT_BLOCK), here_cols]
            )
            ggu[pair, shard_at, :chans] = (grad_gated * conv_value).astype(jnp.bfloat16)
            ggu[pair, shard_at, 2 * chans : 3 * chans] = (grad_gated * in_gate).astype(jnp.bfloat16)

        halo_keep[...] = conv_in[pl.ds(0, 8), :]

        @pl.when(n < blocks - 1)
        def _():
            start(proj_loads(*place_of(n + 1)))

        def shard_grad(j):
            pair, shard_at = shard_rows(j, first, OUT_BLOCK)
            return dot_cols(ggu[pair, shard_at, :], w_in[j][...])

        mixed_buf[...] = sum(shard_grad(j) for j in range(4))

        @pl.when(n > 0)
        def _():
            local, there = hand_out(tokens_out, place_of(n - 1)[2], n - 1)
            local.wait()
            there.wait_send()

        @pl.loop(0, OUT_BLOCK // SUB_ROWS)
        def _(r):
            sub = pl.ds(pl.multiple_of(r * SUB_ROWS, SUB_ROWS), SUB_ROWS)
            whole = pl.ds(pl.multiple_of(first + r * SUB_ROWS, SUB_ROWS), SUB_ROWS)
            inputs = tokens[whole, :].astype(jnp.float32)
            scale = rms_scale(inputs)
            unit = inputs * scale
            grad_in = mixed_buf[sub, :]
            grad_tok[sub, :] = grad_hid[sub, :] + norm_back(grad_in, gain_mix[...], unit, scale)
            small[0:1, :] += jnp.sum(grad_in * unit, axis=0, keepdims=True)

        start(hand_out(tokens_out, first, n))
        summer.tick(FIRST_MIXER_TICK + 2 * n + 1, count)

    in_blocks = width // OUT_BLOCK
    stages = [proj.at[:, i * wide : (i + 1) * wide] for i in range(3)]

    def to_near(src, dst, i):
        return remote(src, dst, weight_sems, i, {"tp": sibling})

    def near_in(m):
        cols = pl.ds(pl.multiple_of(lax.rem(m, 2) * wide, LANES), wide)
        return to_near(proj.at[:, cols], land_in.at[m], m)

    near_out = to_near(grad_hid, land_out, in_blocks)
    near_small = to_near(small, land_small, in_blocks + 1)

    def in_part(m, shard):
        pair, shard_at = shard_rows(shard, 0, half_rows)
        return dot_rows(normed[:, block_at(m)], ggu[pair, shard_at, :])

    def out_part(shard):
        at = pl.ds(pl.multiple_of(shard * chans, LANES), chans)
        return dot_rows(mixed[:, at], grad_mixer[...])

    near_small.start()
    first_tick = FIRST_MIXER_TICK + 2 * blocks

    @pl.loop(0, in_blocks)
    def _(m):
        @pl.when(m >= 2)
        def _():
            near_in(m - 2).wait_send()

        cols = pl.ds(pl.multiple_of(lax.rem(m, 2) * wide, LANES), wide)
        proj[:, cols] = in_part(m, sibling)
        near_in(m).start()
        summer.tick(first_tick + m, count)

    grad_hid[...] = out_part(sibling)
    near_out.start()

    @pl.loop(0, in_blocks)
    def _(m):
        near_in(m).wait_recv()
        fetch = pltpu.make_async_copy(land_in.at[m], stages[2], row_sems.at[0])
        fetch.start()
        part = in_part(m, tp_at)
        fetch.wait()
        for i in range(wide // LANES):
            to = pl.multiple_of(i * width + m * OUT_BLOCK, OUT_BLOCK)
            own[pl.ds(to, OUT_BLOCK), :] = (
                part[:, i * LANES : (i + 1) * LANES]
                + proj[:, 2 * wide + i * LANES : 2 * wide + (i + 1) * LANES]
            )

        summer.tick(first_tick + in_blocks + m, count)

    near_out.wait_recv()
    near_small.wait_recv()
    fetches = [
        pltpu.make_async_copy(land_out, mixed_buf, row_sems.at[0]),
        pltpu.make_async_copy(land_small, small_in, row_sems.at[1]),
    ]
    start(fetches)
    part = out_part(tp_at)
    wait(fetches)
    out_first = wide // LANES * width
    small_first = out_first + width // LANES * chans
    for p in range(width // LANES):
        cols = slice(p * LANES, (p + 1) * LANES)
        own[pl.ds(out_first + p * chans, chans), :] = part[:, cols] + mixed_buf[:, cols]
        own[pl.ds(small_first + 8 * p, 8), :] = small[:, cols] + small_in[:, cols]
    unused = 4 * HALF - 8 * (width // LANES)
    own[pl.ds(small_first + 4 * HALF - unused, unused), :] = jnp.zeros((unused, LANES), jnp.float32)

    local, there = hand_out(tokens_out, place_of(blocks - 1)[2], blocks - 1)
    local.wait()
    there.wait_send()
    done = first_tick + 2 * in_blocks
    pause = BLOCK_TICK

    @pl.loop(done, pause)
    def _(t):
        summer.tick(t, count)

    @pl.loop(0, blocks)
    def _(k):
        ffn_across(k).wait_recv()
        at = block_at(k)
        copies = [
            pltpu.make_async_copy(src.at[at], dst, row_sems.at[i])
            for i, (src, dst) in enumerate(((ffn_chip, chip), (ffn_far, far_rows), (hidden_hbm, hidden_rows)))
        ]
        start(copies)

        @pl.when(k > 0)
        def _():
            local, there = hand_out(block_out, (k - 1) * OUT_BLOCK, blocks + k - 1)
            local.wait()
            there.wait_send()

        wait(copies)
        grad_tok[...] = hidden_rows[...] + (chip[...] + far_rows[...])
        start(hand_out(block_out, k * OUT_BLOCK, blocks + k))
        summer.tick(pause + k, count)

    @pl.loop(pause + blocks, count + summer.P_LAGS[-1][1])
    def _(t):
        summer.tick(t, count)

    local, there = hand_out(block_out, (blocks - 1) * OUT_BLOCK, 2 * blocks - 1)
    local.wait()
    there.wait_send()

    @pl.loop(0, blocks)
    def _(k):
        ffn_across(k).wait_send()
        hand_out(tokens_out, place_of(k)[2], k)[1].wait_recv()
        hand_out(block_out, k * OUT_BLOCK, blocks + k)[1].wait_recv()

    for m in range(max(in_blocks - 2, 0), in_blocks):
        near_in(m).wait_send()
    near_out.wait_send()
    near_small.wait_send()

    @pl.when(here > 0)
    def _():
        for slot in range(slots):
            halo_copy(slot, here - 1).wait_send()


def back_both(hbm, vmem, slots, sum_cols, collective_id):
    normed_mid, _, w_gate, _, w_d, _, _, gated, _, _, _, _, _ = hbm
    rows, width = normed_mid.shape
    half_rows = rows // 2
    local = w_gate.shape[1]
    hidden = local // FFN_PARTS
    chans = 2 * hidden // 3
    blocks = half_rows // OUT_BLOCK
    in_blocks = width // OUT_BLOCK
    f32, low = jnp.float32, jnp.bfloat16
    half = jax.ShapeDtypeStruct((half_rows, width), f32)
    full = jax.ShapeDtypeStruct((rows, width), f32)
    block = pltpu.VMEM((OUT_BLOCK, width), f32)
    row8 = pltpu.VMEM((8, width), f32)
    anywhere = pl.BlockSpec(memory_space=pl.ANY)
    return pl.pallas_call(
        functools.partial(back_kernel, lax.axis_size("seq") // 2, slots),
        out_shape=[jax.ShapeDtypeStruct((width, sum_cols), f32)]
        + [full] * 2
        + [half] * 6
        + [
            jax.ShapeDtypeStruct((in_blocks, OUT_BLOCK, 2 * hidden), f32),
            jax.ShapeDtypeStruct((chans, width), f32),
            jax.ShapeDtypeStruct((8, width), f32),
        ],
        in_specs=[anywhere] * len(hbm)
        + [pl.BlockSpec(memory_space=pltpu.SMEM)]
        + [pl.BlockSpec(memory_space=pltpu.VMEM)] * (len(vmem) - 1),
        out_specs=[anywhere] * 12,
        scratch_shapes=[
            pltpu.VMEM((rows, width), low),
            pltpu.VMEM((rows, width), low),
            pltpu.VMEM((FFN_PARTS, width, 2 * hidden), low),
            pltpu.VMEM(w_d.shape, low),
            pltpu.VMEM((rows, local), low),
            pltpu.VMEM((FFN_PARTS, rows, 2 * hidden), low),
            pltpu.VMEM((3 * local * width // LANES, LANES), f32),
            pltpu.VMEM((2, OUT_BLOCK, width), f32),
            block,
            pltpu.VMEM((OUT_BLOCK, 3 * width), f32),
            pltpu.VMEM((OUT_BLOCK + 8, width), f32),
            block,
            pltpu.VMEM((OUT_BLOCK + 8, width), f32),
            block,
            block,
            pltpu.VMEM((slots, 8, width), f32),
            pltpu.VMEM((slots, 8, width), f32),
            row8,
            row8,
            row8,
            pltpu.SemaphoreType.DMA((3 + 2 * FFN_PARTS,)),
            pltpu.SemaphoreType.DMA((2, 2, blocks)),
            pltpu.SemaphoreType.DMA((2, 2, blocks)),
            pltpu.SemaphoreType.DMA,
            pltpu.SemaphoreType.DMA,
            pltpu.SemaphoreType.DMA((16,)),
            pltpu.SemaphoreType.DMA((5,)),
            pltpu.SemaphoreType.DMA((2, slots)),
            pltpu.SemaphoreType.DMA((2, in_blocks + 2)),
            pltpu.SemaphoreType.DMA((2, 2 * blocks + 1)),
        ]
        + seq_sum_scratch(),
        compiler_params=pltpu.CompilerParams(
            collective_id=collective_id, has_side_effects=True, vmem_limit_bytes=VMEM_LIMIT
        ),
        cost_estimate=pl.CostEstimate(
            flops=18 * rows * width * local, bytes_accessed=800 << 20, transcendentals=0
        ),
        name="back_both",
    )(*hbm, *vmem)


def front_kernel(places, slots, *refs):
    (w_in, w_out, taps, gain_mix, gain_ffn, lengths, tokens_hbm) = refs[0:7]
    (in_hbm, out_hbm, full_taps, mid_hbm, hidden_hbm, proj_hbm, gated_hbm) = refs[7:14]
    (normed_hbm, mixed_hbm) = refs[14:16]
    own_in, own_out, far_in, far_out, sib_in, sib_out, sibfar_in, sibfar_out = refs[16:24]
    own_taps, far_taps, sib_taps, sibfar_taps, share_in, share_out = refs[24:30]
    (full_in, full_out, tokens, normed, mixed, out_gate, gates, gated) = refs[30:38]
    (unit_out, unit_in, hidden) = refs[38:41]
    sends, recvs, once, halo_sems, gate_sems, unit_sems, keep_sems, mid_sems = refs[41:49]
    here = lax.axis_index("seq")
    place, side = here // 2, lax.rem(here, 2)
    last = places - 1
    end = 2 * places - 1
    tp_at = lax.axis_index("tp")
    core = lax.rem(tp_at, 2)
    sibling = tp_at + 1 - 2 * core
    across = lax.rem(tp_at + 2, 4)
    far_sibling = sibling + across - tp_at
    in_rows = w_in.shape[1] // (2 * places)
    out_rows = w_out.shape[0] // (2 * places)
    chans = w_in.shape[2]
    rows, width = tokens.shape
    slot_len = rows // slots
    low = jnp.bfloat16

    load_tokens = pltpu.make_async_copy(
        tokens_hbm.at[pl.ds(pl.multiple_of(core * rows, rows), rows)], tokens, keep_sems.at[0]
    )
    load_tokens.start()
    barrier = pltpu.get_barrier_semaphore()

    def signal(device):
        pl.semaphore_signal(barrier, inc=1, device_id=device, device_id_type=pl.DeviceIdType.MESH)

    pl.when(here > 0)(lambda: signal({"seq": here - 1}))
    pl.when(here < end)(lambda: signal({"seq": here + 1}))
    ends = jnp.where(here > 0, 1, 0) + jnp.where(here < end, 1, 0)
    greet_seq(places, ({"tp": sibling}, {"tp": across}), ends)

    def shares(j):
        return (
            pl.ds(pl.multiple_of(j * in_rows, in_rows), in_rows),
            pl.ds(pl.multiple_of(j * out_rows, out_rows), out_rows),
        )

    def remote(src, dst, send, recv, device):
        return pltpu.make_async_remote_copy(
            src_ref=src,
            dst_ref=dst,
            send_sem=send,
            recv_sem=recv,
            device_id=device,
            device_id_type=pl.DeviceIdType.MESH,
        )

    def copies(source, target, j, kind, device):
        for i, at in enumerate(shares(j)):
            yield remote(
                source[i] if kind == 0 else source[i].at[at],
                target[i].at[at],
                sends.at[kind, i, j],
                recvs.at[0 if kind < 4 else 1, i, j],
                device,
            )

    share, far, sibfar = (share_in, share_out), (far_in, far_out), (sibfar_in, sibfar_out)

    def across_share():
        return copies(share, far, here, 0, {"tp": across})

    def to_right(j):
        return copies(far, far, j, 1, {"seq": here + 2})

    def to_left(j):
        return copies(far, far, j, 2, {"seq": here - 2})

    def to_side(j):
        return copies(far, far, j, 3, {"seq": here + 1 - 2 * side})

    def to_sibling(j):
        return copies(far, sibfar, j, 4, {"tp": sibling})

    def start(group):
        for copy in group:
            copy.start()

    def arrived(group):
        for copy in group:
            copy.wait_recv()

    def left_source(group):
        for copy in group:
            copy.wait_send()

    def single(i, src, dst, device):
        return remote(src, dst, once.at[0, i], once.at[1, i], device)

    in_at, out_at = shares(here)
    for g in range(3):
        share_in[:, g * chans : (g + 1) * chans] = w_in[g, in_at, :].astype(jnp.float32)
    share_out[...] = w_out[out_at, :].astype(jnp.float32)
    start(across_share())
    own_taps[...] = taps[...]
    taps_far = single(0, own_taps, far_taps, {"tp": across})
    taps_sib = single(1, own_taps, sib_taps, {"tp": sibling})
    taps_sibfar = single(2, far_taps, sibfar_taps, {"tp": sibling})
    for g in range(3):
        own_in[:, g * chans : (g + 1) * chans] = w_in[g].astype(jnp.float32)
    own_out[...] = w_out[...].astype(jnp.float32)
    in_sib = single(3, own_in, sib_in, {"tp": sibling})
    out_sib = single(4, own_out, sib_out, {"tp": sibling})
    for copy in (taps_far, taps_sib, in_sib, out_sib):
        copy.start()

    def gate_cols(g, index):
        return pl.ds(pl.multiple_of(g * width + index * chans, LANES), chans)

    def place_shard(shard_in, shard_out, shard_taps, index):
        for g in range(3):
            full_in[:, gate_cols(g, index)] = shard_in[:, g * chans : (g + 1) * chans].astype(low)
        at = pl.ds(pl.multiple_of(index * chans, chans), chans)
        full_out[at, :] = shard_out[...].astype(low)
        full_taps[:, gate_cols(0, index)] = shard_taps[...]

    def gate_out(turn, index, g):
        if g == 1:
            return pltpu.make_async_copy(
                out_gate.at[:, gate_cols(0, index)],
                proj_hbm.at[:, gate_cols(1, index)],
                gate_sems.at[turn, 1],
            )
        return pltpu.make_async_copy(
            gates.at[turn % 2, g // 2], proj_hbm.at[:, gate_cols(g, index)], gate_sems.at[turn, g]
        )

    def halo(turn, index, slot):
        return remote(
            gated.at[slot, pl.ds(slot_len, 8), gate_cols(0, index)],
            gated.at[slot, pl.ds(0, 8), gate_cols(0, index)],
            halo_sems.at[0, turn, slot],
            halo_sems.at[1, turn, slot],
            {"seq": here + 1},
        )

    order = (tp_at, sibling, across, far_sibling)

    def project(turn):
        index = order[turn]
        cols = gate_cols(0, index)
        if turn >= 2:
            gate_out(turn - 2, order[turn - 2], 0).wait()
            gate_out(turn - 2, order[turn - 2], 2).wait()

        @pl.loop(0, slots)
        def _(s):
            at = pl.ds(pl.multiple_of(s * slot_len, slot_len), slot_len)

            def gate(g):
                return jnp.dot(
                    normed[at, :], full_in[:, gate_cols(g, index)],
                    preferred_element_type=jnp.float32,
                )

            at_pos = lax.broadcasted_iota(jnp.int32, (slot_len, 1), 0) + here * slot_len
            mask = (at_pos < lengths[core * slots + s]).astype(jnp.float32)
            in_gate, value = gate(0), gate(2)
            gates[turn % 2, 0, at, :] = in_gate
            gates[turn % 2, 1, at, :] = value
            gated[s, pl.ds(8, slot_len), cols] = mask * in_gate * value
            out_gate[at, cols] = gate(1)

        for g in range(3):
            gate_out(turn, index, g).start()

        @pl.when(here < end)
        def _():
            for slot in range(slots):
                halo(turn, index, slot).start()

    def convolve(turn):
        index = order[turn]
        cols = gate_cols(0, index)

        @pl.when(here > 0)
        def _():
            for slot in range(slots):
                halo(turn, index, slot).wait_recv()

        @pl.loop(0, slots)
        def _(s):
            at = pl.ds(pl.multiple_of(s * slot_len, slot_len), slot_len)
            seen = [gated[s, pl.ds(6 + j, slot_len), cols] for j in range(3)]
            tap = [full_taps[j : j + 1, cols] for j in range(3)]
            conv_sum = tap[0] * seen[0] + tap[1] * seen[1] + tap[2] * seen[2]
            mixed[at, cols] = (out_gate[at, cols] * conv_sum).astype(low)

    @pl.when(here == 0)
    def _():
        for slot in range(slots):
            gated[slot, pl.ds(0, 8), :] = jnp.zeros((8, width), jnp.float32)

    load_tokens.wait()

    @pl.loop(0, rows // SUB_ROWS)
    def _(r):
        at = pl.ds(pl.multiple_of(r * SUB_ROWS, SUB_ROWS), SUB_ROWS)
        inputs = tokens[at, :].astype(jnp.float32)
        normed[at, :] = (gain_mix[...] * (inputs * rms_scale(inputs))).astype(low)

    keep_normed = pltpu.make_async_copy(normed, normed_hbm, keep_sems.at[0])
    keep_normed.start()
    place_shard(own_in, own_out, own_taps, tp_at)
    project(0)

    arrived(across_share())
    pl.when(place < last)(lambda: start(to_right(here)))
    pl.when(place > 0)(lambda: start(to_left(here)))
    start(to_side(here))
    start(to_sibling(here))
    taps_far.wait_recv()
    taps_sibfar.start()
    in_sib.wait_recv()
    out_sib.wait_recv()
    taps_sib.wait_recv()
    place_shard(sib_in, sib_out, sib_taps, sibling)
    project(1)

    def from_side(q):
        j = 2 * q + 1 - side
        arrived(to_side(j))
        start(to_sibling(j))

    @pl.loop(1, places)
    def _(d):
        @pl.when(place - d >= 0)
        def _():
            j = here - 2 * d
            arrived(to_right(j))
            pl.when(place < last)(lambda: start(to_right(j)))
            start(to_side(j))
            start(to_sibling(j))

        @pl.when(place + d <= last)
        def _():
            j = here + 2 * d
            arrived(to_left(j))
            pl.when(place > 0)(lambda: start(to_left(j)))
            start(to_side(j))
            start(to_sibling(j))

        @pl.when(d == 1)
        def _():
            from_side(place)
            convolve(0)
            convolve(1)

        pl.when(place - d >= 0)(lambda: from_side(place - d))
        pl.when(place + d <= last)(lambda: from_side(place + d))

    place_shard(far_in, far_out, far_taps, across)
    project(2)
    taps_sibfar.wait_recv()

    @pl.loop(0, 2 * places)
    def _(j):
        arrived(to_sibling(j))

    place_shard(sibfar_in, sibfar_out, sibfar_taps, far_sibling)
    project(3)
    keep_in = pltpu.make_async_copy(full_in, in_hbm, keep_sems.at[1])
    keep_out = pltpu.make_async_copy(full_out, out_hbm, keep_sems.at[2])
    keep_in.start()
    keep_out.start()
    convolve(2)
    convolve(3)
    keep_gated = pltpu.make_async_copy(gated, gated_hbm, keep_sems.at[3])
    keep_mixed = pltpu.make_async_copy(mixed, mixed_hbm, keep_sems.at[4])
    keep_gated.start()
    keep_mixed.start()
    keep_normed.wait()

    blocks = rows // OUT_BLOCK

    def block_at(k, first=0):
        return pl.ds(pl.multiple_of(first + k * OUT_BLOCK, OUT_BLOCK), OUT_BLOCK)

    def unit_copy(k):
        return remote(
            unit_out.at[block_at(k)], unit_in.at[block_at(k)],
            unit_sems.at[0, k], unit_sems.at[1, k], {"tp": sibling},
        )

    def hidden_copy(k):
        return pltpu.make_async_copy(
            hidden.at[lax.rem(k, 2)], hidden_hbm.at[block_at(k)], mid_sems.at[0, lax.rem(k, 2)]
        )

    def mid_copy(half, held, whose, k):
        return pltpu.make_async_copy(
            held.at[block_at(k)], mid_hbm.at[block_at(k, whose * rows)], mid_sems.at[half, k]
        )

    @pl.loop(0, blocks)
    def _(k):
        slot = lax.rem(k, 2)
        at = block_at(k)
        pl.when(k >= 2)(lambda: hidden_copy(k - 2).wait())
        hidden[slot] = jnp.dot(mixed[at, :], full_out[...], preferred_element_type=jnp.float32)

        @pl.loop(0, OUT_BLOCK // SUB_ROWS)
        def _(r):
            sub = pl.ds(pl.multiple_of(r * SUB_ROWS, SUB_ROWS), SUB_ROWS)
            whole = pl.ds(pl.multiple_of(k * OUT_BLOCK + r * SUB_ROWS, SUB_ROWS), SUB_ROWS)
            hidden_rows = tokens[whole, :].astype(jnp.float32) + hidden[slot, sub, :]
            hidden[slot, sub, :] = hidden_rows
            unit = hidden_rows * rms_scale(hidden_rows)
            unit_out[whole, :] = unit
            normed[whole, :] = (gain_ffn[...] * unit).astype(low)

        unit_copy(k).start()
        hidden_copy(k).start()
        mid_copy(1, normed, core, k).start()

    keep_mixed.wait()

    @pl.loop(0, blocks)
    def _(k):
        unit_copy(k).wait_recv()

        @pl.loop(0, OUT_BLOCK // SUB_ROWS)
        def _(r):
            whole = pl.ds(pl.multiple_of(k * OUT_BLOCK + r * SUB_ROWS, SUB_ROWS), SUB_ROWS)
            mixed[whole, :] = (gain_ffn[...] * unit_in[whole, :]).astype(low)

        mid_copy(2, mixed, 1 - core, k).start()

    @pl.loop(0, blocks)
    def _(k):
        unit_copy(k).wait_send()
        mid_copy(1, normed, core, k).wait()
        mid_copy(2, mixed, 1 - core, k).wait()

    for k in range(max(blocks - 2, 0), blocks):
        hidden_copy(k).wait()
    keep_in.wait()
    keep_out.wait()
    keep_gated.wait()
    for turn in range(4):
        for g in range(3):
            if turn >= 2 or g == 1:
                gate_out(turn, order[turn], g).wait()

    @pl.when(here < end)
    def _():
        for turn in range(4):
            for slot in range(slots):
                halo(turn, order[turn], slot).wait_send()

    left_source(across_share())
    for copy in (taps_far, taps_sib, taps_sibfar, in_sib, out_sib):
        copy.wait_send()

    @pl.loop(0, places)
    def _(q):
        j = 2 * q + side
        left_source(to_side(j))
        pl.when((q <= place) & (place < last))(lambda: left_source(to_right(j)))
        pl.when((q >= place) & (place > 0))(lambda: left_source(to_left(j)))
        left_source(to_sibling(j))
        left_source(to_sibling(2 * q + 1 - side))


def mixer_front(w_in, w_out, taps, gain_mix, gain_ffn, lengths, tokens, slots, collective_id):
    width, _, chans = w_in.shape
    rows = tokens.shape[0] // 2
    count = lax.axis_size("seq")
    group = lax.axis_size("tp")
    f32, low = jnp.float32, jnp.bfloat16
    blocks = rows // OUT_BLOCK
    pair = [pltpu.VMEM((width, 3 * chans), f32), pltpu.VMEM((chans, width), f32)]
    whole = pl.BlockSpec(memory_space=pltpu.VMEM)
    anywhere = pl.BlockSpec(memory_space=pl.ANY)
    padded = (slots, rows // slots + 8, width)
    return pl.pallas_call(
        functools.partial(front_kernel, count // 2, slots),
        out_shape=[
            jax.ShapeDtypeStruct((width, 3 * chans * group), low),
            jax.ShapeDtypeStruct((chans * group, width), low),
            jax.ShapeDtypeStruct((8, chans * group), f32),
            jax.ShapeDtypeStruct((2 * rows, width), low),
            jax.ShapeDtypeStruct((rows, width), f32),
            jax.ShapeDtypeStruct((rows, 3 * width), f32),
            jax.ShapeDtypeStruct(padded, f32),
            jax.ShapeDtypeStruct((rows, width), low),
            jax.ShapeDtypeStruct((rows, width), low),
        ],
        in_specs=[whole] * 5 + [pl.BlockSpec(memory_space=pltpu.SMEM), anywhere],
        out_specs=[anywhere] * 2 + [whole] + [anywhere] * 6,
        scratch_shapes=pair * 4
        + [pltpu.VMEM((8, chans), f32)] * 4
        + [
            pltpu.VMEM((width // count, 3 * chans), f32),
            pltpu.VMEM((chans // count, width), f32),
            pltpu.VMEM((width, 3 * chans * group), low),
            pltpu.VMEM((chans * group, width), low),
            pltpu.VMEM((rows, width), low),
            pltpu.VMEM((rows, width), low),
            pltpu.VMEM((rows, width), low),
            pltpu.VMEM((rows, width), f32),
            pltpu.VMEM((2, 2, rows, chans), f32),
            pltpu.VMEM(padded, f32),
            pltpu.VMEM((rows, width), f32),
            pltpu.VMEM((rows, width), f32),
            pltpu.VMEM((2, OUT_BLOCK, width), f32),
            pltpu.SemaphoreType.DMA((5, 2, count)),
            pltpu.SemaphoreType.DMA((2, 2, count)),
            pltpu.SemaphoreType.DMA((2, 5)),
            pltpu.SemaphoreType.DMA((2, 4, slots)),
            pltpu.SemaphoreType.DMA((4, 3)),
            pltpu.SemaphoreType.DMA((2, blocks)),
            pltpu.SemaphoreType.DMA((5,)),
            pltpu.SemaphoreType.DMA((3, blocks)),
        ],
        compiler_params=pltpu.CompilerParams(
            collective_id=collective_id, has_side_effects=True, vmem_limit_bytes=VMEM_LIMIT
        ),
        name="mixer_front",
    )(
        w_in.transpose(1, 0, 2),
        w_out,
        jnp.pad(taps, ((0, 5), (0, 0))),
        gain_mix,
        gain_ffn,
        lengths,
        tokens,
    )


def finish_kernel(slots, chans, hidden, *refs):
    (sums, tokens_in, block_in, lengths) = refs[0:4]
    (block_out, tokens_out, gains, g_in, g_conv, g_out, g_gate, g_up, g_down) = refs[4:13]
    (held, tokens, block, rounded, turned, in_sems, block_sems, turn_sems, out_sems) = refs[13:22]
    rows, width = block_in.shape
    slot_len = rows // slots
    here = lax.axis_index("seq")
    tp_at = lax.axis_index("tp")
    first = 3 * hidden
    out_first = first + 3 * chans
    small_first = out_first + chans
    blocks = rows // OUT_BLOCK
    turns = hidden // LANES
    half_rows = rows // 2

    def cols(start, size):
        return (slice(None), slice(start, start + size))

    parts = [cols(i * hidden, hidden) for i in range(3)] + [cols(first, held.shape[1] - first)]
    halves = [slice(0, half_rows), slice(half_rows, rows)]
    part_loads = [
        pltpu.make_async_copy(sums.at[at], held.at[at], in_sems.at[i]) for i, at in enumerate(parts)
    ]
    token_loads = [
        pltpu.make_async_copy(tokens_in.at[at], tokens.at[at], in_sems.at[4 + i])
        for i, at in enumerate(halves)
    ]

    def block_at(k):
        return pl.ds(pl.multiple_of(k * OUT_BLOCK, OUT_BLOCK), OUT_BLOCK)

    def block_load(k):
        return pltpu.make_async_copy(
            block_in.at[block_at(k)], block.at[block_at(k)], block_sems.at[0, k]
        )

    def block_store(k):
        return pltpu.make_async_copy(
            rounded.at[block_at(k)], block_out.at[block_at(k)], block_sems.at[1, k]
        )

    def panel_at(k):
        return pl.ds(pl.multiple_of(k * LANES, LANES), LANES)

    def turn_store(k):
        at = panel_at(k)
        return pltpu.make_async_copy(turned.at[at], g_down.at[at], turn_sems.at[k])

    stores = []

    def store(src, dst):
        copy = pltpu.make_async_copy(src, dst, out_sems.at[len(stores)])
        copy.start()
        stores.append(copy)

    part_loads[2].start()

    @pl.loop(0, blocks)
    def _(k):
        block_load(k).start()

    for load in (*token_loads, part_loads[0], part_loads[1], part_loads[3]):
        load.start()

    part_loads[2].wait()

    @pl.loop(0, turns)
    def _(k):
        from_cols = pl.ds(pl.multiple_of(2 * hidden + k * LANES, LANES), LANES)
        turned[panel_at(k), :] = held[:, from_cols].T
        turn_store(k).start()

    @pl.loop(0, blocks)
    def _(k):
        block_load(k).wait()
        per_slot = slot_len // OUT_BLOCK
        at = lax.broadcasted_iota(jnp.int32, (OUT_BLOCK, 1), 0)
        at = at + (here * slot_len + lax.rem(k, per_slot) * OUT_BLOCK)
        mask = (at < lengths[k // per_slot]).astype(jnp.float32)
        rounded[block_at(k), :] = (mask * block[block_at(k), :]).astype(jnp.bfloat16)
        block_store(k).start()

    for load, at in zip(token_loads, halves):
        load.wait()
        store(tokens.at[at], tokens_out.at[at])
    for i, target in ((0, g_gate), (1, g_up)):
        part_loads[i].wait()
        store(held.at[parts[i]], target)
    part_loads[3].wait()
    for g in range(3):
        store(held.at[cols(first + g * chans, chans)], g_in.at[g])
    per_col = width // chans
    for p in range(width // LANES):
        q, r = p // per_col, p % per_col
        at = (slice(r * chans, (r + 1) * chans), slice(out_first + q * LANES, out_first + (q + 1) * LANES))
        store(held.at[at], g_out.at[cols(p * LANES, LANES)])
        gains[cols(p * LANES, LANES)] = held[8 * p : 8 * p + 8, small_first:]
    own = pl.ds(pl.multiple_of(tp_at * chans, LANES), chans)
    g_conv[...] = gains[2:5, own]
    for copy in stores:
        copy.wait()

    @pl.loop(0, turns)
    def _(k):
        turn_store(k).wait()

    @pl.loop(0, blocks)
    def _(k):
        block_store(k).wait()


def finish(sums, tokens_grad, block_sum, lengths, chans, hidden):
    rows, width = block_sum.shape
    f32 = jnp.float32
    anywhere = pl.BlockSpec(memory_space=pl.ANY)
    whole = pl.BlockSpec(memory_space=pltpu.VMEM)
    blocks = rows // OUT_BLOCK
    return pl.pallas_call(
        functools.partial(finish_kernel, lengths.shape[0], chans, hidden),
        out_shape=[
            jax.ShapeDtypeStruct((rows, width), jnp.bfloat16),
            jax.ShapeDtypeStruct((rows, width), f32),
            jax.ShapeDtypeStruct((8, width), f32),
            jax.ShapeDtypeStruct((3, width, chans), f32),
            jax.ShapeDtypeStruct((3, chans), f32),
            jax.ShapeDtypeStruct((chans, width), f32),
            jax.ShapeDtypeStruct((width, hidden), f32),
            jax.ShapeDtypeStruct((width, hidden), f32),
            jax.ShapeDtypeStruct((hidden, width), f32),
        ],
        in_specs=[anywhere] * 3 + [pl.BlockSpec(memory_space=pltpu.SMEM)],
        out_specs=[anywhere] * 2 + [whole, anywhere, whole] + [anywhere] * 4,
        scratch_shapes=[
            pltpu.VMEM(sums.shape, f32),
            pltpu.VMEM((rows, width), f32),
            pltpu.VMEM((rows, width), f32),
            pltpu.VMEM((rows, width), jnp.bfloat16),
            pltpu.VMEM((hidden, width), f32),
            pltpu.SemaphoreType.DMA((6,)),
            pltpu.SemaphoreType.DMA((2, blocks)),
            pltpu.SemaphoreType.DMA((hidden // LANES,)),
            pltpu.SemaphoreType.DMA((7 + width // LANES,)),
        ],
        compiler_params=pltpu.CompilerParams(vmem_limit_bytes=VMEM_LIMIT),
        name="finish",
    )(sums, tokens_grad, block_sum, lengths)


def per_device(
    tokens, lengths, gain_mix, w_in, conv_weight, w_out, gain_ffn, w_gate, w_up, w_down, cotangent
):
    slot_count, local_len, width = tokens.shape
    chans = w_in.shape[2]
    half_slots = slot_count // 2
    row_count = slot_count * local_len

    token_rows = tokens.reshape(row_count, width)
    cot_rows = cotangent.reshape(row_count, width)
    gains = gain_mix.reshape(1, width), gain_ffn.reshape(1, width)
    w_in_all, w_out_all, taps, normed_mid, hidden_res, projected, gated_rows, normed_in, mixed = (
        mixer_front(w_in, w_out, conv_weight, *gains, lengths, token_rows, half_slots, 3)
    )
    mixer_cols = 4 * chans
    sum_cols = FFN_PANELS * LANES + mixer_cols + LANES
    sums, grad_tokens, block_sum = back_both(
        (
            normed_mid,
            cot_rows,
            w_gate,
            w_up,
            w_down,
            hidden_res,
            projected,
            gated_rows,
            normed_in,
            mixed,
            w_in_all,
            w_out_all,
            token_rows,
        ),
        (lengths, taps, *gains),
        half_slots,
        sum_cols,
        1,
    )[:3]
    block_out, grad_tokens, small, g_in, g_conv, g_out, g_gate, g_up, g_down = finish(
        sums, grad_tokens, block_sum, lengths, chans, w_gate.shape[1]
    )
    return (
        block_out.reshape(slot_count, local_len, width),
        grad_tokens.reshape(slot_count, local_len, width),
        small[0],
        g_in.transpose(1, 0, 2),
        g_conv,
        g_out,
        small[1],
        g_gate,
        g_up,
        g_down,
    )


def solution(mesh):
    rows, cols = P("tp", None), P(None, "tp")
    tokens, whole, stacked = P(None, "seq", None), P(), P(None, None, "tp")
    return jax.shard_map(
        per_device,
        mesh=mesh,
        in_specs=(
            tokens, whole, whole, stacked, cols, rows, whole, cols, cols, rows, tokens,
        ),
        out_specs=(
            tokens, tokens, whole, stacked, cols, rows, whole, cols, cols, rows,
        ),
        check_vma=False,
    )
```

```python
import functools

import jax
import jax.numpy as jnp
from jax import lax
from jax.experimental import pallas as pl
from jax.experimental.pallas import tpu as pltpu
from jax.sharding import PartitionSpec as P

NORM_EPS = 1e-05
LANES = 128
VMEM_LIMIT = 64 << 20
HALF = 128
SLOTS_IN_FLIGHT = 10


def rms_scale(values):
    return lax.rsqrt(jnp.mean(values * values, axis=-1, keepdims=True) + NORM_EPS)


def dot_rows(left, right):
    return lax.dot_general(
        left, right, (((0,), (0,)), ((), ())), preferred_element_type=jnp.float32
    )


def dot_cols(left, right):
    return lax.dot_general(
        left, right, (((1,), (1,)), ((), ())), preferred_element_type=jnp.float32
    )


def greet_seq(places, others=(), more=0):
    barrier = pltpu.get_barrier_semaphore()
    here = lax.axis_index("seq")
    place, side = here // 2, lax.rem(here, 2)

    def signal(device):
        pl.semaphore_signal(
            barrier, inc=1, device_id=device, device_id_type=pl.DeviceIdType.MESH
        )

    signal({"seq": here + 1 - 2 * side})
    for other in others:
        signal(other)
    pl.when(place > 0)(lambda: signal({"seq": here - 2}))
    pl.when(place < places - 1)(lambda: signal({"seq": here + 2}))
    ends = jnp.where(place > 0, 1, 0) + jnp.where(place < places - 1, 1, 0)
    pl.semaphore_wait(barrier, 1 + len(others) + ends + more)


class SeqSum:
    def __init__(self, places, own, out, scratch):
        self.places, self.own, self.out = places, own, out
        self.y_in, self.p_left, self.p_right, self.p_acc = scratch[0:4]
        self.q_left, self.q_right, self.q_acc, self.q_in = scratch[4:8]
        self.sems = scratch[8]
        here = lax.axis_index("seq")
        self.place, self.side = here // 2, here % 2

    def remote(self, src, dst, slot, send, recv, place, side):
        return pltpu.make_async_remote_copy(
            src_ref=src,
            dst_ref=dst,
            send_sem=self.sems.at[send, slot],
            recv_sem=self.sems.at[recv, slot],
            device_id={"seq": place * 2 + side},
            device_id_type=pl.DeviceIdType.MESH,
        )

    def chain(self, root):
        last = self.places - 1
        left = jnp.maximum(self.place - 1, 0)
        right = jnp.minimum(self.place + 1, last)
        from_left = (self.place <= root) & (self.place > 0)
        from_right = (self.place >= root) & (self.place < last)
        return left, right, from_left, from_right

    def own_base(self, k):
        held = self.own.shape[0] // (4 * HALF)
        return pl.multiple_of(lax.rem(k, held) * 4 * HALF, 4 * HALF)

    def out_at(self, k, first, size):
        per_panel = self.out.shape[0] // (4 * HALF)
        panel, part = place_in_sums(k, per_panel)
        row = part * 4 * HALF + first
        return self.out.at[
            pl.ds(pl.multiple_of(row, size), size), pl.ds(pl.multiple_of(panel * LANES, LANES), LANES)
        ]

    def p_stage(self, which, k):
        place, side = self.place, self.side
        own = self.own
        slot = lax.rem(k, SLOTS_IN_FLIGHT)
        base = self.own_base(k)
        mine = pl.ds(pl.multiple_of(base + side * HALF, HALF), HALF)
        theirs = pl.ds(pl.multiple_of(base + (1 - side) * HALF, HALF), HALF)
        out_mine = self.out_at(k, side * HALF, HALF)
        root = self.places // 2 - 1 + lax.rem(k, 2)
        left, right, from_left, from_right = self.chain(root)
        acc, y_in = self.p_acc.at[slot], self.y_in.at[slot]
        from_l, from_r = self.p_left.at[slot], self.p_right.at[slot]
        remote = functools.partial(functools.partial, self.remote)

        to_side = remote(own.at[theirs], y_in, slot, 0, 1, place, 1 - side)
        up_right = remote(acc, from_l, slot, 2, 3, right, side)
        up_left = remote(acc, from_r, slot, 2, 4, left, side)

        def down(src):
            return (
                remote(src, out_mine, slot, 5, 7, left, side),
                remote(src, out_mine, slot, 6, 7, right, side),
                remote(src, out_mine, slot, 8, 9, place, 1 - side),
            )

        def keep():
            return pltpu.make_async_copy(acc, out_mine, self.sems.at[10, slot])

        def hand_down(src):
            down_left, down_right, down_side = down(src)
            down_side().start()
            pl.when(from_left)(lambda: down_left().start())
            pl.when(from_right)(lambda: down_right().start())

        if which == "split":
            to_side().start()

        if which == "up":
            to_side().wait_recv()
            acc[...] = own[mine, :] + y_in[...]

            @pl.when(place < root)
            def _():
                @pl.when(from_left)
                def _():
                    up_right().wait_recv()
                    acc[...] += from_l[...]

                up_right().start()

            @pl.when(place > root)
            def _():
                @pl.when(from_right)
                def _():
                    up_left().wait_recv()
                    acc[...] += from_r[...]

                up_left().start()

        if which == "root":

            @pl.when(place == root)
            def _():
                @pl.when(from_left)
                def _():
                    up_right().wait_recv()
                    acc[...] += from_l[...]

                @pl.when(from_right)
                def _():
                    up_left().wait_recv()
                    acc[...] += from_r[...]

                hand_down(acc)
                keep().start()

        if which == "down":

            @pl.when(place != root)
            def _():
                down(acc)[0]().wait_recv()
                hand_down(out_mine)

        if which == "end":
            down_left, down_right, down_side = down(acc)
            down_side().wait()
            to_side().wait_send()
            pl.when(from_left)(lambda: down_left().wait_send())
            pl.when(from_right)(lambda: down_right().wait_send())
            pl.when(place == root)(lambda: keep().wait())
            pl.when(place != root)(lambda: up_left().wait_send())

    def q_stage(self, which, k):
        place, side = self.place, self.side
        own = self.own
        slot = lax.rem(k, SLOTS_IN_FLIGHT)
        base = self.own_base(k)
        wide = pl.ds(pl.multiple_of(base + 2 * HALF, 2 * HALF), 2 * HALF)
        out_wide = self.out_at(k, 2 * HALF, 2 * HALF)
        root = self.places // 2 - lax.rem(k, 2)
        left, right, from_left, from_right = self.chain(root)
        acc, side_in = self.q_acc.at[slot], self.q_in.at[slot]
        from_l, from_r = self.q_left.at[slot], self.q_right.at[slot]
        remote = functools.partial(functools.partial, self.remote)

        up_right = remote(acc, from_l, slot, 11, 12, right, side)
        up_left = remote(acc, from_r, slot, 11, 13, left, side)
        to_side = remote(acc, side_in, slot, 14, 15, place, 1 - side)

        def down(src):
            return (
                remote(src, out_wide, slot, 16, 18, left, side),
                remote(src, out_wide, slot, 17, 18, right, side),
            )

        def keep():
            return pltpu.make_async_copy(side_in, out_wide, self.sems.at[19, slot])

        def hand_down(src):
            down_left, down_right = down(src)
            pl.when(from_left)(lambda: down_left().start())
            pl.when(from_right)(lambda: down_right().start())

        if which == "up":
            acc[...] = own[wide, :]

            @pl.when(place < root)
            def _():
                @pl.when(from_left)
                def _():
                    up_right().wait_recv()
                    acc[...] += from_l[...]

                up_right().start()

            @pl.when(place > root)
            def _():
                @pl.when(from_right)
                def _():
                    up_left().wait_recv()
                    acc[...] += from_r[...]

                up_left().start()

        if which == "root":

            @pl.when(place == root)
            def _():
                @pl.when(from_left)
                def _():
                    up_right().wait_recv()
                    acc[...] += from_l[...]

                @pl.when(from_right)
                def _():
                    up_left().wait_recv()
                    acc[...] += from_r[...]

                to_side().start()

        if which == "side":

            @pl.when(place == root)
            def _():
                to_side().wait_recv()
                side_in[...] += acc[...]
                hand_down(side_in)
                keep().start()

        if which == "down":

            @pl.when(place != root)
            def _():
                down(acc)[0]().wait_recv()
                hand_down(out_wide)

        if which == "end":
            down_left, down_right = down(acc)
            pl.when(from_left)(lambda: down_left().wait_send())
            pl.when(from_right)(lambda: down_right().wait_send())

            @pl.when(place == root)
            def _():
                to_side().wait_send()
                keep().wait()

            pl.when(place != root)(lambda: up_left().wait_send())

    P_LAGS = (("split", 0, 0), ("up", 2, 1), ("root", 3, 3), ("down", 6, 7), ("end", 9, 9))
    Q_LAGS = (("up", 1, 0), ("root", 2, 2), ("side", 4, 4), ("down", 6, 7), ("end", 9, 9))

    def tick(self, t, count):
        middle = (self.place == self.places // 2) | (self.place == self.places // 2 - 1)
        for stage, lags in ((self.p_stage, self.P_LAGS), (self.q_stage, self.Q_LAGS)):
            for which, mid_lag, outer_lag in lags:
                k = t - jnp.where(middle, mid_lag, outer_lag)

                @pl.when((k >= 0) & (k < count))
                def _(stage=stage, which=which, k=k):
                    stage(which, k)

    def run(self, count):
        @pl.loop(0, count + self.P_LAGS[-1][1])
        def _(t):
            self.tick(t, count)


def seq_sum_scratch():
    half = pltpu.VMEM((SLOTS_IN_FLIGHT, HALF, LANES), jnp.float32)
    wide = pltpu.VMEM((SLOTS_IN_FLIGHT, 2 * HALF, LANES), jnp.float32)
    return [half] * 4 + [wide] * 4 + [pltpu.SemaphoreType.DMA((20, SLOTS_IN_FLIGHT))]


SUB_ROWS = 64
STRAIGHT_COPIES = 4
FIRST_MIXER_TICK = 36
BLOCK_TICK = 56
FFN_PANELS = 27
FFN_PARTS = 3
ROW_BLOCK = 256
ROW_TICK = 2
OUT_BLOCK = 256


def place_in_sums(piece, per_panel):
    per_part = FFN_PANELS // FFN_PARTS
    third = per_part // 3
    part, inside = piece // (per_part * per_panel), lax.rem(piece, per_part * per_panel)
    kind = lax.rem(inside, per_part)
    panel = kind // third * (FFN_PANELS // 3) + part * third + lax.rem(kind, third)
    of_ffn = piece < FFN_PANELS * per_panel
    return (
        jnp.where(of_ffn, panel, piece // per_panel),
        jnp.where(of_ffn, inside // per_part, lax.rem(piece, per_panel)),
    )


def norm_back(grad, gain, unit, scale):
    scaled = gain * grad
    return scale * (scaled - unit * jnp.mean(scaled * unit, axis=-1, keepdims=True))


def back_kernel(places, slots, *refs):
    (mid_hbm, cot_hbm, w_gate_hbm, w_up_hbm, w_d_hbm, hidden_hbm, proj_hbm) = refs[0:7]
    (gated_hbm, normed_hbm, mixed_hbm, w_in_hbm, w_out_hbm, tokens_hbm) = refs[7:13]
    (lengths, taps, gain_mix, gain_ffn) = refs[13:17]
    (sums, tokens_out, block_out, mid_chip, mid_far, ffn_chip, ffn_far) = refs[17:24]
    (mid_land, ffn_land, land_in, land_out, land_small) = refs[24:29]
    (mid, cot, w_gu, w_d, act, ggu, own, staged, fetched) = refs[29:38]
    (proj, gated, mixed_buf, conv_in, grad_hid, grad_tok) = refs[38:44]
    (halo_out, halo_in, halo_keep, small, small_in) = refs[44:49]
    load_sems, near_sems, far_sems, keep_sem, fetch_sem = refs[49:54]
    (later_sems, row_sems, halo_sems, weight_sems, out_sems) = refs[54:59]

    summer = SeqSum(places, own, sums, refs[59:])
    here = lax.axis_index("seq")
    last = 2 * places - 1
    tp_at = lax.axis_index("tp")
    core = lax.rem(tp_at, 2)
    sibling = tp_at + 1 - 2 * core
    across = lax.rem(tp_at + 2, 4)
    rows, width = mid.shape
    parts, _, wide = w_gu.shape
    half_rows = rows // 2
    chans = wide // 3
    hidden = wide // 2
    panels = 3 * hidden // LANES

    moves = [(mid_hbm, mid), (cot_hbm, cot), (w_d_hbm, w_d)]
    for c in range(parts):
        for i, source in enumerate((w_gate_hbm, w_up_hbm)):
            move = (
                source.at[:, c * hidden : (c + 1) * hidden],
                w_gu.at[c, :, i * hidden : (i + 1) * hidden],
            )
            moves.insert(i if c == 0 else len(moves), move)
    loads = [
        pltpu.make_async_copy(src, dst, load_sems.at[i]) for i, (src, dst) in enumerate(moves)
    ]
    for load in loads:
        load.start()

    barrier = pltpu.get_barrier_semaphore()

    def signal(device):
        pl.semaphore_signal(barrier, inc=1, device_id=device, device_id_type=pl.DeviceIdType.MESH)

    pl.when(here > 0)(lambda: signal({"seq": here - 1}))
    pl.when(here < last)(lambda: signal({"seq": here + 1}))
    ends = jnp.where(here > 0, 1, 0) + jnp.where(here < last, 1, 0)
    greet_seq(places, ({"tp": sibling}, {"tp": across}), ends)
    ffn_pieces = own.shape[0] // (4 * HALF)
    mixer_pieces = 4 * chans * width // LANES // (4 * HALF) + 1
    count = ffn_pieces + mixer_pieces
    for load in loads[:5]:
        load.wait()

    slot_len = rows // 2 // slots

    def valid_rows(slot, first, size):
        at = lax.broadcasted_iota(jnp.int32, (size, 1), 0) + (here * slot_len + first)
        return (at < lengths[slot]).astype(jnp.float32)

    part_ticks = rows // ROW_BLOCK // ROW_TICK + width // OUT_BLOCK
    first_ticks = width // OUT_BLOCK - 4 * HALF // OUT_BLOCK

    def part_cols(c):
        return pl.ds(pl.multiple_of(c * hidden, LANES), hidden)

    @pl.loop(0, parts)
    def _(c):
        for i in range(1, parts):

            @pl.when(c == i)
            def _(i=i):
                loads[3 + 2 * i].wait()
                loads[4 + 2 * i].wait()

        @pl.loop(0, rows // ROW_BLOCK)
        def _(r):
            at = pl.ds(pl.multiple_of(r * ROW_BLOCK, ROW_BLOCK), ROW_BLOCK)

            @pl.when(c == 0)
            def _():
                per_slot = slot_len // ROW_BLOCK
                mask = valid_rows(r // per_slot, lax.rem(r, per_slot) * ROW_BLOCK, ROW_BLOCK)
                cot[at, :] = (mask * cot[at, :].astype(jnp.float32)).astype(jnp.bfloat16)

            both = jnp.dot(mid[at, :], w_gu[c], preferred_element_type=jnp.float32)
            gate, up = both[:, :hidden], both[:, hidden:]
            grad_act = dot_cols(cot[at, :], w_d[part_cols(c), :])
            sigmoid = 1.0 / (1.0 + jnp.exp(-gate))
            silu = gate * sigmoid
            act[at, part_cols(c)] = (silu * up).astype(jnp.bfloat16)
            slope = sigmoid * (1.0 + gate * (1.0 - sigmoid))
            ggu[c, at, :hidden] = (grad_act * up * slope).astype(jnp.bfloat16)
            ggu[c, at, hidden:] = (grad_act * silu).astype(jnp.bfloat16)

            @pl.when((c > 0) & (lax.rem(r, ROW_TICK) == ROW_TICK - 1))
            def _():
                summer.tick(first_ticks + (c - 1) * part_ticks + r // ROW_TICK, count)

        @pl.loop(0, width // OUT_BLOCK)
        def _(m):
            first = pl.multiple_of(m * OUT_BLOCK, OUT_BLOCK)
            at = pl.ds(first, OUT_BLOCK)
            per_piece = 4 * HALF // OUT_BLOCK
            piece = (c * (width // OUT_BLOCK // per_piece) + m // per_piece) * panels
            base = piece * 4 * HALF + lax.rem(m, per_piece) * OUT_BLOCK

            def put(block, panel):
                for j in range(block.shape[1] // LANES):
                    to = pl.multiple_of(base + (panel + j) * 4 * HALF, OUT_BLOCK)
                    own[pl.ds(to, OUT_BLOCK), :] = block[:, j * LANES : (j + 1) * LANES]

            put(dot_rows(mid[:, at], ggu[c]), 0)
            put(dot_rows(cot[:, at], act[:, part_cols(c)]), wide // LANES)

            step = first_ticks + (c - 1) * part_ticks + rows // ROW_BLOCK // ROW_TICK + m
            step = jnp.where(c > 0, step, m - (width // OUT_BLOCK - first_ticks))

            @pl.when(step >= 0)
            def _():
                summer.tick(step, count)

    early = first_ticks + (parts - 1) * part_ticks
    blocks = rows // 2 // OUT_BLOCK
    def row_block(half, k):
        return pl.ds(pl.multiple_of((half * blocks + k) * OUT_BLOCK, OUT_BLOCK), OUT_BLOCK)

    def mid_part(at):
        return sum(dot_cols(ggu[c, at, :], w_gu[c]) for c in range(parts))

    def ffn_part(at):
        return sum(
            jnp.dot(
                act[at, c * hidden : (c + 1) * hidden],
                w_d[c * hidden : (c + 1) * hidden, :],
                preferred_element_type=jnp.float32,
            )
            for c in range(parts)
        )

    def near(which, land, k):
        return pltpu.make_async_remote_copy(
            src_ref=staged.at[lax.rem(k, 2)],
            dst_ref=land.at[row_block(0, k)],
            send_sem=near_sems.at[which, 0, k],
            recv_sem=near_sems.at[which, 1, k],
            device_id={"tp": sibling},
            device_id_type=pl.DeviceIdType.MESH,
        )

    def far(which, chip, there, k):
        return pltpu.make_async_remote_copy(
            src_ref=chip.at[row_block(0, k)],
            dst_ref=there.at[row_block(0, k)],
            send_sem=far_sems.at[which, 0, k],
            recv_sem=far_sems.at[which, 1, k],
            device_id={"tp": across},
            device_id_type=pl.DeviceIdType.MESH,
        )

    def ffn_across(k):
        return far(1, ffn_chip, ffn_far, k)

    def tp_sum(which, part, land, chip, first_tick):
        @pl.loop(0, blocks)
        def _(k):
            @pl.when(k >= 2)
            def _():
                near(which, land, k - 2).wait_send()

            staged[lax.rem(k, 2)] = part(row_block(1 - core, k))
            near(which, land, k).start()

        for k in range(max(blocks - 2, 0), blocks):
            near(which, land, k).wait_send()

        @pl.loop(0, blocks)
        def _(k):
            near(which, land, k).wait_recv()
            fetch = pltpu.make_async_copy(land.at[row_block(0, k)], fetched, fetch_sem)
            fetch.start()
            staged[0] = part(row_block(core, k))
            fetch.wait()
            staged[0] += fetched[...]
            keep = pltpu.make_async_copy(staged.at[0], chip.at[row_block(0, k)], keep_sem)
            keep.start()
            summer.tick(first_tick + k, count)
            keep.wait()
            if which == 0:
                far(0, mid_chip, mid_far, k).start()

    tp_sum(0, mid_part, mid_land, mid_chip, early)
    tp_sum(1, ffn_part, ffn_land, ffn_chip, early + blocks)

    own_half = pl.ds(pl.multiple_of(core * half_rows, half_rows), half_rows)
    low_half, high_half = pl.ds(0, half_rows), pl.ds(half_rows, half_rows)
    w_out, grad_mixer = mid.at[low_half], mid.at[high_half]
    normed, mixed = act.at[low_half, pl.ds(0, width)], act.at[high_half, pl.ds(0, width)]
    tokens = w_d.at[low_half]
    w_in = (ggu.at[2, low_half], ggu.at[2, high_half], w_gu.at[0], w_gu.at[1])
    moves = [
        (w_out_hbm, w_out),
        (tokens_hbm.at[own_half], tokens),
        (normed_hbm, normed),
        (mixed_hbm, mixed),
    ]
    for j in range(4):
        for g in range(3):
            first = g * width + j * chans
            moves.append(
                (w_in_hbm.at[:, first : first + chans], w_in[j].at[:, g * chans : (g + 1) * chans])
            )
    loads = [
        pltpu.make_async_copy(src, dst, later_sems.at[i]) for i, (src, dst) in enumerate(moves)
    ]
    for load in loads:
        load.start()
    chip, far_rows, hidden_rows = staged.at[0], staged.at[1], fetched
    per_slot = slot_len // OUT_BLOCK
    small[...] = jnp.zeros_like(small)
    ticked = early + 2 * blocks

    @pl.loop(ticked, FIRST_MIXER_TICK)
    def _(t):
        summer.tick(t, count)

    @pl.loop(0, blocks)
    def _(k):
        far(0, mid_chip, mid_far, k).wait()
        ffn_across(k).start()

    for load in loads:
        load.wait()

    def shard_rows(shard, first, size):
        at = lax.rem(shard, 2) * half_rows + first
        return shard // 2, pl.ds(pl.multiple_of(at, size), size)

    def place_of(n):
        slot = n // per_slot
        block = per_slot - 1 - lax.rem(n, per_slot)
        return slot, block, pl.multiple_of(slot * slot_len + block * OUT_BLOCK, OUT_BLOCK)

    def mid_loads(first):
        at = pl.ds(first, OUT_BLOCK)
        return [
            pltpu.make_async_copy(src.at[at], dst, row_sems.at[i])
            for i, (src, dst) in enumerate(((mid_chip, chip), (mid_far, far_rows), (hidden_hbm, hidden_rows)))
        ]

    def proj_loads(slot, block, first):
        return [
            pltpu.make_async_copy(proj_hbm.at[pl.ds(first, OUT_BLOCK)], proj, row_sems.at[3]),
            pltpu.make_async_copy(
                gated_hbm.at[slot, pl.ds(pl.multiple_of(block * OUT_BLOCK, 8), OUT_BLOCK + 8)],
                gated,
                row_sems.at[4],
            ),
        ]

    def start(copies):
        for copy in copies:
            copy.start()

    def wait(copies):
        for copy in copies:
            copy.wait()

    def remote(src, dst, sems, i, device):
        return pltpu.make_async_remote_copy(
            src_ref=src,
            dst_ref=dst,
            send_sem=sems.at[0, i],
            recv_sem=sems.at[1, i],
            device_id=device,
            device_id_type=pl.DeviceIdType.MESH,
        )

    def block_at(k):
        return pl.ds(pl.multiple_of(k * OUT_BLOCK, OUT_BLOCK), OUT_BLOCK)

    def own_rows(first, size):
        return pl.ds(pl.multiple_of(core * half_rows + first, size), size)

    def hidden_grad(chip_part, far_part, hidden_part, cot_part):
        grad_mid = chip_part + far_part
        scale = rms_scale(hidden_part)
        unit = hidden_part * scale
        grad = cot_part.astype(jnp.float32) + norm_back(grad_mid, gain_ffn[...], unit, scale)
        return grad, grad_mid * unit

    def halo_copy(slot, device):
        return remote(halo_out.at[slot], halo_in.at[slot], halo_sems, slot, {"seq": device})

    head = 16
    for slot in range(slots):
        at = pl.ds(slot * slot_len, head)
        top = pl.ds(0, head)
        copies = [
            pltpu.make_async_copy(src.at[at], dst, row_sems.at[i])
            for i, (src, dst) in enumerate(
                (
                    (mid_chip, chip.at[top]),
                    (mid_far, far_rows.at[top]),
                    (hidden_hbm, hidden_rows.at[top]),
                    (proj_hbm, proj.at[top]),
                )
            )
        ]
        start(copies)
        wait(copies)
        grad, _ = hidden_grad(
            chip[top, :], far_rows[top, :], hidden_rows[top, :], cot[own_rows(slot * slot_len, head), :]
        )
        grad_mixed = dot_cols(grad.astype(jnp.bfloat16), w_out[...])
        halo_out[slot] = (grad_mixed * proj[top, width : 2 * width])[:8]
        pl.when(here > 0)(lambda slot=slot: halo_copy(slot, here - 1).start())

    slot, block, first = place_of(0)
    start(mid_loads(first))
    start(proj_loads(slot, block, first))

    @pl.when(here == last)
    def _():
        halo_in[...] = jnp.zeros_like(halo_in)

    @pl.when(here < last)
    def _():
        for slot in range(slots):
            halo_copy(slot, here + 1).wait_recv()

    def out_rows(first):
        return own_rows(first, OUT_BLOCK)

    def hand_out(target, first, i):
        at = out_rows(first)
        return (
            pltpu.make_async_copy(grad_tok, target.at[at], out_sems.at[0, 2 * blocks]),
            remote(grad_tok, target.at[at], out_sems, i, {"tp": sibling}),
        )

    @pl.loop(0, blocks)
    def _(n):
        slot, block, first = place_of(n)
        at = pl.ds(first, OUT_BLOCK)
        wait(mid_loads(first))

        @pl.loop(0, OUT_BLOCK // SUB_ROWS)
        def _(r):
            sub = pl.ds(pl.multiple_of(r * SUB_ROWS, SUB_ROWS), SUB_ROWS)
            whole = pl.ds(pl.multiple_of(first + r * SUB_ROWS, SUB_ROWS), SUB_ROWS)
            grad, for_gain = hidden_grad(
                chip[sub, :],
                far_rows[sub, :],
                hidden_rows[sub, :],
                cot[own_rows(first + r * SUB_ROWS, SUB_ROWS), :],
            )
            grad_hid[sub, :] = grad
            grad_mixer[whole, :] = grad.astype(jnp.bfloat16)
            small[1:2, :] += jnp.sum(for_gain, axis=0, keepdims=True)

        @pl.when(n < blocks - 1)
        def _():
            start(mid_loads(place_of(n + 1)[2]))

        mixed_buf[...] = dot_cols(grad_mixer[at, :], w_out[...])
        wait(proj_loads(slot, block, first))

        @pl.when(block == per_slot - 1)
        def _():
            conv_in[pl.ds(OUT_BLOCK, 8), :] = halo_in[slot]

        @pl.when(block < per_slot - 1)
        def _():
            conv_in[pl.ds(OUT_BLOCK, 8), :] = halo_keep[...]

        summer.tick(FIRST_MIXER_TICK + 2 * n, count)
        mask = valid_rows(core * slots + slot, block * OUT_BLOCK, OUT_BLOCK)

        @pl.loop(0, width // chans)
        def _(c):
            def cols(gate):
                return pl.ds(pl.multiple_of(gate * width + c * chans, chans), chans)

            here_cols = cols(0)
            pair, shard_at = shard_rows(c, first, OUT_BLOCK)
            in_gate, out_gate, conv_value = (proj[:, cols(g)] for g in range(3))
            grad_mixed = mixed_buf[:, here_cols]
            now = grad_mixed * out_gate
            conv_in[pl.ds(0, OUT_BLOCK), here_cols] = now
            seen = [gated[pl.ds(6 + j, OUT_BLOCK), here_cols] for j in range(3)]
            tap = [taps[j : j + 1, here_cols] for j in range(3)]
            conv_sum = tap[0] * seen[0] + tap[1] * seen[1] + tap[2] * seen[2]
            for j in range(3):
                small[2 + j : 3 + j, here_cols] += jnp.sum(now * seen[j], axis=0, keepdims=True)
            ggu[pair, shard_at, chans : 2 * chans] = (grad_mixed * conv_sum).astype(jnp.bfloat16)
            grad_gated = mask * (
                tap[2] * now
                + tap[1] * conv_in[pl.ds(1, OUT_BLOCK), here_cols]
                + tap[0] * conv_in[pl.ds(2, OUT_BLOCK), here_cols]
            )
            ggu[pair, shard_at, :chans] = (grad_gated * conv_value).astype(jnp.bfloat16)
            ggu[pair, shard_at, 2 * chans : 3 * chans] = (grad_gated * in_gate).astype(jnp.bfloat16)

        halo_keep[...] = conv_in[pl.ds(0, 8), :]

        @pl.when(n < blocks - 1)
        def _():
            start(proj_loads(*place_of(n + 1)))

        def shard_grad(j):
            pair, shard_at = shard_rows(j, first, OUT_BLOCK)
            return dot_cols(ggu[pair, shard_at, :], w_in[j][...])

        mixed_buf[...] = sum(shard_grad(j) for j in range(4))

        @pl.when(n > 0)
        def _():
            local, there = hand_out(tokens_out, place_of(n - 1)[2], n - 1)
            local.wait()
            there.wait_send()

        @pl.loop(0, OUT_BLOCK // SUB_ROWS)
        def _(r):
            sub = pl.ds(pl.multiple_of(r * SUB_ROWS, SUB_ROWS), SUB_ROWS)
            whole = pl.ds(pl.multiple_of(first + r * SUB_ROWS, SUB_ROWS), SUB_ROWS)
            inputs = tokens[whole, :].astype(jnp.float32)
            scale = rms_scale(inputs)
            unit = inputs * scale
            grad_in = mixed_buf[sub, :]
            grad_tok[sub, :] = grad_hid[sub, :] + norm_back(grad_in, gain_mix[...], unit, scale)
            small[0:1, :] += jnp.sum(grad_in * unit, axis=0, keepdims=True)

        start(hand_out(tokens_out, first, n))
        summer.tick(FIRST_MIXER_TICK + 2 * n + 1, count)

    in_blocks = width // OUT_BLOCK
    stages = [proj.at[:, i * wide : (i + 1) * wide] for i in range(3)]

    def to_near(src, dst, i):
        return remote(src, dst, weight_sems, i, {"tp": sibling})

    def near_in(m):
        cols = pl.ds(pl.multiple_of(lax.rem(m, 2) * wide, LANES), wide)
        return to_near(proj.at[:, cols], land_in.at[m], m)

    near_out = to_near(grad_hid, land_out, in_blocks)
    near_small = to_near(small, land_small, in_blocks + 1)

    def in_part(m, shard):
        pair, shard_at = shard_rows(shard, 0, half_rows)
        return dot_rows(normed[:, block_at(m)], ggu[pair, shard_at, :])

    def out_part(shard):
        at = pl.ds(pl.multiple_of(shard * chans, LANES), chans)
        return dot_rows(mixed[:, at], grad_mixer[...])

    near_small.start()
    first_tick = FIRST_MIXER_TICK + 2 * blocks

    @pl.loop(0, in_blocks)
    def _(m):
        @pl.when(m >= 2)
        def _():
            near_in(m - 2).wait_send()

        cols = pl.ds(pl.multiple_of(lax.rem(m, 2) * wide, LANES), wide)
        proj[:, cols] = in_part(m, sibling)
        near_in(m).start()
        summer.tick(first_tick + m, count)

    grad_hid[...] = out_part(sibling)
    near_out.start()

    @pl.loop(0, in_blocks)
    def _(m):
        near_in(m).wait_recv()
        fetch = pltpu.make_async_copy(land_in.at[m], stages[2], row_sems.at[0])
        fetch.start()
        part = in_part(m, tp_at)
        fetch.wait()
        for i in range(wide // LANES):
            to = pl.multiple_of(i * width + m * OUT_BLOCK, OUT_BLOCK)
            own[pl.ds(to, OUT_BLOCK), :] = (
                part[:, i * LANES : (i + 1) * LANES]
                + proj[:, 2 * wide + i * LANES : 2 * wide + (i + 1) * LANES]
            )

        summer.tick(first_tick + in_blocks + m, count)

    near_out.wait_recv()
    near_small.wait_recv()
    fetches = [
        pltpu.make_async_copy(land_out, mixed_buf, row_sems.at[0]),
        pltpu.make_async_copy(land_small, small_in, row_sems.at[1]),
    ]
    start(fetches)
    part = out_part(tp_at)
    wait(fetches)
    out_first = wide // LANES * width
    small_first = out_first + width // LANES * chans
    for p in range(width // LANES):
        cols = slice(p * LANES, (p + 1) * LANES)
        own[pl.ds(out_first + p * chans, chans), :] = part[:, cols] + mixed_buf[:, cols]
        own[pl.ds(small_first + 8 * p, 8), :] = small[:, cols] + small_in[:, cols]
    unused = 4 * HALF - 8 * (width // LANES)
    own[pl.ds(small_first + 4 * HALF - unused, unused), :] = jnp.zeros((unused, LANES), jnp.float32)

    local, there = hand_out(tokens_out, place_of(blocks - 1)[2], blocks - 1)
    local.wait()
    there.wait_send()
    done = first_tick + 2 * in_blocks
    pause = BLOCK_TICK

    @pl.loop(done, pause)
    def _(t):
        summer.tick(t, count)

    @pl.loop(0, blocks)
    def _(k):
        ffn_across(k).wait_recv()
        at = block_at(k)
        copies = [
            pltpu.make_async_copy(src.at[at], dst, row_sems.at[i])
            for i, (src, dst) in enumerate(((ffn_chip, chip), (ffn_far, far_rows), (hidden_hbm, hidden_rows)))
        ]
        start(copies)

        @pl.when(k > 0)
        def _():
            local, there = hand_out(block_out, (k - 1) * OUT_BLOCK, blocks + k - 1)
            local.wait()
            there.wait_send()

        wait(copies)
        grad_tok[...] = hidden_rows[...] + (chip[...] + far_rows[...])
        start(hand_out(block_out, k * OUT_BLOCK, blocks + k))
        summer.tick(pause + k, count)

    @pl.loop(pause + blocks, count + summer.P_LAGS[-1][1])
    def _(t):
        summer.tick(t, count)

    local, there = hand_out(block_out, (blocks - 1) * OUT_BLOCK, 2 * blocks - 1)
    local.wait()
    there.wait_send()

    @pl.loop(0, blocks)
    def _(k):
        ffn_across(k).wait_send()
        hand_out(tokens_out, place_of(k)[2], k)[1].wait_recv()
        hand_out(block_out, k * OUT_BLOCK, blocks + k)[1].wait_recv()

    for m in range(max(in_blocks - 2, 0), in_blocks):
        near_in(m).wait_send()
    near_out.wait_send()
    near_small.wait_send()

    @pl.when(here > 0)
    def _():
        for slot in range(slots):
            halo_copy(slot, here - 1).wait_send()


def back_both(hbm, vmem, slots, sum_cols, collective_id):
    normed_mid, _, w_gate, _, w_d, _, _, gated, _, _, _, _, _ = hbm
    rows, width = normed_mid.shape
    half_rows = rows // 2
    local = w_gate.shape[1]
    hidden = local // FFN_PARTS
    chans = 2 * hidden // 3
    blocks = half_rows // OUT_BLOCK
    in_blocks = width // OUT_BLOCK
    f32, low = jnp.float32, jnp.bfloat16
    half = jax.ShapeDtypeStruct((half_rows, width), f32)
    full = jax.ShapeDtypeStruct((rows, width), f32)
    block = pltpu.VMEM((OUT_BLOCK, width), f32)
    row8 = pltpu.VMEM((8, width), f32)
    anywhere = pl.BlockSpec(memory_space=pl.ANY)
    return pl.pallas_call(
        functools.partial(back_kernel, lax.axis_size("seq") // 2, slots),
        out_shape=[jax.ShapeDtypeStruct((width, sum_cols), f32)]
        + [full] * 2
        + [half] * 6
        + [
            jax.ShapeDtypeStruct((in_blocks, OUT_BLOCK, 2 * hidden), f32),
            jax.ShapeDtypeStruct((chans, width), f32),
            jax.ShapeDtypeStruct((8, width), f32),
        ],
        in_specs=[anywhere] * len(hbm)
        + [pl.BlockSpec(memory_space=pltpu.SMEM)]
        + [pl.BlockSpec(memory_space=pltpu.VMEM)] * (len(vmem) - 1),
        out_specs=[anywhere] * 12,
        scratch_shapes=[
            pltpu.VMEM((rows, width), low),
            pltpu.VMEM((rows, width), low),
            pltpu.VMEM((FFN_PARTS, width, 2 * hidden), low),
            pltpu.VMEM(w_d.shape, low),
            pltpu.VMEM((rows, local), low),
            pltpu.VMEM((FFN_PARTS, rows, 2 * hidden), low),
            pltpu.VMEM((3 * local * width // LANES, LANES), f32),
            pltpu.VMEM((2, OUT_BLOCK, width), f32),
            block,
            pltpu.VMEM((OUT_BLOCK, 3 * width), f32),
            pltpu.VMEM((OUT_BLOCK + 8, width), f32),
            block,
            pltpu.VMEM((OUT_BLOCK + 8, width), f32),
            block,
            block,
            pltpu.VMEM((slots, 8, width), f32),
            pltpu.VMEM((slots, 8, width), f32),
            row8,
            row8,
            row8,
            pltpu.SemaphoreType.DMA((3 + 2 * FFN_PARTS,)),
            pltpu.SemaphoreType.DMA((2, 2, blocks)),
            pltpu.SemaphoreType.DMA((2, 2, blocks)),
            pltpu.SemaphoreType.DMA,
            pltpu.SemaphoreType.DMA,
            pltpu.SemaphoreType.DMA((16,)),
            pltpu.SemaphoreType.DMA((5,)),
            pltpu.SemaphoreType.DMA((2, slots)),
            pltpu.SemaphoreType.DMA((2, in_blocks + 2)),
            pltpu.SemaphoreType.DMA((2, 2 * blocks + 1)),
        ]
        + seq_sum_scratch(),
        compiler_params=pltpu.CompilerParams(
            collective_id=collective_id, has_side_effects=True, vmem_limit_bytes=VMEM_LIMIT
        ),
        cost_estimate=pl.CostEstimate(
            flops=18 * rows * width * local, bytes_accessed=800 << 20, transcendentals=0
        ),
        name="back_both",
    )(*hbm, *vmem)


def front_kernel(places, slots, *refs):
    (w_in, w_out, taps, gain_mix, gain_ffn, lengths, tokens_hbm) = refs[0:7]
    (in_hbm, out_hbm, full_taps, mid_hbm, hidden_hbm, proj_hbm, gated_hbm) = refs[7:14]
    (normed_hbm, mixed_hbm) = refs[14:16]
    own_in, own_out, far_in, far_out, sib_in, sib_out, sibfar_in, sibfar_out = refs[16:24]
    own_taps, far_taps, sib_taps, sibfar_taps, share_in, share_out = refs[24:30]
    (full_in, full_out, tokens, normed, mixed, out_gate, gates, gated) = refs[30:38]
    (unit_out, unit_in, hidden) = refs[38:41]
    sends, recvs, once, halo_sems, gate_sems, unit_sems, keep_sems, mid_sems = refs[41:49]
    straight_sems = refs[49]
    here = lax.axis_index("seq")
    place, side = here // 2, lax.rem(here, 2)
    last = places - 1
    end = 2 * places - 1
    tp_at = lax.axis_index("tp")
    core = lax.rem(tp_at, 2)
    sibling = tp_at + 1 - 2 * core
    across = lax.rem(tp_at + 2, 4)
    far_sibling = sibling + across - tp_at
    straight = w_in.shape[1] // 2
    in_rows = (w_in.shape[1] - straight) // (2 * places)
    out_rows = w_out.shape[0] // (2 * places)
    chans = w_in.shape[2]
    rows, width = tokens.shape
    slot_len = rows // slots
    low = jnp.bfloat16

    load_tokens = pltpu.make_async_copy(
        tokens_hbm.at[pl.ds(pl.multiple_of(core * rows, rows), rows)], tokens, keep_sems.at[0]
    )
    load_tokens.start()
    barrier = pltpu.get_barrier_semaphore()

    def signal(device):
        pl.semaphore_signal(barrier, inc=1, device_id=device, device_id_type=pl.DeviceIdType.MESH)

    pl.when(here > 0)(lambda: signal({"seq": here - 1}))
    pl.when(here < end)(lambda: signal({"seq": here + 1}))
    ends = jnp.where(here > 0, 1, 0) + jnp.where(here < end, 1, 0)
    greet_seq(places, ({"tp": sibling}, {"tp": across}), ends)

    def shares(j):
        return (
            pl.ds(pl.multiple_of(j * in_rows, in_rows), in_rows),
            pl.ds(pl.multiple_of(j * out_rows, out_rows), out_rows),
        )

    def remote(src, dst, send, recv, device):
        return pltpu.make_async_remote_copy(
            src_ref=src,
            dst_ref=dst,
            send_sem=send,
            recv_sem=recv,
            device_id=device,
            device_id_type=pl.DeviceIdType.MESH,
        )

    def copies(source, target, j, kind, device):
        for i, at in enumerate(shares(j)):
            yield remote(
                source[i] if kind == 0 else source[i].at[at],
                target[i].at[at],
                sends.at[kind, i, j],
                recvs.at[0 if kind < 4 else 1, i, j],
                device,
            )

    share, far, sibfar = (share_in, share_out), (far_in, far_out), (sibfar_in, sibfar_out)

    def across_share():
        return copies(share, far, here, 0, {"tp": across})

    def to_right(j):
        return copies(far, far, j, 1, {"seq": here + 2})

    def to_left(j):
        return copies(far, far, j, 2, {"seq": here - 2})

    def to_side(j):
        return copies(far, far, j, 3, {"seq": here + 1 - 2 * side})

    def to_sibling(j):
        return copies(far, sibfar, j, 4, {"tp": sibling})

    def straight_rows(q):
        size = straight // STRAIGHT_COPIES
        first = w_in.shape[1] - straight + q * size
        return pl.ds(pl.multiple_of(first, size), size)

    def straight_across(q):
        at = straight_rows(q)
        return remote(
            own_in.at[at], far_in.at[at], straight_sems.at[0, q], straight_sems.at[1, q],
            {"tp": across},
        )

    def straight_sibling(q):
        at = straight_rows(q)
        return remote(
            far_in.at[at], sibfar_in.at[at], straight_sems.at[2, q], straight_sems.at[3, q],
            {"tp": sibling},
        )

    def pass_straight(q):
        straight_across(q).wait_recv()
        straight_sibling(q).start()

    def start(group):
        for copy in group:
            copy.start()

    def arrived(group):
        for copy in group:
            copy.wait_recv()

    def left_source(group):
        for copy in group:
            copy.wait_send()

    def single(i, src, dst, device):
        return remote(src, dst, once.at[0, i], once.at[1, i], device)

    in_at, out_at = shares(here)
    for g in range(3):
        share_in[:, g * chans : (g + 1) * chans] = w_in[g, in_at, :].astype(jnp.float32)
    share_out[...] = w_out[out_at, :].astype(jnp.float32)
    start(across_share())
    own_taps[...] = taps[...]
    taps_far = single(0, own_taps, far_taps, {"tp": across})
    taps_sib = single(1, own_taps, sib_taps, {"tp": sibling})
    taps_sibfar = single(2, far_taps, sibfar_taps, {"tp": sibling})
    for g in range(3):
        own_in[:, g * chans : (g + 1) * chans] = w_in[g].astype(jnp.float32)
    own_out[...] = w_out[...].astype(jnp.float32)
    in_sib = single(3, own_in, sib_in, {"tp": sibling})
    out_sib = single(4, own_out, sib_out, {"tp": sibling})
    for copy in (taps_far, taps_sib, in_sib, out_sib):
        copy.start()
    for q in range(STRAIGHT_COPIES):
        straight_across(q).start()

    def gate_cols(g, index):
        return pl.ds(pl.multiple_of(g * width + index * chans, LANES), chans)

    def place_shard(shard_in, shard_out, shard_taps, index):
        for g in range(3):
            full_in[:, gate_cols(g, index)] = shard_in[:, g * chans : (g + 1) * chans].astype(low)
        at = pl.ds(pl.multiple_of(index * chans, chans), chans)
        full_out[at, :] = shard_out[...].astype(low)
        full_taps[:, gate_cols(0, index)] = shard_taps[...]

    def gate_out(turn, index, g):
        if g == 1:
            return pltpu.make_async_copy(
                out_gate.at[:, gate_cols(0, index)],
                proj_hbm.at[:, gate_cols(1, index)],
                gate_sems.at[turn, 1],
            )
        return pltpu.make_async_copy(
            gates.at[turn % 2, g // 2], proj_hbm.at[:, gate_cols(g, index)], gate_sems.at[turn, g]
        )

    def halo(turn, index, slot):
        return remote(
            gated.at[slot, pl.ds(slot_len, 8), gate_cols(0, index)],
            gated.at[slot, pl.ds(0, 8), gate_cols(0, index)],
            halo_sems.at[0, turn, slot],
            halo_sems.at[1, turn, slot],
            {"seq": here + 1},
        )

    order = (tp_at, sibling, across, far_sibling)

    def project(turn):
        index = order[turn]
        cols = gate_cols(0, index)
        if turn >= 2:
            gate_out(turn - 2, order[turn - 2], 0).wait()
            gate_out(turn - 2, order[turn - 2], 2).wait()

        @pl.loop(0, slots)
        def _(s):
            at = pl.ds(pl.multiple_of(s * slot_len, slot_len), slot_len)

            def gate(g):
                return jnp.dot(
                    normed[at, :], full_in[:, gate_cols(g, index)],
                    preferred_element_type=jnp.float32,
                )

            at_pos = lax.broadcasted_iota(jnp.int32, (slot_len, 1), 0) + here * slot_len
            mask = (at_pos < lengths[core * slots + s]).astype(jnp.float32)
            in_gate, value = gate(0), gate(2)
            gates[turn % 2, 0, at, :] = in_gate
            gates[turn % 2, 1, at, :] = value
            gated[s, pl.ds(8, slot_len), cols] = mask * in_gate * value
            out_gate[at, cols] = gate(1)

        for g in range(3):
            gate_out(turn, index, g).start()

        @pl.when(here < end)
        def _():
            for slot in range(slots):
                halo(turn, index, slot).start()

    def convolve(turn):
        index = order[turn]
        cols = gate_cols(0, index)

        @pl.when(here > 0)
        def _():
            for slot in range(slots):
                halo(turn, index, slot).wait_recv()

        @pl.loop(0, slots)
        def _(s):
            at = pl.ds(pl.multiple_of(s * slot_len, slot_len), slot_len)
            seen = [gated[s, pl.ds(6 + j, slot_len), cols] for j in range(3)]
            tap = [full_taps[j : j + 1, cols] for j in range(3)]
            conv_sum = tap[0] * seen[0] + tap[1] * seen[1] + tap[2] * seen[2]
            mixed[at, cols] = (out_gate[at, cols] * conv_sum).astype(low)

    @pl.when(here == 0)
    def _():
        for slot in range(slots):
            gated[slot, pl.ds(0, 8), :] = jnp.zeros((8, width), jnp.float32)

    load_tokens.wait()

    @pl.loop(0, rows // SUB_ROWS)
    def _(r):
        at = pl.ds(pl.multiple_of(r * SUB_ROWS, SUB_ROWS), SUB_ROWS)
        inputs = tokens[at, :].astype(jnp.float32)
        normed[at, :] = (gain_mix[...] * (inputs * rms_scale(inputs))).astype(low)

    keep_normed = pltpu.make_async_copy(normed, normed_hbm, keep_sems.at[0])
    keep_normed.start()
    place_shard(own_in, own_out, own_taps, tp_at)
    project(0)

    arrived(across_share())
    pl.when(place < last)(lambda: start(to_right(here)))
    pl.when(place > 0)(lambda: start(to_left(here)))
    start(to_side(here))
    start(to_sibling(here))
    taps_far.wait_recv()
    taps_sibfar.start()
    in_sib.wait_recv()
    out_sib.wait_recv()
    taps_sib.wait_recv()
    place_shard(sib_in, sib_out, sib_taps, sibling)
    project(1)

    def from_side(q):
        j = 2 * q + 1 - side
        arrived(to_side(j))
        start(to_sibling(j))

    @pl.loop(1, places)
    def _(d):
        @pl.when(place - d >= 0)
        def _():
            j = here - 2 * d
            arrived(to_right(j))
            pl.when(place < last)(lambda: start(to_right(j)))
            start(to_side(j))
            start(to_sibling(j))

        @pl.when(place + d <= last)
        def _():
            j = here + 2 * d
            arrived(to_left(j))
            pl.when(place > 0)(lambda: start(to_left(j)))
            start(to_side(j))
            start(to_sibling(j))

        @pl.when(d == 1)
        def _():
            from_side(place)
            convolve(0)
            convolve(1)

        pl.when(place - d >= 0)(lambda: from_side(place - d))
        pl.when(place + d <= last)(lambda: from_side(place + d))
        pl.when(d <= STRAIGHT_COPIES)(lambda: pass_straight(d - 1))

    for q in range(min(last, STRAIGHT_COPIES), STRAIGHT_COPIES):
        pass_straight(q)

    place_shard(far_in, far_out, far_taps, across)
    project(2)
    taps_sibfar.wait_recv()

    @pl.loop(0, 2 * places)
    def _(j):
        arrived(to_sibling(j))

    for q in range(STRAIGHT_COPIES):
        straight_sibling(q).wait_recv()
    place_shard(sibfar_in, sibfar_out, sibfar_taps, far_sibling)
    project(3)
    keep_in = pltpu.make_async_copy(full_in, in_hbm, keep_sems.at[1])
    keep_out = pltpu.make_async_copy(full_out, out_hbm, keep_sems.at[2])
    keep_in.start()
    keep_out.start()
    convolve(2)
    convolve(3)
    keep_gated = pltpu.make_async_copy(gated, gated_hbm, keep_sems.at[3])
    keep_mixed = pltpu.make_async_copy(mixed, mixed_hbm, keep_sems.at[4])
    keep_gated.start()
    keep_mixed.start()
    keep_normed.wait()

    blocks = rows // OUT_BLOCK

    def block_at(k, first=0):
        return pl.ds(pl.multiple_of(first + k * OUT_BLOCK, OUT_BLOCK), OUT_BLOCK)

    def unit_copy(k):
        return remote(
            unit_out.at[block_at(k)], unit_in.at[block_at(k)],
            unit_sems.at[0, k], unit_sems.at[1, k], {"tp": sibling},
        )

    def hidden_copy(k):
        return pltpu.make_async_copy(
            hidden.at[lax.rem(k, 2)], hidden_hbm.at[block_at(k)], mid_sems.at[0, lax.rem(k, 2)]
        )

    def mid_copy(half, held, whose, k):
        return pltpu.make_async_copy(
            held.at[block_at(k)], mid_hbm.at[block_at(k, whose * rows)], mid_sems.at[half, k]
        )

    @pl.loop(0, blocks)
    def _(k):
        slot = lax.rem(k, 2)
        at = block_at(k)
        pl.when(k >= 2)(lambda: hidden_copy(k - 2).wait())
        hidden[slot] = jnp.dot(mixed[at, :], full_out[...], preferred_element_type=jnp.float32)

        @pl.loop(0, OUT_BLOCK // SUB_ROWS)
        def _(r):
            sub = pl.ds(pl.multiple_of(r * SUB_ROWS, SUB_ROWS), SUB_ROWS)
            whole = pl.ds(pl.multiple_of(k * OUT_BLOCK + r * SUB_ROWS, SUB_ROWS), SUB_ROWS)
            hidden_rows = tokens[whole, :].astype(jnp.float32) + hidden[slot, sub, :]
            hidden[slot, sub, :] = hidden_rows
            unit = hidden_rows * rms_scale(hidden_rows)
            unit_out[whole, :] = unit
            normed[whole, :] = (gain_ffn[...] * unit).astype(low)

        unit_copy(k).start()
        hidden_copy(k).start()
        mid_copy(1, normed, core, k).start()

    keep_mixed.wait()

    @pl.loop(0, blocks)
    def _(k):
        unit_copy(k).wait_recv()

        @pl.loop(0, OUT_BLOCK // SUB_ROWS)
        def _(r):
            whole = pl.ds(pl.multiple_of(k * OUT_BLOCK + r * SUB_ROWS, SUB_ROWS), SUB_ROWS)
            mixed[whole, :] = (gain_ffn[...] * unit_in[whole, :]).astype(low)

        mid_copy(2, mixed, 1 - core, k).start()

    @pl.loop(0, blocks)
    def _(k):
        unit_copy(k).wait_send()
        mid_copy(1, normed, core, k).wait()
        mid_copy(2, mixed, 1 - core, k).wait()

    for k in range(max(blocks - 2, 0), blocks):
        hidden_copy(k).wait()
    keep_in.wait()
    keep_out.wait()
    keep_gated.wait()
    for turn in range(4):
        for g in range(3):
            if turn >= 2 or g == 1:
                gate_out(turn, order[turn], g).wait()

    @pl.when(here < end)
    def _():
        for turn in range(4):
            for slot in range(slots):
                halo(turn, order[turn], slot).wait_send()

    left_source(across_share())
    for q in range(STRAIGHT_COPIES):
        straight_across(q).wait_send()
        straight_sibling(q).wait_send()
    for copy in (taps_far, taps_sib, taps_sibfar, in_sib, out_sib):
        copy.wait_send()

    @pl.loop(0, places)
    def _(q):
        j = 2 * q + side
        left_source(to_side(j))
        pl.when((q <= place) & (place < last))(lambda: left_source(to_right(j)))
        pl.when((q >= place) & (place > 0))(lambda: left_source(to_left(j)))
        left_source(to_sibling(j))
        left_source(to_sibling(2 * q + 1 - side))


def mixer_front(w_in, w_out, taps, gain_mix, gain_ffn, lengths, tokens, slots, collective_id):
    width, _, chans = w_in.shape
    rows = tokens.shape[0] // 2
    count = lax.axis_size("seq")
    group = lax.axis_size("tp")
    f32, low = jnp.float32, jnp.bfloat16
    blocks = rows // OUT_BLOCK
    pair = [pltpu.VMEM((width, 3 * chans), f32), pltpu.VMEM((chans, width), f32)]
    whole = pl.BlockSpec(memory_space=pltpu.VMEM)
    anywhere = pl.BlockSpec(memory_space=pl.ANY)
    padded = (slots, rows // slots + 8, width)
    return pl.pallas_call(
        functools.partial(front_kernel, count // 2, slots),
        out_shape=[
            jax.ShapeDtypeStruct((width, 3 * chans * group), low),
            jax.ShapeDtypeStruct((chans * group, width), low),
            jax.ShapeDtypeStruct((8, chans * group), f32),
            jax.ShapeDtypeStruct((2 * rows, width), low),
            jax.ShapeDtypeStruct((rows, width), f32),
            jax.ShapeDtypeStruct((rows, 3 * width), f32),
            jax.ShapeDtypeStruct(padded, f32),
            jax.ShapeDtypeStruct((rows, width), low),
            jax.ShapeDtypeStruct((rows, width), low),
        ],
        in_specs=[whole] * 5 + [pl.BlockSpec(memory_space=pltpu.SMEM), anywhere],
        out_specs=[anywhere] * 2 + [whole] + [anywhere] * 6,
        scratch_shapes=pair * 4
        + [pltpu.VMEM((8, chans), f32)] * 4
        + [
            pltpu.VMEM((width // 2 // count, 3 * chans), f32),
            pltpu.VMEM((chans // count, width), f32),
            pltpu.VMEM((width, 3 * chans * group), low),
            pltpu.VMEM((chans * group, width), low),
            pltpu.VMEM((rows, width), low),
            pltpu.VMEM((rows, width), low),
            pltpu.VMEM((rows, width), low),
            pltpu.VMEM((rows, width), f32),
            pltpu.VMEM((2, 2, rows, chans), f32),
            pltpu.VMEM(padded, f32),
            pltpu.VMEM((rows, width), f32),
            pltpu.VMEM((rows, width), f32),
            pltpu.VMEM((2, OUT_BLOCK, width), f32),
            pltpu.SemaphoreType.DMA((5, 2, count)),
            pltpu.SemaphoreType.DMA((2, 2, count)),
            pltpu.SemaphoreType.DMA((2, 5)),
            pltpu.SemaphoreType.DMA((2, 4, slots)),
            pltpu.SemaphoreType.DMA((4, 3)),
            pltpu.SemaphoreType.DMA((2, blocks)),
            pltpu.SemaphoreType.DMA((5,)),
            pltpu.SemaphoreType.DMA((3, blocks)),
            pltpu.SemaphoreType.DMA((4, STRAIGHT_COPIES)),
        ],
        compiler_params=pltpu.CompilerParams(
            collective_id=collective_id, has_side_effects=True, vmem_limit_bytes=VMEM_LIMIT
        ),
        name="mixer_front",
    )(
        w_in.transpose(1, 0, 2),
        w_out,
        jnp.pad(taps, ((0, 5), (0, 0))),
        gain_mix,
        gain_ffn,
        lengths,
        tokens,
    )


def finish_kernel(slots, chans, hidden, *refs):
    (sums, tokens_in, block_in, lengths) = refs[0:4]
    (block_out, tokens_out, gains, g_in, g_conv, g_out, g_gate, g_up, g_down) = refs[4:13]
    (held, tokens, block, rounded, turned, in_sems, block_sems, turn_sems, out_sems) = refs[13:22]
    rows, width = block_in.shape
    slot_len = rows // slots
    here = lax.axis_index("seq")
    tp_at = lax.axis_index("tp")
    first = 3 * hidden
    out_first = first + 3 * chans
    small_first = out_first + chans
    blocks = rows // OUT_BLOCK
    turns = hidden // LANES
    half_rows = rows // 2

    def cols(start, size):
        return (slice(None), slice(start, start + size))

    parts = [cols(i * hidden, hidden) for i in range(3)] + [cols(first, held.shape[1] - first)]
    halves = [slice(0, half_rows), slice(half_rows, rows)]
    part_loads = [
        pltpu.make_async_copy(sums.at[at], held.at[at], in_sems.at[i]) for i, at in enumerate(parts)
    ]
    token_loads = [
        pltpu.make_async_copy(tokens_in.at[at], tokens.at[at], in_sems.at[4 + i])
        for i, at in enumerate(halves)
    ]

    def block_at(k):
        return pl.ds(pl.multiple_of(k * OUT_BLOCK, OUT_BLOCK), OUT_BLOCK)

    def block_load(k):
        return pltpu.make_async_copy(
            block_in.at[block_at(k)], block.at[block_at(k)], block_sems.at[0, k]
        )

    def block_store(k):
        return pltpu.make_async_copy(
            rounded.at[block_at(k)], block_out.at[block_at(k)], block_sems.at[1, k]
        )

    def panel_at(k):
        return pl.ds(pl.multiple_of(k * LANES, LANES), LANES)

    def turn_store(k):
        at = panel_at(k)
        return pltpu.make_async_copy(turned.at[at], g_down.at[at], turn_sems.at[k])

    stores = []

    def store(src, dst):
        copy = pltpu.make_async_copy(src, dst, out_sems.at[len(stores)])
        copy.start()
        stores.append(copy)

    part_loads[2].start()

    @pl.loop(0, blocks)
    def _(k):
        block_load(k).start()

    for load in (*token_loads, part_loads[0], part_loads[1], part_loads[3]):
        load.start()

    part_loads[2].wait()

    @pl.loop(0, turns)
    def _(k):
        from_cols = pl.ds(pl.multiple_of(2 * hidden + k * LANES, LANES), LANES)
        turned[panel_at(k), :] = held[:, from_cols].T
        turn_store(k).start()

    @pl.loop(0, blocks)
    def _(k):
        block_load(k).wait()
        per_slot = slot_len // OUT_BLOCK
        at = lax.broadcasted_iota(jnp.int32, (OUT_BLOCK, 1), 0)
        at = at + (here * slot_len + lax.rem(k, per_slot) * OUT_BLOCK)
        mask = (at < lengths[k // per_slot]).astype(jnp.float32)
        rounded[block_at(k), :] = (mask * block[block_at(k), :]).astype(jnp.bfloat16)
        block_store(k).start()

    for load, at in zip(token_loads, halves):
        load.wait()
        store(tokens.at[at], tokens_out.at[at])
    for i, target in ((0, g_gate), (1, g_up)):
        part_loads[i].wait()
        store(held.at[parts[i]], target)
    part_loads[3].wait()
    for g in range(3):
        store(held.at[cols(first + g * chans, chans)], g_in.at[g])
    per_col = width // chans
    for p in range(width // LANES):
        q, r = p // per_col, p % per_col
        at = (slice(r * chans, (r + 1) * chans), slice(out_first + q * LANES, out_first + (q + 1) * LANES))
        store(held.at[at], g_out.at[cols(p * LANES, LANES)])
        gains[cols(p * LANES, LANES)] = held[8 * p : 8 * p + 8, small_first:]
    own = pl.ds(pl.multiple_of(tp_at * chans, LANES), chans)
    g_conv[...] = gains[2:5, own]
    for copy in stores:
        copy.wait()

    @pl.loop(0, turns)
    def _(k):
        turn_store(k).wait()

    @pl.loop(0, blocks)
    def _(k):
        block_store(k).wait()


def finish(sums, tokens_grad, block_sum, lengths, chans, hidden):
    rows, width = block_sum.shape
    f32 = jnp.float32
    anywhere = pl.BlockSpec(memory_space=pl.ANY)
    whole = pl.BlockSpec(memory_space=pltpu.VMEM)
    blocks = rows // OUT_BLOCK
    return pl.pallas_call(
        functools.partial(finish_kernel, lengths.shape[0], chans, hidden),
        out_shape=[
            jax.ShapeDtypeStruct((rows, width), jnp.bfloat16),
            jax.ShapeDtypeStruct((rows, width), f32),
            jax.ShapeDtypeStruct((8, width), f32),
            jax.ShapeDtypeStruct((3, width, chans), f32),
            jax.ShapeDtypeStruct((3, chans), f32),
            jax.ShapeDtypeStruct((chans, width), f32),
            jax.ShapeDtypeStruct((width, hidden), f32),
            jax.ShapeDtypeStruct((width, hidden), f32),
            jax.ShapeDtypeStruct((hidden, width), f32),
        ],
        in_specs=[anywhere] * 3 + [pl.BlockSpec(memory_space=pltpu.SMEM)],
        out_specs=[anywhere] * 2 + [whole, anywhere, whole] + [anywhere] * 4,
        scratch_shapes=[
            pltpu.VMEM(sums.shape, f32),
            pltpu.VMEM((rows, width), f32),
            pltpu.VMEM((rows, width), f32),
            pltpu.VMEM((rows, width), jnp.bfloat16),
            pltpu.VMEM((hidden, width), f32),
            pltpu.SemaphoreType.DMA((6,)),
            pltpu.SemaphoreType.DMA((2, blocks)),
            pltpu.SemaphoreType.DMA((hidden // LANES,)),
            pltpu.SemaphoreType.DMA((7 + width // LANES,)),
        ],
        compiler_params=pltpu.CompilerParams(vmem_limit_bytes=VMEM_LIMIT),
        name="finish",
    )(sums, tokens_grad, block_sum, lengths)


def per_device(
    tokens, lengths, gain_mix, w_in, conv_weight, w_out, gain_ffn, w_gate, w_up, w_down, cotangent
):
    slot_count, local_len, width = tokens.shape
    chans = w_in.shape[2]
    half_slots = slot_count // 2
    row_count = slot_count * local_len

    token_rows = tokens.reshape(row_count, width)
    cot_rows = cotangent.reshape(row_count, width)
    gains = gain_mix.reshape(1, width), gain_ffn.reshape(1, width)
    w_in_all, w_out_all, taps, normed_mid, hidden_res, projected, gated_rows, normed_in, mixed = (
        mixer_front(w_in, w_out, conv_weight, *gains, lengths, token_rows, half_slots, 3)
    )
    mixer_cols = 4 * chans
    sum_cols = FFN_PANELS * LANES + mixer_cols + LANES
    sums, grad_tokens, block_sum = back_both(
        (
            normed_mid,
            cot_rows,
            w_gate,
            w_up,
            w_down,
            hidden_res,
            projected,
            gated_rows,
            normed_in,
            mixed,
            w_in_all,
            w_out_all,
            token_rows,
        ),
        (lengths, taps, *gains),
        half_slots,
        sum_cols,
        1,
    )[:3]
    block_out, grad_tokens, small, g_in, g_conv, g_out, g_gate, g_up, g_down = finish(
        sums, grad_tokens, block_sum, lengths, chans, w_gate.shape[1]
    )
    return (
        block_out.reshape(slot_count, local_len, width),
        grad_tokens.reshape(slot_count, local_len, width),
        small[0],
        g_in.transpose(1, 0, 2),
        g_conv,
        g_out,
        small[1],
        g_gate,
        g_up,
        g_down,
    )


def solution(mesh):
    rows, cols = P("tp", None), P(None, "tp")
    tokens, whole, stacked = P(None, "seq", None), P(), P(None, None, "tp")
    return jax.shard_map(
        per_device,
        mesh=mesh,
        in_specs=(
            tokens, whole, whole, stacked, cols, rows, whole, cols, cols, rows, tokens,
        ),
        out_specs=(
            tokens, tokens, whole, stacked, cols, rows, whole, cols, cols, rows,
        ),
        check_vma=False,
    )
```

```python
import functools

import jax
import jax.numpy as jnp
from jax import lax
from jax.experimental import pallas as pl
from jax.experimental.pallas import tpu as pltpu
from jax.sharding import PartitionSpec as P

NORM_EPS = 1e-05
LANES = 128
VMEM_LIMIT = 64 << 20
HALF = 128
SLOTS_IN_FLIGHT = 10


def rms_scale(values):
    return lax.rsqrt(jnp.mean(values * values, axis=-1, keepdims=True) + NORM_EPS)


def dot_rows(left, right):
    return lax.dot_general(
        left, right, (((0,), (0,)), ((), ())), preferred_element_type=jnp.float32
    )


def dot_cols(left, right):
    return lax.dot_general(
        left, right, (((1,), (1,)), ((), ())), preferred_element_type=jnp.float32
    )


def greet_seq(places, others=(), more=0):
    barrier = pltpu.get_barrier_semaphore()
    here = lax.axis_index("seq")
    place, side = here // 2, lax.rem(here, 2)

    def signal(device):
        pl.semaphore_signal(
            barrier, inc=1, device_id=device, device_id_type=pl.DeviceIdType.MESH
        )

    signal({"seq": here + 1 - 2 * side})
    for other in others:
        signal(other)
    pl.when(place > 0)(lambda: signal({"seq": here - 2}))
    pl.when(place < places - 1)(lambda: signal({"seq": here + 2}))
    ends = jnp.where(place > 0, 1, 0) + jnp.where(place < places - 1, 1, 0)
    pl.semaphore_wait(barrier, 1 + len(others) + ends + more)


class SeqSum:
    def __init__(self, places, own, out, scratch):
        self.places, self.own, self.out = places, own, out
        self.y_in, self.p_left, self.p_right, self.p_acc = scratch[0:4]
        self.q_left, self.q_right, self.q_acc, self.q_in = scratch[4:8]
        self.sems = scratch[8]
        here = lax.axis_index("seq")
        self.place, self.side = here // 2, here % 2

    def remote(self, src, dst, slot, send, recv, place, side):
        return pltpu.make_async_remote_copy(
            src_ref=src,
            dst_ref=dst,
            send_sem=self.sems.at[send, slot],
            recv_sem=self.sems.at[recv, slot],
            device_id={"seq": place * 2 + side},
            device_id_type=pl.DeviceIdType.MESH,
        )

    def chain(self, root):
        last = self.places - 1
        left = jnp.maximum(self.place - 1, 0)
        right = jnp.minimum(self.place + 1, last)
        from_left = (self.place <= root) & (self.place > 0)
        from_right = (self.place >= root) & (self.place < last)
        return left, right, from_left, from_right

    def own_base(self, k):
        held = self.own.shape[0] // (4 * HALF)
        return pl.multiple_of(lax.rem(k, held) * 4 * HALF, 4 * HALF)

    def out_at(self, k, first, size):
        per_panel = self.out.shape[0] // (4 * HALF)
        panel, part = place_in_sums(k, per_panel)
        row = part * 4 * HALF + first
        return self.out.at[
            pl.ds(pl.multiple_of(row, size), size), pl.ds(pl.multiple_of(panel * LANES, LANES), LANES)
        ]

    def p_stage(self, which, k):
        place, side = self.place, self.side
        own = self.own
        slot = lax.rem(k, SLOTS_IN_FLIGHT)
        base = self.own_base(k)
        mine = pl.ds(pl.multiple_of(base + side * HALF, HALF), HALF)
        theirs = pl.ds(pl.multiple_of(base + (1 - side) * HALF, HALF), HALF)
        out_mine = self.out_at(k, side * HALF, HALF)
        root = self.places // 2 - 1 + lax.rem(k, 2)
        left, right, from_left, from_right = self.chain(root)
        acc, y_in = self.p_acc.at[slot], self.y_in.at[slot]
        from_l, from_r = self.p_left.at[slot], self.p_right.at[slot]
        remote = functools.partial(functools.partial, self.remote)

        to_side = remote(own.at[theirs], y_in, slot, 0, 1, place, 1 - side)
        up_right = remote(acc, from_l, slot, 2, 3, right, side)
        up_left = remote(acc, from_r, slot, 2, 4, left, side)

        def down(src):
            return (
                remote(src, out_mine, slot, 5, 7, left, side),
                remote(src, out_mine, slot, 6, 7, right, side),
                remote(src, out_mine, slot, 8, 9, place, 1 - side),
            )

        def keep():
            return pltpu.make_async_copy(acc, out_mine, self.sems.at[10, slot])

        def hand_down(src):
            down_left, down_right, down_side = down(src)
            down_side().start()
            pl.when(from_left)(lambda: down_left().start())
            pl.when(from_right)(lambda: down_right().start())

        if which == "split":
            to_side().start()

        if which == "up":
            to_side().wait_recv()
            acc[...] = own[mine, :] + y_in[...]

            @pl.when(place < root)
            def _():
                @pl.when(from_left)
                def _():
                    up_right().wait_recv()
                    acc[...] += from_l[...]

                up_right().start()

            @pl.when(place > root)
            def _():
                @pl.when(from_right)
                def _():
                    up_left().wait_recv()
                    acc[...] += from_r[...]

                up_left().start()

        if which == "root":

            @pl.when(place == root)
            def _():
                @pl.when(from_left)
                def _():
                    up_right().wait_recv()
                    acc[...] += from_l[...]

                @pl.when(from_right)
                def _():
                    up_left().wait_recv()
                    acc[...] += from_r[...]

                hand_down(acc)
                keep().start()

        if which == "down":

            @pl.when(place != root)
            def _():
                down(acc)[0]().wait_recv()
                hand_down(out_mine)

        if which == "end":
            down_left, down_right, down_side = down(acc)
            down_side().wait()
            to_side().wait_send()
            pl.when(from_left)(lambda: down_left().wait_send())
            pl.when(from_right)(lambda: down_right().wait_send())
            pl.when(place == root)(lambda: keep().wait())
            pl.when(place != root)(lambda: up_left().wait_send())

    def q_stage(self, which, k):
        place, side = self.place, self.side
        own = self.own
        slot = lax.rem(k, SLOTS_IN_FLIGHT)
        base = self.own_base(k)
        wide = pl.ds(pl.multiple_of(base + 2 * HALF, 2 * HALF), 2 * HALF)
        out_wide = self.out_at(k, 2 * HALF, 2 * HALF)
        root = self.places // 2 - lax.rem(k, 2)
        left, right, from_left, from_right = self.chain(root)
        acc, side_in = self.q_acc.at[slot], self.q_in.at[slot]
        from_l, from_r = self.q_left.at[slot], self.q_right.at[slot]
        remote = functools.partial(functools.partial, self.remote)

        up_right = remote(acc, from_l, slot, 11, 12, right, side)
        up_left = remote(acc, from_r, slot, 11, 13, left, side)
        to_side = remote(acc, side_in, slot, 14, 15, place, 1 - side)

        def down(src):
            return (
                remote(src, out_wide, slot, 16, 18, left, side),
                remote(src, out_wide, slot, 17, 18, right, side),
            )

        def keep():
            return pltpu.make_async_copy(side_in, out_wide, self.sems.at[19, slot])

        def hand_down(src):
            down_left, down_right = down(src)
            pl.when(from_left)(lambda: down_left().start())
            pl.when(from_right)(lambda: down_right().start())

        if which == "up":
            acc[...] = own[wide, :]

            @pl.when(place < root)
            def _():
                @pl.when(from_left)
                def _():
                    up_right().wait_recv()
                    acc[...] += from_l[...]

                up_right().start()

            @pl.when(place > root)
            def _():
                @pl.when(from_right)
                def _():
                    up_left().wait_recv()
                    acc[...] += from_r[...]

                up_left().start()

        if which == "root":

            @pl.when(place == root)
            def _():
                @pl.when(from_left)
                def _():
                    up_right().wait_recv()
                    acc[...] += from_l[...]

                @pl.when(from_right)
                def _():
                    up_left().wait_recv()
                    acc[...] += from_r[...]

                to_side().start()

        if which == "side":

            @pl.when(place == root)
            def _():
                to_side().wait_recv()
                side_in[...] += acc[...]
                hand_down(side_in)
                keep().start()

        if which == "down":

            @pl.when(place != root)
            def _():
                down(acc)[0]().wait_recv()
                hand_down(out_wide)

        if which == "end":
            down_left, down_right = down(acc)
            pl.when(from_left)(lambda: down_left().wait_send())
            pl.when(from_right)(lambda: down_right().wait_send())

            @pl.when(place == root)
            def _():
                to_side().wait_send()
                keep().wait()

            pl.when(place != root)(lambda: up_left().wait_send())

    P_LAGS = (("split", 0, 0), ("up", 2, 1), ("root", 3, 3), ("down", 6, 7), ("end", 9, 9))
    Q_LAGS = (("up", 1, 0), ("root", 2, 2), ("side", 4, 4), ("down", 6, 7), ("end", 9, 9))

    def tick(self, t, count):
        middle = (self.place == self.places // 2) | (self.place == self.places // 2 - 1)
        for stage, lags in ((self.p_stage, self.P_LAGS), (self.q_stage, self.Q_LAGS)):
            for which, mid_lag, outer_lag in lags:
                k = t - jnp.where(middle, mid_lag, outer_lag)

                @pl.when((k >= 0) & (k < count))
                def _(stage=stage, which=which, k=k):
                    stage(which, k)

    def run(self, count):
        @pl.loop(0, count + self.P_LAGS[-1][1])
        def _(t):
            self.tick(t, count)


def seq_sum_scratch():
    half = pltpu.VMEM((SLOTS_IN_FLIGHT, HALF, LANES), jnp.float32)
    wide = pltpu.VMEM((SLOTS_IN_FLIGHT, 2 * HALF, LANES), jnp.float32)
    return [half] * 4 + [wide] * 4 + [pltpu.SemaphoreType.DMA((20, SLOTS_IN_FLIGHT))]


SUB_ROWS = 64
STRAIGHT_COPIES = 4
FIRST_MIXER_TICK = 36
BLOCK_TICK = 56
FFN_PANELS = 27
FFN_PARTS = 3
ROW_BLOCK = 256
ROW_TICK = 2
OUT_BLOCK = 256


def place_in_sums(piece, per_panel):
    per_part = FFN_PANELS // FFN_PARTS
    third = per_part // 3
    part, inside = piece // (per_part * per_panel), lax.rem(piece, per_part * per_panel)
    kind = lax.rem(inside, per_part)
    panel = kind // third * (FFN_PANELS // 3) + part * third + lax.rem(kind, third)
    of_ffn = piece < FFN_PANELS * per_panel
    return (
        jnp.where(of_ffn, panel, piece // per_panel),
        jnp.where(of_ffn, inside // per_part, lax.rem(piece, per_panel)),
    )


def norm_back(grad, gain, unit, scale):
    scaled = gain * grad
    return scale * (scaled - unit * jnp.mean(scaled * unit, axis=-1, keepdims=True))


def back_kernel(places, slots, *refs):
    (mid_hbm, cot_hbm, w_gate_hbm, w_up_hbm, w_d_hbm, hidden_hbm, proj_hbm) = refs[0:7]
    (gated_hbm, normed_hbm, mixed_hbm, w_in_hbm, w_out_hbm, tokens_hbm) = refs[7:13]
    (lengths, taps, gain_mix, gain_ffn) = refs[13:17]
    (sums, tokens_out, block_out, mid_chip, mid_far, ffn_chip, ffn_far) = refs[17:24]
    (mid_land, ffn_land, land_in, land_out, land_small) = refs[24:29]
    (mid, cot, w_gu, w_d, act, ggu, own, staged, fetched) = refs[29:38]
    (proj, gated, mixed_buf, conv_in, grad_hid, grad_tok) = refs[38:44]
    (halo_out, halo_in, halo_keep, small, small_in) = refs[44:49]
    load_sems, near_sems, far_sems, keep_sem, fetch_sem = refs[49:54]
    (later_sems, row_sems, halo_sems, weight_sems, out_sems) = refs[54:59]

    summer = SeqSum(places, own, sums, refs[59:])
    here = lax.axis_index("seq")
    last = 2 * places - 1
    tp_at = lax.axis_index("tp")
    core = lax.rem(tp_at, 2)
    sibling = tp_at + 1 - 2 * core
    across = lax.rem(tp_at + 2, 4)
    rows, width = mid.shape
    parts, _, wide = w_gu.shape
    half_rows = rows // 2
    chans = wide // 3
    hidden = wide // 2
    panels = 3 * hidden // LANES

    moves = [(mid_hbm, mid), (cot_hbm, cot), (w_d_hbm, w_d)]
    for c in range(parts):
        for i, source in enumerate((w_gate_hbm, w_up_hbm)):
            move = (
                source.at[:, c * hidden : (c + 1) * hidden],
                w_gu.at[c, :, i * hidden : (i + 1) * hidden],
            )
            moves.insert(i if c == 0 else len(moves), move)
    loads = [
        pltpu.make_async_copy(src, dst, load_sems.at[i]) for i, (src, dst) in enumerate(moves)
    ]
    for load in loads:
        load.start()

    barrier = pltpu.get_barrier_semaphore()

    def signal(device):
        pl.semaphore_signal(barrier, inc=1, device_id=device, device_id_type=pl.DeviceIdType.MESH)

    pl.when(here > 0)(lambda: signal({"seq": here - 1}))
    pl.when(here < last)(lambda: signal({"seq": here + 1}))
    ends = jnp.where(here > 0, 1, 0) + jnp.where(here < last, 1, 0)
    greet_seq(places, ({"tp": sibling}, {"tp": across}), ends)
    ffn_pieces = own.shape[0] // (4 * HALF)
    mixer_pieces = 4 * chans * width // LANES // (4 * HALF) + 1
    count = ffn_pieces + mixer_pieces
    for load in loads[:5]:
        load.wait()

    slot_len = rows // 2 // slots

    def valid_rows(slot, first, size):
        at = lax.broadcasted_iota(jnp.int32, (size, 1), 0) + (here * slot_len + first)
        return (at < lengths[slot]).astype(jnp.float32)

    row_ticks = rows // ROW_BLOCK // ROW_TICK
    grad_ticks = width // OUT_BLOCK
    first_ticks = grad_ticks - 4 * HALF // OUT_BLOCK
    blocks = rows // 2 // OUT_BLOCK
    before_mid = first_ticks + (parts - 1) * row_ticks
    after_mid = before_mid + blocks
    before_ffn = after_mid + (parts - 1) * grad_ticks

    def part_cols(c):
        return pl.ds(pl.multiple_of(c * hidden, LANES), hidden)

    def row_phase(c):
        for i in range(1, parts):

            @pl.when(jnp.int32(c) == i)
            def _(i=i):
                loads[3 + 2 * i].wait()
                loads[4 + 2 * i].wait()

        @pl.loop(0, rows // ROW_BLOCK)
        def _(r):
            at = pl.ds(pl.multiple_of(r * ROW_BLOCK, ROW_BLOCK), ROW_BLOCK)

            @pl.when(jnp.int32(c) == 0)
            def _():
                per_slot = slot_len // ROW_BLOCK
                mask = valid_rows(r // per_slot, lax.rem(r, per_slot) * ROW_BLOCK, ROW_BLOCK)
                cot[at, :] = (mask * cot[at, :].astype(jnp.float32)).astype(jnp.bfloat16)

            both = jnp.dot(mid[at, :], w_gu[c], preferred_element_type=jnp.float32)
            gate, up = both[:, :hidden], both[:, hidden:]
            grad_act = dot_cols(cot[at, :], w_d[part_cols(c), :])
            sigmoid = 1.0 / (1.0 + jnp.exp(-gate))
            silu = gate * sigmoid
            act[at, part_cols(c)] = (silu * up).astype(jnp.bfloat16)
            slope = sigmoid * (1.0 + gate * (1.0 - sigmoid))
            ggu[c, at, :hidden] = (grad_act * up * slope).astype(jnp.bfloat16)
            ggu[c, at, hidden:] = (grad_act * silu).astype(jnp.bfloat16)

            @pl.when((jnp.int32(c) > 0) & (lax.rem(r, ROW_TICK) == ROW_TICK - 1))
            def _():
                summer.tick(first_ticks + (c - 1) * row_ticks + r // ROW_TICK, count)

    def grad_phase(c):
        @pl.loop(0, width // OUT_BLOCK)
        def _(m):
            first = pl.multiple_of(m * OUT_BLOCK, OUT_BLOCK)
            at = pl.ds(first, OUT_BLOCK)
            per_piece = 4 * HALF // OUT_BLOCK
            piece = (c * (width // OUT_BLOCK // per_piece) + m // per_piece) * panels
            base = piece * 4 * HALF + lax.rem(m, per_piece) * OUT_BLOCK

            def put(block, panel):
                for j in range(block.shape[1] // LANES):
                    to = pl.multiple_of(base + (panel + j) * 4 * HALF, OUT_BLOCK)
                    own[pl.ds(to, OUT_BLOCK), :] = block[:, j * LANES : (j + 1) * LANES]

            put(dot_rows(mid[:, at], ggu[c]), 0)
            put(dot_rows(cot[:, at], act[:, part_cols(c)]), wide // LANES)

            step = jnp.where(jnp.int32(c) > 0, after_mid + (c - 1) * grad_ticks + m, m - grad_ticks + first_ticks)

            @pl.when(step >= 0)
            def _():
                summer.tick(step, count)

    def row_block(half, k):
        return pl.ds(pl.multiple_of((half * blocks + k) * OUT_BLOCK, OUT_BLOCK), OUT_BLOCK)

    def mid_part(at):
        return sum(dot_cols(ggu[c, at, :], w_gu[c]) for c in range(parts))

    def ffn_part(at):
        return sum(
            jnp.dot(
                act[at, c * hidden : (c + 1) * hidden],
                w_d[c * hidden : (c + 1) * hidden, :],
                preferred_element_type=jnp.float32,
            )
            for c in range(parts)
        )

    def near(which, land, k):
        return pltpu.make_async_remote_copy(
            src_ref=staged.at[lax.rem(k, 2)],
            dst_ref=land.at[row_block(0, k)],
            send_sem=near_sems.at[which, 0, k],
            recv_sem=near_sems.at[which, 1, k],
            device_id={"tp": sibling},
            device_id_type=pl.DeviceIdType.MESH,
        )

    def far(which, chip, there, k):
        return pltpu.make_async_remote_copy(
            src_ref=chip.at[row_block(0, k)],
            dst_ref=there.at[row_block(0, k)],
            send_sem=far_sems.at[which, 0, k],
            recv_sem=far_sems.at[which, 1, k],
            device_id={"tp": across},
            device_id_type=pl.DeviceIdType.MESH,
        )

    def ffn_across(k):
        return far(1, ffn_chip, ffn_far, k)

    def tp_sum(which, part, land, chip, first_tick):
        @pl.loop(0, blocks)
        def _(k):
            @pl.when(k >= 2)
            def _():
                near(which, land, k - 2).wait_send()

            staged[lax.rem(k, 2)] = part(row_block(1 - core, k))
            near(which, land, k).start()

        for k in range(max(blocks - 2, 0), blocks):
            near(which, land, k).wait_send()

        @pl.loop(0, blocks)
        def _(k):
            near(which, land, k).wait_recv()
            fetch = pltpu.make_async_copy(land.at[row_block(0, k)], fetched, fetch_sem)
            fetch.start()
            staged[0] = part(row_block(core, k))
            fetch.wait()
            staged[0] += fetched[...]
            keep = pltpu.make_async_copy(staged.at[0], chip.at[row_block(0, k)], keep_sem)
            keep.start()
            summer.tick(first_tick + k, count)
            keep.wait()
            if which == 0:
                far(0, mid_chip, mid_far, k).start()

    row_phase(0)
    grad_phase(0)
    pl.loop(1, parts)(row_phase)
    tp_sum(0, mid_part, mid_land, mid_chip, before_mid)
    pl.loop(1, parts)(grad_phase)
    tp_sum(1, ffn_part, ffn_land, ffn_chip, before_ffn)

    own_half = pl.ds(pl.multiple_of(core * half_rows, half_rows), half_rows)
    low_half, high_half = pl.ds(0, half_rows), pl.ds(half_rows, half_rows)
    w_out, grad_mixer = mid.at[low_half], mid.at[high_half]
    normed, mixed = act.at[low_half, pl.ds(0, width)], act.at[high_half, pl.ds(0, width)]
    tokens = w_d.at[low_half]
    w_in = (ggu.at[2, low_half], ggu.at[2, high_half], w_gu.at[0], w_gu.at[1])
    moves = [
        (w_out_hbm, w_out),
        (tokens_hbm.at[own_half], tokens),
        (normed_hbm, normed),
        (mixed_hbm, mixed),
    ]
    for j in range(4):
        for g in range(3):
            first = g * width + j * chans
            moves.append(
                (w_in_hbm.at[:, first : first + chans], w_in[j].at[:, g * chans : (g + 1) * chans])
            )
    loads = [
        pltpu.make_async_copy(src, dst, later_sems.at[i]) for i, (src, dst) in enumerate(moves)
    ]
    for load in loads:
        load.start()
    chip, far_rows, hidden_rows = staged.at[0], staged.at[1], fetched
    per_slot = slot_len // OUT_BLOCK
    small[...] = jnp.zeros_like(small)
    ticked = before_ffn + blocks

    @pl.loop(ticked, FIRST_MIXER_TICK)
    def _(t):
        summer.tick(t, count)

    @pl.loop(0, blocks)
    def _(k):
        far(0, mid_chip, mid_far, k).wait()
        ffn_across(k).start()

    for load in loads:
        load.wait()

    def shard_rows(shard, first, size):
        at = lax.rem(shard, 2) * half_rows + first
        return shard // 2, pl.ds(pl.multiple_of(at, size), size)

    def place_of(n):
        slot = n // per_slot
        block = per_slot - 1 - lax.rem(n, per_slot)
        return slot, block, pl.multiple_of(slot * slot_len + block * OUT_BLOCK, OUT_BLOCK)

    def mid_loads(first):
        at = pl.ds(first, OUT_BLOCK)
        return [
            pltpu.make_async_copy(src.at[at], dst, row_sems.at[i])
            for i, (src, dst) in enumerate(((mid_chip, chip), (mid_far, far_rows), (hidden_hbm, hidden_rows)))
        ]

    def proj_loads(slot, block, first):
        return [
            pltpu.make_async_copy(proj_hbm.at[pl.ds(first, OUT_BLOCK)], proj, row_sems.at[3]),
            pltpu.make_async_copy(
                gated_hbm.at[slot, pl.ds(pl.multiple_of(block * OUT_BLOCK, 8), OUT_BLOCK + 8)],
                gated,
                row_sems.at[4],
            ),
        ]

    def start(copies):
        for copy in copies:
            copy.start()

    def wait(copies):
        for copy in copies:
            copy.wait()

    def remote(src, dst, sems, i, device):
        return pltpu.make_async_remote_copy(
            src_ref=src,
            dst_ref=dst,
            send_sem=sems.at[0, i],
            recv_sem=sems.at[1, i],
            device_id=device,
            device_id_type=pl.DeviceIdType.MESH,
        )

    def block_at(k):
        return pl.ds(pl.multiple_of(k * OUT_BLOCK, OUT_BLOCK), OUT_BLOCK)

    def own_rows(first, size):
        return pl.ds(pl.multiple_of(core * half_rows + first, size), size)

    def hidden_grad(chip_part, far_part, hidden_part, cot_part):
        grad_mid = chip_part + far_part
        scale = rms_scale(hidden_part)
        unit = hidden_part * scale
        grad = cot_part.astype(jnp.float32) + norm_back(grad_mid, gain_ffn[...], unit, scale)
        return grad, grad_mid * unit

    def halo_copy(slot, device):
        return remote(halo_out.at[slot], halo_in.at[slot], halo_sems, slot, {"seq": device})

    head = 16
    for slot in range(slots):
        at = pl.ds(slot * slot_len, head)
        top = pl.ds(0, head)
        copies = [
            pltpu.make_async_copy(src.at[at], dst, row_sems.at[i])
            for i, (src, dst) in enumerate(
                (
                    (mid_chip, chip.at[top]),
                    (mid_far, far_rows.at[top]),
                    (hidden_hbm, hidden_rows.at[top]),
                    (proj_hbm, proj.at[top]),
                )
            )
        ]
        start(copies)
        wait(copies)
        grad, _ = hidden_grad(
            chip[top, :], far_rows[top, :], hidden_rows[top, :], cot[own_rows(slot * slot_len, head), :]
        )
        grad_mixed = dot_cols(grad.astype(jnp.bfloat16), w_out[...])
        halo_out[slot] = (grad_mixed * proj[top, width : 2 * width])[:8]
        pl.when(here > 0)(lambda slot=slot: halo_copy(slot, here - 1).start())

    slot, block, first = place_of(0)
    start(mid_loads(first))
    start(proj_loads(slot, block, first))

    @pl.when(here == last)
    def _():
        halo_in[...] = jnp.zeros_like(halo_in)

    @pl.when(here < last)
    def _():
        for slot in range(slots):
            halo_copy(slot, here + 1).wait_recv()

    def out_rows(first):
        return own_rows(first, OUT_BLOCK)

    def hand_out(target, first, i):
        at = out_rows(first)
        return (
            pltpu.make_async_copy(grad_tok, target.at[at], out_sems.at[0, 2 * blocks]),
            remote(grad_tok, target.at[at], out_sems, i, {"tp": sibling}),
        )

    @pl.loop(0, blocks)
    def _(n):
        slot, block, first = place_of(n)
        at = pl.ds(first, OUT_BLOCK)
        wait(mid_loads(first))

        @pl.loop(0, OUT_BLOCK // SUB_ROWS)
        def _(r):
            sub = pl.ds(pl.multiple_of(r * SUB_ROWS, SUB_ROWS), SUB_ROWS)
            whole = pl.ds(pl.multiple_of(first + r * SUB_ROWS, SUB_ROWS), SUB_ROWS)
            grad, for_gain = hidden_grad(
                chip[sub, :],
                far_rows[sub, :],
                hidden_rows[sub, :],
                cot[own_rows(first + r * SUB_ROWS, SUB_ROWS), :],
            )
            grad_hid[sub, :] = grad
            grad_mixer[whole, :] = grad.astype(jnp.bfloat16)
            small[1:2, :] += jnp.sum(for_gain, axis=0, keepdims=True)

        @pl.when(n < blocks - 1)
        def _():
            start(mid_loads(place_of(n + 1)[2]))

        mixed_buf[...] = dot_cols(grad_mixer[at, :], w_out[...])
        wait(proj_loads(slot, block, first))

        @pl.when(block == per_slot - 1)
        def _():
            conv_in[pl.ds(OUT_BLOCK, 8), :] = halo_in[slot]

        @pl.when(block < per_slot - 1)
        def _():
            conv_in[pl.ds(OUT_BLOCK, 8), :] = halo_keep[...]

        summer.tick(FIRST_MIXER_TICK + 2 * n, count)
        mask = valid_rows(core * slots + slot, block * OUT_BLOCK, OUT_BLOCK)

        @pl.loop(0, width // chans)
        def _(c):
            def cols(gate):
                return pl.ds(pl.multiple_of(gate * width + c * chans, chans), chans)

            here_cols = cols(0)
            pair, shard_at = shard_rows(c, first, OUT_BLOCK)
            in_gate, out_gate, conv_value = (proj[:, cols(g)] for g in range(3))
            grad_mixed = mixed_buf[:, here_cols]
            now = grad_mixed * out_gate
            conv_in[pl.ds(0, OUT_BLOCK), here_cols] = now
            seen = [gated[pl.ds(6 + j, OUT_BLOCK), here_cols] for j in range(3)]
            tap = [taps[j : j + 1, here_cols] for j in range(3)]
            conv_sum = tap[0] * seen[0] + tap[1] * seen[1] + tap[2] * seen[2]
            for j in range(3):
                small[2 + j : 3 + j, here_cols] += jnp.sum(now * seen[j], axis=0, keepdims=True)
            ggu[pair, shard_at, chans : 2 * chans] = (grad_mixed * conv_sum).astype(jnp.bfloat16)
            grad_gated = mask * (
                tap[2] * now
                + tap[1] * conv_in[pl.ds(1, OUT_BLOCK), here_cols]
                + tap[0] * conv_in[pl.ds(2, OUT_BLOCK), here_cols]
            )
            ggu[pair, shard_at, :chans] = (grad_gated * conv_value).astype(jnp.bfloat16)
            ggu[pair, shard_at, 2 * chans : 3 * chans] = (grad_gated * in_gate).astype(jnp.bfloat16)

        halo_keep[...] = conv_in[pl.ds(0, 8), :]

        @pl.when(n < blocks - 1)
        def _():
            start(proj_loads(*place_of(n + 1)))

        def shard_grad(j):
            pair, shard_at = shard_rows(j, first, OUT_BLOCK)
            return dot_cols(ggu[pair, shard_at, :], w_in[j][...])

        mixed_buf[...] = sum(shard_grad(j) for j in range(4))

        @pl.when(n > 0)
        def _():
            local, there = hand_out(tokens_out, place_of(n - 1)[2], n - 1)
            local.wait()
            there.wait_send()

        @pl.loop(0, OUT_BLOCK // SUB_ROWS)
        def _(r):
            sub = pl.ds(pl.multiple_of(r * SUB_ROWS, SUB_ROWS), SUB_ROWS)
            whole = pl.ds(pl.multiple_of(first + r * SUB_ROWS, SUB_ROWS), SUB_ROWS)
            inputs = tokens[whole, :].astype(jnp.float32)
            scale = rms_scale(inputs)
            unit = inputs * scale
            grad_in = mixed_buf[sub, :]
            grad_tok[sub, :] = grad_hid[sub, :] + norm_back(grad_in, gain_mix[...], unit, scale)
            small[0:1, :] += jnp.sum(grad_in * unit, axis=0, keepdims=True)

        start(hand_out(tokens_out, first, n))
        summer.tick(FIRST_MIXER_TICK + 2 * n + 1, count)

    in_blocks = width // OUT_BLOCK
    stages = [proj.at[:, i * wide : (i + 1) * wide] for i in range(3)]

    def to_near(src, dst, i):
        return remote(src, dst, weight_sems, i, {"tp": sibling})

    def near_in(m):
        cols = pl.ds(pl.multiple_of(lax.rem(m, 2) * wide, LANES), wide)
        return to_near(proj.at[:, cols], land_in.at[m], m)

    near_out = to_near(grad_hid, land_out, in_blocks)
    near_small = to_near(small, land_small, in_blocks + 1)

    def in_part(m, shard):
        pair, shard_at = shard_rows(shard, 0, half_rows)
        return dot_rows(normed[:, block_at(m)], ggu[pair, shard_at, :])

    def out_part(shard):
        at = pl.ds(pl.multiple_of(shard * chans, LANES), chans)
        return dot_rows(mixed[:, at], grad_mixer[...])

    near_small.start()
    first_tick = FIRST_MIXER_TICK + 2 * blocks

    @pl.loop(0, in_blocks)
    def _(m):
        @pl.when(m >= 2)
        def _():
            near_in(m - 2).wait_send()

        cols = pl.ds(pl.multiple_of(lax.rem(m, 2) * wide, LANES), wide)
        proj[:, cols] = in_part(m, sibling)
        near_in(m).start()
        summer.tick(first_tick + m, count)

    grad_hid[...] = out_part(sibling)
    near_out.start()

    @pl.loop(0, in_blocks)
    def _(m):
        near_in(m).wait_recv()
        fetch = pltpu.make_async_copy(land_in.at[m], stages[2], row_sems.at[0])
        fetch.start()
        part = in_part(m, tp_at)
        fetch.wait()
        for i in range(wide // LANES):
            to = pl.multiple_of(i * width + m * OUT_BLOCK, OUT_BLOCK)
            own[pl.ds(to, OUT_BLOCK), :] = (
                part[:, i * LANES : (i + 1) * LANES]
                + proj[:, 2 * wide + i * LANES : 2 * wide + (i + 1) * LANES]
            )

        summer.tick(first_tick + in_blocks + m, count)

    near_out.wait_recv()
    near_small.wait_recv()
    fetches = [
        pltpu.make_async_copy(land_out, mixed_buf, row_sems.at[0]),
        pltpu.make_async_copy(land_small, small_in, row_sems.at[1]),
    ]
    start(fetches)
    part = out_part(tp_at)
    wait(fetches)
    out_first = wide // LANES * width
    small_first = out_first + width // LANES * chans
    for p in range(width // LANES):
        cols = slice(p * LANES, (p + 1) * LANES)
        own[pl.ds(out_first + p * chans, chans), :] = part[:, cols] + mixed_buf[:, cols]
        own[pl.ds(small_first + 8 * p, 8), :] = small[:, cols] + small_in[:, cols]
    unused = 4 * HALF - 8 * (width // LANES)
    own[pl.ds(small_first + 4 * HALF - unused, unused), :] = jnp.zeros((unused, LANES), jnp.float32)

    local, there = hand_out(tokens_out, place_of(blocks - 1)[2], blocks - 1)
    local.wait()
    there.wait_send()
    done = first_tick + 2 * in_blocks
    pause = BLOCK_TICK

    @pl.loop(done, pause)
    def _(t):
        summer.tick(t, count)

    @pl.loop(0, blocks)
    def _(k):
        ffn_across(k).wait_recv()
        at = block_at(k)
        copies = [
            pltpu.make_async_copy(src.at[at], dst, row_sems.at[i])
            for i, (src, dst) in enumerate(((ffn_chip, chip), (ffn_far, far_rows), (hidden_hbm, hidden_rows)))
        ]
        start(copies)

        @pl.when(k > 0)
        def _():
            local, there = hand_out(block_out, (k - 1) * OUT_BLOCK, blocks + k - 1)
            local.wait()
            there.wait_send()

        wait(copies)
        grad_tok[...] = hidden_rows[...] + (chip[...] + far_rows[...])
        start(hand_out(block_out, k * OUT_BLOCK, blocks + k))
        summer.tick(pause + k, count)

    @pl.loop(pause + blocks, count + summer.P_LAGS[-1][1])
    def _(t):
        summer.tick(t, count)

    local, there = hand_out(block_out, (blocks - 1) * OUT_BLOCK, 2 * blocks - 1)
    local.wait()
    there.wait_send()

    @pl.loop(0, blocks)
    def _(k):
        ffn_across(k).wait_send()
        hand_out(tokens_out, place_of(k)[2], k)[1].wait_recv()
        hand_out(block_out, k * OUT_BLOCK, blocks + k)[1].wait_recv()

    for m in range(max(in_blocks - 2, 0), in_blocks):
        near_in(m).wait_send()
    near_out.wait_send()
    near_small.wait_send()

    @pl.when(here > 0)
    def _():
        for slot in range(slots):
            halo_copy(slot, here - 1).wait_send()


def back_both(hbm, vmem, slots, sum_cols, collective_id):
    normed_mid, _, w_gate, _, w_d, _, _, gated, _, _, _, _, _ = hbm
    rows, width = normed_mid.shape
    half_rows = rows // 2
    local = w_gate.shape[1]
    hidden = local // FFN_PARTS
    chans = 2 * hidden // 3
    blocks = half_rows // OUT_BLOCK
    in_blocks = width // OUT_BLOCK
    f32, low = jnp.float32, jnp.bfloat16
    half = jax.ShapeDtypeStruct((half_rows, width), f32)
    full = jax.ShapeDtypeStruct((rows, width), f32)
    block = pltpu.VMEM((OUT_BLOCK, width), f32)
    row8 = pltpu.VMEM((8, width), f32)
    anywhere = pl.BlockSpec(memory_space=pl.ANY)
    return pl.pallas_call(
        functools.partial(back_kernel, lax.axis_size("seq") // 2, slots),
        out_shape=[jax.ShapeDtypeStruct((width, sum_cols), f32)]
        + [full] * 2
        + [half] * 6
        + [
            jax.ShapeDtypeStruct((in_blocks, OUT_BLOCK, 2 * hidden), f32),
            jax.ShapeDtypeStruct((chans, width), f32),
            jax.ShapeDtypeStruct((8, width), f32),
        ],
        in_specs=[anywhere] * len(hbm)
        + [pl.BlockSpec(memory_space=pltpu.SMEM)]
        + [pl.BlockSpec(memory_space=pltpu.VMEM)] * (len(vmem) - 1),
        out_specs=[anywhere] * 12,
        scratch_shapes=[
            pltpu.VMEM((rows, width), low),
            pltpu.VMEM((rows, width), low),
            pltpu.VMEM((FFN_PARTS, width, 2 * hidden), low),
            pltpu.VMEM(w_d.shape, low),
            pltpu.VMEM((rows, local), low),
            pltpu.VMEM((FFN_PARTS, rows, 2 * hidden), low),
            pltpu.VMEM((3 * local * width // LANES, LANES), f32),
            pltpu.VMEM((2, OUT_BLOCK, width), f32),
            block,
            pltpu.VMEM((OUT_BLOCK, 3 * width), f32),
            pltpu.VMEM((OUT_BLOCK + 8, width), f32),
            block,
            pltpu.VMEM((OUT_BLOCK + 8, width), f32),
            block,
            block,
            pltpu.VMEM((slots, 8, width), f32),
            pltpu.VMEM((slots, 8, width), f32),
            row8,
            row8,
            row8,
            pltpu.SemaphoreType.DMA((3 + 2 * FFN_PARTS,)),
            pltpu.SemaphoreType.DMA((2, 2, blocks)),
            pltpu.SemaphoreType.DMA((2, 2, blocks)),
            pltpu.SemaphoreType.DMA,
            pltpu.SemaphoreType.DMA,
            pltpu.SemaphoreType.DMA((16,)),
            pltpu.SemaphoreType.DMA((5,)),
            pltpu.SemaphoreType.DMA((2, slots)),
            pltpu.SemaphoreType.DMA((2, in_blocks + 2)),
            pltpu.SemaphoreType.DMA((2, 2 * blocks + 1)),
        ]
        + seq_sum_scratch(),
        compiler_params=pltpu.CompilerParams(
            collective_id=collective_id, has_side_effects=True, vmem_limit_bytes=VMEM_LIMIT
        ),
        cost_estimate=pl.CostEstimate(
            flops=18 * rows * width * local, bytes_accessed=800 << 20, transcendentals=0
        ),
        name="back_both",
    )(*hbm, *vmem)


def front_kernel(places, slots, *refs):
    (w_in, w_out, taps, gain_mix, gain_ffn, lengths, tokens_hbm) = refs[0:7]
    (in_hbm, out_hbm, full_taps, mid_hbm, hidden_hbm, proj_hbm, gated_hbm) = refs[7:14]
    (normed_hbm, mixed_hbm) = refs[14:16]
    own_in, own_out, far_in, far_out, sib_in, sib_out, sibfar_in, sibfar_out = refs[16:24]
    own_taps, far_taps, sib_taps, sibfar_taps, share_in, share_out = refs[24:30]
    (full_in, full_out, tokens, normed, mixed, out_gate, gates, gated) = refs[30:38]
    (unit_out, unit_in, hidden) = refs[38:41]
    sends, recvs, once, halo_sems, gate_sems, unit_sems, keep_sems, mid_sems = refs[41:49]
    straight_sems = refs[49]
    here = lax.axis_index("seq")
    place, side = here // 2, lax.rem(here, 2)
    last = places - 1
    end = 2 * places - 1
    tp_at = lax.axis_index("tp")
    core = lax.rem(tp_at, 2)
    sibling = tp_at + 1 - 2 * core
    across = lax.rem(tp_at + 2, 4)
    far_sibling = sibling + across - tp_at
    straight = w_in.shape[1] // 2
    in_rows = (w_in.shape[1] - straight) // (2 * places)
    out_rows = w_out.shape[0] // (2 * places)
    chans = w_in.shape[2]
    rows, width = tokens.shape
    slot_len = rows // slots
    low = jnp.bfloat16

    load_tokens = pltpu.make_async_copy(
        tokens_hbm.at[pl.ds(pl.multiple_of(core * rows, rows), rows)], tokens, keep_sems.at[0]
    )
    load_tokens.start()
    barrier = pltpu.get_barrier_semaphore()

    def signal(device):
        pl.semaphore_signal(barrier, inc=1, device_id=device, device_id_type=pl.DeviceIdType.MESH)

    pl.when(here > 0)(lambda: signal({"seq": here - 1}))
    pl.when(here < end)(lambda: signal({"seq": here + 1}))
    ends = jnp.where(here > 0, 1, 0) + jnp.where(here < end, 1, 0)
    greet_seq(places, ({"tp": sibling}, {"tp": across}), ends)

    def shares(j):
        return (
            pl.ds(pl.multiple_of(j * in_rows, in_rows), in_rows),
            pl.ds(pl.multiple_of(j * out_rows, out_rows), out_rows),
        )

    def remote(src, dst, send, recv, device):
        return pltpu.make_async_remote_copy(
            src_ref=src,
            dst_ref=dst,
            send_sem=send,
            recv_sem=recv,
            device_id=device,
            device_id_type=pl.DeviceIdType.MESH,
        )

    def copies(source, target, j, kind, device):
        for i, at in enumerate(shares(j)):
            yield remote(
                source[i] if kind == 0 else source[i].at[at],
                target[i].at[at],
                sends.at[kind, i, j],
                recvs.at[0 if kind < 4 else 1, i, j],
                device,
            )

    share, far, sibfar = (share_in, share_out), (far_in, far_out), (sibfar_in, sibfar_out)

    def across_share():
        return copies(share, far, here, 0, {"tp": across})

    def to_right(j):
        return copies(far, far, j, 1, {"seq": here + 2})

    def to_left(j):
        return copies(far, far, j, 2, {"seq": here - 2})

    def to_side(j):
        return copies(far, far, j, 3, {"seq": here + 1 - 2 * side})

    def to_sibling(j):
        return copies(far, sibfar, j, 4, {"tp": sibling})

    def straight_rows(q):
        size = straight // STRAIGHT_COPIES
        first = w_in.shape[1] - straight + q * size
        return pl.ds(pl.multiple_of(first, size), size)

    def straight_across(q):
        at = straight_rows(q)
        return remote(
            own_in.at[at], far_in.at[at], straight_sems.at[0, q], straight_sems.at[1, q],
            {"tp": across},
        )

    def straight_sibling(q):
        at = straight_rows(q)
        return remote(
            far_in.at[at], sibfar_in.at[at], straight_sems.at[2, q], straight_sems.at[3, q],
            {"tp": sibling},
        )

    def pass_straight(q):
        straight_across(q).wait_recv()
        straight_sibling(q).start()

    def start(group):
        for copy in group:
            copy.start()

    def arrived(group):
        for copy in group:
            copy.wait_recv()

    def left_source(group):
        for copy in group:
            copy.wait_send()

    def single(i, src, dst, device):
        return remote(src, dst, once.at[0, i], once.at[1, i], device)

    in_at, out_at = shares(here)
    for g in range(3):
        share_in[:, g * chans : (g + 1) * chans] = w_in[g, in_at, :].astype(jnp.float32)
    share_out[...] = w_out[out_at, :].astype(jnp.float32)
    start(across_share())
    own_taps[...] = taps[...]
    taps_far = single(0, own_taps, far_taps, {"tp": across})
    taps_sib = single(1, own_taps, sib_taps, {"tp": sibling})
    taps_sibfar = single(2, far_taps, sibfar_taps, {"tp": sibling})
    for g in range(3):
        own_in[:, g * chans : (g + 1) * chans] = w_in[g].astype(jnp.float32)
    own_out[...] = w_out[...].astype(jnp.float32)
    in_sib = single(3, own_in, sib_in, {"tp": sibling})
    out_sib = single(4, own_out, sib_out, {"tp": sibling})
    for copy in (taps_far, taps_sib, in_sib, out_sib):
        copy.start()
    for q in range(STRAIGHT_COPIES):
        straight_across(q).start()

    def gate_cols(g, index):
        return pl.ds(pl.multiple_of(g * width + index * chans, LANES), chans)

    def place_shard(shard_in, shard_out, shard_taps, index):
        for g in range(3):
            full_in[:, gate_cols(g, index)] = shard_in[:, g * chans : (g + 1) * chans].astype(low)
        at = pl.ds(pl.multiple_of(index * chans, chans), chans)
        full_out[at, :] = shard_out[...].astype(low)
        full_taps[:, gate_cols(0, index)] = shard_taps[...]

    def gate_out(turn, index, g):
        if g == 1:
            return pltpu.make_async_copy(
                out_gate.at[:, gate_cols(0, index)],
                proj_hbm.at[:, gate_cols(1, index)],
                gate_sems.at[turn, 1],
            )
        return pltpu.make_async_copy(
            gates.at[turn % 2, g // 2], proj_hbm.at[:, gate_cols(g, index)], gate_sems.at[turn, g]
        )

    def halo(turn, index, slot):
        return remote(
            gated.at[slot, pl.ds(slot_len, 8), gate_cols(0, index)],
            gated.at[slot, pl.ds(0, 8), gate_cols(0, index)],
            halo_sems.at[0, turn, slot],
            halo_sems.at[1, turn, slot],
            {"seq": here + 1},
        )

    order = (tp_at, sibling, across, far_sibling)

    def project(turn):
        index = order[turn]
        cols = gate_cols(0, index)
        if turn >= 2:
            gate_out(turn - 2, order[turn - 2], 0).wait()
            gate_out(turn - 2, order[turn - 2], 2).wait()

        @pl.loop(0, slots)
        def _(s):
            at = pl.ds(pl.multiple_of(s * slot_len, slot_len), slot_len)

            def gate(g):
                return jnp.dot(
                    normed[at, :], full_in[:, gate_cols(g, index)],
                    preferred_element_type=jnp.float32,
                )

            at_pos = lax.broadcasted_iota(jnp.int32, (slot_len, 1), 0) + here * slot_len
            mask = (at_pos < lengths[core * slots + s]).astype(jnp.float32)
            in_gate, value = gate(0), gate(2)
            gates[turn % 2, 0, at, :] = in_gate
            gates[turn % 2, 1, at, :] = value
            gated[s, pl.ds(8, slot_len), cols] = mask * in_gate * value
            out_gate[at, cols] = gate(1)

        for g in range(3):
            gate_out(turn, index, g).start()

        @pl.when(here < end)
        def _():
            for slot in range(slots):
                halo(turn, index, slot).start()

    def convolve(turn):
        index = order[turn]
        cols = gate_cols(0, index)

        @pl.when(here > 0)
        def _():
            for slot in range(slots):
                halo(turn, index, slot).wait_recv()

        @pl.loop(0, slots)
        def _(s):
            at = pl.ds(pl.multiple_of(s * slot_len, slot_len), slot_len)
            seen = [gated[s, pl.ds(6 + j, slot_len), cols] for j in range(3)]
            tap = [full_taps[j : j + 1, cols] for j in range(3)]
            conv_sum = tap[0] * seen[0] + tap[1] * seen[1] + tap[2] * seen[2]
            mixed[at, cols] = (out_gate[at, cols] * conv_sum).astype(low)

    @pl.when(here == 0)
    def _():
        for slot in range(slots):
            gated[slot, pl.ds(0, 8), :] = jnp.zeros((8, width), jnp.float32)

    load_tokens.wait()

    @pl.loop(0, rows // SUB_ROWS)
    def _(r):
        at = pl.ds(pl.multiple_of(r * SUB_ROWS, SUB_ROWS), SUB_ROWS)
        inputs = tokens[at, :].astype(jnp.float32)
        normed[at, :] = (gain_mix[...] * (inputs * rms_scale(inputs))).astype(low)

    keep_normed = pltpu.make_async_copy(normed, normed_hbm, keep_sems.at[0])
    keep_normed.start()
    place_shard(own_in, own_out, own_taps, tp_at)
    project(0)

    arrived(across_share())
    pl.when(place < last)(lambda: start(to_right(here)))
    pl.when(place > 0)(lambda: start(to_left(here)))
    start(to_side(here))
    start(to_sibling(here))
    taps_far.wait_recv()
    taps_sibfar.start()
    in_sib.wait_recv()
    out_sib.wait_recv()
    taps_sib.wait_recv()
    place_shard(sib_in, sib_out, sib_taps, sibling)
    project(1)

    def from_side(q):
        j = 2 * q + 1 - side
        arrived(to_side(j))
        start(to_sibling(j))

    @pl.loop(1, places)
    def _(d):
        @pl.when(place - d >= 0)
        def _():
            j = here - 2 * d
            arrived(to_right(j))
            pl.when(place < last)(lambda: start(to_right(j)))
            start(to_side(j))
            start(to_sibling(j))

        @pl.when(place + d <= last)
        def _():
            j = here + 2 * d
            arrived(to_left(j))
            pl.when(place > 0)(lambda: start(to_left(j)))
            start(to_side(j))
            start(to_sibling(j))

        @pl.when(d == 1)
        def _():
            from_side(place)
            convolve(0)
            convolve(1)

        pl.when(place - d >= 0)(lambda: from_side(place - d))
        pl.when(place + d <= last)(lambda: from_side(place + d))
        pl.when(d <= STRAIGHT_COPIES)(lambda: pass_straight(d - 1))

    for q in range(min(last, STRAIGHT_COPIES), STRAIGHT_COPIES):
        pass_straight(q)

    place_shard(far_in, far_out, far_taps, across)
    project(2)
    taps_sibfar.wait_recv()

    @pl.loop(0, 2 * places)
    def _(j):
        arrived(to_sibling(j))

    for q in range(STRAIGHT_COPIES):
        straight_sibling(q).wait_recv()
    place_shard(sibfar_in, sibfar_out, sibfar_taps, far_sibling)
    project(3)
    keep_in = pltpu.make_async_copy(full_in, in_hbm, keep_sems.at[1])
    keep_out = pltpu.make_async_copy(full_out, out_hbm, keep_sems.at[2])
    keep_in.start()
    keep_out.start()
    convolve(2)
    convolve(3)
    keep_gated = pltpu.make_async_copy(gated, gated_hbm, keep_sems.at[3])
    keep_mixed = pltpu.make_async_copy(mixed, mixed_hbm, keep_sems.at[4])
    keep_gated.start()
    keep_mixed.start()
    keep_normed.wait()

    blocks = rows // OUT_BLOCK

    def block_at(k, first=0):
        return pl.ds(pl.multiple_of(first + k * OUT_BLOCK, OUT_BLOCK), OUT_BLOCK)

    def unit_copy(k):
        return remote(
            unit_out.at[block_at(k)], unit_in.at[block_at(k)],
            unit_sems.at[0, k], unit_sems.at[1, k], {"tp": sibling},
        )

    def hidden_copy(k):
        return pltpu.make_async_copy(
            hidden.at[lax.rem(k, 2)], hidden_hbm.at[block_at(k)], mid_sems.at[0, lax.rem(k, 2)]
        )

    def mid_copy(half, held, whose, k):
        return pltpu.make_async_copy(
            held.at[block_at(k)], mid_hbm.at[block_at(k, whose * rows)], mid_sems.at[half, k]
        )

    @pl.loop(0, blocks)
    def _(k):
        slot = lax.rem(k, 2)
        at = block_at(k)
        pl.when(k >= 2)(lambda: hidden_copy(k - 2).wait())
        hidden[slot] = jnp.dot(mixed[at, :], full_out[...], preferred_element_type=jnp.float32)

        @pl.loop(0, OUT_BLOCK // SUB_ROWS)
        def _(r):
            sub = pl.ds(pl.multiple_of(r * SUB_ROWS, SUB_ROWS), SUB_ROWS)
            whole = pl.ds(pl.multiple_of(k * OUT_BLOCK + r * SUB_ROWS, SUB_ROWS), SUB_ROWS)
            hidden_rows = tokens[whole, :].astype(jnp.float32) + hidden[slot, sub, :]
            hidden[slot, sub, :] = hidden_rows
            unit = hidden_rows * rms_scale(hidden_rows)
            unit_out[whole, :] = unit
            normed[whole, :] = (gain_ffn[...] * unit).astype(low)

        unit_copy(k).start()
        hidden_copy(k).start()
        mid_copy(1, normed, core, k).start()

    keep_mixed.wait()

    @pl.loop(0, blocks)
    def _(k):
        unit_copy(k).wait_recv()

        @pl.loop(0, OUT_BLOCK // SUB_ROWS)
        def _(r):
            whole = pl.ds(pl.multiple_of(k * OUT_BLOCK + r * SUB_ROWS, SUB_ROWS), SUB_ROWS)
            mixed[whole, :] = (gain_ffn[...] * unit_in[whole, :]).astype(low)

        mid_copy(2, mixed, 1 - core, k).start()

    @pl.loop(0, blocks)
    def _(k):
        unit_copy(k).wait_send()
        mid_copy(1, normed, core, k).wait()
        mid_copy(2, mixed, 1 - core, k).wait()

    for k in range(max(blocks - 2, 0), blocks):
        hidden_copy(k).wait()
    keep_in.wait()
    keep_out.wait()
    keep_gated.wait()
    for turn in range(4):
        for g in range(3):
            if turn >= 2 or g == 1:
                gate_out(turn, order[turn], g).wait()

    @pl.when(here < end)
    def _():
        for turn in range(4):
            for slot in range(slots):
                halo(turn, order[turn], slot).wait_send()

    left_source(across_share())
    for q in range(STRAIGHT_COPIES):
        straight_across(q).wait_send()
        straight_sibling(q).wait_send()
    for copy in (taps_far, taps_sib, taps_sibfar, in_sib, out_sib):
        copy.wait_send()

    @pl.loop(0, places)
    def _(q):
        j = 2 * q + side
        left_source(to_side(j))
        pl.when((q <= place) & (place < last))(lambda: left_source(to_right(j)))
        pl.when((q >= place) & (place > 0))(lambda: left_source(to_left(j)))
        left_source(to_sibling(j))
        left_source(to_sibling(2 * q + 1 - side))


def mixer_front(w_in, w_out, taps, gain_mix, gain_ffn, lengths, tokens, slots, collective_id):
    width, _, chans = w_in.shape
    rows = tokens.shape[0] // 2
    count = lax.axis_size("seq")
    group = lax.axis_size("tp")
    f32, low = jnp.float32, jnp.bfloat16
    blocks = rows // OUT_BLOCK
    pair = [pltpu.VMEM((width, 3 * chans), f32), pltpu.VMEM((chans, width), f32)]
    whole = pl.BlockSpec(memory_space=pltpu.VMEM)
    anywhere = pl.BlockSpec(memory_space=pl.ANY)
    padded = (slots, rows // slots + 8, width)
    return pl.pallas_call(
        functools.partial(front_kernel, count // 2, slots),
        out_shape=[
            jax.ShapeDtypeStruct((width, 3 * chans * group), low),
            jax.ShapeDtypeStruct((chans * group, width), low),
            jax.ShapeDtypeStruct((8, chans * group), f32),
            jax.ShapeDtypeStruct((2 * rows, width), low),
            jax.ShapeDtypeStruct((rows, width), f32),
            jax.ShapeDtypeStruct((rows, 3 * width), f32),
            jax.ShapeDtypeStruct(padded, f32),
            jax.ShapeDtypeStruct((rows, width), low),
            jax.ShapeDtypeStruct((rows, width), low),
        ],
        in_specs=[whole] * 5 + [pl.BlockSpec(memory_space=pltpu.SMEM), anywhere],
        out_specs=[anywhere] * 2 + [whole] + [anywhere] * 6,
        scratch_shapes=pair * 4
        + [pltpu.VMEM((8, chans), f32)] * 4
        + [
            pltpu.VMEM((width // 2 // count, 3 * chans), f32),
            pltpu.VMEM((chans // count, width), f32),
            pltpu.VMEM((width, 3 * chans * group), low),
            pltpu.VMEM((chans * group, width), low),
            pltpu.VMEM((rows, width), low),
            pltpu.VMEM((rows, width), low),
            pltpu.VMEM((rows, width), low),
            pltpu.VMEM((rows, width), f32),
            pltpu.VMEM((2, 2, rows, chans), f32),
            pltpu.VMEM(padded, f32),
            pltpu.VMEM((rows, width), f32),
            pltpu.VMEM((rows, width), f32),
            pltpu.VMEM((2, OUT_BLOCK, width), f32),
            pltpu.SemaphoreType.DMA((5, 2, count)),
            pltpu.SemaphoreType.DMA((2, 2, count)),
            pltpu.SemaphoreType.DMA((2, 5)),
            pltpu.SemaphoreType.DMA((2, 4, slots)),
            pltpu.SemaphoreType.DMA((4, 3)),
            pltpu.SemaphoreType.DMA((2, blocks)),
            pltpu.SemaphoreType.DMA((5,)),
            pltpu.SemaphoreType.DMA((3, blocks)),
            pltpu.SemaphoreType.DMA((4, STRAIGHT_COPIES)),
        ],
        compiler_params=pltpu.CompilerParams(
            collective_id=collective_id, has_side_effects=True, vmem_limit_bytes=VMEM_LIMIT
        ),
        name="mixer_front",
    )(
        w_in.transpose(1, 0, 2),
        w_out,
        jnp.pad(taps, ((0, 5), (0, 0))),
        gain_mix,
        gain_ffn,
        lengths,
        tokens,
    )


def finish_kernel(slots, chans, hidden, *refs):
    (sums, tokens_in, block_in, lengths) = refs[0:4]
    (block_out, tokens_out, gains, g_in, g_conv, g_out, g_gate, g_up, g_down) = refs[4:13]
    (held, tokens, block, rounded, turned, in_sems, block_sems, turn_sems, out_sems) = refs[13:22]
    rows, width = block_in.shape
    slot_len = rows // slots
    here = lax.axis_index("seq")
    tp_at = lax.axis_index("tp")
    first = 3 * hidden
    out_first = first + 3 * chans
    small_first = out_first + chans
    blocks = rows // OUT_BLOCK
    turns = hidden // LANES
    half_rows = rows // 2

    def cols(start, size):
        return (slice(None), slice(start, start + size))

    parts = [cols(i * hidden, hidden) for i in range(3)] + [cols(first, held.shape[1] - first)]
    halves = [slice(0, half_rows), slice(half_rows, rows)]
    part_loads = [
        pltpu.make_async_copy(sums.at[at], held.at[at], in_sems.at[i]) for i, at in enumerate(parts)
    ]
    token_loads = [
        pltpu.make_async_copy(tokens_in.at[at], tokens.at[at], in_sems.at[4 + i])
        for i, at in enumerate(halves)
    ]

    def block_at(k):
        return pl.ds(pl.multiple_of(k * OUT_BLOCK, OUT_BLOCK), OUT_BLOCK)

    def block_load(k):
        return pltpu.make_async_copy(
            block_in.at[block_at(k)], block.at[block_at(k)], block_sems.at[0, k]
        )

    def block_store(k):
        return pltpu.make_async_copy(
            rounded.at[block_at(k)], block_out.at[block_at(k)], block_sems.at[1, k]
        )

    def panel_at(k):
        return pl.ds(pl.multiple_of(k * LANES, LANES), LANES)

    def turn_store(k):
        at = panel_at(k)
        return pltpu.make_async_copy(turned.at[at], g_down.at[at], turn_sems.at[k])

    stores = []

    def store(src, dst):
        copy = pltpu.make_async_copy(src, dst, out_sems.at[len(stores)])
        copy.start()
        stores.append(copy)

    part_loads[2].start()

    @pl.loop(0, blocks)
    def _(k):
        block_load(k).start()

    for load in (*token_loads, part_loads[0], part_loads[1], part_loads[3]):
        load.start()

    part_loads[2].wait()

    @pl.loop(0, turns)
    def _(k):
        from_cols = pl.ds(pl.multiple_of(2 * hidden + k * LANES, LANES), LANES)
        turned[panel_at(k), :] = held[:, from_cols].T
        turn_store(k).start()

    @pl.loop(0, blocks)
    def _(k):
        block_load(k).wait()
        per_slot = slot_len // OUT_BLOCK
        at = lax.broadcasted_iota(jnp.int32, (OUT_BLOCK, 1), 0)
        at = at + (here * slot_len + lax.rem(k, per_slot) * OUT_BLOCK)
        mask = (at < lengths[k // per_slot]).astype(jnp.float32)
        rounded[block_at(k), :] = (mask * block[block_at(k), :]).astype(jnp.bfloat16)
        block_store(k).start()

    for load, at in zip(token_loads, halves):
        load.wait()
        store(tokens.at[at], tokens_out.at[at])
    for i, target in ((0, g_gate), (1, g_up)):
        part_loads[i].wait()
        store(held.at[parts[i]], target)
    part_loads[3].wait()
    for g in range(3):
        store(held.at[cols(first + g * chans, chans)], g_in.at[g])
    per_col = width // chans
    for p in range(width // LANES):
        q, r = p // per_col, p % per_col
        at = (slice(r * chans, (r + 1) * chans), slice(out_first + q * LANES, out_first + (q + 1) * LANES))
        store(held.at[at], g_out.at[cols(p * LANES, LANES)])
        gains[cols(p * LANES, LANES)] = held[8 * p : 8 * p + 8, small_first:]
    own = pl.ds(pl.multiple_of(tp_at * chans, LANES), chans)
    g_conv[...] = gains[2:5, own]
    for copy in stores:
        copy.wait()

    @pl.loop(0, turns)
    def _(k):
        turn_store(k).wait()

    @pl.loop(0, blocks)
    def _(k):
        block_store(k).wait()


def finish(sums, tokens_grad, block_sum, lengths, chans, hidden):
    rows, width = block_sum.shape
    f32 = jnp.float32
    anywhere = pl.BlockSpec(memory_space=pl.ANY)
    whole = pl.BlockSpec(memory_space=pltpu.VMEM)
    blocks = rows // OUT_BLOCK
    return pl.pallas_call(
        functools.partial(finish_kernel, lengths.shape[0], chans, hidden),
        out_shape=[
            jax.ShapeDtypeStruct((rows, width), jnp.bfloat16),
            jax.ShapeDtypeStruct((rows, width), f32),
            jax.ShapeDtypeStruct((8, width), f32),
            jax.ShapeDtypeStruct((3, width, chans), f32),
            jax.ShapeDtypeStruct((3, chans), f32),
            jax.ShapeDtypeStruct((chans, width), f32),
            jax.ShapeDtypeStruct((width, hidden), f32),
            jax.ShapeDtypeStruct((width, hidden), f32),
            jax.ShapeDtypeStruct((hidden, width), f32),
        ],
        in_specs=[anywhere] * 3 + [pl.BlockSpec(memory_space=pltpu.SMEM)],
        out_specs=[anywhere] * 2 + [whole, anywhere, whole] + [anywhere] * 4,
        scratch_shapes=[
            pltpu.VMEM(sums.shape, f32),
            pltpu.VMEM((rows, width), f32),
            pltpu.VMEM((rows, width), f32),
            pltpu.VMEM((rows, width), jnp.bfloat16),
            pltpu.VMEM((hidden, width), f32),
            pltpu.SemaphoreType.DMA((6,)),
            pltpu.SemaphoreType.DMA((2, blocks)),
            pltpu.SemaphoreType.DMA((hidden // LANES,)),
            pltpu.SemaphoreType.DMA((7 + width // LANES,)),
        ],
        compiler_params=pltpu.CompilerParams(vmem_limit_bytes=VMEM_LIMIT),
        name="finish",
    )(sums, tokens_grad, block_sum, lengths)


def per_device(
    tokens, lengths, gain_mix, w_in, conv_weight, w_out, gain_ffn, w_gate, w_up, w_down, cotangent
):
    slot_count, local_len, width = tokens.shape
    chans = w_in.shape[2]
    half_slots = slot_count // 2
    row_count = slot_count * local_len

    token_rows = tokens.reshape(row_count, width)
    cot_rows = cotangent.reshape(row_count, width)
    gains = gain_mix.reshape(1, width), gain_ffn.reshape(1, width)
    w_in_all, w_out_all, taps, normed_mid, hidden_res, projected, gated_rows, normed_in, mixed = (
        mixer_front(w_in, w_out, conv_weight, *gains, lengths, token_rows, half_slots, 3)
    )
    mixer_cols = 4 * chans
    sum_cols = FFN_PANELS * LANES + mixer_cols + LANES
    sums, grad_tokens, block_sum = back_both(
        (
            normed_mid,
            cot_rows,
            w_gate,
            w_up,
            w_down,
            hidden_res,
            projected,
            gated_rows,
            normed_in,
            mixed,
            w_in_all,
            w_out_all,
            token_rows,
        ),
        (lengths, taps, *gains),
        half_slots,
        sum_cols,
        1,
    )[:3]
    block_out, grad_tokens, small, g_in, g_conv, g_out, g_gate, g_up, g_down = finish(
        sums, grad_tokens, block_sum, lengths, chans, w_gate.shape[1]
    )
    return (
        block_out.reshape(slot_count, local_len, width),
        grad_tokens.reshape(slot_count, local_len, width),
        small[0],
        g_in.transpose(1, 0, 2),
        g_conv,
        g_out,
        small[1],
        g_gate,
        g_up,
        g_down,
    )


def solution(mesh):
    rows, cols = P("tp", None), P(None, "tp")
    tokens, whole, stacked = P(None, "seq", None), P(), P(None, None, "tp")
    return jax.shard_map(
        per_device,
        mesh=mesh,
        in_specs=(
            tokens, whole, whole, stacked, cols, rows, whole, cols, cols, rows, tokens,
        ),
        out_specs=(
            tokens, tokens, whole, stacked, cols, rows, whole, cols, cols, rows,
        ),
        check_vma=False,
    )
```

```python
import functools

import jax
import jax.numpy as jnp
from jax import lax
from jax.experimental import pallas as pl
from jax.experimental.pallas import tpu as pltpu
from jax.sharding import PartitionSpec as P

NORM_EPS = 1e-05
LANES = 128
VMEM_LIMIT = 64 << 20
HALF = 128
SLOTS_IN_FLIGHT = 10


def rms_scale(values):
    return lax.rsqrt(jnp.mean(values * values, axis=-1, keepdims=True) + NORM_EPS)


def dot_rows(left, right):
    return lax.dot_general(
        left, right, (((0,), (0,)), ((), ())), preferred_element_type=jnp.float32
    )


def dot_cols(left, right):
    return lax.dot_general(
        left, right, (((1,), (1,)), ((), ())), preferred_element_type=jnp.float32
    )


def greet_seq(places, others=(), more=0):
    barrier = pltpu.get_barrier_semaphore()
    here = lax.axis_index("seq")
    place, side = here // 2, lax.rem(here, 2)

    def signal(device):
        pl.semaphore_signal(
            barrier, inc=1, device_id=device, device_id_type=pl.DeviceIdType.MESH
        )

    signal({"seq": here + 1 - 2 * side})
    for other in others:
        signal(other)
    pl.when(place > 0)(lambda: signal({"seq": here - 2}))
    pl.when(place < places - 1)(lambda: signal({"seq": here + 2}))
    ends = jnp.where(place > 0, 1, 0) + jnp.where(place < places - 1, 1, 0)
    pl.semaphore_wait(barrier, 1 + len(others) + ends + more)


class SeqSum:
    def __init__(self, places, own, out, scratch):
        self.places, self.own, self.out = places, own, out
        self.y_in, self.p_left, self.p_right, self.p_acc = scratch[0:4]
        self.q_left, self.q_right, self.q_acc, self.q_in = scratch[4:8]
        self.sems = scratch[8]
        here = lax.axis_index("seq")
        self.place, self.side = here // 2, here % 2

    def remote(self, src, dst, slot, send, recv, place, side):
        return pltpu.make_async_remote_copy(
            src_ref=src,
            dst_ref=dst,
            send_sem=self.sems.at[send, slot],
            recv_sem=self.sems.at[recv, slot],
            device_id={"seq": place * 2 + side},
            device_id_type=pl.DeviceIdType.MESH,
        )

    def chain(self, root):
        last = self.places - 1
        left = jnp.maximum(self.place - 1, 0)
        right = jnp.minimum(self.place + 1, last)
        from_left = (self.place <= root) & (self.place > 0)
        from_right = (self.place >= root) & (self.place < last)
        return left, right, from_left, from_right

    def own_base(self, k):
        held = self.own.shape[0] // (4 * HALF)
        return pl.multiple_of(lax.rem(k, held) * 4 * HALF, 4 * HALF)

    def out_at(self, k, first, size):
        per_panel = self.out.shape[0] // (4 * HALF)
        panel, part = place_in_sums(k, per_panel)
        row = part * 4 * HALF + first
        return self.out.at[
            pl.ds(pl.multiple_of(row, size), size), pl.ds(pl.multiple_of(panel * LANES, LANES), LANES)
        ]

    def p_stage(self, which, k):
        place, side = self.place, self.side
        own = self.own
        slot = lax.rem(k, SLOTS_IN_FLIGHT)
        base = self.own_base(k)
        mine = pl.ds(pl.multiple_of(base + side * HALF, HALF), HALF)
        theirs = pl.ds(pl.multiple_of(base + (1 - side) * HALF, HALF), HALF)
        out_mine = self.out_at(k, side * HALF, HALF)
        root = self.places // 2 - 1 + lax.rem(k, 2)
        left, right, from_left, from_right = self.chain(root)
        acc, y_in = self.p_acc.at[slot], self.y_in.at[slot]
        from_l, from_r = self.p_left.at[slot], self.p_right.at[slot]
        remote = functools.partial(functools.partial, self.remote)

        to_side = remote(own.at[theirs], y_in, slot, 0, 1, place, 1 - side)
        up_right = remote(acc, from_l, slot, 2, 3, right, side)
        up_left = remote(acc, from_r, slot, 2, 4, left, side)

        def down(src):
            return (
                remote(src, out_mine, slot, 5, 7, left, side),
                remote(src, out_mine, slot, 6, 7, right, side),
                remote(src, out_mine, slot, 8, 9, place, 1 - side),
            )

        def keep():
            return pltpu.make_async_copy(acc, out_mine, self.sems.at[10, slot])

        def hand_down(src):
            down_left, down_right, down_side = down(src)
            down_side().start()
            pl.when(from_left)(lambda: down_left().start())
            pl.when(from_right)(lambda: down_right().start())

        if which == "split":
            to_side().start()

        if which == "up":
            to_side().wait_recv()
            acc[...] = own[mine, :] + y_in[...]

            @pl.when(place < root)
            def _():
                @pl.when(from_left)
                def _():
                    up_right().wait_recv()
                    acc[...] += from_l[...]

                up_right().start()

            @pl.when(place > root)
            def _():
                @pl.when(from_right)
                def _():
                    up_left().wait_recv()
                    acc[...] += from_r[...]

                up_left().start()

        if which == "root":

            @pl.when(place == root)
            def _():
                @pl.when(from_left)
                def _():
                    up_right().wait_recv()
                    acc[...] += from_l[...]

                @pl.when(from_right)
                def _():
                    up_left().wait_recv()
                    acc[...] += from_r[...]

                hand_down(acc)
                keep().start()

        if which == "down":

            @pl.when(place != root)
            def _():
                down(acc)[0]().wait_recv()
                hand_down(out_mine)

        if which == "end":
            down_left, down_right, down_side = down(acc)
            down_side().wait()
            to_side().wait_send()
            pl.when(from_left)(lambda: down_left().wait_send())
            pl.when(from_right)(lambda: down_right().wait_send())
            pl.when(place == root)(lambda: keep().wait())
            pl.when(place != root)(lambda: up_left().wait_send())

    def q_stage(self, which, k):
        place, side = self.place, self.side
        own = self.own
        slot = lax.rem(k, SLOTS_IN_FLIGHT)
        base = self.own_base(k)
        wide = pl.ds(pl.multiple_of(base + 2 * HALF, 2 * HALF), 2 * HALF)
        out_wide = self.out_at(k, 2 * HALF, 2 * HALF)
        root = self.places // 2 - lax.rem(k, 2)
        left, right, from_left, from_right = self.chain(root)
        acc, side_in = self.q_acc.at[slot], self.q_in.at[slot]
        from_l, from_r = self.q_left.at[slot], self.q_right.at[slot]
        remote = functools.partial(functools.partial, self.remote)

        up_right = remote(acc, from_l, slot, 11, 12, right, side)
        up_left = remote(acc, from_r, slot, 11, 13, left, side)
        to_side = remote(acc, side_in, slot, 14, 15, place, 1 - side)

        def down(src):
            return (
                remote(src, out_wide, slot, 16, 18, left, side),
                remote(src, out_wide, slot, 17, 18, right, side),
            )

        def keep():
            return pltpu.make_async_copy(side_in, out_wide, self.sems.at[19, slot])

        def hand_down(src):
            down_left, down_right = down(src)
            pl.when(from_left)(lambda: down_left().start())
            pl.when(from_right)(lambda: down_right().start())

        if which == "up":
            acc[...] = own[wide, :]

            @pl.when(place < root)
            def _():
                @pl.when(from_left)
                def _():
                    up_right().wait_recv()
                    acc[...] += from_l[...]

                up_right().start()

            @pl.when(place > root)
            def _():
                @pl.when(from_right)
                def _():
                    up_left().wait_recv()
                    acc[...] += from_r[...]

                up_left().start()

        if which == "root":

            @pl.when(place == root)
            def _():
                @pl.when(from_left)
                def _():
                    up_right().wait_recv()
                    acc[...] += from_l[...]

                @pl.when(from_right)
                def _():
                    up_left().wait_recv()
                    acc[...] += from_r[...]

                to_side().start()

        if which == "side":

            @pl.when(place == root)
            def _():
                to_side().wait_recv()
                side_in[...] += acc[...]
                hand_down(side_in)
                keep().start()

        if which == "down":

            @pl.when(place != root)
            def _():
                down(acc)[0]().wait_recv()
                hand_down(out_wide)

        if which == "end":
            down_left, down_right = down(acc)
            pl.when(from_left)(lambda: down_left().wait_send())
            pl.when(from_right)(lambda: down_right().wait_send())

            @pl.when(place == root)
            def _():
                to_side().wait_send()
                keep().wait()

            pl.when(place != root)(lambda: up_left().wait_send())

    P_LAGS = (("split", 0, 0), ("up", 2, 1), ("root", 3, 3), ("down", 6, 7), ("end", 9, 9))
    Q_LAGS = (("up", 1, 0), ("root", 2, 2), ("side", 4, 4), ("down", 6, 7), ("end", 9, 9))

    def tick(self, t, count):
        middle = (self.place == self.places // 2) | (self.place == self.places // 2 - 1)
        for stage, lags in ((self.p_stage, self.P_LAGS), (self.q_stage, self.Q_LAGS)):
            for which, mid_lag, outer_lag in lags:
                k = t - jnp.where(middle, mid_lag, outer_lag)

                @pl.when((k >= 0) & (k < count))
                def _(stage=stage, which=which, k=k):
                    stage(which, k)

    def run(self, count):
        @pl.loop(0, count + self.P_LAGS[-1][1])
        def _(t):
            self.tick(t, count)


def seq_sum_scratch():
    half = pltpu.VMEM((SLOTS_IN_FLIGHT, HALF, LANES), jnp.float32)
    wide = pltpu.VMEM((SLOTS_IN_FLIGHT, 2 * HALF, LANES), jnp.float32)
    return [half] * 4 + [wide] * 4 + [pltpu.SemaphoreType.DMA((20, SLOTS_IN_FLIGHT))]


SUB_ROWS = 64
STRAIGHT_COPIES = 4
FIRST_MIXER_TICK = 36
BLOCK_TICK = 56
FFN_PANELS = 27
FFN_PARTS = 3
ROW_BLOCK = 256
ROW_TICK = 2
OUT_BLOCK = 256


def place_in_sums(piece, per_panel):
    per_part = FFN_PANELS // FFN_PARTS
    third = per_part // 3
    part, inside = piece // (per_part * per_panel), lax.rem(piece, per_part * per_panel)
    kind = lax.rem(inside, per_part)
    panel = kind // third * (FFN_PANELS // 3) + part * third + lax.rem(kind, third)
    of_ffn = piece < FFN_PANELS * per_panel
    return (
        jnp.where(of_ffn, panel, piece // per_panel),
        jnp.where(of_ffn, inside // per_part, lax.rem(piece, per_panel)),
    )


def norm_back(grad, gain, unit, scale):
    scaled = gain * grad
    return scale * (scaled - unit * jnp.mean(scaled * unit, axis=-1, keepdims=True))


def back_kernel(places, slots, *refs):
    (mid_hbm, cot_hbm, w_gate_hbm, w_up_hbm, w_d_hbm, hidden_hbm, proj_hbm) = refs[0:7]
    (gated_hbm, normed_hbm, mixed_hbm, w_in_hbm, w_out_hbm, tokens_hbm) = refs[7:13]
    (lengths, taps, gain_mix, gain_ffn) = refs[13:17]
    (sums, tokens_out, block_out, mid_chip, mid_far, ffn_chip, ffn_far) = refs[17:24]
    (mid_land, ffn_land, land_in, land_out, land_small) = refs[24:29]
    (mid, cot, w_gu, w_d, act, ggu, own, staged, fetched) = refs[29:38]
    (proj, gated, mixed_buf, conv_in, grad_hid, grad_tok) = refs[38:44]
    (halo_out, halo_in, halo_keep, small, small_in) = refs[44:49]
    load_sems, near_sems, far_sems, keep_sem, fetch_sem = refs[49:54]
    (later_sems, row_sems, halo_sems, weight_sems, out_sems) = refs[54:59]

    summer = SeqSum(places, own, sums, refs[59:])
    here = lax.axis_index("seq")
    last = 2 * places - 1
    tp_at = lax.axis_index("tp")
    core = lax.rem(tp_at, 2)
    sibling = tp_at + 1 - 2 * core
    across = lax.rem(tp_at + 2, 4)
    rows, width = mid.shape
    parts, _, wide = w_gu.shape
    half_rows = rows // 2
    chans = wide // 3
    hidden = wide // 2
    panels = 3 * hidden // LANES

    moves = [(mid_hbm, mid), (cot_hbm, cot), (w_d_hbm, w_d)]
    for c in range(parts):
        for i, source in enumerate((w_gate_hbm, w_up_hbm)):
            move = (
                source.at[:, c * hidden : (c + 1) * hidden],
                w_gu.at[c, :, i * hidden : (i + 1) * hidden],
            )
            moves.insert(i if c == 0 else len(moves), move)
    loads = [
        pltpu.make_async_copy(src, dst, load_sems.at[i]) for i, (src, dst) in enumerate(moves)
    ]
    for load in loads:
        load.start()

    barrier = pltpu.get_barrier_semaphore()

    def signal(device):
        pl.semaphore_signal(barrier, inc=1, device_id=device, device_id_type=pl.DeviceIdType.MESH)

    pl.when(here > 0)(lambda: signal({"seq": here - 1}))
    pl.when(here < last)(lambda: signal({"seq": here + 1}))
    ends = jnp.where(here > 0, 1, 0) + jnp.where(here < last, 1, 0)
    greet_seq(places, ({"tp": sibling}, {"tp": across}), ends)
    ffn_pieces = own.shape[0] // (4 * HALF)
    mixer_pieces = 4 * chans * width // LANES // (4 * HALF) + 1
    count = ffn_pieces + mixer_pieces
    for load in loads[:5]:
        load.wait()

    slot_len = rows // 2 // slots

    def valid_rows(slot, first, size):
        at = lax.broadcasted_iota(jnp.int32, (size, 1), 0) + (here * slot_len + first)
        return (at < lengths[slot]).astype(jnp.float32)

    row_ticks = rows // ROW_BLOCK // ROW_TICK
    grad_ticks = width // OUT_BLOCK
    first_ticks = grad_ticks - 4 * HALF // OUT_BLOCK
    blocks = rows // 2 // OUT_BLOCK
    before_mid = first_ticks + (parts - 1) * row_ticks
    after_mid = before_mid + blocks
    before_ffn = after_mid + (parts - 1) * grad_ticks

    def part_cols(c):
        return pl.ds(pl.multiple_of(c * hidden, LANES), hidden)

    def row_phase(c):
        for i in range(1, parts):

            @pl.when(jnp.int32(c) == i)
            def _(i=i):
                loads[3 + 2 * i].wait()
                loads[4 + 2 * i].wait()

        @pl.loop(0, rows // ROW_BLOCK)
        def _(r):
            at = pl.ds(pl.multiple_of(r * ROW_BLOCK, ROW_BLOCK), ROW_BLOCK)

            @pl.when(jnp.int32(c) == 0)
            def _():
                per_slot = slot_len // ROW_BLOCK
                mask = valid_rows(r // per_slot, lax.rem(r, per_slot) * ROW_BLOCK, ROW_BLOCK)
                cot[at, :] = (mask * cot[at, :].astype(jnp.float32)).astype(jnp.bfloat16)

            both = jnp.dot(mid[at, :], w_gu[c], preferred_element_type=jnp.float32)
            gate, up = both[:, :hidden], both[:, hidden:]
            grad_act = dot_cols(cot[at, :], w_d[part_cols(c), :])
            sigmoid = 1.0 / (1.0 + jnp.exp(-gate))
            silu = gate * sigmoid
            act[at, part_cols(c)] = (silu * up).astype(jnp.bfloat16)
            slope = sigmoid * (1.0 + gate * (1.0 - sigmoid))
            ggu[c, at, :hidden] = (grad_act * up * slope).astype(jnp.bfloat16)
            ggu[c, at, hidden:] = (grad_act * silu).astype(jnp.bfloat16)

            @pl.when((jnp.int32(c) > 0) & (lax.rem(r, ROW_TICK) == ROW_TICK - 1))
            def _():
                summer.tick(first_ticks + (c - 1) * row_ticks + r // ROW_TICK, count)

    def grad_phase(c):
        @pl.loop(0, width // OUT_BLOCK)
        def _(m):
            first = pl.multiple_of(m * OUT_BLOCK, OUT_BLOCK)
            at = pl.ds(first, OUT_BLOCK)
            per_piece = 4 * HALF // OUT_BLOCK
            piece = (c * (width // OUT_BLOCK // per_piece) + m // per_piece) * panels
            base = piece * 4 * HALF + lax.rem(m, per_piece) * OUT_BLOCK

            def put(block, panel):
                for j in range(block.shape[1] // LANES):
                    to = pl.multiple_of(base + (panel + j) * 4 * HALF, OUT_BLOCK)
                    own[pl.ds(to, OUT_BLOCK), :] = block[:, j * LANES : (j + 1) * LANES]

            put(dot_rows(mid[:, at], ggu[c]), 0)
            put(dot_rows(cot[:, at], act[:, part_cols(c)]), wide // LANES)

            step = jnp.where(jnp.int32(c) > 0, after_mid + (c - 1) * grad_ticks + m, m - grad_ticks + first_ticks)

            @pl.when(step >= 0)
            def _():
                summer.tick(step, count)

    def row_block(half, k):
        return pl.ds(pl.multiple_of((half * blocks + k) * OUT_BLOCK, OUT_BLOCK), OUT_BLOCK)

    def mid_part(at):
        return sum(dot_cols(ggu[c, at, :], w_gu[c]) for c in range(parts))

    def ffn_part(at):
        return sum(
            jnp.dot(
                act[at, c * hidden : (c + 1) * hidden],
                w_d[c * hidden : (c + 1) * hidden, :],
                preferred_element_type=jnp.float32,
            )
            for c in range(parts)
        )

    def near(which, land, k):
        return pltpu.make_async_remote_copy(
            src_ref=staged.at[lax.rem(k, 2)],
            dst_ref=land.at[row_block(0, k)],
            send_sem=near_sems.at[which, 0, k],
            recv_sem=near_sems.at[which, 1, k],
            device_id={"tp": sibling},
            device_id_type=pl.DeviceIdType.MESH,
        )

    def far(which, chip, there, k):
        return pltpu.make_async_remote_copy(
            src_ref=chip.at[row_block(0, k)],
            dst_ref=there.at[row_block(0, k)],
            send_sem=far_sems.at[which, 0, k],
            recv_sem=far_sems.at[which, 1, k],
            device_id={"tp": across},
            device_id_type=pl.DeviceIdType.MESH,
        )

    def ffn_across(k):
        return far(1, ffn_chip, ffn_far, k)

    def tp_sum(which, part, land, chip, first_tick):
        @pl.loop(0, blocks)
        def _(k):
            @pl.when(k >= 2)
            def _():
                near(which, land, k - 2).wait_send()

            staged[lax.rem(k, 2)] = part(row_block(1 - core, k))
            near(which, land, k).start()

        for k in range(max(blocks - 2, 0), blocks):
            near(which, land, k).wait_send()

        @pl.loop(0, blocks)
        def _(k):
            near(which, land, k).wait_recv()
            fetch = pltpu.make_async_copy(land.at[row_block(0, k)], fetched, fetch_sem)
            fetch.start()
            staged[0] = part(row_block(core, k))
            fetch.wait()
            staged[0] += fetched[...]
            keep = pltpu.make_async_copy(staged.at[0], chip.at[row_block(0, k)], keep_sem)
            keep.start()
            summer.tick(first_tick + k, count)
            keep.wait()
            if which == 0:
                far(0, mid_chip, mid_far, k).start()

    row_phase(0)
    grad_phase(0)
    pl.loop(1, parts)(row_phase)
    tp_sum(0, mid_part, mid_land, mid_chip, before_mid)
    pl.loop(1, parts)(grad_phase)
    tp_sum(1, ffn_part, ffn_land, ffn_chip, before_ffn)

    own_half = pl.ds(pl.multiple_of(core * half_rows, half_rows), half_rows)
    low_half, high_half = pl.ds(0, half_rows), pl.ds(half_rows, half_rows)
    w_out, grad_mixer = mid.at[low_half], mid.at[high_half]
    normed, mixed = act.at[low_half, pl.ds(0, width)], act.at[high_half, pl.ds(0, width)]
    tokens = w_d.at[low_half]
    w_in = (ggu.at[2, low_half], ggu.at[2, high_half], w_gu.at[0], w_gu.at[1])
    moves = [
        (w_out_hbm, w_out),
        (tokens_hbm.at[own_half], tokens),
        (normed_hbm, normed),
        (mixed_hbm, mixed),
    ]
    for j in range(4):
        for g in range(3):
            first = g * width + j * chans
            moves.append(
                (w_in_hbm.at[:, first : first + chans], w_in[j].at[:, g * chans : (g + 1) * chans])
            )
    loads = [
        pltpu.make_async_copy(src, dst, later_sems.at[i]) for i, (src, dst) in enumerate(moves)
    ]
    for load in loads:
        load.start()
    chip, far_rows, hidden_rows = staged.at[0], staged.at[1], fetched
    per_slot = slot_len // OUT_BLOCK
    small[...] = jnp.zeros_like(small)
    ticked = before_ffn + blocks

    @pl.loop(ticked, FIRST_MIXER_TICK)
    def _(t):
        summer.tick(t, count)

    @pl.loop(0, blocks)
    def _(k):
        far(0, mid_chip, mid_far, k).wait()
        ffn_across(k).start()

    for load in loads:
        load.wait()

    def shard_rows(shard, first, size):
        at = lax.rem(shard, 2) * half_rows + first
        return shard // 2, pl.ds(pl.multiple_of(at, size), size)

    def place_of(n):
        slot = n // per_slot
        block = per_slot - 1 - lax.rem(n, per_slot)
        return slot, block, pl.multiple_of(slot * slot_len + block * OUT_BLOCK, OUT_BLOCK)

    def mid_loads(first):
        at = pl.ds(first, OUT_BLOCK)
        return [
            pltpu.make_async_copy(src.at[at], dst, row_sems.at[i])
            for i, (src, dst) in enumerate(((mid_chip, chip), (mid_far, far_rows), (hidden_hbm, hidden_rows)))
        ]

    def proj_loads(slot, block, first):
        return [
            pltpu.make_async_copy(proj_hbm.at[pl.ds(first, OUT_BLOCK)], proj, row_sems.at[3]),
            pltpu.make_async_copy(
                gated_hbm.at[slot, pl.ds(pl.multiple_of(block * OUT_BLOCK, 8), OUT_BLOCK + 8)],
                gated,
                row_sems.at[4],
            ),
        ]

    def start(copies):
        for copy in copies:
            copy.start()

    def wait(copies):
        for copy in copies:
            copy.wait()

    def remote(src, dst, sems, i, device):
        return pltpu.make_async_remote_copy(
            src_ref=src,
            dst_ref=dst,
            send_sem=sems.at[0, i],
            recv_sem=sems.at[1, i],
            device_id=device,
            device_id_type=pl.DeviceIdType.MESH,
        )

    def block_at(k):
        return pl.ds(pl.multiple_of(k * OUT_BLOCK, OUT_BLOCK), OUT_BLOCK)

    def own_rows(first, size):
        return pl.ds(pl.multiple_of(core * half_rows + first, size), size)

    def hidden_grad(chip_part, far_part, hidden_part, cot_part):
        grad_mid = chip_part + far_part
        scale = rms_scale(hidden_part)
        unit = hidden_part * scale
        grad = cot_part.astype(jnp.float32) + norm_back(grad_mid, gain_ffn[...], unit, scale)
        return grad, grad_mid * unit

    def halo_copy(slot, device):
        return remote(halo_out.at[slot], halo_in.at[slot], halo_sems, slot, {"seq": device})

    head = 16
    for slot in range(slots):
        at = pl.ds(slot * slot_len, head)
        top = pl.ds(0, head)
        copies = [
            pltpu.make_async_copy(src.at[at], dst, row_sems.at[i])
            for i, (src, dst) in enumerate(
                (
                    (mid_chip, chip.at[top]),
                    (mid_far, far_rows.at[top]),
                    (hidden_hbm, hidden_rows.at[top]),
                    (proj_hbm, proj.at[top]),
                )
            )
        ]
        start(copies)
        wait(copies)
        grad, _ = hidden_grad(
            chip[top, :], far_rows[top, :], hidden_rows[top, :], cot[own_rows(slot * slot_len, head), :]
        )
        grad_mixed = dot_cols(grad.astype(jnp.bfloat16), w_out[...])
        halo_out[slot] = (grad_mixed * proj[top, width : 2 * width])[:8]
        pl.when(here > 0)(lambda slot=slot: halo_copy(slot, here - 1).start())

    slot, block, first = place_of(0)
    start(mid_loads(first))
    start(proj_loads(slot, block, first))

    @pl.when(here == last)
    def _():
        halo_in[...] = jnp.zeros_like(halo_in)

    @pl.when(here < last)
    def _():
        for slot in range(slots):
            halo_copy(slot, here + 1).wait_recv()

    def out_rows(first):
        return own_rows(first, OUT_BLOCK)

    def hand_out(target, first, i):
        at = out_rows(first)
        return (
            pltpu.make_async_copy(grad_tok, target.at[at], out_sems.at[0, 2 * blocks]),
            remote(grad_tok, target.at[at], out_sems, i, {"tp": sibling}),
        )

    @pl.loop(0, blocks)
    def _(n):
        slot, block, first = place_of(n)
        at = pl.ds(first, OUT_BLOCK)
        wait(mid_loads(first))

        @pl.loop(0, OUT_BLOCK // SUB_ROWS)
        def _(r):
            sub = pl.ds(pl.multiple_of(r * SUB_ROWS, SUB_ROWS), SUB_ROWS)
            whole = pl.ds(pl.multiple_of(first + r * SUB_ROWS, SUB_ROWS), SUB_ROWS)
            grad, for_gain = hidden_grad(
                chip[sub, :],
                far_rows[sub, :],
                hidden_rows[sub, :],
                cot[own_rows(first + r * SUB_ROWS, SUB_ROWS), :],
            )
            grad_hid[sub, :] = grad
            grad_mixer[whole, :] = grad.astype(jnp.bfloat16)
            small[1:2, :] += jnp.sum(for_gain, axis=0, keepdims=True)

        @pl.when(n < blocks - 1)
        def _():
            start(mid_loads(place_of(n + 1)[2]))

        mixed_buf[...] = dot_cols(grad_mixer[at, :], w_out[...])
        wait(proj_loads(slot, block, first))

        @pl.when(block == per_slot - 1)
        def _():
            conv_in[pl.ds(OUT_BLOCK, 8), :] = halo_in[slot]

        @pl.when(block < per_slot - 1)
        def _():
            conv_in[pl.ds(OUT_BLOCK, 8), :] = halo_keep[...]

        summer.tick(FIRST_MIXER_TICK + 2 * n, count)
        mask = valid_rows(core * slots + slot, block * OUT_BLOCK, OUT_BLOCK)

        @pl.loop(0, width // chans)
        def _(c):
            def cols(gate):
                return pl.ds(pl.multiple_of(gate * width + c * chans, chans), chans)

            here_cols = cols(0)
            pair, shard_at = shard_rows(c, first, OUT_BLOCK)
            in_gate, out_gate, conv_value = (proj[:, cols(g)] for g in range(3))
            grad_mixed = mixed_buf[:, here_cols]
            now = grad_mixed * out_gate
            conv_in[pl.ds(0, OUT_BLOCK), here_cols] = now
            seen = [gated[pl.ds(6 + j, OUT_BLOCK), here_cols] for j in range(3)]
            tap = [taps[j : j + 1, here_cols] for j in range(3)]
            conv_sum = tap[0] * seen[0] + tap[1] * seen[1] + tap[2] * seen[2]
            for j in range(3):
                small[2 + j : 3 + j, here_cols] += jnp.sum(now * seen[j], axis=0, keepdims=True)
            ggu[pair, shard_at, chans : 2 * chans] = (grad_mixed * conv_sum).astype(jnp.bfloat16)
            grad_gated = mask * (
                tap[2] * now
                + tap[1] * conv_in[pl.ds(1, OUT_BLOCK), here_cols]
                + tap[0] * conv_in[pl.ds(2, OUT_BLOCK), here_cols]
            )
            ggu[pair, shard_at, :chans] = (grad_gated * conv_value).astype(jnp.bfloat16)
            ggu[pair, shard_at, 2 * chans : 3 * chans] = (grad_gated * in_gate).astype(jnp.bfloat16)

        halo_keep[...] = conv_in[pl.ds(0, 8), :]

        @pl.when(n < blocks - 1)
        def _():
            start(proj_loads(*place_of(n + 1)))

        def shard_grad(j):
            pair, shard_at = shard_rows(j, first, OUT_BLOCK)
            return dot_cols(ggu[pair, shard_at, :], w_in[j][...])

        mixed_buf[...] = sum(shard_grad(j) for j in range(4))

        @pl.when(n > 0)
        def _():
            local, there = hand_out(tokens_out, place_of(n - 1)[2], n - 1)
            local.wait()
            there.wait_send()

        @pl.loop(0, OUT_BLOCK // SUB_ROWS)
        def _(r):
            sub = pl.ds(pl.multiple_of(r * SUB_ROWS, SUB_ROWS), SUB_ROWS)
            whole = pl.ds(pl.multiple_of(first + r * SUB_ROWS, SUB_ROWS), SUB_ROWS)
            inputs = tokens[whole, :].astype(jnp.float32)
            scale = rms_scale(inputs)
            unit = inputs * scale
            grad_in = mixed_buf[sub, :]
            grad_tok[sub, :] = grad_hid[sub, :] + norm_back(grad_in, gain_mix[...], unit, scale)
            small[0:1, :] += jnp.sum(grad_in * unit, axis=0, keepdims=True)

        start(hand_out(tokens_out, first, n))
        summer.tick(FIRST_MIXER_TICK + 2 * n + 1, count)

    in_blocks = width // OUT_BLOCK
    stages = [proj.at[:, i * wide : (i + 1) * wide] for i in range(3)]

    def to_near(src, dst, i):
        return remote(src, dst, weight_sems, i, {"tp": sibling})

    def near_in(m):
        cols = pl.ds(pl.multiple_of(lax.rem(m, 2) * wide, LANES), wide)
        return to_near(proj.at[:, cols], land_in.at[m], m)

    near_out = to_near(grad_hid, land_out, in_blocks)
    near_small = to_near(small, land_small, in_blocks + 1)

    def in_part(m, shard):
        pair, shard_at = shard_rows(shard, 0, half_rows)
        return dot_rows(normed[:, block_at(m)], ggu[pair, shard_at, :])

    def out_part(shard):
        at = pl.ds(pl.multiple_of(shard * chans, LANES), chans)
        return dot_rows(mixed[:, at], grad_mixer[...])

    near_small.start()
    first_tick = FIRST_MIXER_TICK + 2 * blocks

    @pl.loop(0, in_blocks)
    def _(m):
        @pl.when(m >= 2)
        def _():
            near_in(m - 2).wait_send()

        cols = pl.ds(pl.multiple_of(lax.rem(m, 2) * wide, LANES), wide)
        proj[:, cols] = in_part(m, sibling)
        near_in(m).start()
        summer.tick(first_tick + m, count)

    grad_hid[...] = out_part(sibling)
    near_out.start()

    @pl.loop(0, in_blocks)
    def _(m):
        near_in(m).wait_recv()
        fetch = pltpu.make_async_copy(land_in.at[m], stages[2], row_sems.at[0])
        fetch.start()
        part = in_part(m, tp_at)
        fetch.wait()
        for i in range(wide // LANES):
            to = pl.multiple_of(i * width + m * OUT_BLOCK, OUT_BLOCK)
            own[pl.ds(to, OUT_BLOCK), :] = (
                part[:, i * LANES : (i + 1) * LANES]
                + proj[:, 2 * wide + i * LANES : 2 * wide + (i + 1) * LANES]
            )

        summer.tick(first_tick + in_blocks + m, count)

    near_out.wait_recv()
    near_small.wait_recv()
    fetches = [
        pltpu.make_async_copy(land_out, mixed_buf, row_sems.at[0]),
        pltpu.make_async_copy(land_small, small_in, row_sems.at[1]),
    ]
    start(fetches)
    part = out_part(tp_at)
    wait(fetches)
    out_first = wide // LANES * width
    small_first = out_first + width // LANES * chans
    for p in range(width // LANES):
        cols = slice(p * LANES, (p + 1) * LANES)
        own[pl.ds(out_first + p * chans, chans), :] = part[:, cols] + mixed_buf[:, cols]
        own[pl.ds(small_first + 8 * p, 8), :] = small[:, cols] + small_in[:, cols]
    unused = 4 * HALF - 8 * (width // LANES)
    own[pl.ds(small_first + 4 * HALF - unused, unused), :] = jnp.zeros((unused, LANES), jnp.float32)

    local, there = hand_out(tokens_out, place_of(blocks - 1)[2], blocks - 1)
    local.wait()
    there.wait_send()
    done = first_tick + 2 * in_blocks
    pause = BLOCK_TICK

    @pl.loop(done, pause)
    def _(t):
        summer.tick(t, count)

    @pl.loop(0, blocks)
    def _(k):
        ffn_across(k).wait_recv()
        at = block_at(k)
        copies = [
            pltpu.make_async_copy(src.at[at], dst, row_sems.at[i])
            for i, (src, dst) in enumerate(((ffn_chip, chip), (ffn_far, far_rows), (hidden_hbm, hidden_rows)))
        ]
        start(copies)

        @pl.when(k > 0)
        def _():
            local, there = hand_out(block_out, (k - 1) * OUT_BLOCK, blocks + k - 1)
            local.wait()
            there.wait_send()

        wait(copies)
        grad_tok[...] = hidden_rows[...] + (chip[...] + far_rows[...])
        start(hand_out(block_out, k * OUT_BLOCK, blocks + k))
        summer.tick(pause + k, count)

    @pl.loop(pause + blocks, count + summer.P_LAGS[-1][1])
    def _(t):
        summer.tick(t, count)

    local, there = hand_out(block_out, (blocks - 1) * OUT_BLOCK, 2 * blocks - 1)
    local.wait()
    there.wait_send()

    @pl.loop(0, blocks)
    def _(k):
        ffn_across(k).wait_send()
        hand_out(tokens_out, place_of(k)[2], k)[1].wait_recv()
        hand_out(block_out, k * OUT_BLOCK, blocks + k)[1].wait_recv()

    for m in range(max(in_blocks - 2, 0), in_blocks):
        near_in(m).wait_send()
    near_out.wait_send()
    near_small.wait_send()

    @pl.when(here > 0)
    def _():
        for slot in range(slots):
            halo_copy(slot, here - 1).wait_send()


def back_both(hbm, vmem, slots, sum_cols, collective_id):
    normed_mid, _, w_gate, _, w_d, _, _, gated, _, _, _, _, _ = hbm
    rows, width = normed_mid.shape
    half_rows = rows // 2
    local = w_gate.shape[1]
    hidden = local // FFN_PARTS
    chans = 2 * hidden // 3
    blocks = half_rows // OUT_BLOCK
    in_blocks = width // OUT_BLOCK
    f32, low = jnp.float32, jnp.bfloat16
    half = jax.ShapeDtypeStruct((half_rows, width), f32)
    full = jax.ShapeDtypeStruct((rows, width), f32)
    block = pltpu.VMEM((OUT_BLOCK, width), f32)
    row8 = pltpu.VMEM((8, width), f32)
    anywhere = pl.BlockSpec(memory_space=pl.ANY)
    return pl.pallas_call(
        functools.partial(back_kernel, lax.axis_size("seq") // 2, slots),
        out_shape=[jax.ShapeDtypeStruct((width, sum_cols), f32)]
        + [full] * 2
        + [half] * 6
        + [
            jax.ShapeDtypeStruct((in_blocks, OUT_BLOCK, 2 * hidden), f32),
            jax.ShapeDtypeStruct((chans, width), f32),
            jax.ShapeDtypeStruct((8, width), f32),
        ],
        in_specs=[anywhere] * len(hbm)
        + [pl.BlockSpec(memory_space=pltpu.SMEM)]
        + [pl.BlockSpec(memory_space=pltpu.VMEM)] * (len(vmem) - 1),
        out_specs=[anywhere] * 12,
        scratch_shapes=[
            pltpu.VMEM((rows, width), low),
            pltpu.VMEM((rows, width), low),
            pltpu.VMEM((FFN_PARTS, width, 2 * hidden), low),
            pltpu.VMEM(w_d.shape, low),
            pltpu.VMEM((rows, local), low),
            pltpu.VMEM((FFN_PARTS, rows, 2 * hidden), low),
            pltpu.VMEM((3 * local * width // LANES, LANES), f32),
            pltpu.VMEM((2, OUT_BLOCK, width), f32),
            block,
            pltpu.VMEM((OUT_BLOCK, 3 * width), f32),
            pltpu.VMEM((OUT_BLOCK + 8, width), f32),
            block,
            pltpu.VMEM((OUT_BLOCK + 8, width), f32),
            block,
            block,
            pltpu.VMEM((slots, 8, width), f32),
            pltpu.VMEM((slots, 8, width), f32),
            row8,
            row8,
            row8,
            pltpu.SemaphoreType.DMA((3 + 2 * FFN_PARTS,)),
            pltpu.SemaphoreType.DMA((2, 2, blocks)),
            pltpu.SemaphoreType.DMA((2, 2, blocks)),
            pltpu.SemaphoreType.DMA,
            pltpu.SemaphoreType.DMA,
            pltpu.SemaphoreType.DMA((16,)),
            pltpu.SemaphoreType.DMA((5,)),
            pltpu.SemaphoreType.DMA((2, slots)),
            pltpu.SemaphoreType.DMA((2, in_blocks + 2)),
            pltpu.SemaphoreType.DMA((2, 2 * blocks + 1)),
        ]
        + seq_sum_scratch(),
        compiler_params=pltpu.CompilerParams(
            collective_id=collective_id, has_side_effects=True, vmem_limit_bytes=VMEM_LIMIT
        ),
        cost_estimate=pl.CostEstimate(
            flops=18 * rows * width * local, bytes_accessed=800 << 20, transcendentals=0
        ),
        name="back_both",
    )(*hbm, *vmem)


def front_kernel(places, slots, *refs):
    (w_in, w_out, taps, gain_mix, gain_ffn, lengths, tokens_hbm) = refs[0:7]
    (in_hbm, out_hbm, full_taps, mid_hbm, hidden_hbm, proj_hbm, gated_hbm) = refs[7:14]
    (normed_hbm, mixed_hbm) = refs[14:16]
    own_in, own_out, far_in, far_out, sib_in, sib_out, sibfar_in, sibfar_out = refs[16:24]
    own_taps, far_taps, sib_taps, sibfar_taps, share_in, share_out = refs[24:30]
    (full_in, full_out, tokens, normed, mixed, out_gate, gates, gated) = refs[30:38]
    (unit_out, unit_in, hidden) = refs[38:41]
    sends, recvs, once, halo_sems, gate_sems, unit_sems, keep_sems, mid_sems = refs[41:49]
    straight_sems = refs[49]
    here = lax.axis_index("seq")
    place, side = here // 2, lax.rem(here, 2)
    last = places - 1
    end = 2 * places - 1
    tp_at = lax.axis_index("tp")
    core = lax.rem(tp_at, 2)
    sibling = tp_at + 1 - 2 * core
    across = lax.rem(tp_at + 2, 4)
    far_sibling = sibling + across - tp_at
    in_rows = share_in.shape[0]
    straight = w_in.shape[1] - in_rows * 2 * places
    out_rows = w_out.shape[0] // (2 * places)
    chans = w_in.shape[2]
    rows, width = tokens.shape
    slot_len = rows // slots
    low = jnp.bfloat16

    load_tokens = pltpu.make_async_copy(
        tokens_hbm.at[pl.ds(pl.multiple_of(core * rows, rows), rows)], tokens, keep_sems.at[0]
    )
    load_tokens.start()
    barrier = pltpu.get_barrier_semaphore()

    def signal(device):
        pl.semaphore_signal(barrier, inc=1, device_id=device, device_id_type=pl.DeviceIdType.MESH)

    pl.when(here > 0)(lambda: signal({"seq": here - 1}))
    pl.when(here < end)(lambda: signal({"seq": here + 1}))
    ends = jnp.where(here > 0, 1, 0) + jnp.where(here < end, 1, 0)
    greet_seq(places, ({"tp": sibling}, {"tp": across}), ends)

    def shares(j):
        return (
            pl.ds(pl.multiple_of(j * in_rows, 8), in_rows),
            pl.ds(pl.multiple_of(j * out_rows, out_rows), out_rows),
        )

    def remote(src, dst, send, recv, device):
        return pltpu.make_async_remote_copy(
            src_ref=src,
            dst_ref=dst,
            send_sem=send,
            recv_sem=recv,
            device_id=device,
            device_id_type=pl.DeviceIdType.MESH,
        )

    def copies(source, target, j, kind, device):
        for i, at in enumerate(shares(j)):
            yield remote(
                source[i] if kind == 0 else source[i].at[at],
                target[i].at[at],
                sends.at[kind, i, j],
                recvs.at[0 if kind < 4 else 1, i, j],
                device,
            )

    share, far, sibfar = (share_in, share_out), (far_in, far_out), (sibfar_in, sibfar_out)

    def across_share():
        return copies(share, far, here, 0, {"tp": across})

    def to_right(j):
        return copies(far, far, j, 1, {"seq": here + 2})

    def to_left(j):
        return copies(far, far, j, 2, {"seq": here - 2})

    def to_side(j):
        return copies(far, far, j, 3, {"seq": here + 1 - 2 * side})

    def to_sibling(j):
        return copies(far, sibfar, j, 4, {"tp": sibling})

    def straight_rows(q):
        size = straight // STRAIGHT_COPIES
        first = w_in.shape[1] - straight + q * size
        return pl.ds(pl.multiple_of(first, 8), size)

    def straight_across(q):
        at = straight_rows(q)
        return remote(
            own_in.at[at], far_in.at[at], straight_sems.at[0, q], straight_sems.at[1, q],
            {"tp": across},
        )

    def straight_sibling(q):
        at = straight_rows(q)
        return remote(
            far_in.at[at], sibfar_in.at[at], straight_sems.at[2, q], straight_sems.at[3, q],
            {"tp": sibling},
        )

    def pass_straight(q):
        straight_across(q).wait_recv()
        straight_sibling(q).start()

    def start(group):
        for copy in group:
            copy.start()

    def arrived(group):
        for copy in group:
            copy.wait_recv()

    def left_source(group):
        for copy in group:
            copy.wait_send()

    def relay(incoming, j, on_right, on_left):
        onward = zip(incoming, to_right(j), to_left(j), to_side(j), to_sibling(j))
        for copy, right, left, aside, near in onward:
            copy.wait_recv()
            if on_right:
                pl.when(place < last)(right.start)
            if on_left:
                pl.when(place > 0)(left.start)
            aside.start()
            near.start()

    def single(i, src, dst, device):
        return remote(src, dst, once.at[0, i], once.at[1, i], device)

    in_at, out_at = shares(here)
    for g in range(3):
        share_in[:, g * chans : (g + 1) * chans] = w_in[g, in_at, :].astype(jnp.float32)
    share_out[...] = w_out[out_at, :].astype(jnp.float32)
    start(across_share())
    own_taps[...] = jnp.zeros_like(own_taps)
    own_taps[0:3, :] = taps[...]
    taps_far = single(0, own_taps, far_taps, {"tp": across})
    taps_sib = single(1, own_taps, sib_taps, {"tp": sibling})
    taps_sibfar = single(2, far_taps, sibfar_taps, {"tp": sibling})
    for g in range(3):
        own_in[:, g * chans : (g + 1) * chans] = w_in[g].astype(jnp.float32)
    own_out[...] = w_out[...].astype(jnp.float32)
    in_sib = single(3, own_in, sib_in, {"tp": sibling})
    out_sib = single(4, own_out, sib_out, {"tp": sibling})
    for copy in (taps_far, taps_sib, in_sib, out_sib):
        copy.start()
    for q in range(STRAIGHT_COPIES):
        straight_across(q).start()

    def gate_cols(g, index):
        return pl.ds(pl.multiple_of(g * width + index * chans, LANES), chans)

    def place_shard(shard_in, shard_out, shard_taps, index):
        for g in range(3):
            full_in[:, gate_cols(g, index)] = shard_in[:, g * chans : (g + 1) * chans].astype(low)
        at = pl.ds(pl.multiple_of(index * chans, chans), chans)
        full_out[at, :] = shard_out[...].astype(low)
        full_taps[:, gate_cols(0, index)] = shard_taps[...]

    def gate_out(turn, index, g):
        if g == 1:
            return pltpu.make_async_copy(
                out_gate.at[:, gate_cols(0, index)],
                proj_hbm.at[:, gate_cols(1, index)],
                gate_sems.at[turn, 1],
            )
        return pltpu.make_async_copy(
            gates.at[turn % 2, g // 2], proj_hbm.at[:, gate_cols(g, index)], gate_sems.at[turn, g]
        )

    def halo(turn, index, slot):
        return remote(
            gated.at[slot, pl.ds(slot_len, 8), gate_cols(0, index)],
            gated.at[slot, pl.ds(0, 8), gate_cols(0, index)],
            halo_sems.at[0, turn, slot],
            halo_sems.at[1, turn, slot],
            {"seq": here + 1},
        )

    order = (tp_at, sibling, across, far_sibling)

    def project(turn):
        index = order[turn]
        cols = gate_cols(0, index)
        if turn >= 2:
            gate_out(turn - 2, order[turn - 2], 0).wait()
            gate_out(turn - 2, order[turn - 2], 2).wait()

        @pl.loop(0, slots)
        def _(s):
            at = pl.ds(pl.multiple_of(s * slot_len, slot_len), slot_len)

            def gate(g):
                return jnp.dot(
                    normed[at, :], full_in[:, gate_cols(g, index)],
                    preferred_element_type=jnp.float32,
                )

            at_pos = lax.broadcasted_iota(jnp.int32, (slot_len, 1), 0) + here * slot_len
            mask = (at_pos < lengths[core * slots + s]).astype(jnp.float32)
            in_gate, value = gate(0), gate(2)
            gates[turn % 2, 0, at, :] = in_gate
            gates[turn % 2, 1, at, :] = value
            gated[s, pl.ds(8, slot_len), cols] = mask * in_gate * value
            out_gate[at, cols] = gate(1)

        for g in range(3):
            gate_out(turn, index, g).start()

        @pl.when(here < end)
        def _():
            for slot in range(slots):
                halo(turn, index, slot).start()

    def convolve(turn):
        index = order[turn]
        cols = gate_cols(0, index)

        @pl.when(here > 0)
        def _():
            for slot in range(slots):
                halo(turn, index, slot).wait_recv()

        @pl.loop(0, slots)
        def _(s):
            at = pl.ds(pl.multiple_of(s * slot_len, slot_len), slot_len)
            seen = [gated[s, pl.ds(6 + j, slot_len), cols] for j in range(3)]
            tap = [full_taps[j : j + 1, cols] for j in range(3)]
            conv_sum = tap[0] * seen[0] + tap[1] * seen[1] + tap[2] * seen[2]
            mixed[at, cols] = (out_gate[at, cols] * conv_sum).astype(low)

    @pl.when(here == 0)
    def _():
        for slot in range(slots):
            gated[slot, pl.ds(0, 8), :] = jnp.zeros((8, width), jnp.float32)

    load_tokens.wait()

    @pl.loop(0, rows // SUB_ROWS)
    def _(r):
        at = pl.ds(pl.multiple_of(r * SUB_ROWS, SUB_ROWS), SUB_ROWS)
        inputs = tokens[at, :].astype(jnp.float32)
        normed[at, :] = (gain_mix[...] * (inputs * rms_scale(inputs))).astype(low)

    keep_normed = pltpu.make_async_copy(normed, normed_hbm, keep_sems.at[0])
    keep_normed.start()
    place_shard(own_in, own_out, own_taps, tp_at)
    project(0)

    relay(across_share(), here, True, True)
    taps_far.wait_recv()
    taps_sibfar.start()
    in_sib.wait_recv()
    out_sib.wait_recv()
    taps_sib.wait_recv()
    place_shard(sib_in, sib_out, sib_taps, sibling)
    project(1)

    def from_side(q):
        j = 2 * q + 1 - side
        arrived(to_side(j))
        start(to_sibling(j))

    @pl.loop(1, places)
    def _(d):
        @pl.when(place - d >= 0)
        def _():
            j = here - 2 * d
            relay(to_right(j), j, True, False)

        @pl.when(place + d <= last)
        def _():
            j = here + 2 * d
            relay(to_left(j), j, False, True)

        @pl.when(d == 1)
        def _():
            from_side(place)
            convolve(0)
            convolve(1)

        pl.when(place - d >= 0)(lambda: from_side(place - d))
        pl.when(place + d <= last)(lambda: from_side(place + d))
        pl.when(d <= STRAIGHT_COPIES)(lambda: pass_straight(d - 1))

    for q in range(min(last, STRAIGHT_COPIES), STRAIGHT_COPIES):
        pass_straight(q)

    place_shard(far_in, far_out, far_taps, across)
    project(2)
    taps_sibfar.wait_recv()

    @pl.loop(0, 2 * places)
    def _(j):
        arrived(to_sibling(j))

    for q in range(STRAIGHT_COPIES):
        straight_sibling(q).wait_recv()
    place_shard(sibfar_in, sibfar_out, sibfar_taps, far_sibling)
    project(3)
    keep_in = pltpu.make_async_copy(full_in, in_hbm, keep_sems.at[1])
    keep_out = pltpu.make_async_copy(full_out, out_hbm, keep_sems.at[2])
    keep_in.start()
    keep_out.start()
    convolve(2)
    convolve(3)
    keep_gated = pltpu.make_async_copy(gated, gated_hbm, keep_sems.at[3])
    keep_mixed = pltpu.make_async_copy(mixed, mixed_hbm, keep_sems.at[4])
    keep_gated.start()
    keep_mixed.start()
    keep_normed.wait()

    blocks = rows // OUT_BLOCK

    def block_at(k, first=0):
        return pl.ds(pl.multiple_of(first + k * OUT_BLOCK, OUT_BLOCK), OUT_BLOCK)

    def unit_copy(k):
        return remote(
            unit_out.at[block_at(k)], unit_in.at[block_at(k)],
            unit_sems.at[0, k], unit_sems.at[1, k], {"tp": sibling},
        )

    def hidden_copy(k):
        return pltpu.make_async_copy(
            hidden.at[lax.rem(k, 2)], hidden_hbm.at[block_at(k)], mid_sems.at[0, lax.rem(k, 2)]
        )

    def mid_copy(half, held, whose, k):
        return pltpu.make_async_copy(
            held.at[block_at(k)], mid_hbm.at[block_at(k, whose * rows)], mid_sems.at[half, k]
        )

    @pl.loop(0, blocks)
    def _(k):
        slot = lax.rem(k, 2)
        at = block_at(k)
        pl.when(k >= 2)(lambda: hidden_copy(k - 2).wait())
        hidden[slot] = jnp.dot(mixed[at, :], full_out[...], preferred_element_type=jnp.float32)

        @pl.loop(0, OUT_BLOCK // SUB_ROWS)
        def _(r):
            sub = pl.ds(pl.multiple_of(r * SUB_ROWS, SUB_ROWS), SUB_ROWS)
            whole = pl.ds(pl.multiple_of(k * OUT_BLOCK + r * SUB_ROWS, SUB_ROWS), SUB_ROWS)
            hidden_rows = tokens[whole, :].astype(jnp.float32) + hidden[slot, sub, :]
            hidden[slot, sub, :] = hidden_rows
            unit = hidden_rows * rms_scale(hidden_rows)
            unit_out[whole, :] = unit
            normed[whole, :] = (gain_ffn[...] * unit).astype(low)

        unit_copy(k).start()
        hidden_copy(k).start()
        mid_copy(1, normed, core, k).start()

    keep_mixed.wait()

    @pl.loop(0, blocks)
    def _(k):
        unit_copy(k).wait_recv()

        @pl.loop(0, OUT_BLOCK // SUB_ROWS)
        def _(r):
            whole = pl.ds(pl.multiple_of(k * OUT_BLOCK + r * SUB_ROWS, SUB_ROWS), SUB_ROWS)
            mixed[whole, :] = (gain_ffn[...] * unit_in[whole, :]).astype(low)

        mid_copy(2, mixed, 1 - core, k).start()

    @pl.loop(0, blocks)
    def _(k):
        unit_copy(k).wait_send()
        mid_copy(1, normed, core, k).wait()
        mid_copy(2, mixed, 1 - core, k).wait()

    for k in range(max(blocks - 2, 0), blocks):
        hidden_copy(k).wait()
    keep_in.wait()
    keep_out.wait()
    keep_gated.wait()
    for turn in range(4):
        for g in range(3):
            if turn >= 2 or g == 1:
                gate_out(turn, order[turn], g).wait()

    @pl.when(here < end)
    def _():
        for turn in range(4):
            for slot in range(slots):
                halo(turn, order[turn], slot).wait_send()

    left_source(across_share())
    for q in range(STRAIGHT_COPIES):
        straight_across(q).wait_send()
        straight_sibling(q).wait_send()
    for copy in (taps_far, taps_sib, taps_sibfar, in_sib, out_sib):
        copy.wait_send()

    @pl.loop(0, places)
    def _(q):
        j = 2 * q + side
        left_source(to_side(j))
        pl.when((q <= place) & (place < last))(lambda: left_source(to_right(j)))
        pl.when((q >= place) & (place > 0))(lambda: left_source(to_left(j)))
        left_source(to_sibling(j))
        left_source(to_sibling(2 * q + 1 - side))


def mixer_front(w_in, w_out, taps, gain_mix, gain_ffn, lengths, tokens, slots, collective_id):
    width, _, chans = w_in.shape
    rows = tokens.shape[0] // 2
    count = lax.axis_size("seq")
    group = lax.axis_size("tp")
    f32, low = jnp.float32, jnp.bfloat16
    blocks = rows // OUT_BLOCK
    pair = [pltpu.VMEM((width, 3 * chans), f32), pltpu.VMEM((chans, width), f32)]
    whole = pl.BlockSpec(memory_space=pltpu.VMEM)
    anywhere = pl.BlockSpec(memory_space=pl.ANY)
    padded = (slots, rows // slots + 8, width)
    return pl.pallas_call(
        functools.partial(front_kernel, count // 2, slots),
        out_shape=[
            jax.ShapeDtypeStruct((width, 3 * chans * group), low),
            jax.ShapeDtypeStruct((chans * group, width), low),
            jax.ShapeDtypeStruct((8, chans * group), f32),
            jax.ShapeDtypeStruct((2 * rows, width), low),
            jax.ShapeDtypeStruct((rows, width), f32),
            jax.ShapeDtypeStruct((rows, 3 * width), f32),
            jax.ShapeDtypeStruct(padded, f32),
            jax.ShapeDtypeStruct((rows, width), low),
            jax.ShapeDtypeStruct((rows, width), low),
        ],
        in_specs=[whole] * 5 + [pl.BlockSpec(memory_space=pltpu.SMEM), anywhere],
        out_specs=[anywhere] * 2 + [whole] + [anywhere] * 6,
        scratch_shapes=pair * 4
        + [pltpu.VMEM((8, chans), f32)] * 4
        + [
            pltpu.VMEM((width * 8 // 16 // count // 8 * 8, 3 * chans), f32),
            pltpu.VMEM((chans // count, width), f32),
            pltpu.VMEM((width, 3 * chans * group), low),
            pltpu.VMEM((chans * group, width), low),
            pltpu.VMEM((rows, width), low),
            pltpu.VMEM((rows, width), low),
            pltpu.VMEM((rows, width), low),
            pltpu.VMEM((rows, width), f32),
            pltpu.VMEM((2, 2, rows, chans), f32),
            pltpu.VMEM(padded, f32),
            pltpu.VMEM((rows, width), f32),
            pltpu.VMEM((rows, width), f32),
            pltpu.VMEM((2, OUT_BLOCK, width), f32),
            pltpu.SemaphoreType.DMA((5, 2, count)),
            pltpu.SemaphoreType.DMA((2, 2, count)),
            pltpu.SemaphoreType.DMA((2, 5)),
            pltpu.SemaphoreType.DMA((2, 4, slots)),
            pltpu.SemaphoreType.DMA((4, 3)),
            pltpu.SemaphoreType.DMA((2, blocks)),
            pltpu.SemaphoreType.DMA((5,)),
            pltpu.SemaphoreType.DMA((3, blocks)),
            pltpu.SemaphoreType.DMA((4, STRAIGHT_COPIES)),
        ],
        compiler_params=pltpu.CompilerParams(
            collective_id=collective_id, has_side_effects=True, vmem_limit_bytes=VMEM_LIMIT
        ),
        name="mixer_front",
    )(
        w_in.transpose(1, 0, 2),
        w_out,
        taps,
        gain_mix,
        gain_ffn,
        lengths,
        tokens,
    )


def finish_kernel(slots, chans, hidden, *refs):
    (sums, tokens_in, block_in, lengths) = refs[0:4]
    (block_out, tokens_out, gain_a, gain_b, g_in, g_conv, g_out, g_gate, g_up, g_down) = refs[4:14]
    (held, tokens, block, rounded, turned, gains) = refs[14:20]
    (in_sems, block_sems, turn_sems, out_sems) = refs[20:24]
    rows, width = block_in.shape
    slot_len = rows // slots
    here = lax.axis_index("seq")
    tp_at = lax.axis_index("tp")
    first = 3 * hidden
    out_first = first + 3 * chans
    small_first = out_first + chans
    blocks = rows // OUT_BLOCK
    turns = hidden // LANES
    half_rows = rows // 2

    def cols(start, size):
        return (slice(None), slice(start, start + size))

    parts = [cols(i * hidden, hidden) for i in range(3)] + [cols(first, held.shape[1] - first)]
    halves = [slice(0, half_rows), slice(half_rows, rows)]
    part_loads = [
        pltpu.make_async_copy(sums.at[at], held.at[at], in_sems.at[i]) for i, at in enumerate(parts)
    ]
    token_loads = [
        pltpu.make_async_copy(tokens_in.at[at], tokens.at[at], in_sems.at[4 + i])
        for i, at in enumerate(halves)
    ]

    def block_at(k):
        return pl.ds(pl.multiple_of(k * OUT_BLOCK, OUT_BLOCK), OUT_BLOCK)

    def block_load(k):
        return pltpu.make_async_copy(
            block_in.at[block_at(k)], block.at[block_at(k)], block_sems.at[0, k]
        )

    def block_store(k):
        return pltpu.make_async_copy(
            rounded.at[block_at(k)], block_out.at[block_at(k)], block_sems.at[1, k]
        )

    def panel_at(k):
        return pl.ds(pl.multiple_of(k * LANES, LANES), LANES)

    def turn_store(k):
        at = panel_at(k)
        return pltpu.make_async_copy(turned.at[at], g_down.at[at], turn_sems.at[k])

    stores = []

    def store(src, dst):
        copy = pltpu.make_async_copy(src, dst, out_sems.at[len(stores)])
        copy.start()
        stores.append(copy)

    part_loads[2].start()

    @pl.loop(0, blocks)
    def _(k):
        block_load(k).start()

    for load in (*token_loads, part_loads[0], part_loads[1], part_loads[3]):
        load.start()

    part_loads[2].wait()

    @pl.loop(0, turns)
    def _(k):
        from_cols = pl.ds(pl.multiple_of(2 * hidden + k * LANES, LANES), LANES)
        turned[panel_at(k), :] = held[:, from_cols].T
        turn_store(k).start()

    @pl.loop(0, blocks)
    def _(k):
        block_load(k).wait()
        per_slot = slot_len // OUT_BLOCK
        at = lax.broadcasted_iota(jnp.int32, (OUT_BLOCK, 1), 0)
        at = at + (here * slot_len + lax.rem(k, per_slot) * OUT_BLOCK)
        mask = (at < lengths[k // per_slot]).astype(jnp.float32)
        rounded[block_at(k), :] = (mask * block[block_at(k), :]).astype(jnp.bfloat16)
        block_store(k).start()

    for load, at in zip(token_loads, halves):
        load.wait()
        store(tokens.at[at], tokens_out.at[at])
    for i, target in ((0, g_gate), (1, g_up)):
        part_loads[i].wait()
        store(held.at[parts[i]], target)
    part_loads[3].wait()
    for g in range(3):
        store(held.at[cols(first + g * chans, chans)], g_in.at[g])
    per_col = width // chans
    for p in range(width // LANES):
        q, r = p // per_col, p % per_col
        at = (slice(r * chans, (r + 1) * chans), slice(out_first + q * LANES, out_first + (q + 1) * LANES))
        store(held.at[at], g_out.at[cols(p * LANES, LANES)])
        gains[cols(p * LANES, LANES)] = held[8 * p : 8 * p + 8, small_first:]
    own = pl.ds(pl.multiple_of(tp_at * chans, LANES), chans)
    g_conv[...] = gains[2:5, own]
    gain_a[...] = gains[0:1, :]
    gain_b[...] = gains[1:2, :]
    for copy in stores:
        copy.wait()

    @pl.loop(0, turns)
    def _(k):
        turn_store(k).wait()

    @pl.loop(0, blocks)
    def _(k):
        block_store(k).wait()


def finish(sums, tokens_grad, block_sum, lengths, chans, hidden):
    rows, width = block_sum.shape
    f32 = jnp.float32
    anywhere = pl.BlockSpec(memory_space=pl.ANY)
    whole = pl.BlockSpec(memory_space=pltpu.VMEM)
    blocks = rows // OUT_BLOCK
    return pl.pallas_call(
        functools.partial(finish_kernel, lengths.shape[0], chans, hidden),
        out_shape=[
            jax.ShapeDtypeStruct((rows, width), jnp.bfloat16),
            jax.ShapeDtypeStruct((rows, width), f32),
            jax.ShapeDtypeStruct((1, width), f32),
            jax.ShapeDtypeStruct((1, width), f32),
            jax.ShapeDtypeStruct((3, width, chans), f32),
            jax.ShapeDtypeStruct((3, chans), f32),
            jax.ShapeDtypeStruct((chans, width), f32),
            jax.ShapeDtypeStruct((width, hidden), f32),
            jax.ShapeDtypeStruct((width, hidden), f32),
            jax.ShapeDtypeStruct((hidden, width), f32),
        ],
        in_specs=[anywhere] * 3 + [pl.BlockSpec(memory_space=pltpu.SMEM)],
        out_specs=[anywhere] * 2 + [whole, whole, anywhere, whole] + [anywhere] * 4,
        scratch_shapes=[
            pltpu.VMEM(sums.shape, f32),
            pltpu.VMEM((rows, width), f32),
            pltpu.VMEM((rows, width), f32),
            pltpu.VMEM((rows, width), jnp.bfloat16),
            pltpu.VMEM((hidden, width), f32),
            pltpu.VMEM((8, width), f32),
            pltpu.SemaphoreType.DMA((6,)),
            pltpu.SemaphoreType.DMA((2, blocks)),
            pltpu.SemaphoreType.DMA((hidden // LANES,)),
            pltpu.SemaphoreType.DMA((7 + width // LANES,)),
        ],
        compiler_params=pltpu.CompilerParams(vmem_limit_bytes=VMEM_LIMIT),
        name="finish",
    )(sums, tokens_grad, block_sum, lengths)


def per_device(
    tokens, lengths, gain_mix, w_in, conv_weight, w_out, gain_ffn, w_gate, w_up, w_down, cotangent
):
    slot_count, local_len, width = tokens.shape
    chans = w_in.shape[2]
    half_slots = slot_count // 2
    row_count = slot_count * local_len

    token_rows = tokens.reshape(row_count, width)
    cot_rows = cotangent.reshape(row_count, width)
    gains = gain_mix.reshape(1, width), gain_ffn.reshape(1, width)
    w_in_all, w_out_all, taps, normed_mid, hidden_res, projected, gated_rows, normed_in, mixed = (
        mixer_front(w_in, w_out, conv_weight, *gains, lengths, token_rows, half_slots, 3)
    )
    mixer_cols = 4 * chans
    sum_cols = FFN_PANELS * LANES + mixer_cols + LANES
    sums, grad_tokens, block_sum = back_both(
        (
            normed_mid,
            cot_rows,
            w_gate,
            w_up,
            w_down,
            hidden_res,
            projected,
            gated_rows,
            normed_in,
            mixed,
            w_in_all,
            w_out_all,
            token_rows,
        ),
        (lengths, taps, *gains),
        half_slots,
        sum_cols,
        1,
    )[:3]
    block_out, grad_tokens, g_gain_mix, g_gain_ffn, g_in, g_conv, g_out, g_gate, g_up, g_down = finish(
        sums, grad_tokens, block_sum, lengths, chans, w_gate.shape[1]
    )
    return (
        block_out.reshape(slot_count, local_len, width),
        grad_tokens.reshape(slot_count, local_len, width),
        g_gain_mix.reshape(width),
        g_in.transpose(1, 0, 2),
        g_conv,
        g_out,
        g_gain_ffn.reshape(width),
        g_gate,
        g_up,
        g_down,
    )


def solution(mesh):
    rows, cols = P("tp", None), P(None, "tp")
    tokens, whole, stacked = P(None, "seq", None), P(), P(None, None, "tp")
    return jax.shard_map(
        per_device,
        mesh=mesh,
        in_specs=(
            tokens, whole, whole, stacked, cols, rows, whole, cols, cols, rows, tokens,
        ),
        out_specs=(
            tokens, tokens, whole, stacked, cols, rows, whole, cols, cols, rows,
        ),
        check_vma=False,
    )
```

```python
import functools

import jax
import jax.numpy as jnp
from jax import lax
from jax.experimental import pallas as pl
from jax.experimental.pallas import tpu as pltpu
from jax.sharding import PartitionSpec as P

NORM_EPS = 1e-05
LANES = 128
VMEM_LIMIT = 64 << 20
HALF = 128
SLOTS_IN_FLIGHT = 10


def rms_scale(values):
    return lax.rsqrt(jnp.mean(values * values, axis=-1, keepdims=True) + NORM_EPS)


def dot_rows(left, right):
    return lax.dot_general(
        left, right, (((0,), (0,)), ((), ())), preferred_element_type=jnp.float32
    )


def dot_cols(left, right):
    return lax.dot_general(
        left, right, (((1,), (1,)), ((), ())), preferred_element_type=jnp.float32
    )


def greet_seq(places, others=(), more=0):
    barrier = pltpu.get_barrier_semaphore()
    here = lax.axis_index("seq")
    place, side = here // 2, lax.rem(here, 2)

    def signal(device):
        pl.semaphore_signal(
            barrier, inc=1, device_id=device, device_id_type=pl.DeviceIdType.MESH
        )

    signal({"seq": here + 1 - 2 * side})
    for other in others:
        signal(other)
    pl.when(place > 0)(lambda: signal({"seq": here - 2}))
    pl.when(place < places - 1)(lambda: signal({"seq": here + 2}))
    ends = jnp.where(place > 0, 1, 0) + jnp.where(place < places - 1, 1, 0)
    pl.semaphore_wait(barrier, 1 + len(others) + ends + more)


class SeqSum:
    def __init__(self, places, own, out, scratch):
        self.places, self.own, self.out = places, own, out
        self.y_in, self.p_left, self.p_right, self.p_acc = scratch[0:4]
        self.q_left, self.q_right, self.q_acc, self.q_in = scratch[4:8]
        self.sems = scratch[8]
        here = lax.axis_index("seq")
        self.place, self.side = here // 2, here % 2

    def remote(self, src, dst, slot, send, recv, place, side):
        return pltpu.make_async_remote_copy(
            src_ref=src,
            dst_ref=dst,
            send_sem=self.sems.at[send, slot],
            recv_sem=self.sems.at[recv, slot],
            device_id={"seq": place * 2 + side},
            device_id_type=pl.DeviceIdType.MESH,
        )

    def chain(self, root):
        last = self.places - 1
        left = jnp.maximum(self.place - 1, 0)
        right = jnp.minimum(self.place + 1, last)
        from_left = (self.place <= root) & (self.place > 0)
        from_right = (self.place >= root) & (self.place < last)
        return left, right, from_left, from_right

    def own_base(self, k):
        held = self.own.shape[0] // (4 * HALF)
        return pl.multiple_of(lax.rem(k, held) * 4 * HALF, 4 * HALF)

    def out_at(self, k, first, size):
        per_panel = self.out.shape[0] // (4 * HALF)
        panel, part = place_in_sums(k, per_panel)
        row = part * 4 * HALF + first
        return self.out.at[
            pl.ds(pl.multiple_of(row, size), size), pl.ds(pl.multiple_of(panel * LANES, LANES), LANES)
        ]

    def p_stage(self, which, k):
        place, side = self.place, self.side
        own = self.own
        slot = lax.rem(k, SLOTS_IN_FLIGHT)
        base = self.own_base(k)
        mine = pl.ds(pl.multiple_of(base + side * HALF, HALF), HALF)
        theirs = pl.ds(pl.multiple_of(base + (1 - side) * HALF, HALF), HALF)
        out_mine = self.out_at(k, side * HALF, HALF)
        root = self.places // 2 - 1 + lax.rem(k, 2)
        left, right, from_left, from_right = self.chain(root)
        acc, y_in = self.p_acc.at[slot], self.y_in.at[slot]
        from_l, from_r = self.p_left.at[slot], self.p_right.at[slot]
        remote = functools.partial(functools.partial, self.remote)

        to_side = remote(own.at[theirs], y_in, slot, 0, 1, place, 1 - side)
        up_right = remote(acc, from_l, slot, 2, 3, right, side)
        up_left = remote(acc, from_r, slot, 2, 4, left, side)

        def down(src):
            return (
                remote(src, out_mine, slot, 5, 7, left, side),
                remote(src, out_mine, slot, 6, 7, right, side),
                remote(src, out_mine, slot, 8, 9, place, 1 - side),
            )

        def keep():
            return pltpu.make_async_copy(acc, out_mine, self.sems.at[10, slot])

        def hand_down(src):
            down_left, down_right, down_side = down(src)
            down_side().start()
            pl.when(from_left)(lambda: down_left().start())
            pl.when(from_right)(lambda: down_right().start())

        if which == "split":
            to_side().start()

        if which == "up":
            to_side().wait_recv()
            acc[...] = own[mine, :] + y_in[...]

            @pl.when(place < root)
            def _():
                @pl.when(from_left)
                def _():
                    up_right().wait_recv()
                    acc[...] += from_l[...]

                up_right().start()

            @pl.when(place > root)
            def _():
                @pl.when(from_right)
                def _():
                    up_left().wait_recv()
                    acc[...] += from_r[...]

                up_left().start()

        if which == "root":

            @pl.when(place == root)
            def _():
                @pl.when(from_left)
                def _():
                    up_right().wait_recv()
                    acc[...] += from_l[...]

                @pl.when(from_right)
                def _():
                    up_left().wait_recv()
                    acc[...] += from_r[...]

                hand_down(acc)
                keep().start()

        if which == "down":

            @pl.when(place != root)
            def _():
                down(acc)[0]().wait_recv()
                hand_down(out_mine)

        if which == "end":
            down_left, down_right, down_side = down(acc)
            down_side().wait()
            to_side().wait_send()
            pl.when(from_left)(lambda: down_left().wait_send())
            pl.when(from_right)(lambda: down_right().wait_send())
            pl.when(place == root)(lambda: keep().wait())
            pl.when(place != root)(lambda: up_left().wait_send())

    def q_stage(self, which, k):
        place, side = self.place, self.side
        own = self.own
        slot = lax.rem(k, SLOTS_IN_FLIGHT)
        base = self.own_base(k)
        wide = pl.ds(pl.multiple_of(base + 2 * HALF, 2 * HALF), 2 * HALF)
        out_wide = self.out_at(k, 2 * HALF, 2 * HALF)
        root = self.places // 2 - lax.rem(k, 2)
        left, right, from_left, from_right = self.chain(root)
        acc, side_in = self.q_acc.at[slot], self.q_in.at[slot]
        from_l, from_r = self.q_left.at[slot], self.q_right.at[slot]
        remote = functools.partial(functools.partial, self.remote)

        up_right = remote(acc, from_l, slot, 11, 12, right, side)
        up_left = remote(acc, from_r, slot, 11, 13, left, side)
        to_side = remote(acc, side_in, slot, 14, 15, place, 1 - side)

        def down(src):
            return (
                remote(src, out_wide, slot, 16, 18, left, side),
                remote(src, out_wide, slot, 17, 18, right, side),
            )

        def keep():
            return pltpu.make_async_copy(side_in, out_wide, self.sems.at[19, slot])

        def hand_down(src):
            down_left, down_right = down(src)
            pl.when(from_left)(lambda: down_left().start())
            pl.when(from_right)(lambda: down_right().start())

        if which == "up":
            acc[...] = own[wide, :]

            @pl.when(place < root)
            def _():
                @pl.when(from_left)
                def _():
                    up_right().wait_recv()
                    acc[...] += from_l[...]

                up_right().start()

            @pl.when(place > root)
            def _():
                @pl.when(from_right)
                def _():
                    up_left().wait_recv()
                    acc[...] += from_r[...]

                up_left().start()

        if which == "root":

            @pl.when(place == root)
            def _():
                @pl.when(from_left)
                def _():
                    up_right().wait_recv()
                    acc[...] += from_l[...]

                @pl.when(from_right)
                def _():
                    up_left().wait_recv()
                    acc[...] += from_r[...]

                to_side().start()

        if which == "side":

            @pl.when(place == root)
            def _():
                to_side().wait_recv()
                side_in[...] += acc[...]
                hand_down(side_in)
                keep().start()

        if which == "down":

            @pl.when(place != root)
            def _():
                down(acc)[0]().wait_recv()
                hand_down(out_wide)

        if which == "end":
            down_left, down_right = down(acc)
            pl.when(from_left)(lambda: down_left().wait_send())
            pl.when(from_right)(lambda: down_right().wait_send())

            @pl.when(place == root)
            def _():
                to_side().wait_send()
                keep().wait()

            pl.when(place != root)(lambda: up_left().wait_send())

    P_LAGS = (("split", 0, 0), ("up", 2, 1), ("root", 3, 3), ("down", 6, 7), ("end", 9, 9))
    Q_LAGS = (("up", 1, 0), ("root", 3, 3), ("side", 4, 4), ("down", 6, 7), ("end", 9, 9))

    def tick(self, t, count):
        middle = (self.place == self.places // 2) | (self.place == self.places // 2 - 1)
        for stage, lags in ((self.p_stage, self.P_LAGS), (self.q_stage, self.Q_LAGS)):
            for which, mid_lag, outer_lag in lags:
                k = t - jnp.where(middle, mid_lag, outer_lag)

                @pl.when((k >= 0) & (k < count))
                def _(stage=stage, which=which, k=k):
                    stage(which, k)

    def run(self, count):
        @pl.loop(0, count + self.P_LAGS[-1][1])
        def _(t):
            self.tick(t, count)


def seq_sum_scratch():
    half = pltpu.VMEM((SLOTS_IN_FLIGHT, HALF, LANES), jnp.float32)
    wide = pltpu.VMEM((SLOTS_IN_FLIGHT, 2 * HALF, LANES), jnp.float32)
    return [half] * 4 + [wide] * 4 + [pltpu.SemaphoreType.DMA((20, SLOTS_IN_FLIGHT))]


SUB_ROWS = 64
STRAIGHT_COPIES = 4
FIRST_MIXER_TICK = 36
BLOCK_TICK = 56
FFN_PANELS = 27
FFN_PARTS = 3
ROW_BLOCK = 256
ROW_TICK = 2
OUT_BLOCK = 256


def place_in_sums(piece, per_panel):
    per_part = FFN_PANELS // FFN_PARTS
    third = per_part // 3
    part, inside = piece // (per_part * per_panel), lax.rem(piece, per_part * per_panel)
    kind = lax.rem(inside, per_part)
    panel = kind // third * (FFN_PANELS // 3) + part * third + lax.rem(kind, third)
    of_ffn = piece < FFN_PANELS * per_panel
    return (
        jnp.where(of_ffn, panel, piece // per_panel),
        jnp.where(of_ffn, inside // per_part, lax.rem(piece, per_panel)),
    )


def norm_back(grad, gain, unit, scale):
    scaled = gain * grad
    return scale * (scaled - unit * jnp.mean(scaled * unit, axis=-1, keepdims=True))


def back_kernel(places, slots, *refs):
    (mid_hbm, cot_hbm, w_gate_hbm, w_up_hbm, w_d_hbm, hidden_hbm, proj_hbm) = refs[0:7]
    (gated_hbm, normed_hbm, mixed_hbm, w_in_hbm, w_out_hbm, tokens_hbm) = refs[7:13]
    (lengths, taps, gain_mix, gain_ffn) = refs[13:17]
    (sums, tokens_out, block_out, mid_chip, mid_far, ffn_chip, ffn_far) = refs[17:24]
    (mid_land, ffn_land, land_in, land_out, land_small) = refs[24:29]
    (mid, cot, w_gu, w_d, act, ggu, own, staged, fetched) = refs[29:38]
    (proj, gated, mixed_buf, conv_in, grad_hid, grad_tok) = refs[38:44]
    (halo_out, halo_in, halo_keep, small, small_in) = refs[44:49]
    load_sems, near_sems, far_sems, keep_sem, fetch_sem = refs[49:54]
    (later_sems, row_sems, halo_sems, weight_sems, out_sems) = refs[54:59]

    summer = SeqSum(places, own, sums, refs[59:])
    here = lax.axis_index("seq")
    last = 2 * places - 1
    tp_at = lax.axis_index("tp")
    core = lax.rem(tp_at, 2)
    sibling = tp_at + 1 - 2 * core
    across = lax.rem(tp_at + 2, 4)
    rows, width = mid.shape
    parts, _, wide = w_gu.shape
    half_rows = rows // 2
    chans = wide // 3
    hidden = wide // 2
    panels = 3 * hidden // LANES

    moves = [(mid_hbm, mid), (cot_hbm, cot), (w_d_hbm, w_d)]
    for c in range(parts):
        for i, source in enumerate((w_gate_hbm, w_up_hbm)):
            move = (
                source.at[:, c * hidden : (c + 1) * hidden],
                w_gu.at[c, :, i * hidden : (i + 1) * hidden],
            )
            moves.insert(i if c == 0 else len(moves), move)
    loads = [
        pltpu.make_async_copy(src, dst, load_sems.at[i]) for i, (src, dst) in enumerate(moves)
    ]
    for load in loads:
        load.start()

    barrier = pltpu.get_barrier_semaphore()

    def signal(device):
        pl.semaphore_signal(barrier, inc=1, device_id=device, device_id_type=pl.DeviceIdType.MESH)

    pl.when(here > 0)(lambda: signal({"seq": here - 1}))
    pl.when(here < last)(lambda: signal({"seq": here + 1}))
    ends = jnp.where(here > 0, 1, 0) + jnp.where(here < last, 1, 0)
    greet_seq(places, ({"tp": sibling}, {"tp": across}), ends)
    ffn_pieces = own.shape[0] // (4 * HALF)
    mixer_pieces = 4 * chans * width // LANES // (4 * HALF) + 1
    count = ffn_pieces + mixer_pieces
    for load in loads[:5]:
        load.wait()

    slot_len = rows // 2 // slots

    def valid_rows(slot, first, size):
        at = lax.broadcasted_iota(jnp.int32, (size, 1), 0) + (here * slot_len + first)
        return (at < lengths[slot]).astype(jnp.float32)

    row_ticks = rows // ROW_BLOCK // ROW_TICK
    grad_ticks = width // OUT_BLOCK
    first_ticks = grad_ticks - 4 * HALF // OUT_BLOCK
    blocks = rows // 2 // OUT_BLOCK
    before_mid = first_ticks + (parts - 1) * row_ticks
    after_mid = before_mid + blocks
    before_ffn = after_mid + (parts - 1) * grad_ticks

    def part_cols(c):
        return pl.ds(pl.multiple_of(c * hidden, LANES), hidden)

    def row_phase(c):
        for i in range(1, parts):

            @pl.when(jnp.int32(c) == i)
            def _(i=i):
                loads[3 + 2 * i].wait()
                loads[4 + 2 * i].wait()

        @pl.loop(0, rows // ROW_BLOCK)
        def _(r):
            at = pl.ds(pl.multiple_of(r * ROW_BLOCK, ROW_BLOCK), ROW_BLOCK)

            @pl.when(jnp.int32(c) == 0)
            def _():
                per_slot = slot_len // ROW_BLOCK
                mask = valid_rows(r // per_slot, lax.rem(r, per_slot) * ROW_BLOCK, ROW_BLOCK)
                cot[at, :] = (mask * cot[at, :].astype(jnp.float32)).astype(jnp.bfloat16)

            both = jnp.dot(mid[at, :], w_gu[c], preferred_element_type=jnp.float32)
            gate, up = both[:, :hidden], both[:, hidden:]
            grad_act = dot_cols(cot[at, :], w_d[part_cols(c), :])
            sigmoid = 1.0 / (1.0 + jnp.exp(-gate))
            silu = gate * sigmoid
            act[at, part_cols(c)] = (silu * up).astype(jnp.bfloat16)
            slope = sigmoid * (1.0 + gate * (1.0 - sigmoid))
            ggu[c, at, :hidden] = (grad_act * up * slope).astype(jnp.bfloat16)
            ggu[c, at, hidden:] = (grad_act * silu).astype(jnp.bfloat16)

            @pl.when((jnp.int32(c) > 0) & (lax.rem(r, ROW_TICK) == ROW_TICK - 1))
            def _():
                summer.tick(first_ticks + (c - 1) * row_ticks + r // ROW_TICK, count)

    def grad_phase(c):
        @pl.loop(0, width // OUT_BLOCK)
        def _(m):
            first = pl.multiple_of(m * OUT_BLOCK, OUT_BLOCK)
            at = pl.ds(first, OUT_BLOCK)
            per_piece = 4 * HALF // OUT_BLOCK
            piece = (c * (width // OUT_BLOCK // per_piece) + m // per_piece) * panels
            base = piece * 4 * HALF + lax.rem(m, per_piece) * OUT_BLOCK

            def put(block, panel):
                for j in range(block.shape[1] // LANES):
                    to = pl.multiple_of(base + (panel + j) * 4 * HALF, OUT_BLOCK)
                    own[pl.ds(to, OUT_BLOCK), :] = block[:, j * LANES : (j + 1) * LANES]

            put(dot_rows(mid[:, at], ggu[c]), 0)
            put(dot_rows(cot[:, at], act[:, part_cols(c)]), wide // LANES)

            step = jnp.where(jnp.int32(c) > 0, after_mid + (c - 1) * grad_ticks + m, m - grad_ticks + first_ticks)

            @pl.when(step >= 0)
            def _():
                summer.tick(step, count)

    def row_block(half, k):
        return pl.ds(pl.multiple_of((half * blocks + k) * OUT_BLOCK, OUT_BLOCK), OUT_BLOCK)

    def mid_part(at):
        return sum(dot_cols(ggu[c, at, :], w_gu[c]) for c in range(parts))

    def ffn_part(at):
        return sum(
            jnp.dot(
                act[at, c * hidden : (c + 1) * hidden],
                w_d[c * hidden : (c + 1) * hidden, :],
                preferred_element_type=jnp.float32,
            )
            for c in range(parts)
        )

    def near(which, land, k):
        return pltpu.make_async_remote_copy(
            src_ref=staged.at[lax.rem(k, 2)],
            dst_ref=land.at[row_block(0, k)],
            send_sem=near_sems.at[which, 0, k],
            recv_sem=near_sems.at[which, 1, k],
            device_id={"tp": sibling},
            device_id_type=pl.DeviceIdType.MESH,
        )

    def far(which, chip, there, k):
        return pltpu.make_async_remote_copy(
            src_ref=chip.at[row_block(0, k)],
            dst_ref=there.at[row_block(0, k)],
            send_sem=far_sems.at[which, 0, k],
            recv_sem=far_sems.at[which, 1, k],
            device_id={"tp": across},
            device_id_type=pl.DeviceIdType.MESH,
        )

    def ffn_across(k):
        return far(1, ffn_chip, ffn_far, k)

    def tp_sum(which, part, land, chip, first_tick):
        @pl.loop(0, blocks)
        def _(k):
            @pl.when(k >= 2)
            def _():
                near(which, land, k - 2).wait_send()

            staged[lax.rem(k, 2)] = part(row_block(1 - core, k))
            near(which, land, k).start()

        for k in range(max(blocks - 2, 0), blocks):
            near(which, land, k).wait_send()

        @pl.loop(0, blocks)
        def _(k):
            near(which, land, k).wait_recv()
            fetch = pltpu.make_async_copy(land.at[row_block(0, k)], fetched, fetch_sem)
            fetch.start()
            staged[0] = part(row_block(core, k))
            fetch.wait()
            staged[0] += fetched[...]
            keep = pltpu.make_async_copy(staged.at[0], chip.at[row_block(0, k)], keep_sem)
            keep.start()
            summer.tick(first_tick + k, count)
            keep.wait()
            if which == 0:
                far(0, mid_chip, mid_far, k).start()

    row_phase(0)
    grad_phase(0)
    pl.loop(1, parts)(row_phase)
    tp_sum(0, mid_part, mid_land, mid_chip, before_mid)
    pl.loop(1, parts)(grad_phase)
    tp_sum(1, ffn_part, ffn_land, ffn_chip, before_ffn)

    own_half = pl.ds(pl.multiple_of(core * half_rows, half_rows), half_rows)
    low_half, high_half = pl.ds(0, half_rows), pl.ds(half_rows, half_rows)
    w_out, grad_mixer = mid.at[low_half], mid.at[high_half]
    normed, mixed = act.at[low_half, pl.ds(0, width)], act.at[high_half, pl.ds(0, width)]
    tokens = w_d.at[low_half]
    w_in = (ggu.at[2, low_half], ggu.at[2, high_half], w_gu.at[0], w_gu.at[1])
    moves = [
        (w_out_hbm, w_out),
        (tokens_hbm.at[own_half], tokens),
        (normed_hbm, normed),
        (mixed_hbm, mixed),
    ]
    for j in range(4):
        for g in range(3):
            first = g * width + j * chans
            moves.append(
                (w_in_hbm.at[:, first : first + chans], w_in[j].at[:, g * chans : (g + 1) * chans])
            )
    loads = [
        pltpu.make_async_copy(src, dst, later_sems.at[i]) for i, (src, dst) in enumerate(moves)
    ]
    for load in loads:
        load.start()
    chip, far_rows, hidden_rows = staged.at[0], staged.at[1], fetched
    per_slot = slot_len // OUT_BLOCK
    small[...] = jnp.zeros_like(small)
    ticked = before_ffn + blocks

    @pl.loop(ticked, FIRST_MIXER_TICK)
    def _(t):
        summer.tick(t, count)

    @pl.loop(0, blocks)
    def _(k):
        far(0, mid_chip, mid_far, k).wait()
        ffn_across(k).start()

    for load in loads:
        load.wait()

    def shard_rows(shard, first, size):
        at = lax.rem(shard, 2) * half_rows + first
        return shard // 2, pl.ds(pl.multiple_of(at, size), size)

    def place_of(n):
        slot = n // per_slot
        block = per_slot - 1 - lax.rem(n, per_slot)
        return slot, block, pl.multiple_of(slot * slot_len + block * OUT_BLOCK, OUT_BLOCK)

    def mid_loads(first):
        at = pl.ds(first, OUT_BLOCK)
        return [
            pltpu.make_async_copy(src.at[at], dst, row_sems.at[i])
            for i, (src, dst) in enumerate(((mid_chip, chip), (mid_far, far_rows), (hidden_hbm, hidden_rows)))
        ]

    def proj_loads(slot, block, first):
        return [
            pltpu.make_async_copy(proj_hbm.at[pl.ds(first, OUT_BLOCK)], proj, row_sems.at[3]),
            pltpu.make_async_copy(
                gated_hbm.at[slot, pl.ds(pl.multiple_of(block * OUT_BLOCK, 8), OUT_BLOCK + 8)],
                gated,
                row_sems.at[4],
            ),
        ]

    def start(copies):
        for copy in copies:
            copy.start()

    def wait(copies):
        for copy in copies:
            copy.wait()

    def remote(src, dst, sems, i, device):
        return pltpu.make_async_remote_copy(
            src_ref=src,
            dst_ref=dst,
            send_sem=sems.at[0, i],
            recv_sem=sems.at[1, i],
            device_id=device,
            device_id_type=pl.DeviceIdType.MESH,
        )

    def block_at(k):
        return pl.ds(pl.multiple_of(k * OUT_BLOCK, OUT_BLOCK), OUT_BLOCK)

    def own_rows(first, size):
        return pl.ds(pl.multiple_of(core * half_rows + first, size), size)

    def hidden_grad(chip_part, far_part, hidden_part, cot_part):
        grad_mid = chip_part + far_part
        scale = rms_scale(hidden_part)
        unit = hidden_part * scale
        grad = cot_part.astype(jnp.float32) + norm_back(grad_mid, gain_ffn[...], unit, scale)
        return grad, grad_mid * unit

    def halo_copy(slot, device):
        return remote(halo_out.at[slot], halo_in.at[slot], halo_sems, slot, {"seq": device})

    head = 16
    for slot in range(slots):
        at = pl.ds(slot * slot_len, head)
        top = pl.ds(0, head)
        copies = [
            pltpu.make_async_copy(src.at[at], dst, row_sems.at[i])
            for i, (src, dst) in enumerate(
                (
                    (mid_chip, chip.at[top]),
                    (mid_far, far_rows.at[top]),
                    (hidden_hbm, hidden_rows.at[top]),
                    (proj_hbm, proj.at[top]),
                )
            )
        ]
        start(copies)
        wait(copies)
        grad, _ = hidden_grad(
            chip[top, :], far_rows[top, :], hidden_rows[top, :], cot[own_rows(slot * slot_len, head), :]
        )
        grad_mixed = dot_cols(grad.astype(jnp.bfloat16), w_out[...])
        halo_out[slot] = (grad_mixed * proj[top, width : 2 * width])[:8]
        pl.when(here > 0)(lambda slot=slot: halo_copy(slot, here - 1).start())

    slot, block, first = place_of(0)
    start(mid_loads(first))
    start(proj_loads(slot, block, first))

    @pl.when(here == last)
    def _():
        halo_in[...] = jnp.zeros_like(halo_in)

    @pl.when(here < last)
    def _():
        for slot in range(slots):
            halo_copy(slot, here + 1).wait_recv()

    def out_rows(first):
        return own_rows(first, OUT_BLOCK)

    def hand_out(target, first, i):
        at = out_rows(first)
        return (
            pltpu.make_async_copy(grad_tok, target.at[at], out_sems.at[0, 2 * blocks]),
            remote(grad_tok, target.at[at], out_sems, i, {"tp": sibling}),
        )

    @pl.loop(0, blocks)
    def _(n):
        slot, block, first = place_of(n)
        at = pl.ds(first, OUT_BLOCK)
        wait(mid_loads(first))

        @pl.loop(0, OUT_BLOCK // SUB_ROWS)
        def _(r):
            sub = pl.ds(pl.multiple_of(r * SUB_ROWS, SUB_ROWS), SUB_ROWS)
            whole = pl.ds(pl.multiple_of(first + r * SUB_ROWS, SUB_ROWS), SUB_ROWS)
            grad, for_gain = hidden_grad(
                chip[sub, :],
                far_rows[sub, :],
                hidden_rows[sub, :],
                cot[own_rows(first + r * SUB_ROWS, SUB_ROWS), :],
            )
            grad_hid[sub, :] = grad
            grad_mixer[whole, :] = grad.astype(jnp.bfloat16)
            small[1:2, :] += jnp.sum(for_gain, axis=0, keepdims=True)

        @pl.when(n < blocks - 1)
        def _():
            start(mid_loads(place_of(n + 1)[2]))

        mixed_buf[...] = dot_cols(grad_mixer[at, :], w_out[...])
        wait(proj_loads(slot, block, first))

        @pl.when(block == per_slot - 1)
        def _():
            conv_in[pl.ds(OUT_BLOCK, 8), :] = halo_in[slot]

        @pl.when(block < per_slot - 1)
        def _():
            conv_in[pl.ds(OUT_BLOCK, 8), :] = halo_keep[...]

        summer.tick(FIRST_MIXER_TICK + 2 * n, count)
        mask = valid_rows(core * slots + slot, block * OUT_BLOCK, OUT_BLOCK)

        @pl.loop(0, width // chans)
        def _(c):
            def cols(gate):
                return pl.ds(pl.multiple_of(gate * width + c * chans, chans), chans)

            here_cols = cols(0)
            pair, shard_at = shard_rows(c, first, OUT_BLOCK)
            in_gate, out_gate, conv_value = (proj[:, cols(g)] for g in range(3))
            grad_mixed = mixed_buf[:, here_cols]
            now = grad_mixed * out_gate
            conv_in[pl.ds(0, OUT_BLOCK), here_cols] = now
            seen = [gated[pl.ds(6 + j, OUT_BLOCK), here_cols] for j in range(3)]
            tap = [taps[j : j + 1, here_cols] for j in range(3)]
            conv_sum = tap[0] * seen[0] + tap[1] * seen[1] + tap[2] * seen[2]
            for j in range(3):
                small[2 + j : 3 + j, here_cols] += jnp.sum(now * seen[j], axis=0, keepdims=True)
            ggu[pair, shard_at, chans : 2 * chans] = (grad_mixed * conv_sum).astype(jnp.bfloat16)
            grad_gated = mask * (
                tap[2] * now
                + tap[1] * conv_in[pl.ds(1, OUT_BLOCK), here_cols]
                + tap[0] * conv_in[pl.ds(2, OUT_BLOCK), here_cols]
            )
            ggu[pair, shard_at, :chans] = (grad_gated * conv_value).astype(jnp.bfloat16)
            ggu[pair, shard_at, 2 * chans : 3 * chans] = (grad_gated * in_gate).astype(jnp.bfloat16)

        halo_keep[...] = conv_in[pl.ds(0, 8), :]

        @pl.when(n < blocks - 1)
        def _():
            start(proj_loads(*place_of(n + 1)))

        def shard_grad(j):
            pair, shard_at = shard_rows(j, first, OUT_BLOCK)
            return dot_cols(ggu[pair, shard_at, :], w_in[j][...])

        mixed_buf[...] = sum(shard_grad(j) for j in range(4))

        @pl.when(n > 0)
        def _():
            local, there = hand_out(tokens_out, place_of(n - 1)[2], n - 1)
            local.wait()
            there.wait_send()

        @pl.loop(0, OUT_BLOCK // SUB_ROWS)
        def _(r):
            sub = pl.ds(pl.multiple_of(r * SUB_ROWS, SUB_ROWS), SUB_ROWS)
            whole = pl.ds(pl.multiple_of(first + r * SUB_ROWS, SUB_ROWS), SUB_ROWS)
            inputs = tokens[whole, :].astype(jnp.float32)
            scale = rms_scale(inputs)
            unit = inputs * scale
            grad_in = mixed_buf[sub, :]
            grad_tok[sub, :] = grad_hid[sub, :] + norm_back(grad_in, gain_mix[...], unit, scale)
            small[0:1, :] += jnp.sum(grad_in * unit, axis=0, keepdims=True)

        start(hand_out(tokens_out, first, n))
        summer.tick(FIRST_MIXER_TICK + 2 * n + 1, count)

    in_blocks = width // OUT_BLOCK
    stages = [proj.at[:, i * wide : (i + 1) * wide] for i in range(3)]

    def to_near(src, dst, i):
        return remote(src, dst, weight_sems, i, {"tp": sibling})

    def near_in(m):
        cols = pl.ds(pl.multiple_of(lax.rem(m, 2) * wide, LANES), wide)
        return to_near(proj.at[:, cols], land_in.at[m], m)

    near_out = to_near(grad_hid, land_out, in_blocks)
    near_small = to_near(small, land_small, in_blocks + 1)

    def in_part(m, shard):
        pair, shard_at = shard_rows(shard, 0, half_rows)
        return dot_rows(normed[:, block_at(m)], ggu[pair, shard_at, :])

    def out_part(shard):
        at = pl.ds(pl.multiple_of(shard * chans, LANES), chans)
        return dot_rows(mixed[:, at], grad_mixer[...])

    near_small.start()
    first_tick = FIRST_MIXER_TICK + 2 * blocks

    @pl.loop(0, in_blocks)
    def _(m):
        @pl.when(m >= 2)
        def _():
            near_in(m - 2).wait_send()

        cols = pl.ds(pl.multiple_of(lax.rem(m, 2) * wide, LANES), wide)
        proj[:, cols] = in_part(m, sibling)
        near_in(m).start()
        summer.tick(first_tick + m, count)

    grad_hid[...] = out_part(sibling)
    near_out.start()

    @pl.loop(0, in_blocks)
    def _(m):
        near_in(m).wait_recv()
        fetch = pltpu.make_async_copy(land_in.at[m], stages[2], row_sems.at[0])
        fetch.start()
        part = in_part(m, tp_at)
        fetch.wait()
        for i in range(wide // LANES):
            to = pl.multiple_of(i * width + m * OUT_BLOCK, OUT_BLOCK)
            own[pl.ds(to, OUT_BLOCK), :] = (
                part[:, i * LANES : (i + 1) * LANES]
                + proj[:, 2 * wide + i * LANES : 2 * wide + (i + 1) * LANES]
            )

        summer.tick(first_tick + in_blocks + m, count)

    near_out.wait_recv()
    near_small.wait_recv()
    fetches = [
        pltpu.make_async_copy(land_out, mixed_buf, row_sems.at[0]),
        pltpu.make_async_copy(land_small, small_in, row_sems.at[1]),
    ]
    start(fetches)
    part = out_part(tp_at)
    wait(fetches)
    out_first = wide // LANES * width
    small_first = out_first + width // LANES * chans
    for p in range(width // LANES):
        cols = slice(p * LANES, (p + 1) * LANES)
        own[pl.ds(out_first + p * chans, chans), :] = part[:, cols] + mixed_buf[:, cols]
        own[pl.ds(small_first + 8 * p, 8), :] = small[:, cols] + small_in[:, cols]
    unused = 4 * HALF - 8 * (width // LANES)
    own[pl.ds(small_first + 4 * HALF - unused, unused), :] = jnp.zeros((unused, LANES), jnp.float32)

    local, there = hand_out(tokens_out, place_of(blocks - 1)[2], blocks - 1)
    local.wait()
    there.wait_send()
    done = first_tick + 2 * in_blocks
    pause = BLOCK_TICK

    @pl.loop(done, pause)
    def _(t):
        summer.tick(t, count)

    @pl.loop(0, blocks)
    def _(k):
        ffn_across(k).wait_recv()
        at = block_at(k)
        copies = [
            pltpu.make_async_copy(src.at[at], dst, row_sems.at[i])
            for i, (src, dst) in enumerate(((ffn_chip, chip), (ffn_far, far_rows), (hidden_hbm, hidden_rows)))
        ]
        start(copies)

        @pl.when(k > 0)
        def _():
            local, there = hand_out(block_out, (k - 1) * OUT_BLOCK, blocks + k - 1)
            local.wait()
            there.wait_send()

        wait(copies)
        grad_tok[...] = hidden_rows[...] + (chip[...] + far_rows[...])
        start(hand_out(block_out, k * OUT_BLOCK, blocks + k))
        summer.tick(pause + k, count)

    @pl.loop(pause + blocks, count + summer.P_LAGS[-1][1])
    def _(t):
        summer.tick(t, count)

    local, there = hand_out(block_out, (blocks - 1) * OUT_BLOCK, 2 * blocks - 1)
    local.wait()
    there.wait_send()

    @pl.loop(0, blocks)
    def _(k):
        ffn_across(k).wait_send()
        hand_out(tokens_out, place_of(k)[2], k)[1].wait_recv()
        hand_out(block_out, k * OUT_BLOCK, blocks + k)[1].wait_recv()

    for m in range(max(in_blocks - 2, 0), in_blocks):
        near_in(m).wait_send()
    near_out.wait_send()
    near_small.wait_send()

    @pl.when(here > 0)
    def _():
        for slot in range(slots):
            halo_copy(slot, here - 1).wait_send()


def back_both(hbm, vmem, slots, sum_cols, collective_id):
    normed_mid, _, w_gate, _, w_d, _, _, gated, _, _, _, _, _ = hbm
    rows, width = normed_mid.shape
    half_rows = rows // 2
    local = w_gate.shape[1]
    hidden = local // FFN_PARTS
    chans = 2 * hidden // 3
    blocks = half_rows // OUT_BLOCK
    in_blocks = width // OUT_BLOCK
    f32, low = jnp.float32, jnp.bfloat16
    half = jax.ShapeDtypeStruct((half_rows, width), f32)
    full = jax.ShapeDtypeStruct((rows, width), f32)
    block = pltpu.VMEM((OUT_BLOCK, width), f32)
    row8 = pltpu.VMEM((8, width), f32)
    anywhere = pl.BlockSpec(memory_space=pl.ANY)
    return pl.pallas_call(
        functools.partial(back_kernel, lax.axis_size("seq") // 2, slots),
        out_shape=[jax.ShapeDtypeStruct((width, sum_cols), f32)]
        + [full] * 2
        + [half] * 6
        + [
            jax.ShapeDtypeStruct((in_blocks, OUT_BLOCK, 2 * hidden), f32),
            jax.ShapeDtypeStruct((chans, width), f32),
            jax.ShapeDtypeStruct((8, width), f32),
        ],
        in_specs=[anywhere] * len(hbm)
        + [pl.BlockSpec(memory_space=pltpu.SMEM)]
        + [pl.BlockSpec(memory_space=pltpu.VMEM)] * (len(vmem) - 1),
        out_specs=[anywhere] * 12,
        scratch_shapes=[
            pltpu.VMEM((rows, width), low),
            pltpu.VMEM((rows, width), low),
            pltpu.VMEM((FFN_PARTS, width, 2 * hidden), low),
            pltpu.VMEM(w_d.shape, low),
            pltpu.VMEM((rows, local), low),
            pltpu.VMEM((FFN_PARTS, rows, 2 * hidden), low),
            pltpu.VMEM((3 * local * width // LANES, LANES), f32),
            pltpu.VMEM((2, OUT_BLOCK, width), f32),
            block,
            pltpu.VMEM((OUT_BLOCK, 3 * width), f32),
            pltpu.VMEM((OUT_BLOCK + 8, width), f32),
            block,
            pltpu.VMEM((OUT_BLOCK + 8, width), f32),
            block,
            block,
            pltpu.VMEM((slots, 8, width), f32),
            pltpu.VMEM((slots, 8, width), f32),
            row8,
            row8,
            row8,
            pltpu.SemaphoreType.DMA((3 + 2 * FFN_PARTS,)),
            pltpu.SemaphoreType.DMA((2, 2, blocks)),
            pltpu.SemaphoreType.DMA((2, 2, blocks)),
            pltpu.SemaphoreType.DMA,
            pltpu.SemaphoreType.DMA,
            pltpu.SemaphoreType.DMA((16,)),
            pltpu.SemaphoreType.DMA((5,)),
            pltpu.SemaphoreType.DMA((2, slots)),
            pltpu.SemaphoreType.DMA((2, in_blocks + 2)),
            pltpu.SemaphoreType.DMA((2, 2 * blocks + 1)),
        ]
        + seq_sum_scratch(),
        compiler_params=pltpu.CompilerParams(
            collective_id=collective_id, has_side_effects=True, vmem_limit_bytes=VMEM_LIMIT
        ),
        cost_estimate=pl.CostEstimate(
            flops=18 * rows * width * local, bytes_accessed=800 << 20, transcendentals=0
        ),
        name="back_both",
    )(*hbm, *vmem)


def front_kernel(places, slots, *refs):
    (w_in, w_out, taps, gain_mix, gain_ffn, lengths, tokens_hbm) = refs[0:7]
    (in_hbm, out_hbm, full_taps, mid_hbm, hidden_hbm, proj_hbm, gated_hbm) = refs[7:14]
    (normed_hbm, mixed_hbm) = refs[14:16]
    own_in, own_out, far_in, far_out, sib_in, sib_out, sibfar_in, sibfar_out = refs[16:24]
    own_taps, far_taps, sib_taps, sibfar_taps, share_in, share_out = refs[24:30]
    (full_in, full_out, tokens, normed, mixed, out_gate, gates, gated) = refs[30:38]
    (unit_out, unit_in, hidden) = refs[38:41]
    sends, recvs, once, halo_sems, gate_sems, unit_sems, keep_sems, mid_sems = refs[41:49]
    straight_sems, shard_sems = refs[49:51]
    here = lax.axis_index("seq")
    place, side = here // 2, lax.rem(here, 2)
    last = places - 1
    end = 2 * places - 1
    tp_at = lax.axis_index("tp")
    core = lax.rem(tp_at, 2)
    sibling = tp_at + 1 - 2 * core
    across = lax.rem(tp_at + 2, 4)
    far_sibling = sibling + across - tp_at
    in_rows = share_in.shape[0]
    straight = w_in.shape[1] - in_rows * 2 * places
    out_rows = w_out.shape[0] // (2 * places)
    chans = w_in.shape[2]
    rows, width = tokens.shape
    slot_len = rows // slots
    low = jnp.bfloat16

    load_tokens = pltpu.make_async_copy(
        tokens_hbm.at[pl.ds(pl.multiple_of(core * rows, rows), rows)], tokens, keep_sems.at[0]
    )
    load_tokens.start()
    barrier = pltpu.get_barrier_semaphore()

    def signal(device):
        pl.semaphore_signal(barrier, inc=1, device_id=device, device_id_type=pl.DeviceIdType.MESH)

    pl.when(here > 0)(lambda: signal({"seq": here - 1}))
    pl.when(here < end)(lambda: signal({"seq": here + 1}))
    ends = jnp.where(here > 0, 1, 0) + jnp.where(here < end, 1, 0)
    greet_seq(places, ({"tp": sibling}, {"tp": across}), ends)

    def shares(j):
        return (
            pl.ds(pl.multiple_of(j * in_rows, 8), in_rows),
            pl.ds(pl.multiple_of(j * out_rows, out_rows), out_rows),
        )

    def remote(src, dst, send, recv, device):
        return pltpu.make_async_remote_copy(
            src_ref=src,
            dst_ref=dst,
            send_sem=send,
            recv_sem=recv,
            device_id=device,
            device_id_type=pl.DeviceIdType.MESH,
        )

    def copies(source, target, j, kind, device):
        for i, at in enumerate(shares(j)):
            yield remote(
                source[i] if kind == 0 else source[i].at[at],
                target[i].at[at],
                sends.at[kind, i, j],
                recvs.at[0 if kind < 4 else 1, i, j],
                device,
            )

    share, far, sibfar = (share_in, share_out), (far_in, far_out), (sibfar_in, sibfar_out)

    def across_share():
        return copies(share, far, here, 0, {"tp": across})

    def to_right(j):
        return copies(far, far, j, 1, {"seq": here + 2})

    def to_left(j):
        return copies(far, far, j, 2, {"seq": here - 2})

    def to_side(j):
        return copies(far, far, j, 3, {"seq": here + 1 - 2 * side})

    def to_sibling(j):
        return copies(far, sibfar, j, 4, {"tp": sibling})

    def straight_rows(q):
        size = straight // STRAIGHT_COPIES
        first = w_in.shape[1] - straight + q * size
        return pl.ds(pl.multiple_of(first, 8), size)

    def straight_across(q):
        at = straight_rows(q)
        return remote(
            own_in.at[at], far_in.at[at], straight_sems.at[0, q], straight_sems.at[1, q],
            {"tp": across},
        )

    def straight_sibling(q):
        at = straight_rows(q)
        return remote(
            far_in.at[at], sibfar_in.at[at], straight_sems.at[2, q], straight_sems.at[3, q],
            {"tp": sibling},
        )

    def pass_straight(q):
        straight_across(q).wait_recv()
        straight_sibling(q).start()

    def start(group):
        for copy in group:
            copy.start()

    def arrived(group):
        for copy in group:
            copy.wait_recv()

    def left_source(group):
        for copy in group:
            copy.wait_send()

    def relay(incoming, j, on_right, on_left):
        onward = zip(incoming, to_right(j), to_left(j), to_side(j), to_sibling(j))
        for copy, right, left, aside, near in onward:
            copy.wait_recv()
            if on_right:
                pl.when(place < last)(right.start)
            if on_left:
                pl.when(place > 0)(left.start)
            aside.start()
            near.start()

    def single(i, src, dst, device):
        return remote(src, dst, once.at[0, i], once.at[1, i], device)

    in_at, out_at = shares(here)
    for g in range(3):
        share_in[:, g * chans : (g + 1) * chans] = w_in[g, in_at, :].astype(jnp.float32)
    share_out[...] = w_out[out_at, :].astype(jnp.float32)
    start(across_share())
    own_taps[...] = jnp.zeros_like(own_taps)
    own_taps[0:3, :] = taps[...]
    taps_far = single(0, own_taps, far_taps, {"tp": across})
    taps_sib = single(1, own_taps, sib_taps, {"tp": sibling})
    taps_sibfar = single(2, far_taps, sibfar_taps, {"tp": sibling})
    for g in range(3):
        own_in[:, g * chans : (g + 1) * chans] = w_in[g].astype(jnp.float32)
    own_out[...] = w_out[...].astype(jnp.float32)
    in_sib = single(3, own_in, sib_in, {"tp": sibling})
    out_sib = single(4, own_out, sib_out, {"tp": sibling})
    for copy in (taps_far, taps_sib, in_sib, out_sib):
        copy.start()
    for q in range(STRAIGHT_COPIES):
        straight_across(q).start()

    def gate_cols(g, index):
        return pl.ds(pl.multiple_of(g * width + index * chans, LANES), chans)

    def place_shard(shard_in, shard_out, shard_taps, index):
        for g in range(3):
            full_in[:, gate_cols(g, index)] = shard_in[:, g * chans : (g + 1) * chans].astype(low)
        at = pl.ds(pl.multiple_of(index * chans, chans), chans)
        full_out[at, :] = shard_out[...].astype(low)
        full_taps[:, gate_cols(0, index)] = shard_taps[...]

    def gate_out(turn, index, g):
        if g == 1:
            return pltpu.make_async_copy(
                out_gate.at[:, gate_cols(0, index)],
                proj_hbm.at[:, gate_cols(1, index)],
                gate_sems.at[turn, 1],
            )
        return pltpu.make_async_copy(
            gates.at[turn % 2, g // 2], proj_hbm.at[:, gate_cols(g, index)], gate_sems.at[turn, g]
        )

    def halo(turn, index, slot):
        return remote(
            gated.at[slot, pl.ds(slot_len, 8), gate_cols(0, index)],
            gated.at[slot, pl.ds(0, 8), gate_cols(0, index)],
            halo_sems.at[0, turn, slot],
            halo_sems.at[1, turn, slot],
            {"seq": here + 1},
        )

    order = (tp_at, sibling, across, far_sibling)

    def shard_out(turn, g):
        at = gate_cols(g, order[turn])
        return pltpu.make_async_copy(full_in.at[:, at], in_hbm.at[:, at], shard_sems.at[turn, g])

    def gated_out(turn):
        at = gate_cols(0, order[turn])
        return pltpu.make_async_copy(
            gated.at[:, :, at], gated_hbm.at[:, :, at], shard_sems.at[turn, 3]
        )

    def mixed_out(turn):
        at = gate_cols(0, order[turn])
        return pltpu.make_async_copy(mixed.at[:, at], mixed_hbm.at[:, at], shard_sems.at[turn, 4])

    def project(turn):
        index = order[turn]
        cols = gate_cols(0, index)
        if turn >= 2:
            gate_out(turn - 2, order[turn - 2], 0).wait()
            gate_out(turn - 2, order[turn - 2], 2).wait()

        @pl.loop(0, slots)
        def _(s):
            at = pl.ds(pl.multiple_of(s * slot_len, slot_len), slot_len)

            def gate(g):
                return jnp.dot(
                    normed[at, :], full_in[:, gate_cols(g, index)],
                    preferred_element_type=jnp.float32,
                )

            at_pos = lax.broadcasted_iota(jnp.int32, (slot_len, 1), 0) + here * slot_len
            mask = (at_pos < lengths[core * slots + s]).astype(jnp.float32)
            in_gate, value = gate(0), gate(2)
            gates[turn % 2, 0, at, :] = in_gate
            gates[turn % 2, 1, at, :] = value
            gated[s, pl.ds(8, slot_len), cols] = mask * in_gate * value
            out_gate[at, cols] = gate(1)

        for g in range(3):
            gate_out(turn, index, g).start()
            shard_out(turn, g).start()

        @pl.when(here < end)
        def _():
            for slot in range(slots):
                halo(turn, index, slot).start()

    def convolve(turn):
        index = order[turn]
        cols = gate_cols(0, index)

        @pl.when(here > 0)
        def _():
            for slot in range(slots):
                halo(turn, index, slot).wait_recv()

        @pl.loop(0, slots)
        def _(s):
            at = pl.ds(pl.multiple_of(s * slot_len, slot_len), slot_len)
            seen = [gated[s, pl.ds(6 + j, slot_len), cols] for j in range(3)]
            tap = [full_taps[j : j + 1, cols] for j in range(3)]
            conv_sum = tap[0] * seen[0] + tap[1] * seen[1] + tap[2] * seen[2]
            mixed[at, cols] = (out_gate[at, cols] * conv_sum).astype(low)

        gated_out(turn).start()
        mixed_out(turn).start()

    @pl.when(here == 0)
    def _():
        for slot in range(slots):
            gated[slot, pl.ds(0, 8), :] = jnp.zeros((8, width), jnp.float32)

    load_tokens.wait()

    @pl.loop(0, rows // SUB_ROWS)
    def _(r):
        at = pl.ds(pl.multiple_of(r * SUB_ROWS, SUB_ROWS), SUB_ROWS)
        inputs = tokens[at, :].astype(jnp.float32)
        normed[at, :] = (gain_mix[...] * (inputs * rms_scale(inputs))).astype(low)

    keep_normed = pltpu.make_async_copy(normed, normed_hbm, keep_sems.at[0])
    keep_normed.start()
    place_shard(own_in, own_out, own_taps, tp_at)
    project(0)

    relay(across_share(), here, True, True)
    taps_far.wait_recv()
    taps_sibfar.start()
    in_sib.wait_recv()
    out_sib.wait_recv()
    taps_sib.wait_recv()
    place_shard(sib_in, sib_out, sib_taps, sibling)
    project(1)

    def from_side(q):
        j = 2 * q + 1 - side
        arrived(to_side(j))
        start(to_sibling(j))

    @pl.loop(1, places)
    def _(d):
        @pl.when(place - d >= 0)
        def _():
            j = here - 2 * d
            relay(to_right(j), j, True, False)

        @pl.when(place + d <= last)
        def _():
            j = here + 2 * d
            relay(to_left(j), j, False, True)

        @pl.when(d == 1)
        def _():
            from_side(place)
            convolve(0)
            convolve(1)

        pl.when(place - d >= 0)(lambda: from_side(place - d))
        pl.when(place + d <= last)(lambda: from_side(place + d))
        pl.when(d <= STRAIGHT_COPIES)(lambda: pass_straight(d - 1))

    for q in range(min(last, STRAIGHT_COPIES), STRAIGHT_COPIES):
        pass_straight(q)

    place_shard(far_in, far_out, far_taps, across)
    project(2)
    taps_sibfar.wait_recv()

    @pl.loop(0, 2 * places)
    def _(j):
        arrived(to_sibling(j))

    for q in range(STRAIGHT_COPIES):
        straight_sibling(q).wait_recv()
    place_shard(sibfar_in, sibfar_out, sibfar_taps, far_sibling)
    project(3)
    keep_out = pltpu.make_async_copy(full_out, out_hbm, keep_sems.at[2])
    keep_out.start()
    convolve(2)
    convolve(3)
    keep_normed.wait()

    blocks = rows // OUT_BLOCK

    def block_at(k, first=0):
        return pl.ds(pl.multiple_of(first + k * OUT_BLOCK, OUT_BLOCK), OUT_BLOCK)

    def unit_copy(k):
        return remote(
            unit_out.at[block_at(k)], unit_in.at[block_at(k)],
            unit_sems.at[0, k], unit_sems.at[1, k], {"tp": sibling},
        )

    def hidden_copy(k):
        return pltpu.make_async_copy(
            hidden.at[lax.rem(k, 2)], hidden_hbm.at[block_at(k)], mid_sems.at[0, lax.rem(k, 2)]
        )

    def mid_copy(half, held, whose, k):
        return pltpu.make_async_copy(
            held.at[block_at(k)], mid_hbm.at[block_at(k, whose * rows)], mid_sems.at[half, k]
        )

    @pl.loop(0, blocks)
    def _(k):
        slot = lax.rem(k, 2)
        at = block_at(k)
        pl.when(k >= 2)(lambda: hidden_copy(k - 2).wait())
        hidden[slot] = jnp.dot(mixed[at, :], full_out[...], preferred_element_type=jnp.float32)

        @pl.loop(0, OUT_BLOCK // SUB_ROWS)
        def _(r):
            sub = pl.ds(pl.multiple_of(r * SUB_ROWS, SUB_ROWS), SUB_ROWS)
            whole = pl.ds(pl.multiple_of(k * OUT_BLOCK + r * SUB_ROWS, SUB_ROWS), SUB_ROWS)
            hidden_rows = tokens[whole, :].astype(jnp.float32) + hidden[slot, sub, :]
            hidden[slot, sub, :] = hidden_rows
            unit = hidden_rows * rms_scale(hidden_rows)
            unit_out[whole, :] = unit
            normed[whole, :] = (gain_ffn[...] * unit).astype(low)

        unit_copy(k).start()
        hidden_copy(k).start()
        mid_copy(1, normed, core, k).start()

    for turn in range(4):
        mixed_out(turn).wait()

    @pl.loop(0, blocks)
    def _(k):
        unit_copy(k).wait_recv()

        @pl.loop(0, OUT_BLOCK // SUB_ROWS)
        def _(r):
            whole = pl.ds(pl.multiple_of(k * OUT_BLOCK + r * SUB_ROWS, SUB_ROWS), SUB_ROWS)
            mixed[whole, :] = (gain_ffn[...] * unit_in[whole, :]).astype(low)

        mid_copy(2, mixed, 1 - core, k).start()

    @pl.loop(0, blocks)
    def _(k):
        unit_copy(k).wait_send()
        mid_copy(1, normed, core, k).wait()
        mid_copy(2, mixed, 1 - core, k).wait()

    for k in range(max(blocks - 2, 0), blocks):
        hidden_copy(k).wait()
    keep_out.wait()
    for turn in range(4):
        gated_out(turn).wait()
        for g in range(3):
            shard_out(turn, g).wait()
    for turn in range(4):
        for g in range(3):
            if turn >= 2 or g == 1:
                gate_out(turn, order[turn], g).wait()

    @pl.when(here < end)
    def _():
        for turn in range(4):
            for slot in range(slots):
                halo(turn, order[turn], slot).wait_send()

    left_source(across_share())
    for q in range(STRAIGHT_COPIES):
        straight_across(q).wait_send()
        straight_sibling(q).wait_send()
    for copy in (taps_far, taps_sib, taps_sibfar, in_sib, out_sib):
        copy.wait_send()

    @pl.loop(0, places)
    def _(q):
        j = 2 * q + side
        left_source(to_side(j))
        pl.when((q <= place) & (place < last))(lambda: left_source(to_right(j)))
        pl.when((q >= place) & (place > 0))(lambda: left_source(to_left(j)))
        left_source(to_sibling(j))
        left_source(to_sibling(2 * q + 1 - side))


def mixer_front(w_in, w_out, taps, gain_mix, gain_ffn, lengths, tokens, slots, collective_id):
    width, _, chans = w_in.shape
    rows = tokens.shape[0] // 2
    count = lax.axis_size("seq")
    group = lax.axis_size("tp")
    f32, low = jnp.float32, jnp.bfloat16
    blocks = rows // OUT_BLOCK
    pair = [pltpu.VMEM((width, 3 * chans), f32), pltpu.VMEM((chans, width), f32)]
    whole = pl.BlockSpec(memory_space=pltpu.VMEM)
    anywhere = pl.BlockSpec(memory_space=pl.ANY)
    padded = (slots, rows // slots + 8, width)
    return pl.pallas_call(
        functools.partial(front_kernel, count // 2, slots),
        out_shape=[
            jax.ShapeDtypeStruct((width, 3 * chans * group), low),
            jax.ShapeDtypeStruct((chans * group, width), low),
            jax.ShapeDtypeStruct((8, chans * group), f32),
            jax.ShapeDtypeStruct((2 * rows, width), low),
            jax.ShapeDtypeStruct((rows, width), f32),
            jax.ShapeDtypeStruct((rows, 3 * width), f32),
            jax.ShapeDtypeStruct(padded, f32),
            jax.ShapeDtypeStruct((rows, width), low),
            jax.ShapeDtypeStruct((rows, width), low),
        ],
        in_specs=[whole] * 5 + [pl.BlockSpec(memory_space=pltpu.SMEM), anywhere],
        out_specs=[anywhere] * 2 + [whole] + [anywhere] * 6,
        scratch_shapes=pair * 4
        + [pltpu.VMEM((8, chans), f32)] * 4
        + [
            pltpu.VMEM((width * 8 // 16 // count // 8 * 8, 3 * chans), f32),
            pltpu.VMEM((chans // count, width), f32),
            pltpu.VMEM((width, 3 * chans * group), low),
            pltpu.VMEM((chans * group, width), low),
            pltpu.VMEM((rows, width), low),
            pltpu.VMEM((rows, width), low),
            pltpu.VMEM((rows, width), low),
            pltpu.VMEM((rows, width), f32),
            pltpu.VMEM((2, 2, rows, chans), f32),
            pltpu.VMEM(padded, f32),
            pltpu.VMEM((rows, width), f32),
            pltpu.VMEM((rows, width), f32),
            pltpu.VMEM((2, OUT_BLOCK, width), f32),
            pltpu.SemaphoreType.DMA((5, 2, count)),
            pltpu.SemaphoreType.DMA((2, 2, count)),
            pltpu.SemaphoreType.DMA((2, 5)),
            pltpu.SemaphoreType.DMA((2, 4, slots)),
            pltpu.SemaphoreType.DMA((4, 3)),
            pltpu.SemaphoreType.DMA((2, blocks)),
            pltpu.SemaphoreType.DMA((3,)),
            pltpu.SemaphoreType.DMA((3, blocks)),
            pltpu.SemaphoreType.DMA((4, STRAIGHT_COPIES)),
            pltpu.SemaphoreType.DMA((4, 5)),
        ],
        compiler_params=pltpu.CompilerParams(
            collective_id=collective_id, has_side_effects=True, vmem_limit_bytes=VMEM_LIMIT
        ),
        name="mixer_front",
    )(
        w_in.transpose(1, 0, 2),
        w_out,
        taps,
        gain_mix,
        gain_ffn,
        lengths,
        tokens,
    )


def finish_kernel(slots, chans, hidden, *refs):
    (sums, tokens_in, block_in, lengths) = refs[0:4]
    (block_out, tokens_out, gain_a, gain_b, g_in, g_conv, g_out, g_gate, g_up, g_down) = refs[4:14]
    (held, tokens, block, rounded, turned, gains) = refs[14:20]
    (in_sems, block_sems, turn_sems, out_sems) = refs[20:24]
    rows, width = block_in.shape
    slot_len = rows // slots
    here = lax.axis_index("seq")
    tp_at = lax.axis_index("tp")
    first = 3 * hidden
    out_first = first + 3 * chans
    small_first = out_first + chans
    blocks = rows // OUT_BLOCK
    turns = hidden // LANES
    half_rows = rows // 2

    def cols(start, size):
        return (slice(None), slice(start, start + size))

    parts = [cols(i * hidden, hidden) for i in range(3)] + [cols(first, held.shape[1] - first)]
    halves = [slice(0, half_rows), slice(half_rows, rows)]
    part_loads = [
        pltpu.make_async_copy(sums.at[at], held.at[at], in_sems.at[i]) for i, at in enumerate(parts)
    ]
    token_loads = [
        pltpu.make_async_copy(tokens_in.at[at], tokens.at[at], in_sems.at[4 + i])
        for i, at in enumerate(halves)
    ]

    def block_at(k):
        return pl.ds(pl.multiple_of(k * OUT_BLOCK, OUT_BLOCK), OUT_BLOCK)

    def block_load(k):
        return pltpu.make_async_copy(
            block_in.at[block_at(k)], block.at[block_at(k)], block_sems.at[0, k]
        )

    def block_store(k):
        return pltpu.make_async_copy(
            rounded.at[block_at(k)], block_out.at[block_at(k)], block_sems.at[1, k]
        )

    def panel_at(k):
        return pl.ds(pl.multiple_of(k * LANES, LANES), LANES)

    def turn_store(k):
        at = panel_at(k)
        return pltpu.make_async_copy(turned.at[at], g_down.at[at], turn_sems.at[k])

    stores = []

    def store(src, dst):
        copy = pltpu.make_async_copy(src, dst, out_sems.at[len(stores)])
        copy.start()
        stores.append(copy)

    part_loads[2].start()

    @pl.loop(0, blocks)
    def _(k):
        block_load(k).start()

    for load in (*token_loads, part_loads[0], part_loads[1], part_loads[3]):
        load.start()

    part_loads[2].wait()

    @pl.loop(0, turns)
    def _(k):
        from_cols = pl.ds(pl.multiple_of(2 * hidden + k * LANES, LANES), LANES)
        turned[panel_at(k), :] = held[:, from_cols].T
        turn_store(k).start()

    @pl.loop(0, blocks)
    def _(k):
        block_load(k).wait()
        per_slot = slot_len // OUT_BLOCK
        at = lax.broadcasted_iota(jnp.int32, (OUT_BLOCK, 1), 0)
        at = at + (here * slot_len + lax.rem(k, per_slot) * OUT_BLOCK)
        mask = (at < lengths[k // per_slot]).astype(jnp.float32)
        rounded[block_at(k), :] = (mask * block[block_at(k), :]).astype(jnp.bfloat16)
        block_store(k).start()

    for load, at in zip(token_loads, halves):
        load.wait()
        store(tokens.at[at], tokens_out.at[at])
    for i, target in ((0, g_gate), (1, g_up)):
        part_loads[i].wait()
        store(held.at[parts[i]], target)
    part_loads[3].wait()
    for g in range(3):
        store(held.at[cols(first + g * chans, chans)], g_in.at[g])
    per_col = width // chans
    for p in range(width // LANES):
        q, r = p // per_col, p % per_col
        at = (slice(r * chans, (r + 1) * chans), slice(out_first + q * LANES, out_first + (q + 1) * LANES))
        store(held.at[at], g_out.at[cols(p * LANES, LANES)])
        gains[cols(p * LANES, LANES)] = held[8 * p : 8 * p + 8, small_first:]
    own = pl.ds(pl.multiple_of(tp_at * chans, LANES), chans)
    g_conv[...] = gains[2:5, own]
    gain_a[...] = gains[0:1, :]
    gain_b[...] = gains[1:2, :]
    for copy in stores:
        copy.wait()

    @pl.loop(0, turns)
    def _(k):
        turn_store(k).wait()

    @pl.loop(0, blocks)
    def _(k):
        block_store(k).wait()


def finish(sums, tokens_grad, block_sum, lengths, chans, hidden):
    rows, width = block_sum.shape
    f32 = jnp.float32
    anywhere = pl.BlockSpec(memory_space=pl.ANY)
    whole = pl.BlockSpec(memory_space=pltpu.VMEM)
    blocks = rows // OUT_BLOCK
    return pl.pallas_call(
        functools.partial(finish_kernel, lengths.shape[0], chans, hidden),
        out_shape=[
            jax.ShapeDtypeStruct((rows, width), jnp.bfloat16),
            jax.ShapeDtypeStruct((rows, width), f32),
            jax.ShapeDtypeStruct((1, width), f32),
            jax.ShapeDtypeStruct((1, width), f32),
            jax.ShapeDtypeStruct((3, width, chans), f32),
            jax.ShapeDtypeStruct((3, chans), f32),
            jax.ShapeDtypeStruct((chans, width), f32),
            jax.ShapeDtypeStruct((width, hidden), f32),
            jax.ShapeDtypeStruct((width, hidden), f32),
            jax.ShapeDtypeStruct((hidden, width), f32),
        ],
        in_specs=[anywhere] * 3 + [pl.BlockSpec(memory_space=pltpu.SMEM)],
        out_specs=[anywhere] * 2 + [whole, whole, anywhere, whole] + [anywhere] * 4,
        scratch_shapes=[
            pltpu.VMEM(sums.shape, f32),
            pltpu.VMEM((rows, width), f32),
            pltpu.VMEM((rows, width), f32),
            pltpu.VMEM((rows, width), jnp.bfloat16),
            pltpu.VMEM((hidden, width), f32),
            pltpu.VMEM((8, width), f32),
            pltpu.SemaphoreType.DMA((6,)),
            pltpu.SemaphoreType.DMA((2, blocks)),
            pltpu.SemaphoreType.DMA((hidden // LANES,)),
            pltpu.SemaphoreType.DMA((7 + width // LANES,)),
        ],
        compiler_params=pltpu.CompilerParams(vmem_limit_bytes=VMEM_LIMIT),
        name="finish",
    )(sums, tokens_grad, block_sum, lengths)


def per_device(
    tokens, lengths, gain_mix, w_in, conv_weight, w_out, gain_ffn, w_gate, w_up, w_down, cotangent
):
    slot_count, local_len, width = tokens.shape
    chans = w_in.shape[2]
    half_slots = slot_count // 2
    row_count = slot_count * local_len

    token_rows = tokens.reshape(row_count, width)
    cot_rows = cotangent.reshape(row_count, width)
    gains = gain_mix.reshape(1, width), gain_ffn.reshape(1, width)
    w_in_all, w_out_all, taps, normed_mid, hidden_res, projected, gated_rows, normed_in, mixed = (
        mixer_front(w_in, w_out, conv_weight, *gains, lengths, token_rows, half_slots, 3)
    )
    mixer_cols = 4 * chans
    sum_cols = FFN_PANELS * LANES + mixer_cols + LANES
    sums, grad_tokens, block_sum = back_both(
        (
            normed_mid,
            cot_rows,
            w_gate,
            w_up,
            w_down,
            hidden_res,
            projected,
            gated_rows,
            normed_in,
            mixed,
            w_in_all,
            w_out_all,
            token_rows,
        ),
        (lengths, taps, *gains),
        half_slots,
        sum_cols,
        1,
    )[:3]
    block_out, grad_tokens, g_gain_mix, g_gain_ffn, g_in, g_conv, g_out, g_gate, g_up, g_down = finish(
        sums, grad_tokens, block_sum, lengths, chans, w_gate.shape[1]
    )
    return (
        block_out.reshape(slot_count, local_len, width),
        grad_tokens.reshape(slot_count, local_len, width),
        g_gain_mix.reshape(width),
        g_in.transpose(1, 0, 2),
        g_conv,
        g_out,
        g_gain_ffn.reshape(width),
        g_gate,
        g_up,
        g_down,
    )


def solution(mesh):
    rows, cols = P("tp", None), P(None, "tp")
    tokens, whole, stacked = P(None, "seq", None), P(), P(None, None, "tp")
    return jax.shard_map(
        per_device,
        mesh=mesh,
        in_specs=(
            tokens, whole, whole, stacked, cols, rows, whole, cols, cols, rows, tokens,
        ),
        out_specs=(
            tokens, tokens, whole, stacked, cols, rows, whole, cols, cols, rows,
        ),
        check_vma=False,
    )
```

```python
import functools

import jax
import jax.numpy as jnp
from jax import lax
from jax.experimental import pallas as pl
from jax.experimental.pallas import tpu as pltpu
from jax.sharding import PartitionSpec as P

NORM_EPS = 1e-05
LANES = 128
VMEM_LIMIT = 64 << 20
HALF = 128
SLOTS_IN_FLIGHT = 10


def rms_scale(values):
    return lax.rsqrt(jnp.mean(values * values, axis=-1, keepdims=True) + NORM_EPS)


def dot_rows(left, right):
    return lax.dot_general(
        left, right, (((0,), (0,)), ((), ())), preferred_element_type=jnp.float32
    )


def dot_cols(left, right):
    return lax.dot_general(
        left, right, (((1,), (1,)), ((), ())), preferred_element_type=jnp.float32
    )


def greet_seq(places, others=(), more=0):
    barrier = pltpu.get_barrier_semaphore()
    here = lax.axis_index("seq")
    place, side = here // 2, lax.rem(here, 2)

    def signal(device):
        pl.semaphore_signal(
            barrier, inc=1, device_id=device, device_id_type=pl.DeviceIdType.MESH
        )

    signal({"seq": here + 1 - 2 * side})
    for other in others:
        signal(other)
    pl.when(place > 0)(lambda: signal({"seq": here - 2}))
    pl.when(place < places - 1)(lambda: signal({"seq": here + 2}))
    ends = jnp.where(place > 0, 1, 0) + jnp.where(place < places - 1, 1, 0)
    pl.semaphore_wait(barrier, 1 + len(others) + ends + more)


class SeqSum:
    def __init__(self, places, own, out, scratch):
        self.places, self.own, self.out = places, own, out
        self.y_in, self.p_left, self.p_right, self.p_acc = scratch[0:4]
        self.q_left, self.q_right, self.q_acc, self.q_in = scratch[4:8]
        self.sems = scratch[8]
        here = lax.axis_index("seq")
        self.place, self.side = here // 2, here % 2

    def remote(self, src, dst, slot, send, recv, place, side):
        return pltpu.make_async_remote_copy(
            src_ref=src,
            dst_ref=dst,
            send_sem=self.sems.at[send, slot],
            recv_sem=self.sems.at[recv, slot],
            device_id={"seq": place * 2 + side},
            device_id_type=pl.DeviceIdType.MESH,
        )

    def chain(self, root):
        last = self.places - 1
        left = jnp.maximum(self.place - 1, 0)
        right = jnp.minimum(self.place + 1, last)
        from_left = (self.place <= root) & (self.place > 0)
        from_right = (self.place >= root) & (self.place < last)
        return left, right, from_left, from_right

    def own_base(self, k):
        held = self.own.shape[0] // (4 * HALF)
        return pl.multiple_of(lax.rem(k, held) * 4 * HALF, 4 * HALF)

    def out_at(self, k, first, size):
        per_panel = self.out.shape[0] // (4 * HALF)
        panel, part = place_in_sums(k, per_panel)
        row = part * 4 * HALF + first
        return self.out.at[
            pl.ds(pl.multiple_of(row, size), size), pl.ds(pl.multiple_of(panel * LANES, LANES), LANES)
        ]

    def p_stage(self, which, k):
        place, side = self.place, self.side
        own = self.own
        slot = lax.rem(k, SLOTS_IN_FLIGHT)
        base = self.own_base(k)
        mine = pl.ds(pl.multiple_of(base + side * HALF, HALF), HALF)
        theirs = pl.ds(pl.multiple_of(base + (1 - side) * HALF, HALF), HALF)
        out_mine = self.out_at(k, side * HALF, HALF)
        root = self.places // 2 - 1 + lax.rem(k, 2)
        left, right, from_left, from_right = self.chain(root)
        acc, y_in = self.p_acc.at[slot], self.y_in.at[slot]
        from_l, from_r = self.p_left.at[slot], self.p_right.at[slot]
        remote = functools.partial(functools.partial, self.remote)

        to_side = remote(own.at[theirs], y_in, slot, 0, 1, place, 1 - side)
        up_right = remote(acc, from_l, slot, 2, 3, right, side)
        up_left = remote(acc, from_r, slot, 2, 4, left, side)

        def down(src):
            return (
                remote(src, out_mine, slot, 5, 7, left, side),
                remote(src, out_mine, slot, 6, 7, right, side),
                remote(src, out_mine, slot, 8, 9, place, 1 - side),
            )

        def keep():
            return pltpu.make_async_copy(acc, out_mine, self.sems.at[10, slot])

        def hand_down(src):
            down_left, down_right, down_side = down(src)
            down_side().start()
            pl.when(from_left)(lambda: down_left().start())
            pl.when(from_right)(lambda: down_right().start())

        if which == "split":
            to_side().start()

        if which == "up":
            to_side().wait_recv()
            acc[...] = own[mine, :] + y_in[...]

            @pl.when(place < root)
            def _():
                @pl.when(from_left)
                def _():
                    up_right().wait_recv()
                    acc[...] += from_l[...]

                up_right().start()

            @pl.when(place > root)
            def _():
                @pl.when(from_right)
                def _():
                    up_left().wait_recv()
                    acc[...] += from_r[...]

                up_left().start()

        if which == "root":

            @pl.when(place == root)
            def _():
                @pl.when(from_left)
                def _():
                    up_right().wait_recv()
                    acc[...] += from_l[...]

                @pl.when(from_right)
                def _():
                    up_left().wait_recv()
                    acc[...] += from_r[...]

                hand_down(acc)
                keep().start()

        if which == "down":

            @pl.when(place != root)
            def _():
                down(acc)[0]().wait_recv()
                hand_down(out_mine)

        if which == "end":
            down_left, down_right, down_side = down(acc)
            down_side().wait()
            to_side().wait_send()
            pl.when(from_left)(lambda: down_left().wait_send())
            pl.when(from_right)(lambda: down_right().wait_send())
            pl.when(place == root)(lambda: keep().wait())
            pl.when(place != root)(lambda: up_left().wait_send())

    def q_stage(self, which, k):
        place, side = self.place, self.side
        own = self.own
        slot = lax.rem(k, SLOTS_IN_FLIGHT)
        base = self.own_base(k)
        wide = pl.ds(pl.multiple_of(base + 2 * HALF, 2 * HALF), 2 * HALF)
        out_wide = self.out_at(k, 2 * HALF, 2 * HALF)
        root = self.places // 2 - lax.rem(k, 2)
        left, right, from_left, from_right = self.chain(root)
        acc, side_in = self.q_acc.at[slot], self.q_in.at[slot]
        from_l, from_r = self.q_left.at[slot], self.q_right.at[slot]
        remote = functools.partial(functools.partial, self.remote)

        up_right = remote(acc, from_l, slot, 11, 12, right, side)
        up_left = remote(acc, from_r, slot, 11, 13, left, side)
        to_side = remote(acc, side_in, slot, 14, 15, place, 1 - side)

        def down(src):
            return (
                remote(src, out_wide, slot, 16, 18, left, side),
                remote(src, out_wide, slot, 17, 18, right, side),
            )

        def keep():
            return pltpu.make_async_copy(side_in, out_wide, self.sems.at[19, slot])

        def hand_down(src):
            down_left, down_right = down(src)
            pl.when(from_left)(lambda: down_left().start())
            pl.when(from_right)(lambda: down_right().start())

        if which == "up":
            acc[...] = own[wide, :]

            @pl.when(place < root)
            def _():
                @pl.when(from_left)
                def _():
                    up_right().wait_recv()
                    acc[...] += from_l[...]

                up_right().start()

            @pl.when(place > root)
            def _():
                @pl.when(from_right)
                def _():
                    up_left().wait_recv()
                    acc[...] += from_r[...]

                up_left().start()

        if which == "root":

            @pl.when(place == root)
            def _():
                @pl.when(from_left)
                def _():
                    up_right().wait_recv()
                    acc[...] += from_l[...]

                @pl.when(from_right)
                def _():
                    up_left().wait_recv()
                    acc[...] += from_r[...]

                to_side().start()

        if which == "side":

            @pl.when(place == root)
            def _():
                to_side().wait_recv()
                side_in[...] += acc[...]
                hand_down(side_in)
                keep().start()

        if which == "down":

            @pl.when(place != root)
            def _():
                down(acc)[0]().wait_recv()
                hand_down(out_wide)

        if which == "end":
            down_left, down_right = down(acc)
            pl.when(from_left)(lambda: down_left().wait_send())
            pl.when(from_right)(lambda: down_right().wait_send())

            @pl.when(place == root)
            def _():
                to_side().wait_send()
                keep().wait()

            pl.when(place != root)(lambda: up_left().wait_send())

    P_LAGS = (("split", 0, 0), ("up", 2, 1), ("root", 3, 3), ("down", 6, 7), ("end", 9, 9))
    Q_LAGS = (("up", 1, 0), ("root", 3, 3), ("side", 4, 4), ("down", 6, 7), ("end", 9, 9))

    def tick(self, t, count):
        middle = (self.place == self.places // 2) | (self.place == self.places // 2 - 1)
        for stage, lags in (
            (self.p_stage, self.P_LAGS[:-1]),
            (self.q_stage, self.Q_LAGS[:-1]),
            (self.p_stage, self.P_LAGS[-1:]),
            (self.q_stage, self.Q_LAGS[-1:]),
        ):
            for which, mid_lag, outer_lag in lags:
                k = t - jnp.where(middle, mid_lag, outer_lag)

                @pl.when((k >= 0) & (k < count))
                def _(stage=stage, which=which, k=k):
                    stage(which, k)

    def run(self, count):
        @pl.loop(0, count + self.P_LAGS[-1][1])
        def _(t):
            self.tick(t, count)


def seq_sum_scratch():
    half = pltpu.VMEM((SLOTS_IN_FLIGHT, HALF, LANES), jnp.float32)
    wide = pltpu.VMEM((SLOTS_IN_FLIGHT, 2 * HALF, LANES), jnp.float32)
    return [half] * 4 + [wide] * 4 + [pltpu.SemaphoreType.DMA((20, SLOTS_IN_FLIGHT))]


SUB_ROWS = 64
STRAIGHT_COPIES = 4
FIRST_MIXER_TICK = 36
BLOCK_TICK = 56
FFN_PANELS = 27
FFN_PARTS = 3
ROW_BLOCK = 256
ROW_TICK = 2
OUT_BLOCK = 256


def place_in_sums(piece, per_panel):
    per_part = FFN_PANELS // FFN_PARTS
    third = per_part // 3
    part, inside = piece // (per_part * per_panel), lax.rem(piece, per_part * per_panel)
    kind = lax.rem(inside, per_part)
    panel = kind // third * (FFN_PANELS // 3) + part * third + lax.rem(kind, third)
    of_ffn = piece < FFN_PANELS * per_panel
    return (
        jnp.where(of_ffn, panel, piece // per_panel),
        jnp.where(of_ffn, inside // per_part, lax.rem(piece, per_panel)),
    )


def norm_back(grad, gain, unit, scale):
    scaled = gain * grad
    return scale * (scaled - unit * jnp.mean(scaled * unit, axis=-1, keepdims=True))


def back_kernel(places, slots, *refs):
    (mid_hbm, cot_hbm, w_gate_hbm, w_up_hbm, w_d_hbm, hidden_hbm, proj_hbm) = refs[0:7]
    (gated_hbm, normed_hbm, mixed_hbm, w_in_hbm, w_out_hbm, tokens_hbm) = refs[7:13]
    (lengths, taps, gain_mix, gain_ffn) = refs[13:17]
    (sums, tokens_out, block_out, mid_chip, mid_far, ffn_chip, ffn_far) = refs[17:24]
    (mid_land, ffn_land, land_in, land_out, land_small) = refs[24:29]
    (mid, cot, w_gu, w_d, act, ggu, own, staged, fetched) = refs[29:38]
    (proj, gated, mixed_buf, conv_in, grad_hid, grad_tok) = refs[38:44]
    (halo_out, halo_in, halo_keep, small, small_in) = refs[44:49]
    load_sems, near_sems, far_sems, keep_sem, fetch_sem = refs[49:54]
    (later_sems, row_sems, halo_sems, weight_sems, out_sems) = refs[54:59]

    summer = SeqSum(places, own, sums, refs[59:])
    here = lax.axis_index("seq")
    last = 2 * places - 1
    tp_at = lax.axis_index("tp")
    core = lax.rem(tp_at, 2)
    sibling = tp_at + 1 - 2 * core
    across = lax.rem(tp_at + 2, 4)
    rows, width = mid.shape
    parts, _, wide = w_gu.shape
    half_rows = rows // 2
    chans = wide // 3
    hidden = wide // 2
    panels = 3 * hidden // LANES

    moves = [(mid_hbm, mid), (cot_hbm, cot), (w_d_hbm, w_d)]
    for c in range(parts):
        for i, source in enumerate((w_gate_hbm, w_up_hbm)):
            move = (
                source.at[:, c * hidden : (c + 1) * hidden],
                w_gu.at[c, :, i * hidden : (i + 1) * hidden],
            )
            moves.insert(i if c == 0 else len(moves), move)
    loads = [
        pltpu.make_async_copy(src, dst, load_sems.at[i]) for i, (src, dst) in enumerate(moves)
    ]
    for load in loads:
        load.start()

    barrier = pltpu.get_barrier_semaphore()

    def signal(device):
        pl.semaphore_signal(barrier, inc=1, device_id=device, device_id_type=pl.DeviceIdType.MESH)

    pl.when(here > 0)(lambda: signal({"seq": here - 1}))
    pl.when(here < last)(lambda: signal({"seq": here + 1}))
    ends = jnp.where(here > 0, 1, 0) + jnp.where(here < last, 1, 0)
    greet_seq(places, ({"tp": sibling}, {"tp": across}), ends)
    ffn_pieces = own.shape[0] // (4 * HALF)
    mixer_pieces = 4 * chans * width // LANES // (4 * HALF) + 1
    count = ffn_pieces + mixer_pieces
    for load in loads[:5]:
        load.wait()

    slot_len = rows // 2 // slots

    def valid_rows(slot, first, size):
        at = lax.broadcasted_iota(jnp.int32, (size, 1), 0) + (here * slot_len + first)
        return (at < lengths[slot]).astype(jnp.float32)

    row_ticks = rows // ROW_BLOCK // ROW_TICK
    grad_ticks = width // OUT_BLOCK
    first_ticks = grad_ticks - 4 * HALF // OUT_BLOCK
    blocks = rows // 2 // OUT_BLOCK
    before_mid = first_ticks + (parts - 1) * row_ticks
    after_mid = before_mid + blocks
    before_ffn = after_mid + (parts - 1) * grad_ticks

    def part_cols(c):
        return pl.ds(pl.multiple_of(c * hidden, LANES), hidden)

    def row_phase(c):
        for i in range(1, parts):

            @pl.when(jnp.int32(c) == i)
            def _(i=i):
                loads[3 + 2 * i].wait()
                loads[4 + 2 * i].wait()

        @pl.loop(0, rows // ROW_BLOCK)
        def _(r):
            at = pl.ds(pl.multiple_of(r * ROW_BLOCK, ROW_BLOCK), ROW_BLOCK)

            @pl.when(jnp.int32(c) == 0)
            def _():
                per_slot = slot_len // ROW_BLOCK
                mask = valid_rows(r // per_slot, lax.rem(r, per_slot) * ROW_BLOCK, ROW_BLOCK)
                cot[at, :] = (mask * cot[at, :].astype(jnp.float32)).astype(jnp.bfloat16)

            both = jnp.dot(mid[at, :], w_gu[c], preferred_element_type=jnp.float32)
            gate, up = both[:, :hidden], both[:, hidden:]
            grad_act = dot_cols(cot[at, :], w_d[part_cols(c), :])
            sigmoid = 1.0 / (1.0 + jnp.exp(-gate))
            silu = gate * sigmoid
            act[at, part_cols(c)] = (silu * up).astype(jnp.bfloat16)
            slope = sigmoid * (1.0 + gate * (1.0 - sigmoid))
            ggu[c, at, :hidden] = (grad_act * up * slope).astype(jnp.bfloat16)
            ggu[c, at, hidden:] = (grad_act * silu).astype(jnp.bfloat16)

            @pl.when((jnp.int32(c) > 0) & (lax.rem(r, ROW_TICK) == ROW_TICK - 1))
            def _():
                summer.tick(first_ticks + (c - 1) * row_ticks + r // ROW_TICK, count)

    def grad_phase(c):
        @pl.loop(0, width // OUT_BLOCK)
        def _(m):
            first = pl.multiple_of(m * OUT_BLOCK, OUT_BLOCK)
            at = pl.ds(first, OUT_BLOCK)
            per_piece = 4 * HALF // OUT_BLOCK
            piece = (c * (width // OUT_BLOCK // per_piece) + m // per_piece) * panels
            base = piece * 4 * HALF + lax.rem(m, per_piece) * OUT_BLOCK

            def put(block, panel):
                for j in range(block.shape[1] // LANES):
                    to = pl.multiple_of(base + (panel + j) * 4 * HALF, OUT_BLOCK)
                    own[pl.ds(to, OUT_BLOCK), :] = block[:, j * LANES : (j + 1) * LANES]

            put(dot_rows(mid[:, at], ggu[c]), 0)
            put(dot_rows(cot[:, at], act[:, part_cols(c)]), wide // LANES)

            step = jnp.where(jnp.int32(c) > 0, after_mid + (c - 1) * grad_ticks + m, m - grad_ticks + first_ticks)

            @pl.when(step >= 0)
            def _():
                summer.tick(step, count)

    def row_block(half, k):
        return pl.ds(pl.multiple_of((half * blocks + k) * OUT_BLOCK, OUT_BLOCK), OUT_BLOCK)

    def mid_part(at):
        return sum(dot_cols(ggu[c, at, :], w_gu[c]) for c in range(parts))

    def ffn_part(at):
        return sum(
            jnp.dot(
                act[at, c * hidden : (c + 1) * hidden],
                w_d[c * hidden : (c + 1) * hidden, :],
                preferred_element_type=jnp.float32,
            )
            for c in range(parts)
        )

    def near(which, land, k):
        return pltpu.make_async_remote_copy(
            src_ref=staged.at[lax.rem(k, 2)],
            dst_ref=land.at[row_block(0, k)],
            send_sem=near_sems.at[which, 0, k],
            recv_sem=near_sems.at[which, 1, k],
            device_id={"tp": sibling},
            device_id_type=pl.DeviceIdType.MESH,
        )

    def far(which, chip, there, k):
        return pltpu.make_async_remote_copy(
            src_ref=chip.at[row_block(0, k)],
            dst_ref=there.at[row_block(0, k)],
            send_sem=far_sems.at[which, 0, k],
            recv_sem=far_sems.at[which, 1, k],
            device_id={"tp": across},
            device_id_type=pl.DeviceIdType.MESH,
        )

    def ffn_across(k):
        return far(1, ffn_chip, ffn_far, k)

    def tp_sum(which, part, land, chip, first_tick):
        @pl.loop(0, blocks)
        def _(k):
            @pl.when(k >= 2)
            def _():
                near(which, land, k - 2).wait_send()

            staged[lax.rem(k, 2)] = part(row_block(1 - core, k))
            near(which, land, k).start()

        for k in range(max(blocks - 2, 0), blocks):
            near(which, land, k).wait_send()

        @pl.loop(0, blocks)
        def _(k):
            near(which, land, k).wait_recv()
            fetch = pltpu.make_async_copy(land.at[row_block(0, k)], fetched, fetch_sem)
            fetch.start()
            staged[0] = part(row_block(core, k))
            fetch.wait()
            staged[0] += fetched[...]
            keep = pltpu.make_async_copy(staged.at[0], chip.at[row_block(0, k)], keep_sem)
            keep.start()
            summer.tick(first_tick + k, count)
            keep.wait()
            if which == 0:
                far(0, mid_chip, mid_far, k).start()

    row_phase(0)
    grad_phase(0)
    pl.loop(1, parts)(row_phase)
    tp_sum(0, mid_part, mid_land, mid_chip, before_mid)
    pl.loop(1, parts)(grad_phase)
    tp_sum(1, ffn_part, ffn_land, ffn_chip, before_ffn)

    own_half = pl.ds(pl.multiple_of(core * half_rows, half_rows), half_rows)
    low_half, high_half = pl.ds(0, half_rows), pl.ds(half_rows, half_rows)
    w_out, grad_mixer = mid.at[low_half], mid.at[high_half]
    normed, mixed = act.at[low_half, pl.ds(0, width)], act.at[high_half, pl.ds(0, width)]
    tokens = w_d.at[low_half]
    w_in = (ggu.at[2, low_half], ggu.at[2, high_half], w_gu.at[0], w_gu.at[1])
    moves = [
        (w_out_hbm, w_out),
        (tokens_hbm.at[own_half], tokens),
        (normed_hbm, normed),
        (mixed_hbm, mixed),
    ]
    for j in range(4):
        for g in range(3):
            first = g * width + j * chans
            moves.append(
                (w_in_hbm.at[:, first : first + chans], w_in[j].at[:, g * chans : (g + 1) * chans])
            )
    loads = [
        pltpu.make_async_copy(src, dst, later_sems.at[i]) for i, (src, dst) in enumerate(moves)
    ]
    for load in loads:
        load.start()
    chip, far_rows, hidden_rows = staged.at[0], staged.at[1], fetched
    per_slot = slot_len // OUT_BLOCK
    small[...] = jnp.zeros_like(small)
    ticked = before_ffn + blocks

    @pl.loop(ticked, FIRST_MIXER_TICK)
    def _(t):
        summer.tick(t, count)

    @pl.loop(0, blocks)
    def _(k):
        far(0, mid_chip, mid_far, k).wait()
        ffn_across(k).start()

    for load in loads:
        load.wait()

    def shard_rows(shard, first, size):
        at = lax.rem(shard, 2) * half_rows + first
        return shard // 2, pl.ds(pl.multiple_of(at, size), size)

    def place_of(n):
        slot = n // per_slot
        block = per_slot - 1 - lax.rem(n, per_slot)
        return slot, block, pl.multiple_of(slot * slot_len + block * OUT_BLOCK, OUT_BLOCK)

    def mid_loads(first):
        at = pl.ds(first, OUT_BLOCK)
        return [
            pltpu.make_async_copy(src.at[at], dst, row_sems.at[i])
            for i, (src, dst) in enumerate(((mid_chip, chip), (mid_far, far_rows), (hidden_hbm, hidden_rows)))
        ]

    def proj_loads(slot, block, first):
        return [
            pltpu.make_async_copy(proj_hbm.at[pl.ds(first, OUT_BLOCK)], proj, row_sems.at[3]),
            pltpu.make_async_copy(
                gated_hbm.at[slot, pl.ds(pl.multiple_of(block * OUT_BLOCK, 8), OUT_BLOCK + 8)],
                gated,
                row_sems.at[4],
            ),
        ]

    def start(copies):
        for copy in copies:
            copy.start()

    def wait(copies):
        for copy in copies:
            copy.wait()

    def remote(src, dst, sems, i, device):
        return pltpu.make_async_remote_copy(
            src_ref=src,
            dst_ref=dst,
            send_sem=sems.at[0, i],
            recv_sem=sems.at[1, i],
            device_id=device,
            device_id_type=pl.DeviceIdType.MESH,
        )

    def block_at(k):
        return pl.ds(pl.multiple_of(k * OUT_BLOCK, OUT_BLOCK), OUT_BLOCK)

    def own_rows(first, size):
        return pl.ds(pl.multiple_of(core * half_rows + first, size), size)

    def hidden_grad(chip_part, far_part, hidden_part, cot_part):
        grad_mid = chip_part + far_part
        scale = rms_scale(hidden_part)
        unit = hidden_part * scale
        grad = cot_part.astype(jnp.float32) + norm_back(grad_mid, gain_ffn[...], unit, scale)
        return grad, grad_mid * unit

    def halo_copy(slot, device):
        return remote(halo_out.at[slot], halo_in.at[slot], halo_sems, slot, {"seq": device})

    head = 16
    for slot in range(slots):
        at = pl.ds(slot * slot_len, head)
        top = pl.ds(0, head)
        copies = [
            pltpu.make_async_copy(src.at[at], dst, row_sems.at[i])
            for i, (src, dst) in enumerate(
                (
                    (mid_chip, chip.at[top]),
                    (mid_far, far_rows.at[top]),
                    (hidden_hbm, hidden_rows.at[top]),
                    (proj_hbm, proj.at[top]),
                )
            )
        ]
        start(copies)
        wait(copies)
        grad, _ = hidden_grad(
            chip[top, :], far_rows[top, :], hidden_rows[top, :], cot[own_rows(slot * slot_len, head), :]
        )
        grad_mixed = dot_cols(grad.astype(jnp.bfloat16), w_out[...])
        halo_out[slot] = (grad_mixed * proj[top, width : 2 * width])[:8]
        pl.when(here > 0)(lambda slot=slot: halo_copy(slot, here - 1).start())

    slot, block, first = place_of(0)
    start(mid_loads(first))
    start(proj_loads(slot, block, first))

    @pl.when(here == last)
    def _():
        halo_in[...] = jnp.zeros_like(halo_in)

    @pl.when(here < last)
    def _():
        for slot in range(slots):
            halo_copy(slot, here + 1).wait_recv()

    def out_rows(first):
        return own_rows(first, OUT_BLOCK)

    def hand_out(target, first, i):
        at = out_rows(first)
        return (
            pltpu.make_async_copy(grad_tok, target.at[at], out_sems.at[0, 2 * blocks]),
            remote(grad_tok, target.at[at], out_sems, i, {"tp": sibling}),
        )

    @pl.loop(0, blocks)
    def _(n):
        slot, block, first = place_of(n)
        at = pl.ds(first, OUT_BLOCK)
        wait(mid_loads(first))

        @pl.loop(0, OUT_BLOCK // SUB_ROWS)
        def _(r):
            sub = pl.ds(pl.multiple_of(r * SUB_ROWS, SUB_ROWS), SUB_ROWS)
            whole = pl.ds(pl.multiple_of(first + r * SUB_ROWS, SUB_ROWS), SUB_ROWS)
            grad, for_gain = hidden_grad(
                chip[sub, :],
                far_rows[sub, :],
                hidden_rows[sub, :],
                cot[own_rows(first + r * SUB_ROWS, SUB_ROWS), :],
            )
            grad_hid[sub, :] = grad
            grad_mixer[whole, :] = grad.astype(jnp.bfloat16)
            small[1:2, :] += jnp.sum(for_gain, axis=0, keepdims=True)

        @pl.when(n < blocks - 1)
        def _():
            start(mid_loads(place_of(n + 1)[2]))

        mixed_buf[...] = dot_cols(grad_mixer[at, :], w_out[...])
        wait(proj_loads(slot, block, first))

        @pl.when(block == per_slot - 1)
        def _():
            conv_in[pl.ds(OUT_BLOCK, 8), :] = halo_in[slot]

        @pl.when(block < per_slot - 1)
        def _():
            conv_in[pl.ds(OUT_BLOCK, 8), :] = halo_keep[...]

        summer.tick(FIRST_MIXER_TICK + 2 * n, count)
        mask = valid_rows(core * slots + slot, block * OUT_BLOCK, OUT_BLOCK)

        @pl.loop(0, width // chans)
        def _(c):
            def cols(gate):
                return pl.ds(pl.multiple_of(gate * width + c * chans, chans), chans)

            here_cols = cols(0)
            pair, shard_at = shard_rows(c, first, OUT_BLOCK)
            in_gate, out_gate, conv_value = (proj[:, cols(g)] for g in range(3))
            grad_mixed = mixed_buf[:, here_cols]
            now = grad_mixed * out_gate
            conv_in[pl.ds(0, OUT_BLOCK), here_cols] = now
            seen = [gated[pl.ds(6 + j, OUT_BLOCK), here_cols] for j in range(3)]
            tap = [taps[j : j + 1, here_cols] for j in range(3)]
            conv_sum = tap[0] * seen[0] + tap[1] * seen[1] + tap[2] * seen[2]
            for j in range(3):
                small[2 + j : 3 + j, here_cols] += jnp.sum(now * seen[j], axis=0, keepdims=True)
            ggu[pair, shard_at, chans : 2 * chans] = (grad_mixed * conv_sum).astype(jnp.bfloat16)
            grad_gated = mask * (
                tap[2] * now
                + tap[1] * conv_in[pl.ds(1, OUT_BLOCK), here_cols]
                + tap[0] * conv_in[pl.ds(2, OUT_BLOCK), here_cols]
            )
            ggu[pair, shard_at, :chans] = (grad_gated * conv_value).astype(jnp.bfloat16)
            ggu[pair, shard_at, 2 * chans : 3 * chans] = (grad_gated * in_gate).astype(jnp.bfloat16)

        halo_keep[...] = conv_in[pl.ds(0, 8), :]

        @pl.when(n < blocks - 1)
        def _():
            start(proj_loads(*place_of(n + 1)))

        def shard_grad(j):
            pair, shard_at = shard_rows(j, first, OUT_BLOCK)
            return dot_cols(ggu[pair, shard_at, :], w_in[j][...])

        mixed_buf[...] = sum(shard_grad(j) for j in range(4))

        @pl.when(n > 0)
        def _():
            local, there = hand_out(tokens_out, place_of(n - 1)[2], n - 1)
            local.wait()
            there.wait_send()

        @pl.loop(0, OUT_BLOCK // SUB_ROWS)
        def _(r):
            sub = pl.ds(pl.multiple_of(r * SUB_ROWS, SUB_ROWS), SUB_ROWS)
            whole = pl.ds(pl.multiple_of(first + r * SUB_ROWS, SUB_ROWS), SUB_ROWS)
            inputs = tokens[whole, :].astype(jnp.float32)
            scale = rms_scale(inputs)
            unit = inputs * scale
            grad_in = mixed_buf[sub, :]
            grad_tok[sub, :] = grad_hid[sub, :] + norm_back(grad_in, gain_mix[...], unit, scale)
            small[0:1, :] += jnp.sum(grad_in * unit, axis=0, keepdims=True)

        start(hand_out(tokens_out, first, n))
        summer.tick(FIRST_MIXER_TICK + 2 * n + 1, count)

    in_blocks = width // OUT_BLOCK
    stages = [proj.at[:, i * wide : (i + 1) * wide] for i in range(3)]

    def to_near(src, dst, i):
        return remote(src, dst, weight_sems, i, {"tp": sibling})

    def near_in(m):
        cols = pl.ds(pl.multiple_of(lax.rem(m, 2) * wide, LANES), wide)
        return to_near(proj.at[:, cols], land_in.at[m], m)

    near_out = to_near(grad_hid, land_out, in_blocks)
    near_small = to_near(small, land_small, in_blocks + 1)

    def in_part(m, shard):
        pair, shard_at = shard_rows(shard, 0, half_rows)
        return dot_rows(normed[:, block_at(m)], ggu[pair, shard_at, :])

    def out_part(shard):
        at = pl.ds(pl.multiple_of(shard * chans, LANES), chans)
        return dot_rows(mixed[:, at], grad_mixer[...])

    near_small.start()
    first_tick = FIRST_MIXER_TICK + 2 * blocks

    @pl.loop(0, in_blocks)
    def _(m):
        @pl.when(m >= 2)
        def _():
            near_in(m - 2).wait_send()

        cols = pl.ds(pl.multiple_of(lax.rem(m, 2) * wide, LANES), wide)
        proj[:, cols] = in_part(m, sibling)
        near_in(m).start()
        summer.tick(first_tick + m, count)

    grad_hid[...] = out_part(sibling)
    near_out.start()

    @pl.loop(0, in_blocks)
    def _(m):
        near_in(m).wait_recv()
        fetch = pltpu.make_async_copy(land_in.at[m], stages[2], row_sems.at[0])
        fetch.start()
        part = in_part(m, tp_at)
        fetch.wait()
        for i in range(wide // LANES):
            to = pl.multiple_of(i * width + m * OUT_BLOCK, OUT_BLOCK)
            own[pl.ds(to, OUT_BLOCK), :] = (
                part[:, i * LANES : (i + 1) * LANES]
                + proj[:, 2 * wide + i * LANES : 2 * wide + (i + 1) * LANES]
            )

        summer.tick(first_tick + in_blocks + m, count)

    near_out.wait_recv()
    near_small.wait_recv()
    fetches = [
        pltpu.make_async_copy(land_out, mixed_buf, row_sems.at[0]),
        pltpu.make_async_copy(land_small, small_in, row_sems.at[1]),
    ]
    start(fetches)
    part = out_part(tp_at)
    wait(fetches)
    out_first = wide // LANES * width
    small_first = out_first + width // LANES * chans
    for p in range(width // LANES):
        cols = slice(p * LANES, (p + 1) * LANES)
        own[pl.ds(out_first + p * chans, chans), :] = part[:, cols] + mixed_buf[:, cols]
        own[pl.ds(small_first + 8 * p, 8), :] = small[:, cols] + small_in[:, cols]
    unused = 4 * HALF - 8 * (width // LANES)
    own[pl.ds(small_first + 4 * HALF - unused, unused), :] = jnp.zeros((unused, LANES), jnp.float32)

    local, there = hand_out(tokens_out, place_of(blocks - 1)[2], blocks - 1)
    local.wait()
    there.wait_send()
    done = first_tick + 2 * in_blocks
    pause = BLOCK_TICK

    @pl.loop(done, pause)
    def _(t):
        summer.tick(t, count)

    @pl.loop(0, blocks)
    def _(k):
        ffn_across(k).wait_recv()
        at = block_at(k)
        copies = [
            pltpu.make_async_copy(src.at[at], dst, row_sems.at[i])
            for i, (src, dst) in enumerate(((ffn_chip, chip), (ffn_far, far_rows), (hidden_hbm, hidden_rows)))
        ]
        start(copies)

        @pl.when(k > 0)
        def _():
            local, there = hand_out(block_out, (k - 1) * OUT_BLOCK, blocks + k - 1)
            local.wait()
            there.wait_send()

        wait(copies)
        grad_tok[...] = hidden_rows[...] + (chip[...] + far_rows[...])
        start(hand_out(block_out, k * OUT_BLOCK, blocks + k))
        summer.tick(pause + k, count)

    @pl.loop(pause + blocks, count + summer.P_LAGS[-1][1])
    def _(t):
        summer.tick(t, count)

    local, there = hand_out(block_out, (blocks - 1) * OUT_BLOCK, 2 * blocks - 1)
    local.wait()
    there.wait_send()

    @pl.loop(0, blocks)
    def _(k):
        ffn_across(k).wait_send()
        hand_out(tokens_out, place_of(k)[2], k)[1].wait_recv()
        hand_out(block_out, k * OUT_BLOCK, blocks + k)[1].wait_recv()

    for m in range(max(in_blocks - 2, 0), in_blocks):
        near_in(m).wait_send()
    near_out.wait_send()
    near_small.wait_send()

    @pl.when(here > 0)
    def _():
        for slot in range(slots):
            halo_copy(slot, here - 1).wait_send()


def back_both(hbm, vmem, slots, sum_cols, collective_id):
    normed_mid, _, w_gate, _, w_d, _, _, gated, _, _, _, _, _ = hbm
    rows, width = normed_mid.shape
    half_rows = rows // 2
    local = w_gate.shape[1]
    hidden = local // FFN_PARTS
    chans = 2 * hidden // 3
    blocks = half_rows // OUT_BLOCK
    in_blocks = width // OUT_BLOCK
    f32, low = jnp.float32, jnp.bfloat16
    half = jax.ShapeDtypeStruct((half_rows, width), f32)
    full = jax.ShapeDtypeStruct((rows, width), f32)
    block = pltpu.VMEM((OUT_BLOCK, width), f32)
    row8 = pltpu.VMEM((8, width), f32)
    anywhere = pl.BlockSpec(memory_space=pl.ANY)
    return pl.pallas_call(
        functools.partial(back_kernel, lax.axis_size("seq") // 2, slots),
        out_shape=[jax.ShapeDtypeStruct((width, sum_cols), f32)]
        + [full] * 2
        + [half] * 6
        + [
            jax.ShapeDtypeStruct((in_blocks, OUT_BLOCK, 2 * hidden), f32),
            jax.ShapeDtypeStruct((chans, width), f32),
            jax.ShapeDtypeStruct((8, width), f32),
        ],
        in_specs=[anywhere] * len(hbm)
        + [pl.BlockSpec(memory_space=pltpu.SMEM)]
        + [pl.BlockSpec(memory_space=pltpu.VMEM)] * (len(vmem) - 1),
        out_specs=[anywhere] * 12,
        scratch_shapes=[
            pltpu.VMEM((rows, width), low),
            pltpu.VMEM((rows, width), low),
            pltpu.VMEM((FFN_PARTS, width, 2 * hidden), low),
            pltpu.VMEM(w_d.shape, low),
            pltpu.VMEM((rows, local), low),
            pltpu.VMEM((FFN_PARTS, rows, 2 * hidden), low),
            pltpu.VMEM((3 * local * width // LANES, LANES), f32),
            pltpu.VMEM((2, OUT_BLOCK, width), f32),
            block,
            pltpu.VMEM((OUT_BLOCK, 3 * width), f32),
            pltpu.VMEM((OUT_BLOCK + 8, width), f32),
            block,
            pltpu.VMEM((OUT_BLOCK + 8, width), f32),
            block,
            block,
            pltpu.VMEM((slots, 8, width), f32),
            pltpu.VMEM((slots, 8, width), f32),
            row8,
            row8,
            row8,
            pltpu.SemaphoreType.DMA((3 + 2 * FFN_PARTS,)),
            pltpu.SemaphoreType.DMA((2, 2, blocks)),
            pltpu.SemaphoreType.DMA((2, 2, blocks)),
            pltpu.SemaphoreType.DMA,
            pltpu.SemaphoreType.DMA,
            pltpu.SemaphoreType.DMA((16,)),
            pltpu.SemaphoreType.DMA((5,)),
            pltpu.SemaphoreType.DMA((2, slots)),
            pltpu.SemaphoreType.DMA((2, in_blocks + 2)),
            pltpu.SemaphoreType.DMA((2, 2 * blocks + 1)),
        ]
        + seq_sum_scratch(),
        compiler_params=pltpu.CompilerParams(
            collective_id=collective_id, has_side_effects=True, vmem_limit_bytes=VMEM_LIMIT
        ),
        cost_estimate=pl.CostEstimate(
            flops=18 * rows * width * local, bytes_accessed=800 << 20, transcendentals=0
        ),
        name="back_both",
    )(*hbm, *vmem)


def front_kernel(places, slots, *refs):
    (w_in, w_out, taps, gain_mix, gain_ffn, lengths, tokens_hbm) = refs[0:7]
    (in_hbm, out_hbm, full_taps, mid_hbm, hidden_hbm, proj_hbm, gated_hbm) = refs[7:14]
    (normed_hbm, mixed_hbm) = refs[14:16]
    own_in, own_out, far_in, far_out, sib_in, sib_out, sibfar_in, sibfar_out = refs[16:24]
    own_taps, far_taps, sib_taps, sibfar_taps, share_in, share_out = refs[24:30]
    (full_in, full_out, tokens, normed, mixed, out_gate, gates, gated) = refs[30:38]
    (unit_out, unit_in, hidden) = refs[38:41]
    sends, recvs, once, halo_sems, gate_sems, unit_sems, keep_sems, mid_sems = refs[41:49]
    straight_sems = refs[49]
    here = lax.axis_index("seq")
    place, side = here // 2, lax.rem(here, 2)
    last = places - 1
    end = 2 * places - 1
    tp_at = lax.axis_index("tp")
    core = lax.rem(tp_at, 2)
    sibling = tp_at + 1 - 2 * core
    across = lax.rem(tp_at + 2, 4)
    far_sibling = sibling + across - tp_at
    in_rows = share_in.shape[0]
    straight = w_in.shape[1] - in_rows * 2 * places
    out_rows = w_out.shape[0] // (2 * places)
    chans = w_in.shape[2]
    rows, width = tokens.shape
    slot_len = rows // slots
    low = jnp.bfloat16

    load_tokens = pltpu.make_async_copy(
        tokens_hbm.at[pl.ds(pl.multiple_of(core * rows, rows), rows)], tokens, keep_sems.at[0]
    )
    load_tokens.start()
    barrier = pltpu.get_barrier_semaphore()

    def signal(device):
        pl.semaphore_signal(barrier, inc=1, device_id=device, device_id_type=pl.DeviceIdType.MESH)

    pl.when(here > 0)(lambda: signal({"seq": here - 1}))
    pl.when(here < end)(lambda: signal({"seq": here + 1}))
    ends = jnp.where(here > 0, 1, 0) + jnp.where(here < end, 1, 0)
    greet_seq(places, ({"tp": sibling}, {"tp": across}), ends)

    def shares(j):
        return (
            pl.ds(pl.multiple_of(j * in_rows, 8), in_rows),
            pl.ds(pl.multiple_of(j * out_rows, out_rows), out_rows),
        )

    def remote(src, dst, send, recv, device):
        return pltpu.make_async_remote_copy(
            src_ref=src,
            dst_ref=dst,
            send_sem=send,
            recv_sem=recv,
            device_id=device,
            device_id_type=pl.DeviceIdType.MESH,
        )

    def copies(source, target, j, kind, device):
        for i, at in enumerate(shares(j)):
            yield remote(
                source[i] if kind == 0 else source[i].at[at],
                target[i].at[at],
                sends.at[kind, i, j],
                recvs.at[0 if kind < 4 else 1, i, j],
                device,
            )

    share, far, sibfar = (share_in, share_out), (far_in, far_out), (sibfar_in, sibfar_out)

    def across_share():
        return copies(share, far, here, 0, {"tp": across})

    def to_right(j):
        return copies(far, far, j, 1, {"seq": here + 2})

    def to_left(j):
        return copies(far, far, j, 2, {"seq": here - 2})

    def to_side(j):
        return copies(far, far, j, 3, {"seq": here + 1 - 2 * side})

    def to_sibling(j):
        return copies(far, sibfar, j, 4, {"tp": sibling})

    def straight_rows(q):
        size = straight // STRAIGHT_COPIES
        first = w_in.shape[1] - straight + q * size
        return pl.ds(pl.multiple_of(first, 8), size)

    def straight_across(q):
        at = straight_rows(q)
        return remote(
            own_in.at[at], far_in.at[at], straight_sems.at[0, q], straight_sems.at[1, q],
            {"tp": across},
        )

    def straight_sibling(q):
        at = straight_rows(q)
        return remote(
            far_in.at[at], sibfar_in.at[at], straight_sems.at[2, q], straight_sems.at[3, q],
            {"tp": sibling},
        )

    def pass_straight(q):
        straight_across(q).wait_recv()
        straight_sibling(q).start()

    def start(group):
        for copy in group:
            copy.start()

    def arrived(group):
        for copy in group:
            copy.wait_recv()

    def left_source(group):
        for copy in group:
            copy.wait_send()

    def relay(incoming, j, on_right, on_left):
        onward = zip(incoming, to_right(j), to_left(j), to_side(j), to_sibling(j))
        for copy, right, left, aside, near in onward:
            copy.wait_recv()
            if on_right:
                pl.when(place < last)(right.start)
            if on_left:
                pl.when(place > 0)(left.start)
            aside.start()
            near.start()

    def single(i, src, dst, device):
        return remote(src, dst, once.at[0, i], once.at[1, i], device)

    in_at, out_at = shares(here)
    for g in range(3):
        share_in[:, g * chans : (g + 1) * chans] = w_in[g, in_at, :].astype(jnp.float32)
    share_out[...] = w_out[out_at, :].astype(jnp.float32)
    start(across_share())
    own_taps[...] = jnp.zeros_like(own_taps)
    own_taps[0:3, :] = taps[...]
    taps_far = single(0, own_taps, far_taps, {"tp": across})
    taps_sib = single(1, own_taps, sib_taps, {"tp": sibling})
    taps_sibfar = single(2, far_taps, sibfar_taps, {"tp": sibling})
    for g in range(3):
        own_in[:, g * chans : (g + 1) * chans] = w_in[g].astype(jnp.float32)
    own_out[...] = w_out[...].astype(jnp.float32)
    in_sib = single(3, own_in, sib_in, {"tp": sibling})
    out_sib = single(4, own_out, sib_out, {"tp": sibling})
    for copy in (taps_far, taps_sib, in_sib, out_sib):
        copy.start()
    for q in range(STRAIGHT_COPIES):
        straight_across(q).start()

    def gate_cols(g, index):
        return pl.ds(pl.multiple_of(g * width + index * chans, LANES), chans)

    def place_shard(shard_in, shard_out, shard_taps, index):
        for g in range(3):
            full_in[:, gate_cols(g, index)] = shard_in[:, g * chans : (g + 1) * chans].astype(low)
        at = pl.ds(pl.multiple_of(index * chans, chans), chans)
        full_out[at, :] = shard_out[...].astype(low)
        full_taps[:, gate_cols(0, index)] = shard_taps[...]

    def gate_out(turn, index, g):
        if g == 1:
            return pltpu.make_async_copy(
                out_gate.at[:, gate_cols(0, index)],
                proj_hbm.at[:, gate_cols(1, index)],
                gate_sems.at[turn, 1],
            )
        return pltpu.make_async_copy(
            gates.at[turn % 2, g // 2], proj_hbm.at[:, gate_cols(g, index)], gate_sems.at[turn, g]
        )

    def halo(turn, index, slot):
        return remote(
            gated.at[slot, pl.ds(slot_len, 8), gate_cols(0, index)],
            gated.at[slot, pl.ds(0, 8), gate_cols(0, index)],
            halo_sems.at[0, turn, slot],
            halo_sems.at[1, turn, slot],
            {"seq": here + 1},
        )

    order = (tp_at, sibling, across, far_sibling)

    def project(turn):
        index = order[turn]
        cols = gate_cols(0, index)
        if turn >= 2:
            gate_out(turn - 2, order[turn - 2], 0).wait()
            gate_out(turn - 2, order[turn - 2], 2).wait()

        @pl.loop(0, slots)
        def _(s):
            at = pl.ds(pl.multiple_of(s * slot_len, slot_len), slot_len)

            def gate(g):
                return jnp.dot(
                    normed[at, :], full_in[:, gate_cols(g, index)],
                    preferred_element_type=jnp.float32,
                )

            at_pos = lax.broadcasted_iota(jnp.int32, (slot_len, 1), 0) + here * slot_len
            mask = (at_pos < lengths[core * slots + s]).astype(jnp.float32)
            in_gate, value = gate(0), gate(2)
            gates[turn % 2, 0, at, :] = in_gate
            gates[turn % 2, 1, at, :] = value
            gated[s, pl.ds(8, slot_len), cols] = mask * in_gate * value
            out_gate[at, cols] = gate(1)

        for g in range(3):
            gate_out(turn, index, g).start()

        @pl.when(here < end)
        def _():
            for slot in range(slots):
                halo(turn, index, slot).start()

    def convolve(turn):
        index = order[turn]
        cols = gate_cols(0, index)

        @pl.when(here > 0)
        def _():
            for slot in range(slots):
                halo(turn, index, slot).wait_recv()

        @pl.loop(0, slots)
        def _(s):
            at = pl.ds(pl.multiple_of(s * slot_len, slot_len), slot_len)
            seen = [gated[s, pl.ds(6 + j, slot_len), cols] for j in range(3)]
            tap = [full_taps[j : j + 1, cols] for j in range(3)]
            conv_sum = tap[0] * seen[0] + tap[1] * seen[1] + tap[2] * seen[2]
            mixed[at, cols] = (out_gate[at, cols] * conv_sum).astype(low)

    @pl.when(here == 0)
    def _():
        for slot in range(slots):
            gated[slot, pl.ds(0, 8), :] = jnp.zeros((8, width), jnp.float32)

    load_tokens.wait()

    @pl.loop(0, rows // SUB_ROWS)
    def _(r):
        at = pl.ds(pl.multiple_of(r * SUB_ROWS, SUB_ROWS), SUB_ROWS)
        inputs = tokens[at, :].astype(jnp.float32)
        normed[at, :] = (gain_mix[...] * (inputs * rms_scale(inputs))).astype(low)

    keep_normed = pltpu.make_async_copy(normed, normed_hbm, keep_sems.at[0])
    keep_normed.start()
    place_shard(own_in, own_out, own_taps, tp_at)
    project(0)

    relay(across_share(), here, True, True)
    taps_far.wait_recv()
    taps_sibfar.start()
    in_sib.wait_recv()
    out_sib.wait_recv()
    taps_sib.wait_recv()
    place_shard(sib_in, sib_out, sib_taps, sibling)
    project(1)

    def from_side(q):
        j = 2 * q + 1 - side
        arrived(to_side(j))
        start(to_sibling(j))

    @pl.loop(1, places)
    def _(d):
        @pl.when(place - d >= 0)
        def _():
            j = here - 2 * d
            relay(to_right(j), j, True, False)

        @pl.when(place + d <= last)
        def _():
            j = here + 2 * d
            relay(to_left(j), j, False, True)

        @pl.when(d == 1)
        def _():
            from_side(place)
            convolve(0)
            convolve(1)

        pl.when(place - d >= 0)(lambda: from_side(place - d))
        pl.when(place + d <= last)(lambda: from_side(place + d))
        pl.when(d <= STRAIGHT_COPIES)(lambda: pass_straight(d - 1))

    for q in range(min(last, STRAIGHT_COPIES), STRAIGHT_COPIES):
        pass_straight(q)

    place_shard(far_in, far_out, far_taps, across)
    project(2)
    taps_sibfar.wait_recv()

    @pl.loop(0, 2 * places)
    def _(j):
        arrived(to_sibling(j))

    for q in range(STRAIGHT_COPIES):
        straight_sibling(q).wait_recv()
    place_shard(sibfar_in, sibfar_out, sibfar_taps, far_sibling)
    project(3)
    keep_in = pltpu.make_async_copy(full_in, in_hbm, keep_sems.at[1])
    keep_out = pltpu.make_async_copy(full_out, out_hbm, keep_sems.at[2])
    keep_in.start()
    keep_out.start()
    convolve(2)
    convolve(3)
    keep_gated = pltpu.make_async_copy(gated, gated_hbm, keep_sems.at[3])
    keep_mixed = pltpu.make_async_copy(mixed, mixed_hbm, keep_sems.at[4])
    keep_gated.start()
    keep_mixed.start()
    keep_normed.wait()

    blocks = rows // OUT_BLOCK

    def block_at(k, first=0):
        return pl.ds(pl.multiple_of(first + k * OUT_BLOCK, OUT_BLOCK), OUT_BLOCK)

    def unit_copy(k):
        return remote(
            unit_out.at[block_at(k)], unit_in.at[block_at(k)],
            unit_sems.at[0, k], unit_sems.at[1, k], {"tp": sibling},
        )

    def hidden_copy(k):
        return pltpu.make_async_copy(
            hidden.at[lax.rem(k, 2)], hidden_hbm.at[block_at(k)], mid_sems.at[0, lax.rem(k, 2)]
        )

    def mid_copy(half, held, whose, k):
        return pltpu.make_async_copy(
            held.at[block_at(k)], mid_hbm.at[block_at(k, whose * rows)], mid_sems.at[half, k]
        )

    @pl.loop(0, blocks)
    def _(k):
        slot = lax.rem(k, 2)
        at = block_at(k)
        pl.when(k >= 2)(lambda: hidden_copy(k - 2).wait())
        hidden[slot] = jnp.dot(mixed[at, :], full_out[...], preferred_element_type=jnp.float32)

        @pl.loop(0, OUT_BLOCK // SUB_ROWS)
        def _(r):
            sub = pl.ds(pl.multiple_of(r * SUB_ROWS, SUB_ROWS), SUB_ROWS)
            whole = pl.ds(pl.multiple_of(k * OUT_BLOCK + r * SUB_ROWS, SUB_ROWS), SUB_ROWS)
            hidden_rows = tokens[whole, :].astype(jnp.float32) + hidden[slot, sub, :]
            hidden[slot, sub, :] = hidden_rows
            unit = hidden_rows * rms_scale(hidden_rows)
            unit_out[whole, :] = unit
            normed[whole, :] = (gain_ffn[...] * unit).astype(low)

        unit_copy(k).start()
        hidden_copy(k).start()
        mid_copy(1, normed, core, k).start()

    keep_mixed.wait()

    @pl.loop(0, blocks)
    def _(k):
        unit_copy(k).wait_recv()

        @pl.loop(0, OUT_BLOCK // SUB_ROWS)
        def _(r):
            whole = pl.ds(pl.multiple_of(k * OUT_BLOCK + r * SUB_ROWS, SUB_ROWS), SUB_ROWS)
            mixed[whole, :] = (gain_ffn[...] * unit_in[whole, :]).astype(low)

        mid_copy(2, mixed, 1 - core, k).start()

    @pl.loop(0, blocks)
    def _(k):
        unit_copy(k).wait_send()
        mid_copy(1, normed, core, k).wait()
        mid_copy(2, mixed, 1 - core, k).wait()

    for k in range(max(blocks - 2, 0), blocks):
        hidden_copy(k).wait()
    keep_in.wait()
    keep_out.wait()
    keep_gated.wait()
    for turn in range(4):
        for g in range(3):
            if turn >= 2 or g == 1:
                gate_out(turn, order[turn], g).wait()

    @pl.when(here < end)
    def _():
        for turn in range(4):
            for slot in range(slots):
                halo(turn, order[turn], slot).wait_send()

    left_source(across_share())
    for q in range(STRAIGHT_COPIES):
        straight_across(q).wait_send()
        straight_sibling(q).wait_send()
    for copy in (taps_far, taps_sib, taps_sibfar, in_sib, out_sib):
        copy.wait_send()

    @pl.loop(0, places)
    def _(q):
        j = 2 * q + side
        left_source(to_side(j))
        pl.when((q <= place) & (place < last))(lambda: left_source(to_right(j)))
        pl.when((q >= place) & (place > 0))(lambda: left_source(to_left(j)))
        left_source(to_sibling(j))
        left_source(to_sibling(2 * q + 1 - side))


def mixer_front(w_in, w_out, taps, gain_mix, gain_ffn, lengths, tokens, slots, collective_id):
    width, _, chans = w_in.shape
    rows = tokens.shape[0] // 2
    count = lax.axis_size("seq")
    group = lax.axis_size("tp")
    f32, low = jnp.float32, jnp.bfloat16
    blocks = rows // OUT_BLOCK
    pair = [pltpu.VMEM((width, 3 * chans), f32), pltpu.VMEM((chans, width), f32)]
    whole = pl.BlockSpec(memory_space=pltpu.VMEM)
    anywhere = pl.BlockSpec(memory_space=pl.ANY)
    padded = (slots, rows // slots + 8, width)
    return pl.pallas_call(
        functools.partial(front_kernel, count // 2, slots),
        out_shape=[
            jax.ShapeDtypeStruct((width, 3 * chans * group), low),
            jax.ShapeDtypeStruct((chans * group, width), low),
            jax.ShapeDtypeStruct((8, chans * group), f32),
            jax.ShapeDtypeStruct((2 * rows, width), low),
            jax.ShapeDtypeStruct((rows, width), f32),
            jax.ShapeDtypeStruct((rows, 3 * width), f32),
            jax.ShapeDtypeStruct(padded, f32),
            jax.ShapeDtypeStruct((rows, width), low),
            jax.ShapeDtypeStruct((rows, width), low),
        ],
        in_specs=[whole] * 5 + [pl.BlockSpec(memory_space=pltpu.SMEM), anywhere],
        out_specs=[anywhere] * 2 + [whole] + [anywhere] * 6,
        scratch_shapes=pair * 4
        + [pltpu.VMEM((8, chans), f32)] * 4
        + [
            pltpu.VMEM((width * 8 // 16 // count // 8 * 8, 3 * chans), f32),
            pltpu.VMEM((chans // count, width), f32),
            pltpu.VMEM((width, 3 * chans * group), low),
            pltpu.VMEM((chans * group, width), low),
            pltpu.VMEM((rows, width), low),
            pltpu.VMEM((rows, width), low),
            pltpu.VMEM((rows, width), low),
            pltpu.VMEM((rows, width), f32),
            pltpu.VMEM((2, 2, rows, chans), f32),
            pltpu.VMEM(padded, f32),
            pltpu.VMEM((rows, width), f32),
            pltpu.VMEM((rows, width), f32),
            pltpu.VMEM((2, OUT_BLOCK, width), f32),
            pltpu.SemaphoreType.DMA((5, 2, count)),
            pltpu.SemaphoreType.DMA((2, 2, count)),
            pltpu.SemaphoreType.DMA((2, 5)),
            pltpu.SemaphoreType.DMA((2, 4, slots)),
            pltpu.SemaphoreType.DMA((4, 3)),
            pltpu.SemaphoreType.DMA((2, blocks)),
            pltpu.SemaphoreType.DMA((5,)),
            pltpu.SemaphoreType.DMA((3, blocks)),
            pltpu.SemaphoreType.DMA((4, STRAIGHT_COPIES)),
        ],
        compiler_params=pltpu.CompilerParams(
            collective_id=collective_id, has_side_effects=True, vmem_limit_bytes=VMEM_LIMIT
        ),
        name="mixer_front",
    )(
        w_in.transpose(1, 0, 2),
        w_out,
        taps,
        gain_mix,
        gain_ffn,
        lengths,
        tokens,
    )


def finish_kernel(slots, chans, hidden, *refs):
    (sums, tokens_in, block_in, lengths) = refs[0:4]
    (block_out, tokens_out, gain_a, gain_b, g_in, g_conv, g_out, g_gate, g_up, g_down) = refs[4:14]
    (held, tokens, block, rounded, turned, gains) = refs[14:20]
    (in_sems, block_sems, turn_sems, out_sems) = refs[20:24]
    rows, width = block_in.shape
    slot_len = rows // slots
    here = lax.axis_index("seq")
    tp_at = lax.axis_index("tp")
    first = 3 * hidden
    out_first = first + 3 * chans
    small_first = out_first + chans
    blocks = rows // OUT_BLOCK
    turns = hidden // LANES
    half_rows = rows // 2

    def cols(start, size):
        return (slice(None), slice(start, start + size))

    parts = [cols(i * hidden, hidden) for i in range(3)] + [cols(first, held.shape[1] - first)]
    halves = [slice(0, half_rows), slice(half_rows, rows)]
    part_loads = [
        pltpu.make_async_copy(sums.at[at], held.at[at], in_sems.at[i]) for i, at in enumerate(parts)
    ]
    token_loads = [
        pltpu.make_async_copy(tokens_in.at[at], tokens.at[at], in_sems.at[4 + i])
        for i, at in enumerate(halves)
    ]

    def block_at(k):
        return pl.ds(pl.multiple_of(k * OUT_BLOCK, OUT_BLOCK), OUT_BLOCK)

    def block_load(k):
        return pltpu.make_async_copy(
            block_in.at[block_at(k)], block.at[block_at(k)], block_sems.at[0, k]
        )

    def block_store(k):
        return pltpu.make_async_copy(
            rounded.at[block_at(k)], block_out.at[block_at(k)], block_sems.at[1, k]
        )

    def panel_at(k):
        return pl.ds(pl.multiple_of(k * LANES, LANES), LANES)

    def turn_store(k):
        at = panel_at(k)
        return pltpu.make_async_copy(turned.at[at], g_down.at[at], turn_sems.at[k])

    stores = []

    def store(src, dst):
        copy = pltpu.make_async_copy(src, dst, out_sems.at[len(stores)])
        copy.start()
        stores.append(copy)

    part_loads[2].start()

    @pl.loop(0, blocks)
    def _(k):
        block_load(k).start()

    for load in (*token_loads, part_loads[0], part_loads[1], part_loads[3]):
        load.start()

    part_loads[2].wait()

    @pl.loop(0, turns)
    def _(k):
        from_cols = pl.ds(pl.multiple_of(2 * hidden + k * LANES, LANES), LANES)
        turned[panel_at(k), :] = held[:, from_cols].T
        turn_store(k).start()

    @pl.loop(0, blocks)
    def _(k):
        block_load(k).wait()
        per_slot = slot_len // OUT_BLOCK
        at = lax.broadcasted_iota(jnp.int32, (OUT_BLOCK, 1), 0)
        at = at + (here * slot_len + lax.rem(k, per_slot) * OUT_BLOCK)
        mask = (at < lengths[k // per_slot]).astype(jnp.float32)
        rounded[block_at(k), :] = (mask * block[block_at(k), :]).astype(jnp.bfloat16)
        block_store(k).start()

    for load, at in zip(token_loads, halves):
        load.wait()
        store(tokens.at[at], tokens_out.at[at])
    for i, target in ((0, g_gate), (1, g_up)):
        part_loads[i].wait()
        store(held.at[parts[i]], target)
    part_loads[3].wait()
    for g in range(3):
        store(held.at[cols(first + g * chans, chans)], g_in.at[g])
    per_col = width // chans
    for p in range(width // LANES):
        q, r = p // per_col, p % per_col
        at = (slice(r * chans, (r + 1) * chans), slice(out_first + q * LANES, out_first + (q + 1) * LANES))
        store(held.at[at], g_out.at[cols(p * LANES, LANES)])
        gains[cols(p * LANES, LANES)] = held[8 * p : 8 * p + 8, small_first:]
    own = pl.ds(pl.multiple_of(tp_at * chans, LANES), chans)
    g_conv[...] = gains[2:5, own]
    gain_a[...] = gains[0:1, :]
    gain_b[...] = gains[1:2, :]
    for copy in stores:
        copy.wait()

    @pl.loop(0, turns)
    def _(k):
        turn_store(k).wait()

    @pl.loop(0, blocks)
    def _(k):
        block_store(k).wait()


def finish(sums, tokens_grad, block_sum, lengths, chans, hidden):
    rows, width = block_sum.shape
    f32 = jnp.float32
    anywhere = pl.BlockSpec(memory_space=pl.ANY)
    whole = pl.BlockSpec(memory_space=pltpu.VMEM)
    blocks = rows // OUT_BLOCK
    return pl.pallas_call(
        functools.partial(finish_kernel, lengths.shape[0], chans, hidden),
        out_shape=[
            jax.ShapeDtypeStruct((rows, width), jnp.bfloat16),
            jax.ShapeDtypeStruct((rows, width), f32),
            jax.ShapeDtypeStruct((1, width), f32),
            jax.ShapeDtypeStruct((1, width), f32),
            jax.ShapeDtypeStruct((3, width, chans), f32),
            jax.ShapeDtypeStruct((3, chans), f32),
            jax.ShapeDtypeStruct((chans, width), f32),
            jax.ShapeDtypeStruct((width, hidden), f32),
            jax.ShapeDtypeStruct((width, hidden), f32),
            jax.ShapeDtypeStruct((hidden, width), f32),
        ],
        in_specs=[anywhere] * 3 + [pl.BlockSpec(memory_space=pltpu.SMEM)],
        out_specs=[anywhere] * 2 + [whole, whole, anywhere, whole] + [anywhere] * 4,
        scratch_shapes=[
            pltpu.VMEM(sums.shape, f32),
            pltpu.VMEM((rows, width), f32),
            pltpu.VMEM((rows, width), f32),
            pltpu.VMEM((rows, width), jnp.bfloat16),
            pltpu.VMEM((hidden, width), f32),
            pltpu.VMEM((8, width), f32),
            pltpu.SemaphoreType.DMA((6,)),
            pltpu.SemaphoreType.DMA((2, blocks)),
            pltpu.SemaphoreType.DMA((hidden // LANES,)),
            pltpu.SemaphoreType.DMA((7 + width // LANES,)),
        ],
        compiler_params=pltpu.CompilerParams(vmem_limit_bytes=VMEM_LIMIT),
        name="finish",
    )(sums, tokens_grad, block_sum, lengths)


def per_device(
    tokens, lengths, gain_mix, w_in, conv_weight, w_out, gain_ffn, w_gate, w_up, w_down, cotangent
):
    slot_count, local_len, width = tokens.shape
    chans = w_in.shape[2]
    half_slots = slot_count // 2
    row_count = slot_count * local_len

    token_rows = tokens.reshape(row_count, width)
    cot_rows = cotangent.reshape(row_count, width)
    gains = gain_mix.reshape(1, width), gain_ffn.reshape(1, width)
    w_in_all, w_out_all, taps, normed_mid, hidden_res, projected, gated_rows, normed_in, mixed = (
        mixer_front(w_in, w_out, conv_weight, *gains, lengths, token_rows, half_slots, 3)
    )
    mixer_cols = 4 * chans
    sum_cols = FFN_PANELS * LANES + mixer_cols + LANES
    sums, grad_tokens, block_sum = back_both(
        (
            normed_mid,
            cot_rows,
            w_gate,
            w_up,
            w_down,
            hidden_res,
            projected,
            gated_rows,
            normed_in,
            mixed,
            w_in_all,
            w_out_all,
            token_rows,
        ),
        (lengths, taps, *gains),
        half_slots,
        sum_cols,
        1,
    )[:3]
    block_out, grad_tokens, g_gain_mix, g_gain_ffn, g_in, g_conv, g_out, g_gate, g_up, g_down = finish(
        sums, grad_tokens, block_sum, lengths, chans, w_gate.shape[1]
    )
    return (
        block_out.reshape(slot_count, local_len, width),
        grad_tokens.reshape(slot_count, local_len, width),
        g_gain_mix.reshape(width),
        g_in.transpose(1, 0, 2),
        g_conv,
        g_out,
        g_gain_ffn.reshape(width),
        g_gate,
        g_up,
        g_down,
    )


def solution(mesh):
    rows, cols = P("tp", None), P(None, "tp")
    tokens, whole, stacked = P(None, "seq", None), P(), P(None, None, "tp")
    return jax.shard_map(
        per_device,
        mesh=mesh,
        in_specs=(
            tokens, whole, whole, stacked, cols, rows, whole, cols, cols, rows, tokens,
        ),
        out_specs=(
            tokens, tokens, whole, stacked, cols, rows, whole, cols, cols, rows,
        ),
        check_vma=False,
    )
```
